32 devices in a mesh: dp: 2 (over core), fsdp: 16 (over z, y, x).
Axes of the slice: x: 2, y: 2, z: 4, core: 2. Of those that a mesh axis runs over, the one named last changes fastest.
Arguments:
- tokens: bfloat16 [65536, 768], P(('dp', 'fsdp')), may hold values from -6 to 6
- sensor_tag: int32 [64], P(('dp', 'fsdp')), may hold values from 0 to 1
- owner_order: int32 [32, 2048], P(('dp', 'fsdp')), may hold values from 0 to 2047, each once within a row
- ln1_gain: bfloat16 [768], P('fsdp'), may hold values from 0.25 to 1.75
- ln1_bias: bfloat16 [768], P('fsdp'), may hold values from -3 to 3
- w_qkv: bfloat16 [768, 2304], P('fsdp'), may hold values from -0.21875 to 0.21875
- b_query: bfloat16 [768], P('fsdp'), may hold values from -4 to 4
- b_value: bfloat16 [768], P('fsdp'), may hold values from -4 to 4
- w_out: bfloat16 [768, 768], P('fsdp'), may hold values from -0.625 to 0.625
- b_out: bfloat16 [768], P('fsdp'), may hold values from -3 to 3
- ln2_gain: bfloat16 [768], P('fsdp'), may hold values from 0.25 to 1.75
- ln2_bias: bfloat16 [768], P('fsdp'), may hold values from -3 to 3
- w_up: bfloat16 [768, 3072], P('fsdp'), may hold values from -0.21875 to 0.21875
- b_up: bfloat16 [3072], P('fsdp'), may hold values from -4 to 4
- w_down: bfloat16 [3072, 768], P('fsdp'), may hold values from -0.109375 to 0.109375
- b_down: bfloat16 [768], P('fsdp'), may hold values from -3 to 3
- out_grad: float32 [65536, 768], P(('dp', 'fsdp')), may hold values from -6 to 6
Outputs:
- encoded: float32 [65536, 768], P(('dp', 'fsdp'))
- tokens_grad: float32 [65536, 768], P(('dp', 'fsdp'))
- grad_ln1_gain: float32 [768], P('fsdp')
- grad_ln1_bias: float32 [768], P('fsdp')
- grad_w_qkv: float32 [768, 2304], P('fsdp')
- grad_b_query: float32 [768], P('fsdp')
- grad_b_value: float32 [768], P('fsdp')
- grad_w_out: float32 [768, 768], P('fsdp')
- grad_b_out: float32 [768], P('fsdp')
- grad_ln2_gain: float32 [768], P('fsdp')
- grad_ln2_bias: float32 [768], P('fsdp')
- grad_w_up: float32 [768, 3072], P('fsdp')
- grad_b_up: float32 [3072], P('fsdp')
- grad_w_down: float32 [3072, 768], P('fsdp')
- grad_b_down: float32 [768], P('fsdp')
The draws below stay inside these ranges and needn't reach their ends.
Inputs may be any that keep to these rules, and one draw needn't show every extreme that they name: `sensor_tag`: 0 marks a row holding one chip of 1024 tokens, 1 a row of four chips of 256 tokens. `owner_order`: each row is a permutation of 0 to 2047.
All inputs are finite; a program needn't handle non-finite values.
Results may differ from the reference program's by a relative error of at most 0.025.
Values may be sent and summed in bfloat16 or wider, within the bound.
No kernel may reach another device: no remote copies, remote signals or barrier semaphores. Data moves between devices by JAX's collectives and lax.ppermute only.
A program may use at most 320 MiB of HBM per device.

```python
import math
import jax
import jax.numpy as jnp
from jax import lax

D = 768
HEADS = 12
HEAD_DIM = 64
FF = 3072
ROW_LEN = 1024
TOK_DEV = 2048
ROWS = 64
TOKENS = 65536
N_DP = 2
N_FSDP = 16


def touch_ends(array, rng, smallest, top_value):
    shape = array.shape
    index_at = [jax.random.randint(jax.random.fold_in(rng, axis), (), 0, shape[axis]) for axis in range(len(shape))]
    array = array.at[tuple(index_at)].set(smallest)
    longest = shape.index(max(shape))
    index_at[longest] = (index_at[longest] + 1) % shape[longest]
    return array.at[tuple(index_at)].set(top_value)


def shard_levels(key, shape, shards, smallest, high):
    def one(position, blocks):
        heights = jax.random.uniform(jax.random.fold_in(jax.random.fold_in(key, 6), position), (blocks,), jnp.float32, smallest / len(shards), high / len(shards))
        return jnp.repeat(jnp.exp(heights), shape[position] // blocks).reshape((-1,) + (1,) * (len(shape) - position - 1))

    gain = one(*shards[0])
    for cut in shards[1:]:
        gain = gain * one(*cut)
    return gain


def gaussian(own_key, dims, width, bound, split=(), held_as=jnp.bfloat16):
    gain = shard_levels(own_key, dims, split, -0.22, 0.18) if split else 1.0
    drawn = jax.random.normal(own_key, dims, jnp.float32) * width * gain
    return jnp.minimum(jnp.maximum(drawn, -bound), bound).astype(held_as)


def setup_inputs(seed: int = 0) -> dict:
    seeds = jax.random.split(jax.random.key(seed), 18)
    return {
        "tokens": gaussian(seeds[0], (TOKENS, D), 1.0, 6.0, ((0, 32),)),
        "sensor_tag": touch_ends(jax.random.randint(seeds[1], (ROWS,), 0, 2), jax.random.fold_in(seeds[1], 1), 0, 1).astype(jnp.int32),
        "owner_order": jax.vmap(lambda own: jax.random.permutation(own, TOK_DEV))(jax.random.split(seeds[2], (N_DP * N_FSDP))).reshape((N_DP * N_FSDP, TOK_DEV)).astype(jnp.int32),
        "ln1_gain": jnp.clip(1.0 + 0.15 * jax.random.normal(seeds[3], (D,), jnp.float32), 0.25, 1.75).astype(jnp.bfloat16),
        "ln1_bias": gaussian(seeds[4], (D,), 0.3, 3.0, ((0, 16),)),
        "w_qkv": gaussian(seeds[5], (D, 3 * D), D ** -0.5, 0.21875, ((0, 16),)),
        "b_query": gaussian(seeds[6], (D,), 0.5, 4.0, ((0, 16),)),
        "b_value": gaussian(seeds[7], (D,), 0.5, 4.0, ((0, 16),)),
        "w_out": gaussian(seeds[8], (D, D), (D // 8) ** -0.5, 0.625, ((0, 16),)),
        "b_out": gaussian(seeds[9], (D,), 0.3, 3.0, ((0, 16),)),
        "ln2_gain": jnp.clip(1.0 + 0.15 * jax.random.normal(seeds[10], (D,), jnp.float32), 0.25, 1.75).astype(jnp.bfloat16),
        "ln2_bias": gaussian(seeds[11], (D,), 0.3, 3.0, ((0, 16),)),
        "w_up": gaussian(seeds[12], (D, FF), D ** -0.5, 0.21875, ((0, 16),)),
        "b_up": gaussian(seeds[13], (FF,), 0.5, 4.0, ((0, 16),)),
        "w_down": gaussian(seeds[14], (FF, D), FF ** -0.5, 0.109375, ((0, 16),)),
        "b_down": gaussian(seeds[15], (D,), 0.3, 3.0, ((0, 16),)),
        "out_grad": gaussian(seeds[16], (TOKENS, D), 1.0, 6.0, ((0, 32),), jnp.float32),
    }


@jax.custom_vjp
def low(v):
    return lax.optimization_barrier(v.astype(jnp.bfloat16)).astype(jnp.float32)

@jax.custom_vjp
def low_back(v):
    return v

def low_keep(v):
    return (low(v), None)

def low_pass(kept, grad):
    return (grad,)

def back_keep(v):
    return (v, None)

def back_low(kept, grad):
    return (low(grad),)
low.defvjp(low_keep, low_pass)
low_back.defvjp(back_keep, back_low)
highest = lax.Precision.HIGHEST
norm_eps = 1e-06
masked_score = -1e+30

def norm_rows(values, gain_vec, shift_vec):
    center = values - lax.optimization_barrier(jnp.mean(values, axis=-1, keepdims=True))
    spread = lax.optimization_barrier(jnp.mean(center * center, axis=-1, keepdims=True))
    return center * lax.rsqrt(spread + norm_eps) * gain_vec + shift_vec

def chip_mask(tag_rows, length):
    chip_len = jnp.where(tag_rows == 0, length, length // 4).astype(jnp.int32)
    places = jnp.arange(length, dtype=jnp.int32)
    return places[None, :, None] // chip_len[:, None, None] == places[None, None, :] // chip_len[:, None, None]

def layer_rows(params, stream, tag_rows):
    gain_one, shift_one, w_qkv, b_query, b_value, w_out, b_out, gain_two, shift_two, w_up, b_up, w_down, b_down = params
    row_count, length, model_width = stream.shape
    score_scale = HEAD_DIM ** (-0.5)
    normed = low(norm_rows(stream, gain_one, shift_one))
    joined = jnp.einsum('rld,de->rle', normed, w_qkv, precision=highest)
    queries = low_back(low((joined[..., :model_width] + b_query) * score_scale))
    key_rows = low_back(low(joined[..., model_width:2 * model_width]))
    value_rows = low_back(low(joined[..., 2 * model_width:] + b_value))
    shape_four = (row_count, length, HEADS, HEAD_DIM)
    scores = jnp.einsum('rqhe,rkhe->rhqk', queries.reshape(shape_four), key_rows.reshape(shape_four), precision=highest)
    scores = low_back(scores)
    scores = jnp.where(chip_mask(tag_rows, length)[:, None], scores, masked_score)
    row_peak = lax.optimization_barrier(jnp.max(scores, axis=-1, keepdims=True))
    weights = jnp.exp(scores - row_peak)
    soft_weights = low(weights / lax.optimization_barrier(jnp.sum(weights, axis=-1, keepdims=True)))
    mixed_heads = jnp.einsum('rhqk,rkhe->rqhe', soft_weights, value_rows.reshape(shape_four), precision=highest)
    mixed_heads = low_back(low(mixed_heads.reshape(row_count, length, model_width)))
    branch = low_back(jnp.einsum('rld,de->rle', mixed_heads, w_out, precision=highest) + b_out)
    middle = stream + branch
    normed_two = low(norm_rows(middle, gain_two, shift_two))
    hidden = low_back(jnp.einsum('rld,df->rlf', normed_two, w_up, precision=highest) + b_up)
    active = low(jax.nn.gelu(hidden, approximate=False))
    output = low_back(jnp.einsum('rlf,fd->rld', active, w_down, precision=highest) + b_down)
    return middle + output

def forward(stream_all, params, sensor_tag, owner_order):
    group_rows = math.gcd(ROWS, max(1, 4096 // ROW_LEN))
    blocks = stream_all.reshape(ROWS // group_rows, group_rows, ROW_LEN, D)
    tag_blocks = sensor_tag.reshape(ROWS // group_rows, group_rows)
    block_fn = jax.checkpoint(lambda rows_in, tags_in: layer_rows(params, rows_in, tags_in))

    def advance(carried, pair_in):
        return (carried, block_fn(pair_in[0], pair_in[1]))
    _, outputs = lax.scan(advance, None, (blocks, tag_blocks))
    devices = N_DP * N_FSDP
    share_rows = TOK_DEV // N_FSDP
    per_device = outputs.reshape(devices, TOK_DEV, D)
    picked = jnp.take_along_axis(per_device, owner_order[:, :, None], axis=1)
    picked = picked.reshape(N_DP, N_FSDP, N_FSDP, share_rows, D)
    return jnp.swapaxes(picked, 1, 2).reshape(TOKENS, D)

def reference(tokens, sensor_tag, owner_order, ln1_gain, ln1_bias, w_qkv, b_query, b_value, w_out, b_out, ln2_gain, ln2_bias, w_up, b_up, w_down, b_down, out_grad):
    params = tuple((member.astype(jnp.float32) for member in (ln1_gain, ln1_bias, w_qkv, b_query, b_value, w_out, b_out, ln2_gain, ln2_bias, w_up, b_up, w_down, b_down)))
    stream = tokens.astype(jnp.float32)
    encoded, pull_back = jax.vjp(lambda stream_in, params_in: forward(stream_in, params_in, sensor_tag, owner_order), stream, params)
    stream_grad, param_grads = pull_back(out_grad.astype(jnp.float32))
    return (encoded, stream_grad, param_grads[0], param_grads[1], param_grads[2], param_grads[3], param_grads[4], param_grads[5], param_grads[6], param_grads[7], param_grads[8], param_grads[9], param_grads[10], param_grads[11], param_grads[12])
```

```python
import functools
import math

import jax
import jax.numpy as jnp
from jax import lax
from jax.experimental import pallas as pl
from jax.experimental.pallas import tpu as pltpu
from jax.sharding import PartitionSpec as P

F32 = jnp.float32
BF = jnp.bfloat16
EPS = 1e-6
LOG2E = math.log2(math.e)
LN2 = math.log(2.0)
NT = (((1,), (1,)), ((), ()))
TN = (((0,), (0,)), ((), ()))
NN = (((1,), (0,)), ((), ()))
ANY = pl.BlockSpec(memory_space=pl.ANY)
VECS = 16
SDS = jax.ShapeDtypeStruct


def dg(a, b, dims):
    return lax.dot_general(a, b, dims, preferred_element_type=F32)


def params(axes=1):
    return pltpu.CompilerParams(
        vmem_limit_bytes=58 * 2**20, dimension_semantics=("arbitrary",) * axes
    )


def cost(flops, nbytes, trans=0):
    return pl.CostEstimate(flops=int(flops), bytes_accessed=int(nbytes), transcendentals=int(trans))


def rows_of(height, width):
    return pl.BlockSpec((height, width), lambda i, *_: (i, 0))


def whole(shape):
    zeros = (0,) * len(shape)
    return pl.BlockSpec(shape, lambda *_: zeros, pipeline_mode=pl.Buffered(1))


def fixed(shape):
    zeros = (0,) * len(shape)
    return pl.BlockSpec(shape, lambda *_: zeros)


def norm_stats(x):
    n = x.shape[-1]
    c = x - jnp.sum(x, axis=-1, keepdims=True) * (1.0 / n)
    var = jnp.sum(c * c, axis=-1, keepdims=True) * (1.0 / n)
    return c, lax.rsqrt(var + EPS)


def xor_pp(x, b, n):
    return lax.ppermute(x, "fsdp", [(i, i ^ b) for i in range(n)])


def core_swap(x, m):
    return lax.ppermute(x, "dp", [(i, i ^ 1) for i in range(m)])


def gather_near(x, n):
    q = n // 4
    return jnp.stack([x] + [xor_pp(x, d * q, n) for d in (1, 2, 3)])


def gather_far(s, n, m):
    own = [s] + [xor_pp(s, e, n) for e in range(1, n // 4)]
    return own + [core_swap(t, m) for t in own]


def settle(pieces, f, c, n, rep=1):
    q = n // 4
    rows = pieces[0].shape[1]
    if rows % 16 == 0 and q == 4:
        return pieces
    order = f ^ jnp.arange(n)
    halves = []
    for side in (pieces[:q], pieces[q:]):
        rel = jnp.stack(side, axis=1).reshape((n,) + side[0].shape[1:])
        halves.append(jnp.take(rel, order, axis=0))
    left = jnp.where(c == 0, halves[0], halves[1])
    right = jnp.where(c == 0, halves[1], halves[0])
    out = []
    for side in (left, right):
        four = side.reshape(4, 4, n * rows // 16, side.shape[-1])
        out += [four[:, e] for e in range(4)]
    return out


def load_pieces(idx_ref, pieces, dst, sem, width):
    f = idx_ref[0]
    c = idx_ref[1]
    rows = pieces[0].shape[1]
    started = []
    for e in range(4):
        for d in range(4):
            s = lax.bitwise_xor(f, jnp.int32(d * 4 + e))
            at = pl.ds(pl.multiple_of(s * rows, 16), rows)
            for h, src in ((c, pieces[e]), (1 - c, pieces[4 + e])):
                cols = pl.ds(pl.multiple_of(h * width, 128), width)
                cp = pltpu.make_async_copy(src.at[d, :, pl.ds(0, width)], dst.at[at, cols], sem)
                cp.start()
                started.append(cp)
    return started


def load_vecs(idx_ref, pieces, dst, sem, width):
    f = idx_ref[0]
    rows = pieces[0].shape[1]
    started = []
    for e in range(4):
        for d in range(4):
            s = lax.bitwise_xor(f, jnp.int32(d * 4 + e))
            at = pl.ds(pl.multiple_of(s * rows, 16), rows)
            cp = pltpu.make_async_copy(pieces[e].at[d, :, pl.ds(width, 128)], dst.at[at, :], sem)
            cp.start()
            started.append(cp)
    return started


def qkv_kernel(idx_ref, x_ref, *refs):
    pieces = refs[:8]
    q_ref, k_ref, v_ref, vt_ref, w_ref, vec_ref, sem = refs[8:]
    d = x_ref.shape[1]

    @pl.when(pl.program_id(0) == 0)
    def _():
        going = load_pieces(idx_ref, pieces, w_ref, sem.at[0], 3 * d // 2)
        vecs = load_vecs(idx_ref, pieces, vec_ref, sem.at[1], 3 * d // 2)
        for cp in vecs:
            cp.wait()
        vt_ref[...] = vec_ref[...].astype(F32).T[:VECS]
        for cp in going:
            cp.wait()

    c, r = norm_stats(x_ref[...].astype(F32))
    h = (c * r * vt_ref[0:1, :] + vt_ref[1:2, :]).astype(BF)
    q = dg(h, w_ref[:, :d], NN)
    q_ref[...] = ((q + vt_ref[2:3, :]) * (0.125 * LOG2E)).astype(BF)
    k_ref[...] = dg(h, w_ref[:, d : 2 * d], NN).astype(BF)
    v_ref[...] = (dg(h, w_ref[:, 2 * d :], NN) + vt_ref[3:4, :]).astype(BF)


def qkv(idx, x, pieces, tb=512):
    t, d = x.shape
    return pl.pallas_call(
        qkv_kernel,
        grid_spec=pltpu.PrefetchScalarGridSpec(
            num_scalar_prefetch=1,
            grid=(t // tb,),
            in_specs=[rows_of(tb, d)] + [ANY] * 8,
            out_specs=[rows_of(tb, d)] * 3 + [fixed((VECS, d))],
            scratch_shapes=[
                pltpu.VMEM((d, 3 * d), BF),
                pltpu.VMEM((d, 128), BF),
                pltpu.SemaphoreType.DMA((2,)),
            ],
        ),
        out_shape=[SDS((t, d), BF)] * 3 + [SDS((VECS, d), F32)],
        compiler_params=params(),
        cost_estimate=cost(6 * t * d * d, t * d * 8 + d * d * 6),
        name="qkv",
    )(idx, x, *pieces)


def attend_kernel(tag_ref, q_ref, k_ref, v_ref, o_ref, l_ref, *, qb):
    r = pl.program_id(0)
    length = q_ref.shape[0]
    low = lax.broadcasted_iota(jnp.int32, (1, 128), 1) < 64

    def block(qs, qn, ks, kn):
        q = q_ref[pl.ds(qs, qn), :]
        k = k_ref[pl.ds(ks, kn), :]
        v = v_ref[pl.ds(ks, kn), :]
        outs = []
        for h in range(2):
            sel = low if h == 0 else jnp.logical_not(low)
            qm = jnp.where(sel, q, jnp.asarray(0, BF))
            vm = jnp.where(sel, v, jnp.asarray(1, BF))
            s = dg(qm, k, NT)
            m = jnp.max(s, axis=1, keepdims=True)
            outs.append((dg(jnp.exp2(s - m).astype(BF), vm, NN), m))
        (a, ma), (b, mb) = outs
        acc = jnp.where(low, a, b)
        total = pltpu.roll(jnp.where(low, b, a), 64, 1)
        o_ref[pl.ds(qs, qn), :] = (acc / total).astype(o_ref.dtype)
        lse = (jnp.where(low, ma, mb) + jnp.log2(total)).T
        l_ref[0, 0, 0:1, pl.ds(qs, qn)] = lse[0:1]
        l_ref[0, 0, 1:2, pl.ds(qs, qn)] = lse[64:65]

    @pl.when(tag_ref[r] == 0)
    def _():
        for i in range(length // qb):
            block(i * qb, qb, 0, length)

    @pl.when(tag_ref[r] != 0)
    def _():
        c = length // 4
        for i in range(4):
            block(i * c, c, i * c, c)


def attend(tag, q, k, v, qb=512):
    t, d = q.shape
    rows = tag.shape[0]
    length = t // rows
    pairs = d // 128
    blk = pl.BlockSpec((length, 128), lambda r, p, _: (r, p))
    lse = pl.BlockSpec((1, 1, 2, length), lambda r, p, _: (r, p, 0, 0))
    return pl.pallas_call(
        functools.partial(attend_kernel, qb=qb),
        grid_spec=pltpu.PrefetchScalarGridSpec(
            num_scalar_prefetch=1, grid=(rows, pairs), in_specs=[blk] * 3, out_specs=[blk, lse]
        ),
        out_shape=[SDS((t, d), BF), SDS((rows, pairs, 2, length), F32)],
        compiler_params=params(2),
        cost_estimate=cost(16 * t * length * d, t * d * 8, t * length * 12),
        name="attend",
    )(tag, q, k, v)


def gelu_both(u):
    t = 1.0 + jnp.abs(u) * (0.3275911 / math.sqrt(2.0))
    r = pl.reciprocal(t, approx=True)
    r = r * (2.0 - t * r)
    e = jnp.exp2(u * u * (-0.5 * LOG2E))
    p = -0.5 * 1.453152027 + r * (0.5 * 1.061405429)
    p = 0.5 * 1.421413741 + r * p
    p = -0.5 * 0.284496736 + r * p
    p = 0.5 * 0.254829592 + r * p
    tail = r * p * e
    phi = jnp.where(u >= 0.0, 1.0 - tail, tail)
    return u * phi, phi + u * e * (1.0 / math.sqrt(2.0 * math.pi))


def mlp_kernel(idx_ref, x_ref, o_ref, vt_ref, bu_ref, *refs, fc):
    p1 = refs[:8]
    p2 = refs[8:16]
    x2_ref, gl_ref, gp_ref, y_ref, w1_ref, w2_ref, sem = refs[16:]
    d = x_ref.shape[1]
    ff = w2_ref.shape[0]

    @pl.when(pl.program_id(0) == 0)
    def _():
        going = load_pieces(idx_ref, p1, w1_ref, sem.at[0], w1_ref.shape[1] // 2)
        going += load_pieces(idx_ref, p2, w2_ref, sem.at[1], d // 2)
        for cp in going:
            cp.wait()

    x2 = x_ref[...].astype(F32) + dg(o_ref[...], w1_ref[:, :d], NN) + vt_ref[4:5, :]
    x2_ref[...] = x2
    c, r = norm_stats(x2)
    h = (c * r * vt_ref[5:6, :] + vt_ref[6:7, :]).astype(BF)
    y = x2 + vt_ref[7:8, :]
    for f in range(0, ff, fc):
        u = dg(h, w1_ref[:, d + f : d + f + fc], NN) + bu_ref[:, f : f + fc]
        g, gp = gelu_both(u)
        g = g.astype(BF)
        gl_ref[:, f : f + fc] = g
        gp_ref[:, f : f + fc] = gp.astype(BF)
        y = y + dg(g, w2_ref[f : f + fc, :], NN)
    y_ref[...] = y.astype(BF)


def mlp(idx, x, o, vt, bu, p1, p2, tb=256, fc=768):
    t, d = x.shape
    ff = bu.shape[1]
    return pl.pallas_call(
        functools.partial(mlp_kernel, fc=fc),
        grid_spec=pltpu.PrefetchScalarGridSpec(
            num_scalar_prefetch=1,
            grid=(t // tb,),
            in_specs=[rows_of(tb, d)] * 2 + [whole(vt.shape), whole(bu.shape)] + [ANY] * 16,
            out_specs=[rows_of(tb, d), rows_of(tb, ff), rows_of(tb, ff), rows_of(tb, d)],
            scratch_shapes=[
                pltpu.VMEM((d, d + ff), BF),
                pltpu.VMEM((ff, d), BF),
                pltpu.SemaphoreType.DMA((2,)),
            ],
        ),
        out_shape=[SDS((t, d), F32), SDS((t, ff), BF), SDS((t, ff), BF), SDS((t, d), BF)],
        compiler_params=params(),
        cost_estimate=cost(4 * t * d * (d + 2 * ff), t * (10 * d + 4 * ff) + 4 * d * ff, 2 * t * ff),
        name="mlp",
    )(idx, x, o, vt, bu, *p1, *p2)


def permute_kernel(ord_ref, y_ref, o_ref):
    jb = o_ref.shape[0]
    t = y_ref.shape[0]
    hot = jnp.where(ord_ref[...] == lax.broadcasted_iota(jnp.int32, (jb, t), 1), 1.0, 0.0)
    o_ref[...] = dg(hot.astype(BF), y_ref[...], NN).astype(BF)


def permute(order_col, y, jb=512):
    t, d = y.shape
    return pl.pallas_call(
        permute_kernel,
        grid=(t // jb,),
        in_specs=[rows_of(jb, 1), whole((t, d))],
        out_specs=rows_of(jb, d),
        out_shape=SDS((t, d), BF),
        compiler_params=params(),
        cost_estimate=cost(2 * t * t * d, t * d * 4),
        name="permute",
    )(order_col, y)


def mlp_back_kernel(idx_ref, ord_ref, ret_ref, gp_ref, x2_ref, vt_ref, *refs, fc):
    p1 = refs[:8]
    p2 = refs[8:16]
    (dm_ref, du_ref, dx2_ref, da_ref, do_ref, h2_ref, sums_ref, gbu_ref, w1_ref, w2_ref, sem) = refs[16:]
    i = pl.program_id(0)
    tb, ff = gp_ref.shape
    t, d = ret_ref.shape

    @pl.when(i == 0)
    def _():
        going = load_pieces(idx_ref, p1, w1_ref, sem.at[0], w1_ref.shape[1] // 2)
        going += load_pieces(idx_ref, p2, w2_ref, sem.at[1], d // 2)
        sums_ref[...] = jnp.zeros_like(sums_ref)
        gbu_ref[...] = jnp.zeros_like(gbu_ref)
        for cp in going:
            cp.wait()

    at = lax.broadcasted_iota(jnp.int32, (tb, t), 0) + i * tb
    hot = jnp.where(ord_ref[...] == at, 1.0, 0.0).astype(BF)
    dy = dg(hot, ret_ref[...], NN)
    dm = dy.astype(BF)
    dm_ref[...] = dm
    sums_ref[0:1, :] += jnp.sum(dy, axis=0, keepdims=True)
    dh = jnp.zeros((tb, d), F32)
    for f in range(0, ff, fc):
        du = (dg(dm, w2_ref[f : f + fc, :], NT) * gp_ref[:, f : f + fc].astype(F32)).astype(BF)
        du_ref[:, f : f + fc] = du
        gbu_ref[:, f : f + fc] += jnp.sum(du.astype(F32), axis=0, keepdims=True)
        dh = dh + dg(du, w1_ref[:, d + f : d + f + fc], NT)
    c, r = norm_stats(x2_ref[...])
    xh = c * r
    gain = vt_ref[5:6, :]
    h2_ref[...] = (xh * gain + vt_ref[6:7, :]).astype(BF)
    sums_ref[1:2, :] += jnp.sum(dh * xh, axis=0, keepdims=True)
    sums_ref[2:3, :] += jnp.sum(dh, axis=0, keepdims=True)
    dz = dh * gain
    m1 = jnp.sum(dz, axis=-1, keepdims=True) * (1.0 / d)
    m2 = jnp.sum(dz * xh, axis=-1, keepdims=True) * (1.0 / d)
    dx2 = dy + r * (dz - m1 - xh * m2)
    dx2_ref[...] = dx2
    da = dx2.astype(BF)
    da_ref[...] = da
    sums_ref[3:4, :] += jnp.sum(da.astype(F32), axis=0, keepdims=True)
    do_ref[...] = dg(da, w1_ref[:, :d], NT).astype(BF)


def mlp_back(idx, order_row, ret, gp, x2, vt, p1, p2, tb=256, fc=768):
    t, d = x2.shape
    ff = gp.shape[1]
    return pl.pallas_call(
        functools.partial(mlp_back_kernel, fc=fc),
        grid_spec=pltpu.PrefetchScalarGridSpec(
            num_scalar_prefetch=1,
            grid=(t // tb,),
            in_specs=[whole((1, t)), whole((t, d)), rows_of(tb, ff), rows_of(tb, d), whole(vt.shape)]
            + [ANY] * 16,
            out_specs=[
                rows_of(tb, d),
                rows_of(tb, ff),
                rows_of(tb, d),
                rows_of(tb, d),
                rows_of(tb, d),
                rows_of(tb, d),
                fixed((8, d)),
                fixed((1, ff)),
            ],
            scratch_shapes=[
                pltpu.VMEM((d, d + ff), BF),
                pltpu.VMEM((ff, d), BF),
                pltpu.SemaphoreType.DMA((2,)),
            ],
        ),
        out_shape=[
            SDS((t, d), BF),
            SDS((t, ff), BF),
            SDS((t, d), F32),
            SDS((t, d), BF),
            SDS((t, d), BF),
            SDS((t, d), BF),
            SDS((8, d), F32),
            SDS((1, ff), F32),
        ],
        compiler_params=params(),
        cost_estimate=cost(2 * t * d * (d + 2 * ff + t) * 1.5, t * (20 * d + 4 * ff)),
        name="mlp_back",
    )(idx, order_row, ret, gp, x2, vt, *p1, *p2)


def split_halves(c, r, mine_ref, theirs_ref):
    h = r.shape[1] // 2
    left, right = r[:, :h], r[:, h:]
    mine_ref[...] = jnp.where(c == 0, left, right)
    theirs_ref[...] = jnp.where(c == 0, right, left)


def grad_down_kernel(idx_ref, g_ref, dm_ref, mine_ref, theirs_ref):
    split_halves(idx_ref[1], dg(g_ref[...], dm_ref[...], TN).astype(BF), mine_ref, theirs_ref)


def grad_down(idx, g, dm, mb=768):
    t, ff = g.shape
    d = dm.shape[1]
    return pl.pallas_call(
        grad_down_kernel,
        grid_spec=pltpu.PrefetchScalarGridSpec(
            num_scalar_prefetch=1,
            grid=(ff // mb,),
            in_specs=[pl.BlockSpec((t, mb), lambda i, _: (0, i)), whole((t, d))],
            out_specs=[rows_of(mb, d // 2)] * 2,
        ),
        out_shape=[SDS((ff, d // 2), BF)] * 2,
        compiler_params=params(),
        cost_estimate=cost(3 * t * ff * d, 2 * t * (ff + d) + 2 * ff * d),
        name="grad_down",
    )(idx, g, dm)


def grad_up_kernel(idx_ref, h2_ref, o_ref, du_ref, da_ref, mine_ref, theirs_ref, *, steps):
    i = pl.program_id(0)

    @pl.when(i < steps)
    def _():
        split_halves(idx_ref[1], dg(h2_ref[...], du_ref[...], TN).astype(BF), mine_ref, theirs_ref)

    @pl.when(i == steps)
    def _():
        split_halves(idx_ref[1], dg(o_ref[...], da_ref[...], TN).astype(BF), mine_ref, theirs_ref)


def grad_up(idx, h2, o, du, da):
    t, d = h2.shape
    ff = du.shape[1]
    steps = ff // d
    return pl.pallas_call(
        functools.partial(grad_up_kernel, steps=steps),
        grid_spec=pltpu.PrefetchScalarGridSpec(
            num_scalar_prefetch=1,
            grid=(steps + 1,),
            in_specs=[
                whole((t, d)),
                whole((t, d)),
                pl.BlockSpec((t, d), lambda i, _: (0, jnp.minimum(i, steps - 1))),
                whole((t, d)),
            ],
            out_specs=[pl.BlockSpec((d, d // 2), lambda i, _: (0, i))] * 2,
        ),
        out_shape=[SDS((d, (d + ff) // 2), BF)] * 2,
        compiler_params=params(),
        cost_estimate=cost(3 * t * (ff + d) * d, 2 * t * (ff + 3 * d) + 2 * ff * d),
        name="grad_up",
    )(idx, h2, o, du, da)


def attend_back_kernel(
    tag_ref, q_ref, k_ref, v_ref, do_ref, o_ref, l_ref, dq_ref, dk_ref, dv_ref, dl_ref, dqt_ref, *, kb, qb
):
    r = pl.program_id(0)
    length = q_ref.shape[0]
    low = lax.broadcasted_iota(jnp.int32, (1, 128), 1) < 64
    prod = (do_ref[...].astype(F32) * o_ref[...].astype(F32)).T
    dl_ref[0:1, :] = jnp.sum(prod[0:64], axis=0, keepdims=True)
    dl_ref[1:2, :] = jnp.sum(prod[64:128], axis=0, keepdims=True)

    def block(ks, kn, qs, qn):
        k = k_ref[pl.ds(ks, kn), :]
        v = v_ref[pl.ds(ks, kn), :]
        q = q_ref[pl.ds(qs, qn), :]
        do = do_ref[pl.ds(qs, qn), :]
        dks = []
        dvs = []
        dqs = []
        for h in range(2):
            sel = low if h == 0 else jnp.logical_not(low)
            km = jnp.where(sel, k, jnp.asarray(0, BF))
            vm = jnp.where(sel, v, jnp.asarray(0, BF))
            pt = jnp.exp2(dg(km, q, NT) - l_ref[0, 0, h : h + 1, pl.ds(qs, qn)])
            dst = (pt * (dg(vm, do, NT) - dl_ref[h : h + 1, pl.ds(qs, qn)])).astype(BF)
            dvs.append(dg(pt.astype(BF), do, NN))
            dks.append(dg(dst, q, NN))
            dqs.append(dg(km.T, dst, NN))
        return jnp.where(low, dks[0], dks[1]), jnp.where(low, dvs[0], dvs[1]), dqs[0] + dqs[1]

    def run(kn, qn, plan):
        seen = set()
        for ks, starts in plan:
            dk = dv = None
            for qs in starts:
                a, b, dq = block(ks, kn, qs, qn)
                dk = a if dk is None else dk + a
                dv = b if dv is None else dv + b
                if qs in seen:
                    dqt_ref[:, pl.ds(qs, qn)] += dq
                else:
                    dqt_ref[:, pl.ds(qs, qn)] = dq
                seen.add(qs)
            dk_ref[pl.ds(ks, kn), :] = (dk * LN2).astype(BF)
            dv_ref[pl.ds(ks, kn), :] = dv.astype(BF)
        dq_ref[...] = (dqt_ref[...].T * 0.125).astype(BF)

    @pl.when(tag_ref[r] == 0)
    def _():
        run(kb, qb, [(ks, range(0, length, qb)) for ks in range(0, length, kb)])

    @pl.when(tag_ref[r] != 0)
    def _():
        c = length // 4
        run(c, c, [(ks, [ks]) for ks in range(0, length, c)])


def attend_back(tag, q, k, v, do, o, lse, kb=512, qb=512):
    t, d = q.shape
    rows = tag.shape[0]
    length = t // rows
    pairs = d // 128
    blk = pl.BlockSpec((length, 128), lambda r, p, _: (r, p))
    lse_spec = pl.BlockSpec((1, 1, 2, length), lambda r, p, _: (r, p, 0, 0))
    return pl.pallas_call(
        functools.partial(attend_back_kernel, kb=kb, qb=qb),
        grid_spec=pltpu.PrefetchScalarGridSpec(
            num_scalar_prefetch=1,
            grid=(rows, pairs),
            in_specs=[blk] * 5 + [lse_spec],
            out_specs=[blk] * 3,
            scratch_shapes=[pltpu.VMEM((2, length), F32), pltpu.VMEM((128, length), F32)],
        ),
        out_shape=[SDS((t, d), BF)] * 3,
        compiler_params=params(2),
        cost_estimate=cost(40 * t * length * d, t * d * 16, t * length * 12),
        name="attend_back",
    )(tag, q, k, v, do, o, lse)


def grad_qkv_kernel(idx_ref, x_ref, vt_ref, dq_ref, dk_ref, dv_ref, mine_ref, theirs_ref, s_ref, h_ref):
    i = pl.program_id(0)

    @pl.when(i == 0)
    def _():
        c, r = norm_stats(x_ref[...].astype(F32))
        h_ref[...] = (c * r * vt_ref[0:1, :] + vt_ref[1:2, :]).astype(BF)
        s_ref[...] = jnp.zeros_like(s_ref)

    for m, ref in enumerate((dq_ref, dk_ref, dv_ref)):

        @pl.when(i == m)
        def _(m=m, ref=ref):
            dj = ref[...]
            split_halves(idx_ref[1], dg(h_ref[...], dj, TN).astype(BF), mine_ref, theirs_ref)
            if m != 1:
                s_ref[m // 2 : m // 2 + 1, :] = jnp.sum(dj.astype(F32), axis=0, keepdims=True)


def grad_qkv(idx, x, vt, dq, dk, dv):
    t, d = x.shape
    return pl.pallas_call(
        grad_qkv_kernel,
        grid_spec=pltpu.PrefetchScalarGridSpec(
            num_scalar_prefetch=1,
            grid=(3,),
            in_specs=[whole((t, d)), whole(vt.shape)] + [whole((t, d))] * 3,
            out_specs=[pl.BlockSpec((d, d // 2), lambda i, _: (0, i))] * 2 + [fixed((8, d))],
            scratch_shapes=[pltpu.VMEM((t, d), BF)],
        ),
        out_shape=[SDS((d, 3 * d // 2), BF)] * 2 + [SDS((8, d), F32)],
        compiler_params=params(),
        cost_estimate=cost(9 * t * d * d, t * d * 10),
        name="grad_qkv",
    )(idx, x, vt, dq, dk, dv)


def tokens_back_kernel(idx_ref, dq_ref, dk_ref, dv_ref, x_ref, vt_ref, dx2_ref, *refs):
    pieces = refs[:8]
    tg_ref, s_ref, w_ref, sem = refs[8:]
    d = x_ref.shape[1]

    @pl.when(pl.program_id(0) == 0)
    def _():
        going = load_pieces(idx_ref, pieces, w_ref, sem, 3 * d // 2)
        s_ref[...] = jnp.zeros_like(s_ref)
        for cp in going:
            cp.wait()

    dh = dg(dq_ref[...], w_ref[:, :d], NT)
    dh = dh + dg(dk_ref[...], w_ref[:, d : 2 * d], NT)
    dh = dh + dg(dv_ref[...], w_ref[:, 2 * d :], NT)
    c, r = norm_stats(x_ref[...].astype(F32))
    xh = c * r
    s_ref[0:1, :] += jnp.sum(dh * xh, axis=0, keepdims=True)
    s_ref[1:2, :] += jnp.sum(dh, axis=0, keepdims=True)
    dz = dh * vt_ref[0:1, :]
    m1 = jnp.sum(dz, axis=-1, keepdims=True) * (1.0 / d)
    m2 = jnp.sum(dz * xh, axis=-1, keepdims=True) * (1.0 / d)
    tg_ref[...] = dx2_ref[...] + r * (dz - m1 - xh * m2)


def tokens_back(idx, dq, dk, dv, x, vt, dx2, pieces, tb=512):
    t, d = x.shape
    return pl.pallas_call(
        tokens_back_kernel,
        grid_spec=pltpu.PrefetchScalarGridSpec(
            num_scalar_prefetch=1,
            grid=(t // tb,),
            in_specs=[rows_of(tb, d)] * 4 + [whole(vt.shape), rows_of(tb, d)] + [ANY] * 8,
            out_specs=[rows_of(tb, d), fixed((8, d))],
            scratch_shapes=[pltpu.VMEM((d, 3 * d), BF), pltpu.SemaphoreType.DMA],
        ),
        out_shape=[SDS((t, d), F32), SDS((8, d), F32)],
        compiler_params=params(),
        cost_estimate=cost(9 * t * d * d, t * d * 16 + d * d * 6),
        name="tokens_back",
    )(idx, dq, dk, dv, x, vt, dx2, *pieces)


def sum_far_kernel(idx_ref, *refs, q):
    for e in range(q):
        a, b, o = refs[e], refs[q + e], refs[2 * q + e]
        o[...] = (a[...].astype(F32) + b[...].astype(F32)).astype(BF)


def sum_far(idx, mine, recv, n):
    q = n // 4
    _, rows, ch = mine.shape

    def spec(e):
        return pl.BlockSpec((1, rows, ch), lambda z, ix: (z * q + lax.bitwise_xor(ix[0] % q, jnp.int32(e)), 0, 0))

    specs = [spec(e) for e in range(q)]
    return pl.pallas_call(
        functools.partial(sum_far_kernel, q=q),
        grid_spec=pltpu.PrefetchScalarGridSpec(
            num_scalar_prefetch=1,
            grid=(4,),
            in_specs=specs * 2,
            out_specs=[pl.BlockSpec((1, rows, ch), lambda z, ix: (z, 0, 0))] * q,
        ),
        out_shape=[SDS((4, rows, ch), BF)] * q,
        compiler_params=params(),
        cost_estimate=cost(n * rows * ch, n * rows * ch * 6),
        name="sum_far",
    )(idx, *([mine] * q), *([recv] * q))


def sum_near_kernel(idx_ref, *refs, q):
    for d in range(4):
        total = refs[d * q][...].astype(F32)
        for e in range(1, q):
            total = total + refs[d * q + e][...].astype(F32)
        refs[4 * q + d][...] = total[0].astype(BF)


def sum_near(idx, parts, n):
    q = n // 4
    _, rows, ch = parts[0].shape

    def spec(d):
        return pl.BlockSpec((1, rows, ch), lambda i, ix: (lax.bitwise_xor(ix[0] // q, jnp.int32(d)), 0, 0))

    return pl.pallas_call(
        functools.partial(sum_near_kernel, q=q),
        grid_spec=pltpu.PrefetchScalarGridSpec(
            num_scalar_prefetch=1,
            grid=(1,),
            in_specs=[spec(d) for d in range(4) for _ in range(q)],
            out_specs=[fixed((rows, ch))] * 4,
        ),
        out_shape=[SDS((rows, ch), BF)] * 4,
        compiler_params=params(),
        cost_estimate=cost(n * rows * ch, n * rows * ch * 3),
        name="sum_near",
    )(idx, *(list(parts) * 4))


def reduce_steps(idx, mine, recv, n, m):
    q = n // 4
    outs = sum_far(idx, mine, recv, n)
    parts = [outs[0]] + [xor_pp(outs[e], e, n) for e in range(1, q)]
    near = sum_near(idx, parts, n)
    total = near[0].astype(F32)
    for d in range(1, 4):
        total = total + xor_pp(near[d], d * q, n).astype(F32)
    b = 2
    while b < m:
        total = total + lax.ppermute(total.astype(BF), "dp", [(i, i ^ b) for i in range(m)]).astype(F32)
        b *= 2
    return total


def reduce_grad(idx, mine, theirs, n, m):
    rows, ch = mine.shape[0] // n, mine.shape[1]
    recv = core_swap(theirs, m)
    low = reduce_steps(idx, mine.reshape(n, rows, ch), recv.reshape(n, rows, ch), n, m).astype(BF)
    other = core_swap(low, m)
    first = idx[1] == 0
    return (
        jnp.where(first, low, other).astype(F32),
        jnp.where(first, other, low).astype(F32),
    )


def vec_table_kernel(*refs):
    a, b, c, u, o = refs
    d = a.shape[1]
    rows = jnp.concatenate(
        [c[0:2, :], b[0:2, :], a[3:4, :], a[1:3, :], a[0:1, :], u[...], jnp.zeros((116, d), F32)], axis=0
    )
    o[...] = rows.T.astype(BF)


def vec_table(s_mlp, s_qkv, s_tok, gbu):
    d = s_mlp.shape[1]
    return pl.pallas_call(
        vec_table_kernel, out_shape=SDS((d, 128), BF), compiler_params=params(0), name="vec_table"
    )(s_mlp, s_qkv, s_tok, gbu)


def local(
    tokens,
    sensor_tag,
    owner_order,
    ln1_gain,
    ln1_bias,
    w_qkv,
    b_query,
    b_value,
    w_out,
    b_out,
    ln2_gain,
    ln2_bias,
    w_up,
    b_up,
    w_down,
    b_down,
    out_grad,
    *,
    n,
    m,
):
    t, d = tokens.shape
    ff = w_up.shape[1]
    rows = d // n
    wide = ff // d
    f = lax.axis_index("fsdp")
    c = lax.axis_index("dp") % 2
    idx = jnp.stack([f, c]).astype(jnp.int32)
    use = idx if rows % 16 == 0 and n == 16 else jnp.zeros_like(idx)

    def core_half(x):
        h = x.shape[1] // 2
        return jnp.where(c == 0, x[:, :h], x[:, h:])

    vec = jnp.stack([ln1_gain, ln1_bias, b_query, b_value, b_out, ln2_gain, ln2_bias, b_down], axis=1)
    vec = jnp.concatenate([vec, b_up.reshape(wide, rows).T], axis=1)
    vec = jnp.pad(vec, ((0, 0), (0, 128 - vec.shape[1])))
    shard_a = jnp.concatenate([core_half(w_qkv), vec], axis=1)
    shard_b = core_half(jnp.concatenate([w_out, w_up], axis=1))
    shard_c = core_half(w_down)
    near_a = gather_near(shard_a, n)
    pieces_a = settle(gather_far(near_a, n, m), f, c, n)
    near_b = gather_near(shard_b, n)
    near_c = gather_near(shard_c, n)
    pieces_b = settle(gather_far(near_b, n, m), f, c, n)
    pieces_c = settle(gather_far(near_c, n, m), f, c, n)

    returned = lax.all_to_all(out_grad.astype(BF), "fsdp", split_axis=0, concat_axis=0, tiled=True)

    q, k, v, vt = qkv(use, tokens, pieces_a)
    mixed, lse = attend(sensor_tag, q, k, v)
    bu = vt[8 : 8 + wide].reshape(wide, n, rows).transpose(1, 0, 2).reshape(1, ff)
    x2, active, slope, y = mlp(use, tokens, mixed, vt, bu, pieces_b, pieces_c)
    sent = permute(owner_order.reshape(t, 1), y)
    encoded = lax.all_to_all(sent, "fsdp", split_axis=0, concat_axis=0, tiled=True).astype(F32)

    dm, du, dx2, da, do, h2, s_mlp, gbu = mlp_back(
        use, owner_order, returned, slope, x2, vt, pieces_b, pieces_c
    )
    down_mine, down_theirs = grad_down(idx, active, dm)
    g_down = reduce_grad(idx, down_mine, down_theirs, n, m)
    up_mine, up_theirs = grad_up(idx, h2, mixed, du, da)
    g_up = reduce_grad(idx, up_mine, up_theirs, n, m)
    dq, dk, dv = attend_back(sensor_tag, q, k, v, do, mixed, lse)
    qkv_mine, qkv_theirs, s_qkv = grad_qkv(idx, tokens, vt, dq, dk, dv)
    g_qkv = reduce_grad(idx, qkv_mine, qkv_theirs, n, m)
    tokens_grad, s_tok = tokens_back(use, dq, dk, dv, tokens, vt, dx2, pieces_a)

    gbu = gbu.reshape(n, wide, rows).transpose(1, 0, 2).reshape(wide, d)
    table = vec_table(s_mlp, s_qkv, s_tok, gbu)
    table_swap = core_swap(table, m)
    vecs = reduce_steps(idx, table.reshape(n, rows, 128), table_swap.reshape(n, rows, 128), n, m)
    vecs = vecs.T

    def join(pair, parts, width):
        out = []
        for p in range(parts):
            out += [pair[0][:, p * width : (p + 1) * width], pair[1][:, p * width : (p + 1) * width]]
        return jnp.concatenate(out, axis=1)

    h = d // 2
    grad_qkv_out = join(g_qkv, 3, h)
    grad_up_out = join((g_up[0][:, : ff // 2], g_up[1][:, : ff // 2]), wide, h)
    grad_out_out = join((g_up[0][:, ff // 2 :], g_up[1][:, ff // 2 :]), 1, h)
    grad_down_out = join(g_down, 1, h)
    return (
        encoded,
        tokens_grad,
        vecs[0],
        vecs[1],
        grad_qkv_out,
        vecs[2],
        vecs[3],
        grad_out_out,
        vecs[4],
        vecs[5],
        vecs[6],
        grad_up_out,
        vecs[8 : 8 + wide].reshape(ff // n),
        grad_down_out,
        vecs[7],
    )


def solution(mesh):
    n = mesh.shape["fsdp"]
    m = mesh.shape["dp"]
    both = P(("dp", "fsdp"), None)
    vec = P("fsdp")
    mat = P("fsdp", None)
    in_specs = (both, P(("dp", "fsdp")), both, vec, vec, mat, vec, vec, mat, vec, vec, vec, mat, vec, mat, vec, both)
    out_specs = (both, both, vec, vec, mat, vec, vec, mat, vec, vec, vec, mat, vec, mat, vec)
    return jax.shard_map(
        functools.partial(local, n=n, m=m), mesh=mesh, in_specs=in_specs, out_specs=out_specs, check_vma=False
    )
```

```python
import functools
import math

import jax
import jax.numpy as jnp
from jax import lax
from jax.experimental import pallas as pl
from jax.experimental.pallas import tpu as pltpu
from jax.sharding import PartitionSpec as P

F32 = jnp.float32
BF = jnp.bfloat16
EPS = 1e-6
LOG2E = math.log2(math.e)
LN2 = math.log(2.0)
NT = (((1,), (1,)), ((), ()))
TN = (((0,), (0,)), ((), ()))
NN = (((1,), (0,)), ((), ()))
ANY = pl.BlockSpec(memory_space=pl.ANY)
VECS = 16
SDS = jax.ShapeDtypeStruct


def dg(a, b, dims):
    return lax.dot_general(a, b, dims, preferred_element_type=F32)


def params(axes=1):
    return pltpu.CompilerParams(
        vmem_limit_bytes=58 * 2**20, dimension_semantics=("arbitrary",) * axes
    )


def cost(flops, nbytes, trans=0):
    return pl.CostEstimate(flops=int(flops) >> 10, bytes_accessed=int(nbytes) >> 10, transcendentals=int(trans) >> 10)


def rows_of(height, width):
    return pl.BlockSpec((height, width), lambda i, *_: (i, 0))


def whole(shape):
    zeros = (0,) * len(shape)
    return pl.BlockSpec(shape, lambda *_: zeros, pipeline_mode=pl.Buffered(1))


def fixed(shape):
    zeros = (0,) * len(shape)
    return pl.BlockSpec(shape, lambda *_: zeros)


def norm_stats(x):
    n = x.shape[-1]
    c = x - jnp.sum(x, axis=-1, keepdims=True) * (1.0 / n)
    var = jnp.sum(c * c, axis=-1, keepdims=True) * (1.0 / n)
    return c, lax.rsqrt(var + EPS)


def after(x, *deps):
    return lax.optimization_barrier((x,) + deps)[0]


def xor_pp(x, b, n):
    return lax.ppermute(x, "fsdp", [(i, i ^ b) for i in range(n)])


def core_swap(x, m):
    return lax.ppermute(x, "dp", [(i, i ^ 1) for i in range(m)])


def gather_near(x, n):
    q = n // 4
    return jnp.stack([x] + [xor_pp(x, d * q, n) for d in (1, 2, 3)])


def tops(n):
    q = n // 4
    return [[low + z * q for z in range(4)] for low in range(q)]


def gather_far(s, n):
    return [s] + [xor_pp(s, e, n) for e in range(1, n // 4)]


def settle(pieces, order, c, n, tall=None):
    q = n // 4
    rows = pieces[0].shape[1]
    if rows % 16 == 0 and q == 4:
        return pieces
    height = n * rows // 16
    halves = []
    for side in (pieces[:q], pieces[q:]):
        rel = jnp.stack(side, axis=1).reshape((n,) + side[0].shape[1:])
        halves.append(jnp.take(rel, order, axis=0))
    left = jnp.where(c == 0, halves[0], halves[1])
    right = jnp.where(c == 0, halves[1], halves[0])
    out = []
    for side in (left, right):
        cut = side.shape[-1] if tall is None else tall
        flat = side[..., :cut].reshape(16, height, cut)
        if tall is not None:
            w = (side.shape[-1] - cut) // 4
            low = side[..., cut:].reshape(n, rows, 4, w).transpose(0, 2, 1, 3)
            low = low.reshape(16, 4, height, w).transpose(0, 2, 1, 3).reshape(16, height, 4 * w)
            flat = jnp.concatenate([flat, low], axis=2)
        four = flat.reshape(4, 4, height, side.shape[-1])
        out += [four[:, e] for e in range(4)]
    return out


def piece(pieces, side, e, d):
    return pieces[side].at[e, d] if len(pieces) == 2 else pieces[4 * side + e].at[d]


def load_pieces(idx_ref, pieces, plan, sem, relative=False):
    f = idx_ref[0]
    c = idx_ref[1]
    rows = pieces[0].shape[-2]
    started = []
    for start, width, dst, height, first, two in plan:
        for e in range(4):
            for d in range(4):
                s = lax.bitwise_xor(f if relative else f % 4 + d * 4, jnp.int32(d * 4 + e if relative else e))
                at = pl.ds(pl.multiple_of(s * height + first, 16), rows)
                src = pl.ds(start, width)
                if two:
                    for side, h in ((0, c), (1, 1 - c)):
                        cols = pl.ds(pl.multiple_of(h * width, 128), width)
                        block = piece(pieces, side, e, d)
                        started.append(pltpu.make_async_copy(block.at[:, src], dst.at[at, cols], sem))
                else:
                    block = piece(pieces, 0, e, d)
                    started.append(pltpu.make_async_copy(block.at[:, src], dst.at[at, :], sem))
    for cp in started:
        cp.start()
    return started


def plan_mlp(rows, w1_ref, w2_ref):
    half = w1_ref.shape[1] // 2
    w = w2_ref.shape[1] // 2
    return [(0, half, w1_ref, rows, 0, True)], [
        (half + j * w, w, w2_ref, 4 * rows, j * rows, True) for j in range(4)
    ]


def qkv_kernel(idx_ref, x_ref, *refs):
    pieces = refs[:2]
    q_ref, k_ref, v_ref, h_ref, vt_ref, w_ref, vec_ref, sem = refs[2:]
    d = x_ref.shape[1]

    @pl.when(pl.program_id(0) == 0)
    def _():
        rows = pieces[0].shape[-2]
        vecs = load_pieces(idx_ref, pieces, [(3 * d // 2, 128, vec_ref, rows, 0, False)], sem.at[1], True)
        going = load_pieces(idx_ref, pieces, [(0, 3 * d // 2, w_ref, rows, 0, True)], sem.at[0], True)
        for cp in vecs:
            cp.wait()
        vt_ref[...] = vec_ref[...].astype(F32).T[:VECS]
        for cp in going:
            cp.wait()

    c, r = norm_stats(x_ref[...].astype(F32))
    h = (c * r * vt_ref[0:1, :] + vt_ref[1:2, :]).astype(BF)
    h_ref[...] = h
    q = dg(h, w_ref[:, :d], NN)
    q_ref[...] = ((q + vt_ref[2:3, :]) * (0.125 * LOG2E)).astype(BF)
    k_ref[...] = dg(h, w_ref[:, d : 2 * d], NN).astype(BF)
    v_ref[...] = (dg(h, w_ref[:, 2 * d :], NN) + vt_ref[3:4, :]).astype(BF)


def qkv(idx, x, pieces, tb=512):
    t, d = x.shape
    return pl.pallas_call(
        qkv_kernel,
        grid_spec=pltpu.PrefetchScalarGridSpec(
            num_scalar_prefetch=1,
            grid=(t // tb,),
            in_specs=[rows_of(tb, d)] + [ANY] * 2,
            out_specs=[rows_of(tb, d)] * 4 + [fixed((VECS, d))],
            scratch_shapes=[
                pltpu.VMEM((d, 3 * d), BF),
                pltpu.VMEM((d, 128), BF),
                pltpu.SemaphoreType.DMA((2,)),
            ],
        ),
        out_shape=[SDS((t, d), BF)] * 4 + [SDS((VECS, d), F32)],
        compiler_params=params(),
        cost_estimate=cost(6 * t * d * d, t * d * 8 + d * d * 6),
        name="qkv",
    )(idx, x, *pieces)


def attend_kernel(tag_ref, q_ref, k_ref, v_ref, o_ref, l_ref, *, qb):
    r = pl.program_id(0)
    length = q_ref.shape[0]
    low = lax.broadcasted_iota(jnp.int32, (1, 128), 1) < 64

    def block(qs, qn, ks, kn):
        q = q_ref[pl.ds(qs, qn), :]
        k = k_ref[pl.ds(ks, kn), :]
        v = v_ref[pl.ds(ks, kn), :]
        outs = []
        for h in range(2):
            sel = low if h == 0 else jnp.logical_not(low)
            qm = jnp.where(sel, q, jnp.asarray(0, BF))
            vm = jnp.where(sel, v, jnp.asarray(1, BF))
            s = dg(qm, k, NT)
            m = jnp.max(s, axis=1, keepdims=True)
            outs.append((dg(jnp.exp2(s - m).astype(BF), vm, NN), m))
        (a, ma), (b, mb) = outs
        acc = jnp.where(low, a, b)
        total = pltpu.roll(jnp.where(low, b, a), 64, 1)
        o_ref[pl.ds(qs, qn), :] = (acc / total).astype(o_ref.dtype)
        lse = (jnp.where(low, ma, mb) + jnp.log2(total)).T
        l_ref[0, 0, 0:1, pl.ds(qs, qn)] = lse[0:1]
        l_ref[0, 0, 1:2, pl.ds(qs, qn)] = lse[64:65]

    @pl.when(tag_ref[r] == 0)
    def _():
        for i in range(length // qb):
            block(i * qb, qb, 0, length)

    @pl.when(tag_ref[r] != 0)
    def _():
        c = length // 4
        for i in range(4):
            block(i * c, c, i * c, c)


def attend(tag, q, k, v, qb=512):
    t, d = q.shape
    rows = tag.shape[0]
    length = t // rows
    pairs = d // 128
    blk = pl.BlockSpec((length, 128), lambda r, p, _: (r, p))
    lse = pl.BlockSpec((1, 1, 2, length), lambda r, p, _: (r, p, 0, 0))
    return pl.pallas_call(
        functools.partial(attend_kernel, qb=qb),
        grid_spec=pltpu.PrefetchScalarGridSpec(
            num_scalar_prefetch=1, grid=(rows, pairs), in_specs=[blk] * 3, out_specs=[blk, lse]
        ),
        out_shape=[SDS((t, d), BF), SDS((rows, pairs, 2, length), F32)],
        compiler_params=params(2),
        cost_estimate=cost(16 * t * length * d, t * d * 8, t * length * 12),
        name="attend",
    )(tag, q, k, v)


def gelu_both(u):
    t = 1.0 + jnp.abs(u) * (0.3275911 / math.sqrt(2.0))
    r = pl.reciprocal(t, approx=True)
    r = r * (2.0 - t * r)
    e = jnp.exp2(u * u * (-0.5 * LOG2E))
    p = -0.5 * 1.453152027 + r * (0.5 * 1.061405429)
    p = 0.5 * 1.421413741 + r * p
    p = -0.5 * 0.284496736 + r * p
    p = 0.5 * 0.254829592 + r * p
    tail = r * p * e
    phi = jnp.where(u >= 0.0, 1.0 - tail, tail)
    return u * phi, phi + u * e * (1.0 / math.sqrt(2.0 * math.pi))


def mlp_kernel(idx_ref, x_ref, o_ref, vt_ref, bu_ref, *refs, fc):
    pieces = refs[:8]
    x2_ref, gl_ref, gp_ref, y_ref, w1_ref, w2_ref, sem = refs[8:]
    d = x_ref.shape[1]
    ff = w2_ref.shape[0]

    @pl.when(pl.program_id(0) == 0)
    def _():
        first, second = plan_mlp(pieces[0].shape[1], w1_ref, w2_ref)
        going = load_pieces(idx_ref, pieces, first, sem.at[0])
        going += load_pieces(idx_ref, pieces, second, sem.at[1])
        for cp in going:
            cp.wait()

    x2 = x_ref[...].astype(F32) + dg(o_ref[...], w1_ref[:, :d], NN) + vt_ref[4:5, :]
    x2_ref[...] = x2
    c, r = norm_stats(x2)
    h = (c * r * vt_ref[5:6, :] + vt_ref[6:7, :]).astype(BF)
    y = x2 + vt_ref[7:8, :]
    for f in range(0, ff, fc):
        u = dg(h, w1_ref[:, d + f : d + f + fc], NN) + bu_ref[:, f : f + fc]
        g, gp = gelu_both(u)
        g = g.astype(BF)
        gl_ref[:, f : f + fc] = g
        gp_ref[:, f : f + fc] = gp.astype(BF)
        y = y + dg(g, w2_ref[f : f + fc, :], NN)
    y_ref[...] = y.astype(BF)


def mlp(idx, x, o, vt, bu, pieces, tb=256, fc=768):
    t, d = x.shape
    ff = bu.shape[1]
    return pl.pallas_call(
        functools.partial(mlp_kernel, fc=fc),
        grid_spec=pltpu.PrefetchScalarGridSpec(
            num_scalar_prefetch=1,
            grid=(t // tb,),
            in_specs=[rows_of(tb, d)] * 2 + [whole(vt.shape), whole(bu.shape)] + [ANY] * 8,
            out_specs=[rows_of(tb, d), rows_of(tb, ff), rows_of(tb, ff), rows_of(tb, d)],
            scratch_shapes=[
                pltpu.VMEM((d, d + ff), BF),
                pltpu.VMEM((ff, d), BF),
                pltpu.SemaphoreType.DMA((2,)),
            ],
        ),
        out_shape=[SDS((t, d), F32), SDS((t, ff), BF), SDS((t, ff), BF), SDS((t, d), BF)],
        compiler_params=params(),
        cost_estimate=cost(4 * t * d * (d + 2 * ff), t * (10 * d + 4 * ff) + 4 * d * ff, 2 * t * ff),
        name="mlp",
    )(idx, x, o, vt, bu, *pieces)


def permute_kernel(ord_ref, y_ref, o_ref):
    jb = o_ref.shape[0]
    t = y_ref.shape[0]
    hot = jnp.where(ord_ref[...] == lax.broadcasted_iota(jnp.int32, (jb, t), 1), 1.0, 0.0)
    o_ref[...] = dg(hot.astype(BF), y_ref[...], NN).astype(BF)


def permute(order_col, y, jb=512):
    t, d = y.shape
    return pl.pallas_call(
        permute_kernel,
        grid=(t // jb,),
        in_specs=[rows_of(jb, 1), whole((t, d))],
        out_specs=rows_of(jb, d),
        out_shape=SDS((t, d), BF),
        compiler_params=params(),
        cost_estimate=cost(2 * t * t * d, t * d * 4),
        name="permute",
    )(order_col, y)


def mlp_back_kernel(idx_ref, ord_ref, ret_ref, gp_ref, x2_ref, vt_ref, *refs, fc):
    pieces = refs[:8]
    (dm_ref, du_ref, dx2_ref, da_ref, do_ref, h2_ref, sums_ref, gbu_ref, w1_ref, w2_ref, sem) = refs[8:]
    i = pl.program_id(0)
    tb, ff = gp_ref.shape
    t, d = ret_ref.shape

    @pl.when(i == 0)
    def _():
        first, second = plan_mlp(pieces[0].shape[1], w1_ref, w2_ref)
        going = load_pieces(idx_ref, pieces, first, sem.at[0])
        going += load_pieces(idx_ref, pieces, second, sem.at[1])
        sums_ref[...] = jnp.zeros_like(sums_ref)
        gbu_ref[...] = jnp.zeros_like(gbu_ref)
        for cp in going:
            cp.wait()

    at = lax.broadcasted_iota(jnp.int32, (tb, t), 0) + i * tb
    hot = jnp.where(ord_ref[...] == at, 1.0, 0.0).astype(BF)
    dy = dg(hot, ret_ref[...], NN)
    dm = dy.astype(BF)
    dm_ref[...] = dm
    sums_ref[0:1, :] += jnp.sum(dy, axis=0, keepdims=True)
    dh = jnp.zeros((tb, d), F32)
    for f in range(0, ff, fc):
        du = (dg(dm, w2_ref[f : f + fc, :], NT) * gp_ref[:, f : f + fc].astype(F32)).astype(BF)
        du_ref[:, f : f + fc] = du
        gbu_ref[:, f : f + fc] += jnp.sum(du.astype(F32), axis=0, keepdims=True)
        dh = dh + dg(du, w1_ref[:, d + f : d + f + fc], NT)
    c, r = norm_stats(x2_ref[...])
    xh = c * r
    gain = vt_ref[5:6, :]
    h2_ref[...] = (xh * gain + vt_ref[6:7, :]).astype(BF)
    sums_ref[1:2, :] += jnp.sum(dh * xh, axis=0, keepdims=True)
    sums_ref[2:3, :] += jnp.sum(dh, axis=0, keepdims=True)
    dz = dh * gain
    m1 = jnp.sum(dz, axis=-1, keepdims=True) * (1.0 / d)
    m2 = jnp.sum(dz * xh, axis=-1, keepdims=True) * (1.0 / d)
    dx2 = dy + r * (dz - m1 - xh * m2)
    dx2_ref[...] = dx2
    da = dx2.astype(BF)
    da_ref[...] = da
    sums_ref[3:4, :] += jnp.sum(da.astype(F32), axis=0, keepdims=True)
    do_ref[...] = dg(da, w1_ref[:, :d], NT).astype(BF)


def mlp_back(idx, order_row, ret, gp, x2, vt, pieces, tb=256, fc=768):
    t, d = x2.shape
    ff = gp.shape[1]
    return pl.pallas_call(
        functools.partial(mlp_back_kernel, fc=fc),
        grid_spec=pltpu.PrefetchScalarGridSpec(
            num_scalar_prefetch=1,
            grid=(t // tb,),
            in_specs=[whole((1, t)), whole((t, d)), rows_of(tb, ff), rows_of(tb, d), whole(vt.shape)]
            + [ANY] * 8,
            out_specs=[
                rows_of(tb, d),
                rows_of(tb, ff),
                rows_of(tb, d),
                rows_of(tb, d),
                rows_of(tb, d),
                rows_of(tb, d),
                fixed((8, d)),
                fixed((1, ff)),
            ],
            scratch_shapes=[
                pltpu.VMEM((d, d + ff), BF),
                pltpu.VMEM((ff, d), BF),
                pltpu.SemaphoreType.DMA((2,)),
            ],
        ),
        out_shape=[
            SDS((t, d), BF),
            SDS((t, ff), BF),
            SDS((t, d), F32),
            SDS((t, d), BF),
            SDS((t, d), BF),
            SDS((t, d), BF),
            SDS((8, d), F32),
            SDS((1, ff), F32),
        ],
        compiler_params=params(),
        cost_estimate=cost(2 * t * d * (d + 2 * ff + t) * 1.5, t * (20 * d + 4 * ff)),
        name="mlp_back",
    )(idx, order_row, ret, gp, x2, vt, *pieces)


def split_halves(c, r, mine_ref, theirs_ref):
    h = r.shape[1] // 2
    left, right = r[:, :h], r[:, h:]
    mine_ref[...] = jnp.where(c == 0, left, right)
    theirs_ref[...] = jnp.where(c == 0, right, left)


def grad_down_kernel(idx_ref, g_ref, dm_ref, mine_ref, theirs_ref):
    split_halves(idx_ref[1], dg(g_ref[...], dm_ref[...], TN).astype(BF), mine_ref, theirs_ref)


def grad_down(idx, g, dm, mb=768):
    t, ff = g.shape
    d = dm.shape[1]
    return pl.pallas_call(
        grad_down_kernel,
        grid_spec=pltpu.PrefetchScalarGridSpec(
            num_scalar_prefetch=1,
            grid=(ff // mb,),
            in_specs=[pl.BlockSpec((t, mb), lambda i, _: (0, i)), whole((t, d))],
            out_specs=[rows_of(mb, d // 2)] * 2,
        ),
        out_shape=[SDS((ff, d // 2), BF)] * 2,
        compiler_params=params(),
        cost_estimate=cost(3 * t * ff * d, 2 * t * (ff + d) + 2 * ff * d),
        name="grad_down",
    )(idx, g, dm)


def grad_up_kernel(idx_ref, h2_ref, o_ref, du_ref, da_ref, mine_ref, theirs_ref, *, steps):
    i = pl.program_id(0)

    @pl.when(i < steps)
    def _():
        split_halves(idx_ref[1], dg(h2_ref[...], du_ref[...], TN).astype(BF), mine_ref, theirs_ref)

    @pl.when(i == steps)
    def _():
        split_halves(idx_ref[1], dg(o_ref[...], da_ref[...], TN).astype(BF), mine_ref, theirs_ref)


def grad_up(idx, h2, o, du, da):
    t, d = h2.shape
    ff = du.shape[1]
    steps = ff // d
    return pl.pallas_call(
        functools.partial(grad_up_kernel, steps=steps),
        grid_spec=pltpu.PrefetchScalarGridSpec(
            num_scalar_prefetch=1,
            grid=(steps + 1,),
            in_specs=[
                whole((t, d)),
                whole((t, d)),
                pl.BlockSpec((t, d), lambda i, _: (0, jnp.minimum(i, steps - 1))),
                whole((t, d)),
            ],
            out_specs=[pl.BlockSpec((d, d // 2), lambda i, _: (0, i))] * 2,
        ),
        out_shape=[SDS((d, (d + ff) // 2), BF)] * 2,
        compiler_params=params(),
        cost_estimate=cost(3 * t * (ff + d) * d, 2 * t * (ff + 3 * d) + 2 * ff * d),
        name="grad_up",
    )(idx, h2, o, du, da)


def attend_back_kernel(
    tag_ref, q_ref, k_ref, v_ref, do_ref, o_ref, l_ref, dq_ref, dk_ref, dv_ref, dl_ref, dqt_ref, *, kb, qb
):
    r = pl.program_id(0)
    length = q_ref.shape[0]
    low = lax.broadcasted_iota(jnp.int32, (1, 128), 1) < 64
    prod = (do_ref[...].astype(F32) * o_ref[...].astype(F32)).T
    dl_ref[0:1, :] = jnp.sum(prod[0:64], axis=0, keepdims=True)
    dl_ref[1:2, :] = jnp.sum(prod[64:128], axis=0, keepdims=True)

    def block(ks, kn, qs, qn):
        k = k_ref[pl.ds(ks, kn), :]
        v = v_ref[pl.ds(ks, kn), :]
        q = q_ref[pl.ds(qs, qn), :]
        do = do_ref[pl.ds(qs, qn), :]
        dks = []
        dvs = []
        dqs = []
        for h in range(2):
            sel = low if h == 0 else jnp.logical_not(low)
            km = jnp.where(sel, k, jnp.asarray(0, BF))
            vm = jnp.where(sel, v, jnp.asarray(0, BF))
            pt = jnp.exp2(dg(km, q, NT) - l_ref[0, 0, h : h + 1, pl.ds(qs, qn)])
            dst = (pt * (dg(vm, do, NT) - dl_ref[h : h + 1, pl.ds(qs, qn)])).astype(BF)
            dvs.append(dg(pt.astype(BF), do, NN))
            dks.append(dg(dst, q, NN))
            dqs.append(dg(km.T, dst, NN))
        return jnp.where(low, dks[0], dks[1]), jnp.where(low, dvs[0], dvs[1]), dqs[0] + dqs[1]

    def run(kn, qn, plan):
        seen = set()
        for ks, starts in plan:
            dk = dv = None
            for qs in starts:
                a, b, dq = block(ks, kn, qs, qn)
                dk = a if dk is None else dk + a
                dv = b if dv is None else dv + b
                if qs in seen:
                    dqt_ref[:, pl.ds(qs, qn)] += dq
                else:
                    dqt_ref[:, pl.ds(qs, qn)] = dq
                seen.add(qs)
            dk_ref[pl.ds(ks, kn), :] = (dk * LN2).astype(BF)
            dv_ref[pl.ds(ks, kn), :] = dv.astype(BF)
        dq_ref[...] = (dqt_ref[...].T * 0.125).astype(BF)

    @pl.when(tag_ref[r] == 0)
    def _():
        run(kb, qb, [(ks, range(0, length, qb)) for ks in range(0, length, kb)])

    @pl.when(tag_ref[r] != 0)
    def _():
        c = length // 4
        run(c, c, [(ks, [ks]) for ks in range(0, length, c)])


def attend_back(tag, q, k, v, do, o, lse, first, pairs, kb=512, qb=512):
    t = q.shape[0]
    d = pairs * 128
    rows = tag.shape[0]
    length = t // rows
    blk = pl.BlockSpec((length, 128), lambda r, p, _: (r, p + first))
    out = pl.BlockSpec((length, 128), lambda r, p, _: (r, p))
    lse_spec = pl.BlockSpec((1, 1, 2, length), lambda r, p, _: (r, p + first, 0, 0))
    return pl.pallas_call(
        functools.partial(attend_back_kernel, kb=kb, qb=qb),
        grid_spec=pltpu.PrefetchScalarGridSpec(
            num_scalar_prefetch=1,
            grid=(rows, pairs),
            in_specs=[blk] * 5 + [lse_spec],
            out_specs=[out] * 3,
            scratch_shapes=[pltpu.VMEM((2, length), F32), pltpu.VMEM((128, length), F32)],
        ),
        out_shape=[SDS((t, d), BF)] * 3,
        compiler_params=params(2),
        cost_estimate=cost(40 * t * length * d, t * d * 16, t * length * 12),
        name="attend_back",
    )(tag, q, k, v, do, o, lse)


def grad_qkv_kernel(idx_ref, h_ref, dq_ref, dk_ref, dv_ref, o_ref):
    w = dq_ref.shape[1]
    for m, ref in enumerate((dq_ref, dk_ref, dv_ref)):
        o_ref[:, m * w : (m + 1) * w] = dg(h_ref[...], ref[...], TN).astype(BF)


def grad_qkv(idx, h1, dq, dk, dv, other):
    t, d = h1.shape
    w = d // 2
    half = pl.BlockSpec((t, w), lambda i, ix: (0, lax.bitwise_xor(ix[1], jnp.int32(other))))
    return pl.pallas_call(
        grad_qkv_kernel,
        grid_spec=pltpu.PrefetchScalarGridSpec(
            num_scalar_prefetch=1,
            grid=(1,),
            in_specs=[whole((t, d)), half, half, half],
            out_specs=fixed((d, 3 * w)),
        ),
        out_shape=SDS((d, 3 * w), BF),
        compiler_params=params(),
        cost_estimate=cost(6 * t * d * w, t * d * 6),
        name="grad_qkv_other" if other else "grad_qkv_own",
    )(idx, h1, dq, dk, dv)


def tokens_back_kernel(idx_ref, x_ref, vt_ref, dx2_ref, dq_ref, dk_ref, dv_ref, *refs):
    pieces = refs[:2]
    tg_ref, s_ref, w_ref, sem = refs[2:]
    d = x_ref.shape[1]

    @pl.when(pl.program_id(0) == 0)
    def _():
        plan = [(0, 3 * d // 2, w_ref, pieces[0].shape[-2], 0, True)]
        going = load_pieces(idx_ref, pieces, plan, sem, True)
        s_ref[...] = jnp.zeros_like(s_ref)
        for cp in going:
            cp.wait()

    dh = dg(dq_ref[...], w_ref[:, :d], NT)
    dh = dh + dg(dk_ref[...], w_ref[:, d : 2 * d], NT)
    dh = dh + dg(dv_ref[...], w_ref[:, 2 * d :], NT)
    s_ref[2:3, :] += jnp.sum(dq_ref[...].astype(F32), axis=0, keepdims=True)
    s_ref[3:4, :] += jnp.sum(dv_ref[...].astype(F32), axis=0, keepdims=True)
    c, r = norm_stats(x_ref[...].astype(F32))
    xh = c * r
    s_ref[0:1, :] += jnp.sum(dh * xh, axis=0, keepdims=True)
    s_ref[1:2, :] += jnp.sum(dh, axis=0, keepdims=True)
    dz = dh * vt_ref[0:1, :]
    m1 = jnp.sum(dz, axis=-1, keepdims=True) * (1.0 / d)
    m2 = jnp.sum(dz * xh, axis=-1, keepdims=True) * (1.0 / d)
    tg_ref[...] = dx2_ref[...] + r * (dz - m1 - xh * m2)


def tokens_back(idx, dq, dk, dv, x, vt, dx2, pieces, tb=512):
    t, d = x.shape
    return pl.pallas_call(
        tokens_back_kernel,
        grid_spec=pltpu.PrefetchScalarGridSpec(
            num_scalar_prefetch=1,
            grid=(t // tb,),
            in_specs=[rows_of(tb, d), whole(vt.shape)] + [rows_of(tb, d)] * 4 + [ANY] * 2,
            out_specs=[rows_of(tb, d), fixed((8, d))],
            scratch_shapes=[pltpu.VMEM((d, 3 * d), BF), pltpu.SemaphoreType.DMA],
        ),
        out_shape=[SDS((t, d), F32), SDS((8, d), F32)],
        compiler_params=params(),
        cost_estimate=cost(9 * t * d * d, t * d * 16 + d * d * 6),
        name="tokens_back",
    )(idx, x, vt, dx2, dq, dk, dv, *pieces)


def sum_far_kernel(idx_ref, *refs, q, groups):
    outs = refs[2 * groups * q :]
    for e in range(q):
        start = 0
        for g in range(groups):
            a, b = refs[2 * g * q + e], refs[(2 * g + 1) * q + e]
            total = (a[0].astype(F32) + b[0].astype(F32)).astype(BF)
            rows = outs[e].shape[1]
            w = total.shape[1]
            for j in range(total.shape[0] // rows):
                outs[e][0, :, start : start + w] = total[j * rows : (j + 1) * rows]
                start += w


def reduce_far(idx, pairs, rows, n):
    q = n // 4
    ops, specs, width = [], [], 0

    def spec(e, shape):
        return pl.BlockSpec(
            (1,) + shape, lambda z, ix: (z * q + lax.bitwise_xor(ix[0] % q, jnp.int32(e)), 0, 0)
        )

    for pair in pairs:
        shape = (pair[0].shape[0] // n, pair[0].shape[1])
        width += shape[0] // rows * shape[1]
        for x in pair:
            ops += [x.reshape((n,) + shape)] * q
            specs += [spec(e, shape) for e in range(q)]
    outs = pl.pallas_call(
        functools.partial(sum_far_kernel, q=q, groups=len(pairs)),
        grid_spec=pltpu.PrefetchScalarGridSpec(
            num_scalar_prefetch=1,
            grid=(4,),
            in_specs=specs,
            out_specs=[pl.BlockSpec((1, rows, width), lambda z, ix: (z, 0, 0))] * q,
        ),
        out_shape=[SDS((4, rows, width), BF)] * q,
        compiler_params=params(),
        cost_estimate=cost(n * rows * width, n * rows * width * 6),
        name="sum_far",
    )(idx, *ops)
    return [outs[0]] + [xor_pp(outs[e], e, n) for e in range(1, q)]


def sum_parts_kernel(*refs):
    total = refs[0][...].astype(F32)
    for x in refs[1:-1]:
        total = total + x[...].astype(F32)
    refs[-1][...] = total.astype(BF)


def sum_parts(parts):
    shape = (1,) + parts[0].shape[1:]
    spec = pl.BlockSpec(shape, lambda i: (i, 0, 0))
    return pl.pallas_call(
        sum_parts_kernel,
        grid=(4,),
        in_specs=[spec] * len(parts),
        out_specs=spec,
        out_shape=SDS(parts[0].shape, BF),
        compiler_params=params(),
        cost_estimate=cost(4 * len(parts) * math.prod(shape), 8 * len(parts) * math.prod(shape)),
        name="sum_parts",
    )(*parts)


def sum_near_kernel(idx_ref, *refs, q, groups):
    outs = refs[4 * q * groups :]
    for d in range(4):
        start = 0
        for g in range(groups):
            at = (g * 4 + d) * q
            total = refs[at][0].astype(F32)
            for e in range(1, q):
                total = total + refs[at + e][0].astype(F32)
            w = total.shape[1]
            outs[d][:, start : start + w] = total.astype(BF)
            start += w


def reduce_near(idx, groups, n):
    q = n // 4
    ops, specs, width = [], [], 0

    def spec(d, shape):
        return pl.BlockSpec((1,) + shape, lambda i, ix: (lax.bitwise_xor(ix[0] // q, jnp.int32(d)), 0, 0))

    for parts in groups:
        shape = parts[0].shape[1:]
        rows = shape[0]
        width += shape[1]
        ops += list(parts) * 4
        specs += [spec(d, shape) for d in range(4) for _ in range(q)]
    near = pl.pallas_call(
        functools.partial(sum_near_kernel, q=q, groups=len(groups)),
        grid_spec=pltpu.PrefetchScalarGridSpec(
            num_scalar_prefetch=1,
            grid=(1,),
            in_specs=specs,
            out_specs=[fixed((rows, width))] * 4,
        ),
        out_shape=[SDS((rows, width), BF)] * 4,
        compiler_params=params(),
        cost_estimate=cost(n * rows * width, n * rows * width * 3),
        name="sum_near",
    )(idx, *ops)
    return [near[0]] + [xor_pp(near[d], d * q, n) for d in range(1, 4)]


def reduce_last(near, n, m):
    total = near[0].astype(F32)
    for x in near[1:]:
        total = total + x.astype(F32)
    return over_pairs(total, m)


def over_pairs(total, m):
    b = 2
    while b < m:
        total = total + lax.ppermute(total.astype(BF), "dp", [(i, i ^ b) for i in range(m)]).astype(F32)
        b *= 2
    return total


def vec_table_kernel(*refs):
    a, c, u, o = refs
    d = a.shape[1]
    rows = jnp.concatenate(
        [c[0:4, :], a[3:4, :], a[1:3, :], a[0:1, :], u[...], jnp.zeros((116, d), F32)], axis=0
    )
    o[...] = rows.T.astype(BF)


def vec_table(s_mlp, s_tok, gbu):
    d = s_mlp.shape[1]
    return pl.pallas_call(
        vec_table_kernel, out_shape=SDS((d, 128), BF), compiler_params=params(0), name="vec_table"
    )(s_mlp, s_tok, gbu)


def local(
    tokens,
    sensor_tag,
    owner_order,
    ln1_gain,
    ln1_bias,
    w_qkv,
    b_query,
    b_value,
    w_out,
    b_out,
    ln2_gain,
    ln2_bias,
    w_up,
    b_up,
    w_down,
    b_down,
    out_grad,
    *,
    n,
    m,
):
    t, d = tokens.shape
    ff = w_up.shape[1]
    rows = d // n
    wide = ff // d
    f = lax.axis_index("fsdp")
    c = lax.axis_index("dp") % 2
    idx = jnp.stack([f, c]).astype(jnp.int32)
    use = idx if rows % 16 == 0 and n == 16 else jnp.zeros_like(idx)

    def core_half(x):
        h = x.shape[1] // 2
        return jnp.where(c == 0, x[:, :h], x[:, h:])

    vec = jnp.stack([ln1_gain, ln1_bias, b_query, b_value, b_out, ln2_gain, ln2_bias, b_down], axis=1)
    vec = jnp.concatenate([vec, b_up.reshape(wide, rows).T], axis=1)
    vec = jnp.pad(vec, ((0, 0), (0, 128 - vec.shape[1])))
    shard_a = jnp.concatenate([core_half(w_qkv), vec], axis=1)
    shard_b = jnp.concatenate(
        [core_half(jnp.concatenate([w_out, w_up], axis=1))]
        + [core_half(w_down[j * rows : (j + 1) * rows]) for j in range(wide)],
        axis=1,
    )
    q = n // 4
    near_a = gather_near(shard_a, n)
    near_b = lax.all_to_all(
        jnp.broadcast_to(after(shard_b, near_a)[None], (4,) + shard_b.shape),
        "fsdp",
        split_axis=0,
        concat_axis=0,
        tiled=True,
        axis_index_groups=tops(n),
    )
    own_a = gather_far(near_a, n)
    everyone = jnp.arange(n)
    own_a = jnp.stack(own_a)
    pieces_a = [own_a, core_swap(own_a, m)]
    if use is not idx:
        pieces_a = settle([x[e] for x in pieces_a for e in range(q)], f ^ everyone, c, n)
        pieces_a = [jnp.stack(pieces_a[:4]), jnp.stack(pieces_a[4:])]
    own_b = gather_far(near_b, n)
    swap_b = [core_swap(near_b, m)]

    qh, kh, vh, h1, vt = qkv(use, after(tokens, near_b), pieces_a)
    mixed, lse = attend(sensor_tag, qh, kh, vh)
    bu = vt[8 : 8 + wide].reshape(wide, n, rows).transpose(1, 0, 2).reshape(1, ff)
    own_b = [after(x, mixed) for x in own_b]
    cast = after(out_grad.astype(BF), own_b)
    returned = lax.all_to_all(cast, "fsdp", split_axis=0, concat_axis=0, tiled=True)
    swap_b += [core_swap(x, m) for x in own_b[1:]]
    pieces_b = settle(own_b + swap_b, everyone // q * q + (everyone ^ f) % q, c, n, (d + ff) // 2)

    x2, active, slope, y = mlp(use, tokens, mixed, vt, bu, pieces_b)
    sent = permute(owner_order.reshape(t, 1), y)
    encoded = lax.all_to_all(sent, "fsdp", split_axis=0, concat_axis=0, tiled=True)

    returned = after(returned, sent)
    dm, du, dx2, da, do, h2, s_mlp, gbu = mlp_back(use, owner_order, returned, slope, x2, vt, pieces_b)
    gbu = gbu.reshape(n, wide, rows).transpose(1, 0, 2).reshape(wide, d)
    up_own, up_other = grad_up(idx, h2, mixed, du, da)
    up_recv = core_swap(up_other, m)
    down_own, down_other = grad_down(idx, *after((active, dm), up_own))
    down_recv = core_swap(down_other, m)
    encoded = after(encoded, down_own).astype(F32)
    up_recv, down_recv = after((up_recv, down_recv), encoded)
    far_b = reduce_far(idx, [(up_own, up_recv), (down_own, down_recv)], rows, n)
    do, gbu = after((do, gbu), far_b[0])
    dj = attend_back(sensor_tag, qh, kh, vh, do, mixed, lse, 0, d // 128)
    far_b = sum_parts(after(far_b, dj))
    total_b = lax.all_to_all(
        far_b, "fsdp", split_axis=0, concat_axis=0, tiled=True, axis_index_groups=tops(n)
    )
    dj = after(dj, far_b)
    qkv_other = grad_qkv(idx, h1, *dj, 1)
    qkv_recv = core_swap(qkv_other, m)
    qkv_own = grad_qkv(idx, after(h1, qkv_other), *dj, 0)
    far_a = reduce_far(idx, [(qkv_own, after(qkv_recv, qkv_own))], rows, n)
    tokens_grad, s_tok = tokens_back(use, *after(dj, far_a[0]), tokens, vt, dx2, pieces_a)
    table = vec_table(s_mlp, s_tok, gbu).reshape(4, q, rows, 128)
    far_v = [lax.dynamic_index_in_dim(table, (f % q) ^ e, 1, keepdims=False) for e in range(q)]
    far_v = [far_v[0]] + [xor_pp(far_v[e], e, n) for e in range(1, q)]
    total_b = over_pairs(jnp.sum(after(total_b, tokens_grad).astype(F32), axis=0), m).astype(BF)
    other_b = core_swap(total_b, m)

    near_a = reduce_near(idx, [far_a, far_v], n)
    total_a = reduce_last(near_a, n, m)
    other_a = core_swap(total_a.astype(BF), m)
    cut = 3 * d // 2
    vecs = (total_a[:, cut:] + other_a[:, cut:].astype(F32)).T
    total_a, other_a = total_a[:, :cut].astype(BF), other_a[:, :cut]

    def both(mine, other):
        first = c == 0
        return jnp.where(first, mine, other).astype(F32), jnp.where(first, other, mine).astype(F32)

    def join(pair, start, width, parts, axis=1):
        out = []
        for p in range(parts):
            at = slice(start + p * width, start + (p + 1) * width)
            out.append(jnp.concatenate([pair[0][:, at], pair[1][:, at]], axis=1))
        return jnp.concatenate(out, axis=axis)

    h = d // 2
    g_mlp = both(total_b, other_b)
    grad_qkv_out = join(both(total_a, other_a), 0, h, 3)
    grad_up_out = join(g_mlp, 0, h, wide)
    grad_out_out = join(g_mlp, ff // 2, h, 1)
    grad_down_out = join(g_mlp, (d + ff) // 2, h, wide, 0)
    return (
        encoded,
        tokens_grad,
        vecs[0],
        vecs[1],
        grad_qkv_out,
        vecs[2],
        vecs[3],
        grad_out_out,
        vecs[4],
        vecs[5],
        vecs[6],
        grad_up_out,
        vecs[8 : 8 + wide].reshape(ff // n),
        grad_down_out,
        vecs[7],
    )


def solution(mesh):
    n = mesh.shape["fsdp"]
    m = mesh.shape["dp"]
    both = P(("dp", "fsdp"), None)
    vec = P("fsdp")
    mat = P("fsdp", None)
    in_specs = (both, P(("dp", "fsdp")), both, vec, vec, mat, vec, vec, mat, vec, vec, vec, mat, vec, mat, vec, both)
    out_specs = (both, both, vec, vec, mat, vec, vec, mat, vec, vec, vec, mat, vec, mat, vec)
    return jax.shard_map(
        functools.partial(local, n=n, m=m), mesh=mesh, in_specs=in_specs, out_specs=out_specs, check_vma=False
    )
```

```python
import functools
import math

import jax
import jax.numpy as jnp
from jax import lax
from jax.experimental import pallas as pl
from jax.experimental.pallas import tpu as pltpu
from jax.sharding import PartitionSpec as P

F32 = jnp.float32
BF = jnp.bfloat16
EPS = 1e-6
LOG2E = math.log2(math.e)
LN2 = math.log(2.0)
NT = (((1,), (1,)), ((), ()))
TN = (((0,), (0,)), ((), ()))
NN = (((1,), (0,)), ((), ()))
ANY = pl.BlockSpec(memory_space=pl.ANY)
VECS = 16
SDS = jax.ShapeDtypeStruct


def dg(a, b, dims):
    return lax.dot_general(a, b, dims, preferred_element_type=F32)


def params(axes=1):
    return pltpu.CompilerParams(
        vmem_limit_bytes=58 * 2**20, dimension_semantics=("arbitrary",) * axes
    )


def cost(flops, nbytes, trans=0):
    return pl.CostEstimate(flops=int(flops) >> 10, bytes_accessed=int(nbytes) >> 10, transcendentals=int(trans) >> 10)


def rows_of(height, width):
    return pl.BlockSpec((height, width), lambda i, *_: (i, 0))


def whole(shape):
    zeros = (0,) * len(shape)
    return pl.BlockSpec(shape, lambda *_: zeros, pipeline_mode=pl.Buffered(1))


def fixed(shape):
    zeros = (0,) * len(shape)
    return pl.BlockSpec(shape, lambda *_: zeros)


def norm_stats(x):
    n = x.shape[-1]
    c = x - jnp.sum(x, axis=-1, keepdims=True) * (1.0 / n)
    var = jnp.sum(c * c, axis=-1, keepdims=True) * (1.0 / n)
    return c, lax.rsqrt(var + EPS)


def after(x, *deps):
    return lax.optimization_barrier((x,) + deps)[0]


def xor_pp(x, b, n):
    return lax.ppermute(x, "fsdp", [(i, i ^ b) for i in range(n)])


def core_swap(x, m):
    return lax.ppermute(x, "dp", [(i, i ^ 1) for i in range(m)])


def gather_near(x, n):
    q = n // 4
    return jnp.stack([x] + [xor_pp(x, d * q, n) for d in (1, 2, 3)])


def tops(n):
    q = n // 4
    return [[low + z * q for z in range(4)] for low in range(q)]


def gather_far(s, n):
    return [s] + [xor_pp(s, e, n) for e in range(1, n // 4)]


def fits(rows, n):
    return rows % 16 == 0 and n == 16


def settle(pieces, order, c, n, wide=None):
    q = n // 4
    rows, width = pieces[0].shape[1:]
    if fits(rows, n):
        return pieces
    height = n * rows // 16
    halves = []
    for side in (pieces[:q], pieces[q:]):
        rel = jnp.stack(side, axis=1).reshape((n, rows, width))
        whole_side = jnp.take(rel, order, axis=0)
        flat = whole_side.reshape(16, height, width)
        if wide is not None:
            cut = width * (wide + 1) // (2 * wide + 1)
            low = whole_side[..., cut:].reshape(n, rows, wide, -1).transpose(0, 2, 1, 3)
            low = low.reshape(16, wide, height, -1).transpose(0, 2, 1, 3).reshape(16, height, -1)
            flat = jnp.concatenate([flat[..., :cut], low], axis=2)
        halves.append(flat.reshape(4, 4, height, width))
    left, right = jnp.where(c == 0, halves[0], halves[1]), jnp.where(c == 0, halves[1], halves[0])
    return [side[:, e] for side in (left, right) for e in range(4)]


def load_pieces(idx_ref, plan, sem):
    c = idx_ref[1]
    started = []
    for find, shard, start, width, dst, height, first in plan:
        for e in range(4):
            for d in range(4):
                for block, h in zip(find(e, d), (c, 1 - c), strict=False):
                    rows = block.shape[0]
                    at = pl.ds(pl.multiple_of(shard(e, d) * height + first, 16), rows)
                    cols = pl.ds(pl.multiple_of(h * width, 128), width) if dst.shape[1] > width else slice(None)
                    started.append(pltpu.make_async_copy(block.at[:, pl.ds(start, width)], dst.at[at, cols], sem))
    for cp in started:
        cp.start()
    return started


def relative(idx_ref):
    return lambda e, d: lax.bitwise_xor(idx_ref[0], jnp.int32(d * 4 + e))


def by_top(idx_ref):
    return lambda e, d: lax.bitwise_xor(idx_ref[0] % 4, jnp.int32(e)) + d * 4


def load_qkv(idx_ref, pieces, w_ref, sem, vec_ref=None):
    def find(e, d):
        if len(pieces) == 8:
            return pieces[e].at[d], pieces[4 + e].at[d]
        return pieces[e].at[d], pieces[5].at[e - 1, d] if e else pieces[4].at[d]

    where = relative(idx_ref)
    rows, half = pieces[0].shape[1], w_ref.shape[1] // 2
    if vec_ref is not None:
        return load_pieces(idx_ref, [(lambda e, d: find(e, d)[:1], where, half, 128, vec_ref, rows, 0)], sem)
    return load_pieces(idx_ref, [(find, where, 0, half, w_ref, rows, 0)], sem)


def load_mlp(idx_ref, pieces, w1_ref, w2_ref, sem):
    where = by_top(idx_ref)

    def find1(e, d):
        return pieces[e // 2].at[e % 2, d], pieces[2 + e // 2].at[e % 2, d]

    def find2(e, d):
        return pieces[4 + e % 2].at[e // 2, d], pieces[6 + e % 2].at[e // 2, d]

    rows = pieces[0].shape[2]
    w = w2_ref.shape[1] // 2
    plan = [(find1, where, 0, w1_ref.shape[1] // 2, w1_ref, rows, 0)]
    plan += [(find2, where, j * w, w, w2_ref, 4 * rows, j * rows) for j in range(4)]
    return load_pieces(idx_ref, plan, sem.at[0])


def qkv_kernel(idx_ref, x_ref, *refs):
    pieces = refs[:-9]
    q_ref, k_ref, v_ref, h_ref, vt_ref, bu_ref, w_ref, vec_ref, sem = refs[-9:]
    d = x_ref.shape[1]

    @pl.when(pl.program_id(0) == 0)
    def _():
        rows = pieces[0].shape[1]
        vecs = load_qkv(idx_ref, pieces, w_ref, sem.at[1], vec_ref)
        going = load_qkv(idx_ref, pieces, w_ref, sem.at[0])
        for cp in vecs:
            cp.wait()
        table = vec_ref[...].astype(F32).T[:VECS]
        vt_ref[...] = table
        bu_ref[...] = jnp.concatenate(
            [table[8 + j : 9 + j, s * rows : (s + 1) * rows] for s in range(d // rows) for j in range(4)], axis=1
        )
        for cp in going:
            cp.wait()

    c, r = norm_stats(x_ref[...].astype(F32))
    h = (c * r * vt_ref[0:1, :] + vt_ref[1:2, :]).astype(BF)
    h_ref[...] = h
    q = dg(h, w_ref[:, :d], NN)
    q_ref[...] = ((q + vt_ref[2:3, :]) * (0.125 * LOG2E)).astype(BF)
    k_ref[...] = dg(h, w_ref[:, d : 2 * d], NN).astype(BF)
    v_ref[...] = (dg(h, w_ref[:, 2 * d :], NN) + vt_ref[3:4, :]).astype(BF)


def qkv(idx, x, pieces, tb=512):
    t, d = x.shape
    return pl.pallas_call(
        qkv_kernel,
        grid_spec=pltpu.PrefetchScalarGridSpec(
            num_scalar_prefetch=1,
            grid=(t // tb,),
            in_specs=[rows_of(tb, d)] + [ANY] * len(pieces),
            out_specs=[rows_of(tb, d)] * 4 + [fixed((VECS, d)), fixed((1, 4 * d))],
            scratch_shapes=[
                pltpu.VMEM((d, 3 * d), BF),
                pltpu.VMEM((d, 128), BF),
                pltpu.SemaphoreType.DMA((2,)),
            ],
        ),
        out_shape=[SDS((t, d), BF)] * 4 + [SDS((VECS, d), F32), SDS((1, 4 * d), F32)],
        compiler_params=params(),
        cost_estimate=cost(6 * t * d * d, t * d * 8 + d * d * 6),
        name="qkv",
    )(idx, x, *pieces)


def attend_kernel(tag_ref, q_ref, k_ref, v_ref, *refs, qb):
    o_ref, l_ref = refs[-2:]
    r = pl.program_id(0)
    length = q_ref.shape[0]
    low = lax.broadcasted_iota(jnp.int32, (1, 128), 1) < 64

    def block(qs, qn, ks, kn):
        q = q_ref[pl.ds(qs, qn), :]
        k = k_ref[pl.ds(ks, kn), :]
        v = v_ref[pl.ds(ks, kn), :]
        outs = []
        for h in range(2):
            sel = low if h == 0 else jnp.logical_not(low)
            qm = jnp.where(sel, q, jnp.asarray(0, BF))
            vm = jnp.where(sel, v, jnp.asarray(1, BF))
            s = dg(qm, k, NT)
            m = jnp.max(s, axis=1, keepdims=True)
            outs.append((dg(jnp.exp2(s - m).astype(BF), vm, NN), m))
        (a, ma), (b, mb) = outs
        acc = jnp.where(low, a, b)
        total = pltpu.roll(jnp.where(low, b, a), 64, 1)
        o_ref[pl.ds(qs, qn), :] = (acc / total).astype(o_ref.dtype)
        lse = (jnp.where(low, ma, mb) + jnp.log2(total)).T
        l_ref[0, 0, 0:1, pl.ds(qs, qn)] = lse[0:1]
        l_ref[0, 0, 1:2, pl.ds(qs, qn)] = lse[64:65]

    @pl.when(tag_ref[r] == 0)
    def _():
        for i in range(length // qb):
            block(i * qb, qb, 0, length)

    @pl.when(tag_ref[r] != 0)
    def _():
        c = length // 4
        for i in range(4):
            block(i * c, c, i * c, c)


def attend(tag, q, k, v, first, pairs, before=(), qb=512):
    t, d = q.shape
    rows = tag.shape[0]
    length = t // rows
    blk = pl.BlockSpec((length, 128), lambda r, p, _: (r, p + first))
    lse = pl.BlockSpec((1, 1, 2, length), lambda r, p, _: (r, p + first, 0, 0))
    return pl.pallas_call(
        functools.partial(attend_kernel, qb=qb),
        grid_spec=pltpu.PrefetchScalarGridSpec(
            num_scalar_prefetch=1,
            grid=(rows, pairs),
            in_specs=[blk] * 3 + [ANY] * len(before),
            out_specs=[blk, lse],
        ),
        out_shape=[SDS((t, d), BF), SDS((rows, d // 128, 2, length), F32)],
        input_output_aliases={4: 0, 5: 1} if before else {},
        compiler_params=params(2),
        cost_estimate=cost(2048 * t * length * pairs, t * d * 8, t * length * 12),
        name="attend",
    )(tag, q, k, v, *before)


ODDS = (2.3021649, 1.05007451e-1, -2.545477e-4, -1.0560537e-4, 4.093017e-6)


def gelu_both(u):
    z = u * u
    odds = ODDS[3] + z * ODDS[4]
    odds = ODDS[2] + z * odds
    odds = ODDS[1] + z * odds
    odds = ODDS[0] + z * odds
    phi = pltpu.reciprocal(1.0 + jnp.exp2(-u * odds), approx=True)
    density = jnp.exp2(z * (-0.5 * LOG2E) - 0.5 * math.log2(2.0 * math.pi))
    return u * phi, phi + u * density


def mlp_kernel(idx_ref, x_ref, o_ref, vt_ref, bu_ref, *refs, fc):
    pieces = refs[:8]
    x2_ref, gl_ref, gp_ref, y_ref, w1_ref, w2_ref, sem = refs[8:]
    d = x_ref.shape[1]
    ff = w2_ref.shape[0]

    @pl.when(pl.program_id(0) == 0)
    def _():
        going = load_mlp(idx_ref, pieces, w1_ref, w2_ref, sem)
        for cp in going:
            cp.wait()

    x2 = x_ref[...].astype(F32) + dg(o_ref[...], w1_ref[:, :d], NN) + vt_ref[4:5, :]
    x2_ref[...] = x2
    c, r = norm_stats(x2)
    h = (c * r * vt_ref[5:6, :] + vt_ref[6:7, :]).astype(BF)
    y = x2 + vt_ref[7:8, :]
    for f in range(0, ff, fc):
        u = dg(h, w1_ref[:, d + f : d + f + fc], NN) + bu_ref[:, f : f + fc]
        g, gp = gelu_both(u)
        g = g.astype(BF)
        gl_ref[:, f : f + fc] = g
        gp_ref[:, f : f + fc] = gp.astype(BF)
        y = y + dg(g, w2_ref[f : f + fc, :], NN)
    y_ref[...] = y.astype(BF)


def mlp(idx, x, o, vt, bu, pieces, tb=256, fc=768):
    t, d = x.shape
    ff = bu.shape[1]
    return pl.pallas_call(
        functools.partial(mlp_kernel, fc=fc),
        grid_spec=pltpu.PrefetchScalarGridSpec(
            num_scalar_prefetch=1,
            grid=(t // tb,),
            in_specs=[rows_of(tb, d)] * 2 + [whole(vt.shape), whole(bu.shape)] + [ANY] * 8,
            out_specs=[rows_of(tb, d), rows_of(tb, ff), rows_of(tb, ff), rows_of(tb, d)],
            scratch_shapes=[
                pltpu.VMEM((d, d + ff), BF),
                pltpu.VMEM((ff, d), BF),
                pltpu.SemaphoreType.DMA((2,)),
            ],
        ),
        out_shape=[SDS((t, d), F32), SDS((t, ff), BF), SDS((t, ff), BF), SDS((t, d), BF)],
        compiler_params=params(),
        cost_estimate=cost(4 * t * d * (d + 2 * ff), t * (10 * d + 4 * ff) + 4 * d * ff, 2 * t * ff),
        name="mlp",
    )(idx, x, o, vt, bu, *pieces)


def permute_kernel(ord_ref, y_ref, o_ref):
    jb = o_ref.shape[0]
    t = y_ref.shape[0]
    order = jnp.broadcast_to(ord_ref[...].astype(F32), (8, jb)).T[:, 0:1]
    hot = jnp.where(order == lax.broadcasted_iota(jnp.int32, (jb, t), 1).astype(F32), 1.0, 0.0)
    o_ref[...] = dg(hot.astype(BF), y_ref[...], NN).astype(BF)


def permute(order, y, jb=512):
    t, d = y.shape
    return pl.pallas_call(
        permute_kernel,
        grid=(t // jb,),
        in_specs=[pl.BlockSpec((1, jb), lambda i: (0, i)), whole((t, d))],
        out_specs=rows_of(jb, d),
        out_shape=SDS((t, d), BF),
        compiler_params=params(),
        cost_estimate=cost(2 * t * t * d, t * d * 4),
        name="permute",
    )(order, y)


def split_halves(c, r, mine_ref, theirs_ref):
    h = r.shape[1] // 2
    left, right = r[:, :h], r[:, h:]
    mine_ref[...] = jnp.where(c == 0, left, right)
    theirs_ref[...] = jnp.where(c == 0, right, left)


def mlp_back_kernel(idx_ref, ord_ref, ret_ref, gp_ref, x2_ref, o_ref, vt_ref, *refs, fc):
    pieces = refs[:8]
    (dm_ref, du_ref, dx2_ref, do_ref, h2_ref, sums_ref, gbu_ref, mine_ref, theirs_ref) = refs[8:17]
    w1_ref, w2_ref, acc_ref, sem = refs[17:]
    i = pl.program_id(0)
    tb, ff = gp_ref.shape
    t, d = ret_ref.shape

    @pl.when(i == 0)
    def _():
        going = load_mlp(idx_ref, pieces, w1_ref, w2_ref, sem)
        sums_ref[...] = jnp.zeros_like(sums_ref)
        gbu_ref[...] = jnp.zeros_like(gbu_ref)
        acc_ref[...] = jnp.zeros_like(acc_ref)
        for cp in going:
            cp.wait()

    at = lax.broadcasted_iota(jnp.int32, (tb, t), 0) + i * tb
    hot = jnp.where(ord_ref[...] == at, 1.0, 0.0).astype(BF)
    dy = dg(hot, ret_ref[...], NN)
    dm = dy.astype(BF)
    dm_ref[...] = dm
    sums_ref[0:1, :] += jnp.sum(dy, axis=0, keepdims=True)
    dh = jnp.zeros((tb, d), F32)
    for f in range(0, ff, fc):
        du = dg(dm, w2_ref[f : f + fc, :], NT) * gp_ref[:, f : f + fc].astype(F32)
        gbu_ref[:, f : f + fc] += jnp.sum(du, axis=0, keepdims=True)
        du = du.astype(BF)
        du_ref[:, f : f + fc] = du
        dh = dh + dg(du, w1_ref[:, d + f : d + f + fc], NT)
    c, r = norm_stats(x2_ref[...])
    xh = c * r
    gain = vt_ref[5:6, :]
    h2_ref[...] = (xh * gain + vt_ref[6:7, :]).astype(BF)
    sums_ref[1:2, :] += jnp.sum(dh * xh, axis=0, keepdims=True)
    sums_ref[2:3, :] += jnp.sum(dh, axis=0, keepdims=True)
    dz = dh * gain
    m1 = jnp.sum(dz, axis=-1, keepdims=True) * (1.0 / d)
    m2 = jnp.sum(dz * xh, axis=-1, keepdims=True) * (1.0 / d)
    dx2 = dy + r * (dz - m1 - xh * m2)
    dx2_ref[...] = dx2
    da = dx2.astype(BF)
    sums_ref[3:4, :] += jnp.sum(da.astype(F32), axis=0, keepdims=True)
    do_ref[...] = dg(da, w1_ref[:, :d], NT).astype(BF)
    acc_ref[...] += dg(o_ref[...], da, TN)

    @pl.when(i == pl.num_programs(0) - 1)
    def _():
        split_halves(idx_ref[1], acc_ref[...].astype(BF), mine_ref, theirs_ref)


def mlp_back(idx, order_row, ret, gp, x2, o, vt, pieces, tb=256, fc=768):
    t, d = x2.shape
    ff = gp.shape[1]
    return pl.pallas_call(
        functools.partial(mlp_back_kernel, fc=fc),
        grid_spec=pltpu.PrefetchScalarGridSpec(
            num_scalar_prefetch=1,
            grid=(t // tb,),
            in_specs=[whole((1, t)), whole((t, d)), rows_of(tb, ff), rows_of(tb, d), rows_of(tb, d), whole(vt.shape)]
            + [ANY] * 8,
            out_specs=[rows_of(tb, d), rows_of(tb, ff)]
            + [rows_of(tb, d)] * 3
            + [fixed((8, d)), fixed((1, ff))]
            + [fixed((d, d // 2))] * 2,
            scratch_shapes=[
                pltpu.VMEM((d, d + ff), BF),
                pltpu.VMEM((ff, d), BF),
                pltpu.VMEM((d, d), F32),
                pltpu.SemaphoreType.DMA((2,)),
            ],
        ),
        out_shape=[
            SDS((t, d), BF),
            SDS((t, ff), BF),
            SDS((t, d), F32),
            SDS((t, d), BF),
            SDS((t, d), BF),
            SDS((8, d), F32),
            SDS((1, ff), F32),
            SDS((d, d // 2), BF),
            SDS((d, d // 2), BF),
        ],
        compiler_params=params(),
        cost_estimate=cost(2 * t * d * (d + 2 * ff + t) * 1.5, t * (20 * d + 4 * ff)),
        name="mlp_back",
    )(idx, order_row, ret, gp, x2, o, vt, *pieces)


def grad_down_kernel(idx_ref, g_ref, dm_ref, mine_ref, theirs_ref):
    split_halves(idx_ref[1], dg(g_ref[...], dm_ref[...], TN).astype(BF), mine_ref, theirs_ref)


def grad_down(idx, g, dm, mb=768):
    t, ff = g.shape
    d = dm.shape[1]
    return pl.pallas_call(
        grad_down_kernel,
        grid_spec=pltpu.PrefetchScalarGridSpec(
            num_scalar_prefetch=1,
            grid=(ff // mb,),
            in_specs=[pl.BlockSpec((t, mb), lambda i, _: (0, i)), whole((t, d))],
            out_specs=[rows_of(mb, d // 2)] * 2,
        ),
        out_shape=[SDS((ff, d // 2), BF)] * 2,
        compiler_params=params(),
        cost_estimate=cost(3 * t * ff * d, 2 * t * (ff + d) + 2 * ff * d),
        name="grad_down",
    )(idx, g, dm)


def grad_wide_kernel(idx_ref, a_ref, b_ref, mine_ref, theirs_ref):
    split_halves(idx_ref[1], dg(a_ref[...], b_ref[...], TN).astype(BF), mine_ref, theirs_ref)


def grad_wide(idx, a, b, name):
    t, d = a.shape
    width = b.shape[1]
    return pl.pallas_call(
        grad_wide_kernel,
        grid_spec=pltpu.PrefetchScalarGridSpec(
            num_scalar_prefetch=1,
            grid=(width // d,),
            in_specs=[whole((t, d)), pl.BlockSpec((t, d), lambda i, _: (0, i))],
            out_specs=[pl.BlockSpec((d, d // 2), lambda i, _: (0, i))] * 2,
        ),
        out_shape=[SDS((d, width // 2), BF)] * 2,
        compiler_params=params(),
        cost_estimate=cost(3 * t * width * d, 2 * t * (width + d) + 2 * width * d),
        name=name,
    )(idx, a, b)


def attend_back_kernel(
    tag_ref, q_ref, k_ref, v_ref, do_ref, o_ref, l_ref, dq_ref, dk_ref, dv_ref, dl_ref, dqt_ref, *, kb, qb
):
    r = pl.program_id(0)
    length = q_ref.shape[0]
    low = lax.broadcasted_iota(jnp.int32, (1, 128), 1) < 64
    prod = (do_ref[...].astype(F32) * o_ref[...].astype(F32)).T
    dl_ref[0:1, :] = jnp.sum(prod[0:64], axis=0, keepdims=True)
    dl_ref[1:2, :] = jnp.sum(prod[64:128], axis=0, keepdims=True)

    def block(ks, kn, qs, qn):
        k = k_ref[pl.ds(ks, kn), :]
        v = v_ref[pl.ds(ks, kn), :]
        q = q_ref[pl.ds(qs, qn), :]
        do = do_ref[pl.ds(qs, qn), :]
        dks = []
        dvs = []
        dqs = []
        for h in range(2):
            sel = low if h == 0 else jnp.logical_not(low)
            km = jnp.where(sel, k, jnp.asarray(0, BF))
            vm = jnp.where(sel, v, jnp.asarray(0, BF))
            pt = jnp.exp2(dg(km, q, NT) - l_ref[0, 0, h : h + 1, pl.ds(qs, qn)])
            dst = (pt * (dg(vm, do, NT) - dl_ref[h : h + 1, pl.ds(qs, qn)])).astype(BF)
            dvs.append(dg(pt.astype(BF), do, NN))
            dks.append(dg(dst, q, NN))
            dqs.append(dg(km.T, dst, NN))
        return jnp.where(low, dks[0], dks[1]), jnp.where(low, dvs[0], dvs[1]), dqs[0] + dqs[1]

    def run(kn, qn, plan):
        seen = set()
        for ks, starts in plan:
            dk = dv = None
            for qs in starts:
                a, b, dq = block(ks, kn, qs, qn)
                dk = a if dk is None else dk + a
                dv = b if dv is None else dv + b
                if qs in seen:
                    dqt_ref[:, pl.ds(qs, qn)] += dq
                else:
                    dqt_ref[:, pl.ds(qs, qn)] = dq
                seen.add(qs)
            dk_ref[pl.ds(ks, kn), :] = (dk * LN2).astype(BF)
            dv_ref[pl.ds(ks, kn), :] = dv.astype(BF)
        dq_ref[...] = (dqt_ref[...].T * 0.125).astype(BF)

    @pl.when(tag_ref[r] == 0)
    def _():
        run(kb, qb, [(ks, range(0, length, qb)) for ks in range(0, length, kb)])

    @pl.when(tag_ref[r] != 0)
    def _():
        c = length // 4
        run(c, c, [(ks, [ks]) for ks in range(0, length, c)])


def attend_back(tag, q, k, v, do, o, lse, first, pairs, kb=512, qb=512):
    t = q.shape[0]
    d = pairs * 128
    rows = tag.shape[0]
    length = t // rows
    blk = pl.BlockSpec((length, 128), lambda r, p, _: (r, p + first))
    out = pl.BlockSpec((length, 128), lambda r, p, _: (r, p))
    lse_spec = pl.BlockSpec((1, 1, 2, length), lambda r, p, _: (r, p + first, 0, 0))
    return pl.pallas_call(
        functools.partial(attend_back_kernel, kb=kb, qb=qb),
        grid_spec=pltpu.PrefetchScalarGridSpec(
            num_scalar_prefetch=1,
            grid=(rows, pairs),
            in_specs=[blk] * 5 + [lse_spec],
            out_specs=[out] * 3,
            scratch_shapes=[pltpu.VMEM((2, length), F32), pltpu.VMEM((128, length), F32)],
        ),
        out_shape=[SDS((t, d), BF)] * 3,
        compiler_params=params(2),
        cost_estimate=cost(40 * t * length * d, t * d * 16, t * length * 12),
        name="attend_back",
    )(tag, q, k, v, do, o, lse)


def grad_qkv_kernel(idx_ref, h_ref, dq_ref, dk_ref, dv_ref, *refs, rows):
    w = dq_ref.shape[1]
    for m, ref in enumerate((dq_ref, dk_ref, dv_ref)):
        at = slice(m * w, (m + 1) * w)
        part = dg(h_ref[...], ref[...], TN)
        if rows is None:
            refs[0][:, at] = part.astype(BF)
        else:
            outs, sum_ref = refs[1:-1], refs[-1]
            q = len(outs)
            sum_ref[...] = part + refs[0][:, at].astype(F32)
            for e in range(q):
                for z in range(4):
                    s = z * q + lax.bitwise_xor(idx_ref[0] % q, jnp.int32(e))
                    outs[e][z, :, at] = sum_ref[pl.ds(pl.multiple_of(s * rows, 8), rows), :].astype(BF)


def grad_qkv(idx, h1, dq, dk, dv, recv=None, n=None):
    t, d = h1.shape
    w = d // 2
    own = recv is not None
    half = pl.BlockSpec((t, w), lambda i, ix: (0, lax.bitwise_xor(ix[1], jnp.int32(0 if own else 1))))
    outs = [(4, d // n, 3 * w)] * (n // 4) if own else [(d, 3 * w)]
    return pl.pallas_call(
        functools.partial(grad_qkv_kernel, rows=d // n if own else None),
        grid_spec=pltpu.PrefetchScalarGridSpec(
            num_scalar_prefetch=1,
            grid=(1,),
            in_specs=[whole((t, d)), half, half, half] + [whole((d, 3 * w))] * own,
            out_specs=[fixed(o) for o in outs],
            scratch_shapes=[pltpu.VMEM((d, w), F32)] * own,
        ),
        out_shape=[SDS(o, BF) for o in outs],
        compiler_params=params(),
        cost_estimate=cost(6 * t * d * w, t * d * 6),
        name="grad_qkv_own" if own else "grad_qkv_other",
    )(idx, h1, dq, dk, dv, *([recv] * own))


def tokens_back_kernel(idx_ref, x_ref, vt_ref, dx2_ref, dq_ref, dk_ref, dv_ref, *refs):
    pieces = refs[:-4]
    tg_ref, s_ref, w_ref, sem = refs[-4:]
    d = x_ref.shape[1]

    @pl.when(pl.program_id(0) == 0)
    def _():
        going = load_qkv(idx_ref, pieces, w_ref, sem)
        s_ref[...] = jnp.zeros_like(s_ref)
        for cp in going:
            cp.wait()

    dh = dg(dq_ref[...], w_ref[:, :d], NT)
    dh = dh + dg(dk_ref[...], w_ref[:, d : 2 * d], NT)
    dh = dh + dg(dv_ref[...], w_ref[:, 2 * d :], NT)
    s_ref[2:3, :] += jnp.sum(dq_ref[...].astype(F32), axis=0, keepdims=True)
    s_ref[3:4, :] += jnp.sum(dv_ref[...].astype(F32), axis=0, keepdims=True)
    c, r = norm_stats(x_ref[...].astype(F32))
    xh = c * r
    s_ref[0:1, :] += jnp.sum(dh * xh, axis=0, keepdims=True)
    s_ref[1:2, :] += jnp.sum(dh, axis=0, keepdims=True)
    dz = dh * vt_ref[0:1, :]
    m1 = jnp.sum(dz, axis=-1, keepdims=True) * (1.0 / d)
    m2 = jnp.sum(dz * xh, axis=-1, keepdims=True) * (1.0 / d)
    tg_ref[...] = dx2_ref[...] + r * (dz - m1 - xh * m2)


def tokens_back(idx, dq, dk, dv, x, vt, dx2, pieces, tb=512):
    t, d = x.shape
    return pl.pallas_call(
        tokens_back_kernel,
        grid_spec=pltpu.PrefetchScalarGridSpec(
            num_scalar_prefetch=1,
            grid=(t // tb,),
            in_specs=[rows_of(tb, d), whole(vt.shape)] + [rows_of(tb, d)] * 4 + [ANY] * len(pieces),
            out_specs=[rows_of(tb, d), fixed((8, d))],
            scratch_shapes=[pltpu.VMEM((d, 3 * d), BF), pltpu.SemaphoreType.DMA],
        ),
        out_shape=[SDS((t, d), F32), SDS((8, d), F32)],
        compiler_params=params(),
        cost_estimate=cost(9 * t * d * d, t * d * 16 + d * d * 6),
        name="tokens_back",
    )(idx, x, vt, dx2, dq, dk, dv, *pieces)


def hop(x, groups):
    return lax.all_to_all(x, "fsdp", split_axis=0, concat_axis=0, tiled=True, axis_index_groups=groups)


def sum_cores_kernel(idx_ref, *refs, q):
    outs = refs[-q:]
    rows = outs[0].shape[1]
    for e in range(q):
        at = lax.bitwise_xor(idx_ref[0] % q, jnp.int32(e))
        start = 0
        for a_ref, b_ref in zip(refs[:-q:2], refs[1:-q:2], strict=True):
            total = (a_ref[at].astype(F32) + b_ref[at].astype(F32)).astype(BF)
            w = total.shape[1]
            for j in range(total.shape[0] // rows):
                outs[e][0, :, start : start + w] = total[j * rows : (j + 1) * rows]
                start += w


def sum_cores(idx, pairs, rows, n):
    q = n // 4
    ops, specs, width = [], [], 0
    for pair in pairs:
        shape = (pair[0].shape[0] // n, pair[0].shape[1])
        width += shape[0] // rows * shape[1]
        ops += [x.reshape((n,) + shape) for x in pair]
        specs += [pl.BlockSpec((q,) + shape, lambda z, _: (z, 0, 0))] * 2
    return pl.pallas_call(
        functools.partial(sum_cores_kernel, q=q),
        grid_spec=pltpu.PrefetchScalarGridSpec(
            num_scalar_prefetch=1,
            grid=(4,),
            in_specs=specs,
            out_specs=[pl.BlockSpec((1, rows, width), lambda z, _: (z, 0, 0))] * q,
        ),
        out_shape=[SDS((4, rows, width), BF)] * q,
        compiler_params=params(),
        cost_estimate=cost(n * rows * width, n * rows * width * 6),
        name="sum_cores",
    )(idx, *ops)


def spread(parts, n):
    return [parts[0]] + [xor_pp(parts[e], e, n) for e in range(1, n // 4)]


def sum_parts_kernel(*refs):
    total = refs[0][...].astype(F32)
    for x in refs[1:-1]:
        total = total + x[...].astype(F32)
    refs[-1][...] = total.astype(BF)


def sum_parts(parts):
    shape = (1,) + parts[0].shape[1:]
    spec = pl.BlockSpec(shape, lambda i: (i, 0, 0))
    return pl.pallas_call(
        sum_parts_kernel,
        grid=(4,),
        in_specs=[spec] * len(parts),
        out_specs=spec,
        out_shape=SDS(parts[0].shape, BF),
        compiler_params=params(),
        cost_estimate=cost(4 * len(parts) * math.prod(shape), 8 * len(parts) * math.prod(shape)),
        name="sum_parts",
    )(*parts)


def sum_qkv_kernel(idx_ref, *refs, q):
    for d in range(4):
        at = lax.bitwise_xor(idx_ref[0] // q, jnp.int32(d))
        start = 0
        for parts in (refs[:q], refs[q : 2 * q]):
            total = parts[0][at].astype(F32)
            for x in parts[1:]:
                total = total + x[at].astype(F32)
            w = total.shape[1]
            refs[2 * q + d][:, start : start + w] = total.astype(BF)
            start += w


def sum_qkv(idx, far, vecs, n):
    _, rows, w = far[0].shape
    width = w + vecs[0].shape[2]
    ops = list(far) + list(vecs)
    near = pl.pallas_call(
        functools.partial(sum_qkv_kernel, q=n // 4),
        grid_spec=pltpu.PrefetchScalarGridSpec(
            num_scalar_prefetch=1,
            grid=(1,),
            in_specs=[whole(x.shape) for x in ops],
            out_specs=[fixed((rows, width))] * 4,
        ),
        out_shape=[SDS((rows, width), BF)] * 4,
        compiler_params=params(),
        cost_estimate=cost(n * rows * width, n * rows * width * 3),
        name="sum_qkv",
    )(idx, *ops)
    return near


def reduce_last(near, n, m):
    total = near[0].astype(F32)
    for x in near[1:]:
        total = total + x.astype(F32)
    return over_pairs(total, m)


def over_pairs(total, m):
    b = 2
    while b < m:
        total = total + lax.ppermute(total.astype(BF), "dp", [(i, i ^ b) for i in range(m)]).astype(F32)
        b *= 2
    return total


def vec_table_kernel(idx_ref, a, c, u, *refs, q):
    table_ref = refs[q]
    d = a.shape[1]
    rows = refs[0].shape[1]
    wide = u.shape[1] // d
    bias = [
        jnp.concatenate(
            [u[:, (s * wide + j) * rows : (s * wide + j + 1) * rows] for s in range(4 * q)], axis=1
        )
        for j in range(wide)
    ]
    lines = [c[0:4, :], a[3:4, :], a[1:3, :], a[0:1, :]] + bias + [jnp.zeros((120 - wide, d), F32)]
    table_ref[...] = jnp.concatenate(lines, axis=0).T
    for e in range(q):
        for z in range(4):
            s = z * q + lax.bitwise_xor(idx_ref[0] % q, jnp.int32(e))
            refs[e][z] = table_ref[pl.ds(pl.multiple_of(s * rows, 8), rows), :].astype(BF)


def vec_table(idx, s_mlp, s_tok, gbu, n):
    d = s_mlp.shape[1]
    q = n // 4
    return pl.pallas_call(
        functools.partial(vec_table_kernel, q=q),
        grid_spec=pltpu.PrefetchScalarGridSpec(
            num_scalar_prefetch=1,
            grid=(1,),
            in_specs=[whole(s_mlp.shape), whole(s_tok.shape), whole(gbu.shape)],
            out_specs=[fixed((4, d // n, 128))] * q,
            scratch_shapes=[pltpu.VMEM((d, 128), F32)],
        ),
        out_shape=[SDS((4, d // n, 128), BF)] * q,
        compiler_params=params(),
        cost_estimate=cost(d * 128, d * 1024),
        name="vec_table",
    )(idx, s_mlp, s_tok, gbu)


def local(
    tokens,
    sensor_tag,
    owner_order,
    ln1_gain,
    ln1_bias,
    w_qkv,
    b_query,
    b_value,
    w_out,
    b_out,
    ln2_gain,
    ln2_bias,
    w_up,
    b_up,
    w_down,
    b_down,
    out_grad,
    *,
    n,
    m,
):
    t, d = tokens.shape
    ff = w_up.shape[1]
    rows = d // n
    wide = ff // d
    f = lax.axis_index("fsdp")
    c = lax.axis_index("dp") % 2
    idx = jnp.stack([f, c]).astype(jnp.int32)
    use = idx if fits(rows, n) else jnp.zeros_like(idx)

    def core_half(x):
        h = x.shape[1] // 2
        return jnp.where(c == 0, x[:, :h], x[:, h:])

    vec = jnp.stack([ln1_gain, ln1_bias, b_query, b_value, b_out, ln2_gain, ln2_bias, b_down], axis=1)
    vec = jnp.concatenate([vec, b_up.reshape(wide, rows).T], axis=1)
    vec = jnp.pad(vec, ((0, 0), (0, 128 - vec.shape[1])))
    shard_a = jnp.concatenate([core_half(w_qkv), vec], axis=1)
    shard_b = jnp.concatenate(
        [core_half(jnp.concatenate([w_out, w_up], axis=1))]
        + [core_half(w_down[j * rows : (j + 1) * rows]) for j in range(wide)],
        axis=1,
    )
    q = n // 4
    everyone = jnp.arange(n)

    near_a = gather_near(shard_a, n)
    near_b = hop(jnp.broadcast_to(after(shard_b, near_a)[None], (4,) + shard_b.shape), tops(n))
    own_a = gather_far(near_a, n)
    cast = after(out_grad, near_a).astype(BF)
    own_a[1:] = after(own_a[1:], cast)
    swap_a = [core_swap(near_a, m), core_swap(jnp.stack(own_a[1:]), m)]
    if fits(rows, n):
        pieces_a = own_a + swap_a
    else:
        pieces_a = settle(own_a + swap_a[:1] + [swap_a[1][e] for e in range(q - 1)], f ^ everyone, c, n)
    near_b = after(near_b, own_a[1:])
    qh, kh, vh, h1, vt, bu = qkv(use, after(tokens, near_b), pieces_a)
    pairs = d // 128
    early = pairs * 2 // 3
    if fits(rows, n):
        first = [near_b[..., : (d + ff) // 2], near_b[..., (d + ff) // 2 :]]
        bits = (1, 2)
        second = [xor_pp(x, b, n) for x, b in zip(first, bits, strict=True)]
        both_b = [jnp.stack([x, y]) for x, y in zip(first, after(second, vt), strict=True)]
        far_b = [xor_pp(x, b, n) for x, b in zip(both_b, bits[::-1], strict=True)]
        part = attend(sensor_tag, after(qh, both_b), kh, vh, 0, early)
        far_b = after(far_b, part[0])
        pieces_b = []
        for x, y in zip(both_b, far_b, strict=True):
            pieces_b += [x, y, core_swap(x, m), core_swap(y, m)]
    else:
        far_b = gather_far(near_b, n)
        side = settle(
            far_b + [core_swap(x, m) for x in far_b], everyone // q * q + (everyone ^ f) % q, c, n, wide
        )
        part = attend(sensor_tag, qh, kh, vh, 0, early)
        cut = (d + ff) // 2
        one = [x[..., :cut] for x in side]
        two = [x[..., cut:] for x in side]
        pieces_b = [jnp.stack(one[i : i + 2]) for i in (0, 2, 4, 6)]
        pieces_b += [jnp.stack([two[i], two[i + 2]]) for i in (0, 1, 4, 5)]
    returned = lax.all_to_all(after(cast, far_b), "fsdp", split_axis=0, concat_axis=0, tiled=True)
    mixed, lse = attend(sensor_tag, qh, kh, vh, early, pairs - early, part)

    x2, active, slope, y = mlp(use, tokens, mixed, vt, bu, pieces_b)
    sent = permute(owner_order, y)
    encoded = lax.all_to_all(sent, "fsdp", split_axis=0, concat_axis=0, tiled=True)

    returned = after(returned, sent)
    dm, du, dx2, do, h2, s_mlp, gbu, out_own, out_other = mlp_back(
        use, owner_order, returned, slope, x2, mixed, vt, pieces_b
    )
    out_recv = core_swap(out_other, m)
    down_own, down_other = grad_down(idx, active, dm)
    down_recv = core_swap(down_other, m)
    up_own, up_other = grad_wide(idx, after(h2, down_own), du, "grad_up")
    up_recv = core_swap(up_other, m)
    encoded = after(encoded, up_own).astype(F32)
    out_recv, down_recv, up_recv = after((out_recv, down_recv, up_recv), encoded)
    pairs = [(up_own, up_recv), (out_own, out_recv), (down_own, down_recv)]
    far_b = sum_cores(idx, pairs, rows, n)
    do = after(do, far_b[0])
    far_b = spread(far_b, n)
    dj = attend_back(sensor_tag, qh, kh, vh, do, mixed, lse, 0, d // 128)
    (qkv_other,) = grad_qkv(idx, h1, *dj)
    qkv_recv = core_swap(qkv_other, m)
    far_b = after(far_b, dj[0])
    near_b = sum_parts([after(far_b[0], qkv_other)] + far_b[1:])
    total_b = hop(near_b, tops(n))
    far_a = grad_qkv(idx, after(h1, near_b), *dj, qkv_recv, n)
    dj = after(dj, far_a[0])
    far_a = spread(far_a, n)
    tokens_grad, s_tok = tokens_back(use, *dj, tokens, vt, dx2, pieces_a)
    far_a, total_b = after((far_a, total_b), tokens_grad)
    total_b = over_pairs(jnp.sum(total_b.astype(F32), axis=0), m).astype(BF)
    other_b = core_swap(total_b, m)
    far_v = spread(vec_table(idx, s_mlp, s_tok, after(gbu, far_a), n), n)

    near_a = sum_qkv(idx, after(far_a, total_b), far_v, n)
    near_a = [near_a[0]] + [xor_pp(near_a[i], i * q, n) for i in range(1, 4)]
    def both(mine, other):
        first = c == 0
        return jnp.where(first, mine, other).astype(F32), jnp.where(first, other, mine).astype(F32)

    def join(pair, start, width, parts, axis=1):
        out = []
        for p in range(parts):
            at = slice(start + p * width, start + (p + 1) * width)
            out.append(jnp.concatenate([pair[0][:, at], pair[1][:, at]], axis=1))
        return jnp.concatenate(out, axis=axis)

    h = d // 2
    g_mlp = both(total_b, other_b)
    grad_up_out = join(g_mlp, 0, h, wide)
    grad_out_out = join(g_mlp, ff // 2, h, 1)
    grad_down_out = join(g_mlp, (d + ff) // 2, h, wide, 0)
    near_a = after(near_a, grad_up_out, grad_out_out, grad_down_out)
    total_a = reduce_last(near_a, n, m)
    other_a = core_swap(total_a.astype(BF), m)
    cut = 3 * d // 2
    vecs = (total_a[:, cut:] + other_a[:, cut:].astype(F32)).T
    total_a, other_a = total_a[:, :cut].astype(BF), other_a[:, :cut]

    grad_qkv_out = join(both(total_a, other_a), 0, h, 3)
    return (
        encoded,
        tokens_grad,
        vecs[0],
        vecs[1],
        grad_qkv_out,
        vecs[2],
        vecs[3],
        grad_out_out,
        vecs[4],
        vecs[5],
        vecs[6],
        grad_up_out,
        vecs[8 : 8 + wide].reshape(ff // n),
        grad_down_out,
        vecs[7],
    )


def solution(mesh):
    n = mesh.shape["fsdp"]
    m = mesh.shape["dp"]
    both = P(("dp", "fsdp"), None)
    vec = P("fsdp")
    mat = P("fsdp", None)
    in_specs = (both, P(("dp", "fsdp")), both, vec, vec, mat, vec, vec, mat, vec, vec, vec, mat, vec, mat, vec, both)
    out_specs = (both, both, vec, vec, mat, vec, vec, mat, vec, vec, vec, mat, vec, mat, vec)
    return jax.shard_map(
        functools.partial(local, n=n, m=m), mesh=mesh, in_specs=in_specs, out_specs=out_specs, check_vma=False
    )
```

```python
import functools
import math

import jax
import jax.numpy as jnp
from jax import lax
from jax.experimental import pallas as pl
from jax.experimental.pallas import tpu as pltpu
from jax.sharding import PartitionSpec as P

F32 = jnp.float32
BF = jnp.bfloat16
EPS = 1e-6
LOG2E = math.log2(math.e)
LN2 = math.log(2.0)
NT = (((1,), (1,)), ((), ()))
TN = (((0,), (0,)), ((), ()))
NN = (((1,), (0,)), ((), ()))
ANY = pl.BlockSpec(memory_space=pl.ANY)
VECS = 16
SDS = jax.ShapeDtypeStruct


def dg(a, b, dims):
    return lax.dot_general(a, b, dims, preferred_element_type=F32)


def params(axes=1):
    return pltpu.CompilerParams(
        vmem_limit_bytes=58 * 2**20, dimension_semantics=("arbitrary",) * axes
    )


def cost(flops, nbytes, trans=0):
    return pl.CostEstimate(flops=int(flops) >> 10, bytes_accessed=int(nbytes) >> 10, transcendentals=int(trans) >> 10)


def rows_of(height, width):
    return pl.BlockSpec((height, width), lambda i, *_: (i, 0))


def whole(shape):
    zeros = (0,) * len(shape)
    return pl.BlockSpec(shape, lambda *_: zeros, pipeline_mode=pl.Buffered(1))


def fixed(shape):
    zeros = (0,) * len(shape)
    return pl.BlockSpec(shape, lambda *_: zeros)


def norm_stats(x):
    n = x.shape[-1]
    c = x - jnp.sum(x, axis=-1, keepdims=True) * (1.0 / n)
    var = jnp.sum(c * c, axis=-1, keepdims=True) * (1.0 / n)
    return c, lax.rsqrt(var + EPS)


def after(x, *deps):
    return lax.optimization_barrier((x,) + deps)[0]


def xor_pp(x, b, n):
    return lax.ppermute(x, "fsdp", [(i, i ^ b) for i in range(n)])


def core_swap(x, m):
    return lax.ppermute(x, "dp", [(i, i ^ 1) for i in range(m)])


def gather_near(x, n):
    q = n // 4
    return jnp.stack([x] + [xor_pp(x, d * q, n) for d in (1, 2, 3)])


def tops(n):
    q = n // 4
    return [[low + z * q for z in range(4)] for low in range(q)]


def gather_far(s, n):
    return [s] + [xor_pp(s, e, n) for e in range(1, n // 4)]


def fits(rows, n):
    return rows % 16 == 0 and n == 16


def settle(pieces, order, c, n, wide=None):
    q = n // 4
    rows, width = pieces[0].shape[1:]
    if fits(rows, n):
        return pieces
    height = n * rows // 16
    halves = []
    for side in (pieces[:q], pieces[q:]):
        rel = jnp.stack(side, axis=1).reshape((n, rows, width))
        whole_side = jnp.take(rel, order, axis=0)
        flat = whole_side.reshape(16, height, width)
        if wide is not None:
            cut = width * (wide + 1) // (2 * wide + 1)
            low = whole_side[..., cut:].reshape(n, rows, wide, -1).transpose(0, 2, 1, 3)
            low = low.reshape(16, wide, height, -1).transpose(0, 2, 1, 3).reshape(16, height, -1)
            flat = jnp.concatenate([flat[..., :cut], low], axis=2)
        halves.append(flat.reshape(4, 4, height, width))
    left, right = jnp.where(c == 0, halves[0], halves[1]), jnp.where(c == 0, halves[1], halves[0])
    return [side[:, e] for side in (left, right) for e in range(4)]


def load_pieces(idx_ref, plan, sem):
    c = idx_ref[1]
    started = []
    for find, shard, start, width, dst, height, first in plan:
        for e in range(4):
            for d in range(4):
                for block, h in zip(find(e, d), (c, 1 - c), strict=False):
                    rows = block.shape[0]
                    at = pl.ds(pl.multiple_of(shard(e, d) * height + first, 16), rows)
                    cols = pl.ds(pl.multiple_of(h * width, 128), width) if dst.shape[1] > width else slice(None)
                    started.append(pltpu.make_async_copy(block.at[:, pl.ds(start, width)], dst.at[at, cols], sem))
    for cp in started:
        cp.start()
    return started


def relative(idx_ref):
    return lambda e, d: lax.bitwise_xor(idx_ref[0], jnp.int32(d * 4 + e))


def by_top(idx_ref):
    return lambda e, d: lax.bitwise_xor(idx_ref[0] % 4, jnp.int32(e)) + d * 4


def load_qkv(idx_ref, pieces, w_ref, sem, vec_ref=None):
    def find(e, d):
        if len(pieces) == 8:
            return pieces[e].at[d], pieces[4 + e].at[d]
        return pieces[e].at[d], pieces[5].at[e - 1, d] if e else pieces[4].at[d]

    where = relative(idx_ref)
    rows, half = pieces[0].shape[1], w_ref.shape[1] // 2
    if vec_ref is not None:
        return load_pieces(idx_ref, [(lambda e, d: find(e, d)[:1], where, half, 128, vec_ref, rows, 0)], sem)
    return load_pieces(idx_ref, [(find, where, 0, half, w_ref, rows, 0)], sem)


def load_mlp(idx_ref, pieces, w1_ref, w2_ref, sem):
    where = by_top(idx_ref)

    def find1(e, d):
        return pieces[e // 2].at[e % 2, d], pieces[2 + e // 2].at[e % 2, d]

    def find2(e, d):
        return pieces[4 + e % 2].at[e // 2, d], pieces[6 + e % 2].at[e // 2, d]

    rows = pieces[0].shape[2]
    w = w2_ref.shape[1] // 2
    plan = [(find1, where, 0, w1_ref.shape[1] // 2, w1_ref, rows, 0)]
    plan += [(find2, where, j * w, w, w2_ref, 4 * rows, j * rows) for j in range(4)]
    return load_pieces(idx_ref, plan, sem.at[0])


def qkv_kernel(idx_ref, x_ref, *refs):
    pieces = refs[:-9]
    q_ref, k_ref, v_ref, h_ref, vt_ref, bu_ref, w_ref, vec_ref, sem = refs[-9:]
    d = x_ref.shape[1]

    @pl.when(pl.program_id(0) == 0)
    def _():
        rows = pieces[0].shape[1]
        vecs = load_qkv(idx_ref, pieces, w_ref, sem.at[1], vec_ref)
        going = load_qkv(idx_ref, pieces, w_ref, sem.at[0])
        for cp in vecs:
            cp.wait()
        table = vec_ref[...].astype(F32).T[:VECS]
        vt_ref[...] = table
        bu_ref[...] = jnp.concatenate(
            [table[8 + j : 9 + j, s * rows : (s + 1) * rows] for s in range(d // rows) for j in range(4)], axis=1
        )
        for cp in going:
            cp.wait()

    c, r = norm_stats(x_ref[...].astype(F32))
    h = (c * r * vt_ref[0:1, :] + vt_ref[1:2, :]).astype(BF)
    h_ref[...] = h
    q = dg(h, w_ref[:, :d], NN)
    q_ref[...] = ((q + vt_ref[2:3, :]) * (0.125 * LOG2E)).astype(BF)
    k_ref[...] = dg(h, w_ref[:, d : 2 * d], NN).astype(BF)
    v_ref[...] = (dg(h, w_ref[:, 2 * d :], NN) + vt_ref[3:4, :]).astype(BF)


def qkv(idx, x, pieces, tb=512):
    t, d = x.shape
    return pl.pallas_call(
        qkv_kernel,
        grid_spec=pltpu.PrefetchScalarGridSpec(
            num_scalar_prefetch=1,
            grid=(t // tb,),
            in_specs=[rows_of(tb, d)] + [ANY] * len(pieces),
            out_specs=[rows_of(tb, d)] * 4 + [fixed((VECS, d)), fixed((1, 4 * d))],
            scratch_shapes=[
                pltpu.VMEM((d, 3 * d), BF),
                pltpu.VMEM((d, 128), BF),
                pltpu.SemaphoreType.DMA((2,)),
            ],
        ),
        out_shape=[SDS((t, d), BF)] * 4 + [SDS((VECS, d), F32), SDS((1, 4 * d), F32)],
        compiler_params=params(),
        cost_estimate=cost(6 * t * d * d, t * d * 8 + d * d * 6),
        name="qkv",
    )(idx, x, *pieces)


def attend_kernel(tag_ref, q_ref, k_ref, v_ref, *refs, qb):
    o_ref, l_ref = refs[-2:]
    r = pl.program_id(0)
    length = q_ref.shape[0]
    low = lax.broadcasted_iota(jnp.int32, (1, 128), 1) < 64

    def block(qs, qn, ks, kn):
        q = q_ref[pl.ds(qs, qn), :]
        k = k_ref[pl.ds(ks, kn), :]
        v = v_ref[pl.ds(ks, kn), :]
        outs = []
        for h in range(2):
            sel = low if h == 0 else jnp.logical_not(low)
            qm = jnp.where(sel, q, jnp.asarray(0, BF))
            vm = jnp.where(sel, v, jnp.asarray(1, BF))
            s = dg(qm, k, NT)
            m = jnp.max(s, axis=1, keepdims=True)
            outs.append((dg(jnp.exp2(s - m).astype(BF), vm, NN), m))
        (a, ma), (b, mb) = outs
        acc = jnp.where(low, a, b)
        total = pltpu.roll(jnp.where(low, b, a), 64, 1)
        o_ref[pl.ds(qs, qn), :] = (acc / total).astype(o_ref.dtype)
        lse = (jnp.where(low, ma, mb) + jnp.log2(total)).T
        l_ref[0, 0, 0:1, pl.ds(qs, qn)] = lse[0:1]
        l_ref[0, 0, 1:2, pl.ds(qs, qn)] = lse[64:65]

    @pl.when(tag_ref[r] == 0)
    def _():
        for i in range(length // qb):
            block(i * qb, qb, 0, length)

    @pl.when(tag_ref[r] != 0)
    def _():
        c = length // 4
        for i in range(4):
            block(i * c, c, i * c, c)


def attend(tag, q, k, v, first, pairs, before=(), qb=512):
    t, d = q.shape
    rows = tag.shape[0]
    length = t // rows
    blk = pl.BlockSpec((length, 128), lambda r, p, _: (r, p + first))
    lse = pl.BlockSpec((1, 1, 2, length), lambda r, p, _: (r, p + first, 0, 0))
    return pl.pallas_call(
        functools.partial(attend_kernel, qb=qb),
        grid_spec=pltpu.PrefetchScalarGridSpec(
            num_scalar_prefetch=1,
            grid=(rows, pairs),
            in_specs=[blk] * 3 + [ANY] * len(before),
            out_specs=[blk, lse],
        ),
        out_shape=[SDS((t, d), BF), SDS((rows, d // 128, 2, length), F32)],
        input_output_aliases={4: 0, 5: 1} if before else {},
        compiler_params=params(2),
        cost_estimate=cost(2048 * t * length * pairs, t * d * 8, t * length * 12),
        name="attend",
    )(tag, q, k, v, *before)


ODDS = (2.3021649, 1.05007451e-1, -2.545477e-4, -1.0560537e-4, 4.093017e-6)


def gelu_both(u):
    z = u * u
    odds = ODDS[3] + z * ODDS[4]
    odds = ODDS[2] + z * odds
    odds = ODDS[1] + z * odds
    odds = ODDS[0] + z * odds
    phi = pltpu.reciprocal(1.0 + jnp.exp2(-u * odds), approx=True)
    density = jnp.exp2(z * (-0.5 * LOG2E) - 0.5 * math.log2(2.0 * math.pi))
    return u * phi, phi + u * density


def mlp_kernel(idx_ref, x_ref, o_ref, vt_ref, bu_ref, *refs, fc):
    pieces = refs[:8]
    x2_ref, gl_ref, gp_ref, y_ref, w1_ref, w2_ref, sem = refs[8:]
    d = x_ref.shape[1]
    ff = w2_ref.shape[0]

    @pl.when(pl.program_id(0) == 0)
    def _():
        going = load_mlp(idx_ref, pieces, w1_ref, w2_ref, sem)
        for cp in going:
            cp.wait()

    x2 = x_ref[...].astype(F32) + dg(o_ref[...], w1_ref[:, :d], NN) + vt_ref[4:5, :]
    x2_ref[...] = x2
    c, r = norm_stats(x2)
    h = (c * r * vt_ref[5:6, :] + vt_ref[6:7, :]).astype(BF)
    y = x2 + vt_ref[7:8, :]
    for f in range(0, ff, fc):
        u = dg(h, w1_ref[:, d + f : d + f + fc], NN) + bu_ref[:, f : f + fc]
        g, gp = gelu_both(u)
        g = g.astype(BF)
        gl_ref[:, f : f + fc] = g
        gp_ref[:, f : f + fc] = gp.astype(BF)
        y = y + dg(g, w2_ref[f : f + fc, :], NN)
    y_ref[...] = y.astype(BF)


def mlp(idx, x, o, vt, bu, pieces, tb=256, fc=768):
    t, d = x.shape
    ff = bu.shape[1]
    return pl.pallas_call(
        functools.partial(mlp_kernel, fc=fc),
        grid_spec=pltpu.PrefetchScalarGridSpec(
            num_scalar_prefetch=1,
            grid=(t // tb,),
            in_specs=[rows_of(tb, d)] * 2 + [whole(vt.shape), whole(bu.shape)] + [ANY] * 8,
            out_specs=[rows_of(tb, d), rows_of(tb, ff), rows_of(tb, ff), rows_of(tb, d)],
            scratch_shapes=[
                pltpu.VMEM((d, d + ff), BF),
                pltpu.VMEM((ff, d), BF),
                pltpu.SemaphoreType.DMA((2,)),
            ],
        ),
        out_shape=[SDS((t, d), F32), SDS((t, ff), BF), SDS((t, ff), BF), SDS((t, d), BF)],
        compiler_params=params(),
        cost_estimate=cost(4 * t * d * (d + 2 * ff), t * (10 * d + 4 * ff) + 4 * d * ff, 2 * t * ff),
        name="mlp",
    )(idx, x, o, vt, bu, *pieces)


def permute_kernel(ord_ref, y_ref, o_ref):
    jb = o_ref.shape[0]
    t = y_ref.shape[0]
    order = jnp.broadcast_to(ord_ref[...].astype(F32), (8, jb)).T[:, 0:1]
    hot = jnp.where(order == lax.broadcasted_iota(jnp.int32, (jb, t), 1).astype(F32), 1.0, 0.0)
    o_ref[...] = dg(hot.astype(BF), y_ref[...], NN).astype(BF)


def permute(order, y, jb=512):
    t, d = y.shape
    return pl.pallas_call(
        permute_kernel,
        grid=(t // jb,),
        in_specs=[pl.BlockSpec((1, jb), lambda i: (0, i)), whole((t, d))],
        out_specs=rows_of(jb, d),
        out_shape=pltpu.HBM((t, d), BF),
        compiler_params=params(),
        cost_estimate=cost(2 * t * t * d, t * d * 4),
        name="permute",
    )(order, y)


def split_halves(c, r, mine_ref, theirs_ref):
    h = r.shape[1] // 2
    left, right = r[:, :h], r[:, h:]
    mine_ref[...] = jnp.where(c == 0, left, right)
    theirs_ref[...] = jnp.where(c == 0, right, left)


def mlp_back_kernel(idx_ref, ord_ref, ret_ref, gp_ref, x2_ref, o_ref, vt_ref, *refs, fc):
    pieces = refs[:8]
    (dm_ref, du_ref, dx2_ref, do_ref, h2_ref, sums_ref, gbu_ref, mine_ref, theirs_ref) = refs[8:17]
    w1_ref, w2_ref, acc_ref, sem = refs[17:]
    i = pl.program_id(0)
    tb, ff = gp_ref.shape
    t, d = ret_ref.shape

    @pl.when(i == 0)
    def _():
        going = load_mlp(idx_ref, pieces, w1_ref, w2_ref, sem)
        sums_ref[...] = jnp.zeros_like(sums_ref)
        gbu_ref[...] = jnp.zeros_like(gbu_ref)
        acc_ref[...] = jnp.zeros_like(acc_ref)
        for cp in going:
            cp.wait()

    at = lax.broadcasted_iota(jnp.int32, (tb, t), 0) + i * tb
    hot = jnp.where(ord_ref[...] == at, 1.0, 0.0).astype(BF)
    dy = dg(hot, ret_ref[...], NN)
    dm = dy.astype(BF)
    dm_ref[...] = dm
    sums_ref[0:1, :] += jnp.sum(dy, axis=0, keepdims=True)
    dh = jnp.zeros((tb, d), F32)
    for f in range(0, ff, fc):
        du = dg(dm, w2_ref[f : f + fc, :], NT) * gp_ref[:, f : f + fc].astype(F32)
        gbu_ref[:, f : f + fc] += jnp.sum(du, axis=0, keepdims=True)
        du = du.astype(BF)
        du_ref[:, f : f + fc] = du
        dh = dh + dg(du, w1_ref[:, d + f : d + f + fc], NT)
    c, r = norm_stats(x2_ref[...])
    xh = c * r
    gain = vt_ref[5:6, :]
    h2_ref[...] = (xh * gain + vt_ref[6:7, :]).astype(BF)
    sums_ref[1:2, :] += jnp.sum(dh * xh, axis=0, keepdims=True)
    sums_ref[2:3, :] += jnp.sum(dh, axis=0, keepdims=True)
    dz = dh * gain
    m1 = jnp.sum(dz, axis=-1, keepdims=True) * (1.0 / d)
    m2 = jnp.sum(dz * xh, axis=-1, keepdims=True) * (1.0 / d)
    dx2 = dy + r * (dz - m1 - xh * m2)
    dx2_ref[...] = dx2
    da = dx2.astype(BF)
    sums_ref[3:4, :] += jnp.sum(da.astype(F32), axis=0, keepdims=True)
    do_ref[...] = dg(da, w1_ref[:, :d], NT).astype(BF)
    acc_ref[...] += dg(o_ref[...], da, TN)

    @pl.when(i == pl.num_programs(0) - 1)
    def _():
        split_halves(idx_ref[1], acc_ref[...].astype(BF), mine_ref, theirs_ref)


def mlp_back(idx, order_row, ret, gp, x2, o, vt, pieces, tb=256, fc=768):
    t, d = x2.shape
    ff = gp.shape[1]
    return pl.pallas_call(
        functools.partial(mlp_back_kernel, fc=fc),
        grid_spec=pltpu.PrefetchScalarGridSpec(
            num_scalar_prefetch=1,
            grid=(t // tb,),
            in_specs=[whole((1, t)), whole((t, d)), rows_of(tb, ff), rows_of(tb, d), rows_of(tb, d), whole(vt.shape)]
            + [ANY] * 8,
            out_specs=[rows_of(tb, d), rows_of(tb, ff)]
            + [rows_of(tb, d)] * 3
            + [fixed((8, d)), fixed((1, ff))]
            + [fixed((d, d // 2))] * 2,
            scratch_shapes=[
                pltpu.VMEM((d, d + ff), BF),
                pltpu.VMEM((ff, d), BF),
                pltpu.VMEM((d, d), F32),
                pltpu.SemaphoreType.DMA((2,)),
            ],
        ),
        out_shape=[
            SDS((t, d), BF),
            SDS((t, ff), BF),
            SDS((t, d), F32),
            SDS((t, d), BF),
            SDS((t, d), BF),
            SDS((8, d), F32),
            SDS((1, ff), F32),
            pltpu.HBM((d, d // 2), BF),
            pltpu.HBM((d, d // 2), BF),
        ],
        compiler_params=params(),
        cost_estimate=cost(2 * t * d * (d + 2 * ff + t) * 1.5, t * (20 * d + 4 * ff)),
        name="mlp_back",
    )(idx, order_row, ret, gp, x2, o, vt, *pieces)


def grad_down_kernel(idx_ref, g_ref, dm_ref, mine_ref, theirs_ref):
    split_halves(idx_ref[1], dg(g_ref[...], dm_ref[...], TN).astype(BF), mine_ref, theirs_ref)


def grad_down(idx, g, dm, mb=768):
    t, ff = g.shape
    d = dm.shape[1]
    return pl.pallas_call(
        grad_down_kernel,
        grid_spec=pltpu.PrefetchScalarGridSpec(
            num_scalar_prefetch=1,
            grid=(ff // mb,),
            in_specs=[pl.BlockSpec((t, mb), lambda i, _: (0, i)), whole((t, d))],
            out_specs=[rows_of(mb, d // 2)] * 2,
        ),
        out_shape=[pltpu.HBM((ff, d // 2), BF)] * 2,
        compiler_params=params(),
        cost_estimate=cost(3 * t * ff * d, 2 * t * (ff + d) + 2 * ff * d),
        name="grad_down",
    )(idx, g, dm)


def grad_wide_kernel(idx_ref, a_ref, b_ref, mine_ref, theirs_ref):
    split_halves(idx_ref[1], dg(a_ref[...], b_ref[...], TN).astype(BF), mine_ref, theirs_ref)


def grad_wide(idx, a, b, name):
    t, d = a.shape
    width = b.shape[1]
    return pl.pallas_call(
        grad_wide_kernel,
        grid_spec=pltpu.PrefetchScalarGridSpec(
            num_scalar_prefetch=1,
            grid=(width // d,),
            in_specs=[whole((t, d)), pl.BlockSpec((t, d), lambda i, _: (0, i))],
            out_specs=[pl.BlockSpec((d, d // 2), lambda i, _: (0, i))] * 2,
        ),
        out_shape=[pltpu.HBM((d, width // 2), BF)] * 2,
        compiler_params=params(),
        cost_estimate=cost(3 * t * width * d, 2 * t * (width + d) + 2 * width * d),
        name=name,
    )(idx, a, b)


def attend_back_kernel(
    tag_ref, q_ref, k_ref, v_ref, do_ref, o_ref, l_ref, *refs, kb, qb
):
    dq_ref, dk_ref, dv_ref, dl_ref, dqt_ref = refs[-5:]
    r = pl.program_id(0)
    length = q_ref.shape[0]
    low = lax.broadcasted_iota(jnp.int32, (1, 128), 1) < 64
    prod = (do_ref[...].astype(F32) * o_ref[...].astype(F32)).T
    dl_ref[0:1, :] = jnp.sum(prod[0:64], axis=0, keepdims=True)
    dl_ref[1:2, :] = jnp.sum(prod[64:128], axis=0, keepdims=True)

    def block(ks, kn, qs, qn):
        k = k_ref[pl.ds(ks, kn), :]
        v = v_ref[pl.ds(ks, kn), :]
        q = q_ref[pl.ds(qs, qn), :]
        do = do_ref[pl.ds(qs, qn), :]
        dks = []
        dvs = []
        dqs = []
        for h in range(2):
            sel = low if h == 0 else jnp.logical_not(low)
            km = jnp.where(sel, k, jnp.asarray(0, BF))
            vm = jnp.where(sel, v, jnp.asarray(0, BF))
            pt = jnp.exp2(dg(km, q, NT) - l_ref[0, 0, h : h + 1, pl.ds(qs, qn)])
            dst = (pt * (dg(vm, do, NT) - dl_ref[h : h + 1, pl.ds(qs, qn)])).astype(BF)
            dvs.append(dg(pt.astype(BF), do, NN))
            dks.append(dg(dst, q, NN))
            dqs.append(dg(km.T, dst, NN))
        return jnp.where(low, dks[0], dks[1]), jnp.where(low, dvs[0], dvs[1]), dqs[0] + dqs[1]

    def run(kn, qn, plan):
        seen = set()
        for ks, starts in plan:
            dk = dv = None
            for qs in starts:
                a, b, dq = block(ks, kn, qs, qn)
                dk = a if dk is None else dk + a
                dv = b if dv is None else dv + b
                if qs in seen:
                    dqt_ref[:, pl.ds(qs, qn)] += dq
                else:
                    dqt_ref[:, pl.ds(qs, qn)] = dq
                seen.add(qs)
            dk_ref[pl.ds(ks, kn), :] = (dk * LN2).astype(BF)
            dv_ref[pl.ds(ks, kn), :] = dv.astype(BF)
        dq_ref[...] = (dqt_ref[...].T * 0.125).astype(BF)

    @pl.when(tag_ref[r] == 0)
    def _():
        run(kb, qb, [(ks, range(0, length, qb)) for ks in range(0, length, kb)])

    @pl.when(tag_ref[r] != 0)
    def _():
        c = length // 4
        run(c, c, [(ks, [ks]) for ks in range(0, length, c)])


def attend_back(tag, q, k, v, do, o, lse, first, pairs, before=(), kb=512, qb=512):
    t, d = q.shape
    rows = tag.shape[0]
    length = t // rows
    blk = pl.BlockSpec((length, 128), lambda r, p, _: (r, p + first))
    lse_spec = pl.BlockSpec((1, 1, 2, length), lambda r, p, _: (r, p + first, 0, 0))
    return pl.pallas_call(
        functools.partial(attend_back_kernel, kb=kb, qb=qb),
        grid_spec=pltpu.PrefetchScalarGridSpec(
            num_scalar_prefetch=1,
            grid=(rows, pairs),
            in_specs=[blk] * 5 + [lse_spec] + [ANY] * len(before),
            out_specs=[blk] * 3,
            scratch_shapes=[pltpu.VMEM((2, length), F32), pltpu.VMEM((128, length), F32)],
        ),
        out_shape=[SDS((t, d), BF)] * 3,
        input_output_aliases={7: 0, 8: 1, 9: 2} if before else {},
        compiler_params=params(2),
        cost_estimate=cost(5120 * t * length * pairs, t * d * 16, t * length * 12),
        name="attend_back",
    )(tag, q, k, v, do, o, lse, *before)


def grad_qkv_kernel(idx_ref, h_ref, dq_ref, dk_ref, dv_ref, *refs, rows):
    w = dq_ref.shape[1]
    for m, ref in enumerate((dq_ref, dk_ref, dv_ref)):
        at = slice(m * w, (m + 1) * w)
        part = dg(h_ref[...], ref[...], TN)
        if rows is None:
            refs[0][:, at] = part.astype(BF)
        else:
            outs, sum_ref = refs[1:-1], refs[-1]
            q = len(outs)
            sum_ref[...] = part + refs[0][:, at].astype(F32)
            for e in range(q):
                for z in range(4):
                    s = z * q + lax.bitwise_xor(idx_ref[0] % q, jnp.int32(e))
                    outs[e][z, :, at] = sum_ref[pl.ds(pl.multiple_of(s * rows, 8), rows), :].astype(BF)


def grad_qkv(idx, h1, dq, dk, dv, recv=None, n=None):
    t, d = h1.shape
    w = d // 2
    own = recv is not None
    half = pl.BlockSpec((t, w), lambda i, ix: (0, lax.bitwise_xor(ix[1], jnp.int32(0 if own else 1))))
    outs = [(4, d // n, 3 * w)] * (n // 4) if own else [(d, 3 * w)]
    return pl.pallas_call(
        functools.partial(grad_qkv_kernel, rows=d // n if own else None),
        grid_spec=pltpu.PrefetchScalarGridSpec(
            num_scalar_prefetch=1,
            grid=(1,),
            in_specs=[whole((t, d)), half, half, half] + [whole((d, 3 * w))] * own,
            out_specs=[fixed(o) for o in outs],
            scratch_shapes=[pltpu.VMEM((d, w), F32)] * own,
        ),
        out_shape=[pltpu.HBM(o, BF) for o in outs],
        compiler_params=params(),
        cost_estimate=cost(6 * t * d * w, t * d * 6),
        name="grad_qkv_own" if own else "grad_qkv_other",
    )(idx, h1, dq, dk, dv, *([recv] * own))


def tokens_back_kernel(idx_ref, x_ref, vt_ref, dx2_ref, dq_ref, dk_ref, dv_ref, *refs):
    pieces = refs[:-4]
    tg_ref, s_ref, w_ref, sem = refs[-4:]
    d = x_ref.shape[1]

    @pl.when(pl.program_id(0) == 0)
    def _():
        going = load_qkv(idx_ref, pieces, w_ref, sem)
        s_ref[...] = jnp.zeros_like(s_ref)
        for cp in going:
            cp.wait()

    dh = dg(dq_ref[...], w_ref[:, :d], NT)
    dh = dh + dg(dk_ref[...], w_ref[:, d : 2 * d], NT)
    dh = dh + dg(dv_ref[...], w_ref[:, 2 * d :], NT)
    s_ref[2:3, :] += jnp.sum(dq_ref[...].astype(F32), axis=0, keepdims=True)
    s_ref[3:4, :] += jnp.sum(dv_ref[...].astype(F32), axis=0, keepdims=True)
    c, r = norm_stats(x_ref[...].astype(F32))
    xh = c * r
    s_ref[0:1, :] += jnp.sum(dh * xh, axis=0, keepdims=True)
    s_ref[1:2, :] += jnp.sum(dh, axis=0, keepdims=True)
    dz = dh * vt_ref[0:1, :]
    m1 = jnp.sum(dz, axis=-1, keepdims=True) * (1.0 / d)
    m2 = jnp.sum(dz * xh, axis=-1, keepdims=True) * (1.0 / d)
    tg_ref[...] = dx2_ref[...] + r * (dz - m1 - xh * m2)


def tokens_back(idx, dq, dk, dv, x, vt, dx2, pieces, tb=512):
    t, d = x.shape
    return pl.pallas_call(
        tokens_back_kernel,
        grid_spec=pltpu.PrefetchScalarGridSpec(
            num_scalar_prefetch=1,
            grid=(t // tb,),
            in_specs=[rows_of(tb, d), whole(vt.shape)] + [rows_of(tb, d)] * 4 + [ANY] * len(pieces),
            out_specs=[rows_of(tb, d), fixed((8, d))],
            scratch_shapes=[pltpu.VMEM((d, 3 * d), BF), pltpu.SemaphoreType.DMA],
        ),
        out_shape=[SDS((t, d), F32), SDS((8, d), F32)],
        compiler_params=params(),
        cost_estimate=cost(9 * t * d * d, t * d * 16 + d * d * 6),
        name="tokens_back",
    )(idx, x, vt, dx2, dq, dk, dv, *pieces)


def hop(x, groups):
    return lax.all_to_all(x, "fsdp", split_axis=0, concat_axis=0, tiled=True, axis_index_groups=groups)


def sum_cores_kernel(idx_ref, *refs, q):
    outs = refs[-q:]
    rows = outs[0].shape[1]
    for e in range(q):
        at = lax.bitwise_xor(idx_ref[0] % q, jnp.int32(e))
        start = 0
        for a_ref, b_ref in zip(refs[:-q:2], refs[1:-q:2], strict=True):
            total = a_ref[at] + b_ref[at]
            w = total.shape[1]
            for j in range(total.shape[0] // rows):
                outs[e][0, :, start : start + w] = total[j * rows : (j + 1) * rows]
                start += w


def sum_cores(idx, pairs, rows, n):
    q = n // 4
    ops, specs, width = [], [], 0
    for pair in pairs:
        shape = (pair[0].shape[0] // n, pair[0].shape[1])
        width += shape[0] // rows * shape[1]
        ops += [x.reshape((n,) + shape) for x in pair]
        specs += [pl.BlockSpec((q,) + shape, lambda z, _: (z, 0, 0))] * 2
    return pl.pallas_call(
        functools.partial(sum_cores_kernel, q=q),
        grid_spec=pltpu.PrefetchScalarGridSpec(
            num_scalar_prefetch=1,
            grid=(4,),
            in_specs=specs,
            out_specs=[pl.BlockSpec((1, rows, width), lambda z, _: (z, 0, 0))] * q,
        ),
        out_shape=[pltpu.HBM((4, rows, width), BF)] * q,
        compiler_params=params(),
        cost_estimate=cost(n * rows * width, n * rows * width * 6),
        name="sum_cores",
    )(idx, *ops)


def spread(parts, n):
    return [parts[0]] + [xor_pp(parts[e], e, n) for e in range(1, n // 4)]


def sum_parts_kernel(*refs):
    total = refs[0][...].astype(F32)
    for x in refs[1:-1]:
        total = total + x[...].astype(F32)
    refs[-1][...] = total.astype(BF)


def sum_parts(parts):
    shape = (1,) + parts[0].shape[1:]
    spec = pl.BlockSpec(shape, lambda i: (i, 0, 0))
    return pl.pallas_call(
        sum_parts_kernel,
        grid=(4,),
        in_specs=[spec] * len(parts),
        out_specs=spec,
        out_shape=pltpu.HBM(parts[0].shape, BF),
        compiler_params=params(),
        cost_estimate=cost(4 * len(parts) * math.prod(shape), 8 * len(parts) * math.prod(shape)),
        name="sum_parts",
    )(*parts)


def sum_qkv_kernel(idx_ref, *refs, q):
    for d in range(4):
        at = lax.bitwise_xor(idx_ref[0] // q, jnp.int32(d))
        start = 0
        for parts in (refs[:q], refs[q : 2 * q]):
            total = parts[0][at].astype(F32)
            for x in parts[1:]:
                total = total + x[at].astype(F32)
            w = total.shape[1]
            refs[2 * q + d][:, start : start + w] = total.astype(BF)
            start += w


def sum_qkv(idx, far, vecs, n):
    _, rows, w = far[0].shape
    width = w + vecs[0].shape[2]
    ops = list(far) + list(vecs)
    near = pl.pallas_call(
        functools.partial(sum_qkv_kernel, q=n // 4),
        grid_spec=pltpu.PrefetchScalarGridSpec(
            num_scalar_prefetch=1,
            grid=(1,),
            in_specs=[whole(x.shape) for x in ops],
            out_specs=[fixed((rows, width))] * 4,
        ),
        out_shape=[pltpu.HBM((rows, width), BF)] * 4,
        compiler_params=params(),
        cost_estimate=cost(n * rows * width, n * rows * width * 3),
        name="sum_qkv",
    )(idx, *ops)
    return near


def reduce_last(near, n, m):
    total = near[0].astype(F32)
    for x in near[1:]:
        total = total + x.astype(F32)
    return over_pairs(total, m)


def over_pairs(total, m):
    b = 2
    while b < m:
        total = total + lax.ppermute(total.astype(BF), "dp", [(i, i ^ b) for i in range(m)]).astype(F32)
        b *= 2
    return total


def vec_table_kernel(idx_ref, a, c, u, *refs, q):
    table_ref = refs[q]
    d = a.shape[1]
    rows = refs[0].shape[1]
    wide = u.shape[1] // d
    bias = [
        jnp.concatenate(
            [u[:, (s * wide + j) * rows : (s * wide + j + 1) * rows] for s in range(4 * q)], axis=1
        )
        for j in range(wide)
    ]
    lines = [c[0:4, :], a[3:4, :], a[1:3, :], a[0:1, :]] + bias + [jnp.zeros((120 - wide, d), F32)]
    table_ref[...] = jnp.concatenate(lines, axis=0).T
    for e in range(q):
        for z in range(4):
            s = z * q + lax.bitwise_xor(idx_ref[0] % q, jnp.int32(e))
            refs[e][z] = table_ref[pl.ds(pl.multiple_of(s * rows, 8), rows), :].astype(BF)


def vec_table(idx, s_mlp, s_tok, gbu, n):
    d = s_mlp.shape[1]
    q = n // 4
    return pl.pallas_call(
        functools.partial(vec_table_kernel, q=q),
        grid_spec=pltpu.PrefetchScalarGridSpec(
            num_scalar_prefetch=1,
            grid=(1,),
            in_specs=[whole(s_mlp.shape), whole(s_tok.shape), whole(gbu.shape)],
            out_specs=[fixed((4, d // n, 128))] * q,
            scratch_shapes=[pltpu.VMEM((d, 128), F32)],
        ),
        out_shape=[SDS((4, d // n, 128), BF)] * q,
        compiler_params=params(),
        cost_estimate=cost(d * 128, d * 1024),
        name="vec_table",
    )(idx, s_mlp, s_tok, gbu)


def local(
    tokens,
    sensor_tag,
    owner_order,
    ln1_gain,
    ln1_bias,
    w_qkv,
    b_query,
    b_value,
    w_out,
    b_out,
    ln2_gain,
    ln2_bias,
    w_up,
    b_up,
    w_down,
    b_down,
    out_grad,
    *,
    n,
    m,
):
    t, d = tokens.shape
    ff = w_up.shape[1]
    rows = d // n
    wide = ff // d
    f = lax.axis_index("fsdp")
    c = lax.axis_index("dp") % 2
    idx = jnp.stack([f, c]).astype(jnp.int32)
    use = idx if fits(rows, n) else jnp.zeros_like(idx)

    def core_half(x):
        h = x.shape[1] // 2
        return jnp.where(c == 0, x[:, :h], x[:, h:])

    vec = jnp.stack([ln1_gain, ln1_bias, b_query, b_value, b_out, ln2_gain, ln2_bias, b_down], axis=1)
    vec = jnp.concatenate([vec, b_up.reshape(wide, rows).T], axis=1)
    vec = jnp.pad(vec, ((0, 0), (0, 128 - vec.shape[1])))
    shard_a = jnp.concatenate([core_half(w_qkv), vec], axis=1)
    shard_b = jnp.concatenate(
        [core_half(jnp.concatenate([w_out, w_up], axis=1))]
        + [core_half(w_down[j * rows : (j + 1) * rows]) for j in range(wide)],
        axis=1,
    )
    q = n // 4
    everyone = jnp.arange(n)

    near_a = gather_near(shard_a, n)
    near_b = hop(jnp.broadcast_to(after(shard_b, near_a)[None], (4,) + shard_b.shape), tops(n))
    own_a = gather_far(near_a, n)
    cast = after(out_grad, near_a).astype(BF)
    own_a[1:] = after(own_a[1:], cast)
    swap_a = [core_swap(near_a, m), core_swap(jnp.stack(own_a[1:]), m)]
    if fits(rows, n):
        pieces_a = own_a + swap_a
    else:
        pieces_a = settle(own_a + swap_a[:1] + [swap_a[1][e] for e in range(q - 1)], f ^ everyone, c, n)
    near_b = after(near_b, own_a[1:])
    qh, kh, vh, h1, vt, bu = qkv(use, after(tokens, near_b), pieces_a)
    pairs = d // 128
    early = pairs * 2 // 3
    if fits(rows, n):
        first = [near_b[..., : (d + ff) // 2], near_b[..., (d + ff) // 2 :]]
        bits = (1, 2)
        second = [xor_pp(x, b, n) for x, b in zip(first, bits, strict=True)]
        both_b = [jnp.stack([x, y]) for x, y in zip(first, after(second, vt), strict=True)]
        far_b = [xor_pp(x, b, n) for x, b in zip(both_b, bits[::-1], strict=True)]
        part = attend(sensor_tag, after(qh, both_b), kh, vh, 0, early)
        far_b = after(far_b, part[0])
        pieces_b = []
        for x, y in zip(both_b, far_b, strict=True):
            pieces_b += [x, y, core_swap(x, m), core_swap(y, m)]
    else:
        far_b = gather_far(near_b, n)
        side = settle(
            far_b + [core_swap(x, m) for x in far_b], everyone // q * q + (everyone ^ f) % q, c, n, wide
        )
        part = attend(sensor_tag, qh, kh, vh, 0, early)
        cut = (d + ff) // 2
        one = [x[..., :cut] for x in side]
        two = [x[..., cut:] for x in side]
        pieces_b = [jnp.stack(one[i : i + 2]) for i in (0, 2, 4, 6)]
        pieces_b += [jnp.stack([two[i], two[i + 2]]) for i in (0, 1, 4, 5)]
    returned = lax.all_to_all(after(cast, far_b), "fsdp", split_axis=0, concat_axis=0, tiled=True)
    mixed, lse = attend(sensor_tag, qh, kh, vh, early, pairs - early, part)

    x2, active, slope, y = mlp(use, tokens, mixed, vt, bu, pieces_b)
    sent = permute(owner_order, y)
    encoded = lax.all_to_all(sent, "fsdp", split_axis=0, concat_axis=0, tiled=True)

    returned = after(returned, sent)
    dm, du, dx2, do, h2, s_mlp, gbu, out_own, out_other = mlp_back(
        use, owner_order, returned, slope, x2, mixed, vt, pieces_b
    )
    out_recv = core_swap(out_other, m)
    down_own, down_other = grad_down(idx, active, dm)
    down_recv = core_swap(down_other, m)
    up_own, up_other = grad_wide(idx, after(h2, down_own), du, "grad_up")
    up_recv = core_swap(up_other, m)
    part = attend_back(sensor_tag, qh, kh, vh, after(do, up_own, encoded), mixed, lse, 0, 1)
    out_recv, down_recv, up_recv = after((out_recv, down_recv, up_recv), part[0])
    pairs_b = [(up_own, up_recv), (out_own, out_recv), (down_own, down_recv)]
    far_b = sum_cores(idx, pairs_b, rows, n)
    do = after(do, far_b[0])
    far_b = spread(far_b, n)
    dj = attend_back(sensor_tag, qh, kh, vh, do, mixed, lse, 1, pairs - 1, part)
    (qkv_other,) = grad_qkv(idx, h1, *dj)
    qkv_recv = core_swap(qkv_other, m)
    far_b = after(far_b, dj[0])
    near_b = sum_parts([after(far_b[0], qkv_other)] + far_b[1:])
    total_b = hop(near_b, tops(n))
    far_a = grad_qkv(idx, after(h1, near_b), *dj, qkv_recv, n)
    dj = after(dj, far_a[0])
    far_a = spread(far_a, n)
    tokens_grad, s_tok = tokens_back(use, *dj, tokens, vt, dx2, pieces_a)
    far_a, total_b = after((far_a, total_b), tokens_grad)
    total_b = over_pairs(jnp.sum(total_b.astype(F32), axis=0), m).astype(BF)
    other_b = core_swap(total_b, m)
    far_v = spread(vec_table(idx, s_mlp, s_tok, after(gbu, far_a), n), n)

    near_a = sum_qkv(idx, after(far_a, total_b), far_v, n)
    encoded = after(encoded, near_a[0]).astype(F32)
    near_a = [near_a[0]] + [xor_pp(near_a[i], i * q, n) for i in range(1, 4)]
    def both(mine, other):
        first = c == 0
        return jnp.where(first, mine, other).astype(F32), jnp.where(first, other, mine).astype(F32)

    def join(pair, start, width, parts, axis=1):
        out = []
        for p in range(parts):
            at = slice(start + p * width, start + (p + 1) * width)
            out.append(jnp.concatenate([pair[0][:, at], pair[1][:, at]], axis=1))
        return jnp.concatenate(out, axis=axis)

    h = d // 2
    g_mlp = both(total_b, other_b)
    grad_up_out = join(g_mlp, 0, h, wide)
    grad_out_out = join(g_mlp, ff // 2, h, 1)
    grad_down_out = join(g_mlp, (d + ff) // 2, h, wide, 0)
    near_a = after(near_a, grad_up_out, grad_out_out, grad_down_out, encoded)
    total_a = reduce_last(near_a, n, m)
    other_a = core_swap(total_a.astype(BF), m)
    cut = 3 * d // 2
    vecs = (total_a[:, cut:] + other_a[:, cut:].astype(F32)).T
    total_a, other_a = total_a[:, :cut].astype(BF), other_a[:, :cut]

    grad_qkv_out = join(both(total_a, other_a), 0, h, 3)
    return (
        encoded,
        tokens_grad,
        vecs[0],
        vecs[1],
        grad_qkv_out,
        vecs[2],
        vecs[3],
        grad_out_out,
        vecs[4],
        vecs[5],
        vecs[6],
        grad_up_out,
        vecs[8 : 8 + wide].reshape(ff // n),
        grad_down_out,
        vecs[7],
    )


def solution(mesh):
    n = mesh.shape["fsdp"]
    m = mesh.shape["dp"]
    both = P(("dp", "fsdp"), None)
    vec = P("fsdp")
    mat = P("fsdp", None)
    in_specs = (both, P(("dp", "fsdp")), both, vec, vec, mat, vec, vec, mat, vec, vec, vec, mat, vec, mat, vec, both)
    out_specs = (both, both, vec, vec, mat, vec, vec, mat, vec, vec, vec, mat, vec, mat, vec)
    return jax.shard_map(
        functools.partial(local, n=n, m=m), mesh=mesh, in_specs=in_specs, out_specs=out_specs, check_vma=False
    )
```

```python
import functools
import math

import jax
import jax.numpy as jnp
from jax import lax
from jax.experimental import pallas as pl
from jax.experimental.pallas import tpu as pltpu
from jax.sharding import PartitionSpec as P

F32 = jnp.float32
BF = jnp.bfloat16
EPS = 1e-6
LOG2E = math.log2(math.e)
LN2 = math.log(2.0)
NT = (((1,), (1,)), ((), ()))
TN = (((0,), (0,)), ((), ()))
NN = (((1,), (0,)), ((), ()))
ANY = pl.BlockSpec(memory_space=pl.ANY)
VECS = 16
SDS = jax.ShapeDtypeStruct


def dg(a, b, dims):
    return lax.dot_general(a, b, dims, preferred_element_type=F32)


def params(axes=1):
    return pltpu.CompilerParams(
        vmem_limit_bytes=58 * 2**20, dimension_semantics=("arbitrary",) * axes
    )


def cost(flops, nbytes, trans=0):
    return pl.CostEstimate(flops=int(flops) >> 10, bytes_accessed=int(nbytes) >> 10, transcendentals=int(trans) >> 10)


def rows_of(height, width):
    return pl.BlockSpec((height, width), lambda i, *_: (i, 0))


def whole(shape):
    zeros = (0,) * len(shape)
    return pl.BlockSpec(shape, lambda *_: zeros, pipeline_mode=pl.Buffered(1))


def fixed(shape):
    zeros = (0,) * len(shape)
    return pl.BlockSpec(shape, lambda *_: zeros)


def norm_stats(x):
    n = x.shape[-1]
    c = x - jnp.sum(x, axis=-1, keepdims=True) * (1.0 / n)
    var = jnp.sum(c * c, axis=-1, keepdims=True) * (1.0 / n)
    return c, lax.rsqrt(var + EPS)


def after(x, *deps):
    return lax.optimization_barrier((x,) + deps)[0]


def xor_pp(x, b, n):
    return lax.ppermute(x, "fsdp", [(i, i ^ b) for i in range(n)])


def core_swap(x, m):
    return lax.ppermute(x, "dp", [(i, i ^ 1) for i in range(m)])


def gather_near(x, n):
    q = n // 4
    return jnp.stack([x] + [xor_pp(x, d * q, n) for d in (1, 2, 3)])


def tops(n):
    q = n // 4
    return [[low + z * q for z in range(4)] for low in range(q)]


def gather_far(s, n):
    return [s] + [xor_pp(s, e, n) for e in range(1, n // 4)]


def fits(rows, n):
    return rows % 16 == 0 and n == 16


def settle(pieces, order, c, n, wide=None):
    q = n // 4
    rows, width = pieces[0].shape[1:]
    if fits(rows, n):
        return pieces
    height = n * rows // 16
    halves = []
    for side in (pieces[:q], pieces[q:]):
        rel = jnp.stack(side, axis=1).reshape((n, rows, width))
        whole_side = jnp.take(rel, order, axis=0)
        flat = whole_side.reshape(16, height, width)
        if wide is not None:
            cut = width * (wide + 1) // (2 * wide + 1)
            low = whole_side[..., cut:].reshape(n, rows, wide, -1).transpose(0, 2, 1, 3)
            low = low.reshape(16, wide, height, -1).transpose(0, 2, 1, 3).reshape(16, height, -1)
            flat = jnp.concatenate([flat[..., :cut], low], axis=2)
        halves.append(flat.reshape(4, 4, height, width))
    left, right = jnp.where(c == 0, halves[0], halves[1]), jnp.where(c == 0, halves[1], halves[0])
    return [side[:, e] for side in (left, right) for e in range(4)]


def load_pieces(idx_ref, plan, sem):
    c = idx_ref[1]
    started = []
    for find, shard, start, width, dst, height, first in plan:
        for e in range(4):
            for d in range(4):
                for block, h in zip(find(e, d), (c, 1 - c), strict=False):
                    rows = block.shape[0]
                    at = pl.ds(pl.multiple_of(shard(e, d) * height + first, 16), rows)
                    cols = pl.ds(pl.multiple_of(h * width, 128), width) if dst.shape[1] > width else slice(None)
                    started.append(pltpu.make_async_copy(block.at[:, pl.ds(start, width)], dst.at[at, cols], sem))
    for cp in started:
        cp.start()
    return started


def relative(idx_ref):
    return lambda e, d: lax.bitwise_xor(idx_ref[0], jnp.int32(d * 4 + e))


def by_top(idx_ref):
    return lambda e, d: lax.bitwise_xor(idx_ref[0] % 4, jnp.int32(e)) + d * 4


def load_qkv(idx_ref, pieces, w_ref, sem, vec_ref=None):
    def find(e, d):
        if len(pieces) == 8:
            return pieces[e].at[d], pieces[4 + e].at[d]
        return pieces[e].at[d], pieces[5].at[e - 1, d] if e else pieces[4].at[d]

    where = relative(idx_ref)
    rows, half = pieces[0].shape[1], w_ref.shape[1] // 2
    if vec_ref is not None:
        return load_pieces(idx_ref, [(lambda e, d: find(e, d)[:1], where, half, 128, vec_ref, rows, 0)], sem)
    return load_pieces(idx_ref, [(find, where, 0, half, w_ref, rows, 0)], sem)


def load_mlp(idx_ref, pieces, w1_ref, w2_ref, sem):
    where = by_top(idx_ref)

    def find1(e, d):
        return pieces[e // 2].at[e % 2, d], pieces[2 + e // 2].at[e % 2, d]

    def find2(e, d):
        return pieces[4 + e % 2].at[e // 2, d], pieces[6 + e % 2].at[e // 2, d]

    rows = pieces[0].shape[2]
    w = w2_ref.shape[1] // 2
    one = [(find1, where, 0, w1_ref.shape[1] // 2, w1_ref, rows, 0)]
    two = [(find2, where, j * w, w, w2_ref, 4 * rows, j * rows) for j in range(4)]
    return load_pieces(idx_ref, one, sem.at[0]), load_pieces(idx_ref, two, sem.at[1])


def wait_mlp(w_ref, sem):
    pltpu.make_async_copy(w_ref, w_ref, sem).wait()


def qkv_kernel(idx_ref, x_ref, *refs):
    pieces = refs[:-9]
    q_ref, k_ref, v_ref, h_ref, vt_ref, bu_ref, w_ref, vec_ref, sem = refs[-9:]
    d = x_ref.shape[1]

    @pl.when(pl.program_id(0) == 0)
    def _():
        rows = pieces[0].shape[1]
        vecs = load_qkv(idx_ref, pieces, w_ref, sem.at[1], vec_ref)
        going = load_qkv(idx_ref, pieces, w_ref, sem.at[0])
        for cp in vecs:
            cp.wait()
        table = vec_ref[...].astype(F32).T[:VECS]
        vt_ref[...] = table
        bu_ref[...] = jnp.concatenate(
            [table[8 + j : 9 + j, s * rows : (s + 1) * rows] for s in range(d // rows) for j in range(4)], axis=1
        )
        for cp in going:
            cp.wait()

    c, r = norm_stats(x_ref[...].astype(F32))
    h = (c * r * vt_ref[0:1, :] + vt_ref[1:2, :]).astype(BF)
    h_ref[...] = h
    q = dg(h, w_ref[:, :d], NN)
    q_ref[...] = ((q + vt_ref[2:3, :]) * (0.125 * LOG2E)).astype(BF)
    k_ref[...] = dg(h, w_ref[:, d : 2 * d], NN).astype(BF)
    v_ref[...] = (dg(h, w_ref[:, 2 * d :], NN) + vt_ref[3:4, :]).astype(BF)


def qkv(idx, x, pieces, tb=512):
    t, d = x.shape
    return pl.pallas_call(
        qkv_kernel,
        grid_spec=pltpu.PrefetchScalarGridSpec(
            num_scalar_prefetch=1,
            grid=(t // tb,),
            in_specs=[rows_of(tb, d)] + [ANY] * len(pieces),
            out_specs=[rows_of(tb, d)] * 4 + [fixed((VECS, d)), fixed((1, 4 * d))],
            scratch_shapes=[
                pltpu.VMEM((d, 3 * d), BF),
                pltpu.VMEM((d, 128), BF),
                pltpu.SemaphoreType.DMA((2,)),
            ],
        ),
        out_shape=[SDS((t, d), BF)] * 4 + [SDS((VECS, d), F32), SDS((1, 4 * d), F32)],
        compiler_params=params(),
        cost_estimate=cost(6 * t * d * d, t * d * 8 + d * d * 6),
        name="qkv",
    )(idx, x, *pieces)


def attend_kernel(tag_ref, q_ref, k_ref, v_ref, *refs, qb):
    o_ref, l_ref = refs[-2:]
    r = pl.program_id(0)
    length = q_ref.shape[0]
    low = lax.broadcasted_iota(jnp.int32, (1, 128), 1) < 64

    def block(qs, qn, ks, kn):
        q = q_ref[pl.ds(qs, qn), :]
        k = k_ref[pl.ds(ks, kn), :]
        v = v_ref[pl.ds(ks, kn), :]
        outs = []
        for h in range(2):
            sel = low if h == 0 else jnp.logical_not(low)
            qm = jnp.where(sel, q, jnp.asarray(0, BF))
            vm = jnp.where(sel, v, jnp.asarray(1, BF))
            s = dg(qm, k, NT)
            m = jnp.max(s, axis=1, keepdims=True)
            outs.append((dg(jnp.exp2(s - m).astype(BF), vm, NN), m))
        (a, ma), (b, mb) = outs
        acc = jnp.where(low, a, b)
        total = pltpu.roll(jnp.where(low, b, a), 64, 1)
        o_ref[pl.ds(qs, qn), :] = (acc / total).astype(o_ref.dtype)
        lse = (jnp.where(low, ma, mb) + jnp.log2(total)).T
        l_ref[0, 0, 0:1, pl.ds(qs, qn)] = lse[0:1]
        l_ref[0, 0, 1:2, pl.ds(qs, qn)] = lse[64:65]

    @pl.when(tag_ref[r] == 0)
    def _():
        for i in range(length // qb):
            block(i * qb, qb, 0, length)

    @pl.when(tag_ref[r] != 0)
    def _():
        c = length // 4
        for i in range(4):
            block(i * c, c, i * c, c)


def attend(tag, q, k, v, first, pairs, before=(), qb=512):
    t, d = q.shape
    rows = tag.shape[0]
    length = t // rows
    blk = pl.BlockSpec((length, 128), lambda r, p, _: (r, p + first))
    lse = pl.BlockSpec((1, 1, 2, length), lambda r, p, _: (r, p + first, 0, 0))
    return pl.pallas_call(
        functools.partial(attend_kernel, qb=qb),
        grid_spec=pltpu.PrefetchScalarGridSpec(
            num_scalar_prefetch=1,
            grid=(rows, pairs),
            in_specs=[blk] * 3 + [ANY] * len(before),
            out_specs=[blk, lse],
        ),
        out_shape=[SDS((t, d), BF), SDS((rows, d // 128, 2, length), F32)],
        input_output_aliases={4: 0, 5: 1} if before else {},
        compiler_params=params(2),
        cost_estimate=cost(2048 * t * length * pairs, t * d * 8, t * length * 12),
        name="attend",
    )(tag, q, k, v, *before)


ODDS = (2.3021649, 1.05007451e-1, -2.545477e-4, -1.0560537e-4, 4.093017e-6)


def gelu_both(u):
    z = u * u
    odds = ODDS[3] + z * ODDS[4]
    odds = ODDS[2] + z * odds
    odds = ODDS[1] + z * odds
    odds = ODDS[0] + z * odds
    phi = pltpu.reciprocal(1.0 + jnp.exp2(-u * odds), approx=True)
    density = jnp.exp2(z * (-0.5 * LOG2E) - 0.5 * math.log2(2.0 * math.pi))
    return u * phi, phi + u * density


def mlp_kernel(idx_ref, x_ref, o_ref, vt_ref, bu_ref, *refs, fc):
    pieces = refs[:8]
    x2_ref, gl_ref, gp_ref, y_ref, w1_ref, w2_ref, sem = refs[8:]
    d = x_ref.shape[1]
    ff = w2_ref.shape[0]

    @pl.when(pl.program_id(0) == 0)
    def _():
        going, _ = load_mlp(idx_ref, pieces, w1_ref, w2_ref, sem)
        for cp in going:
            cp.wait()

    x2 = x_ref[...].astype(F32) + dg(o_ref[...], w1_ref[:, :d], NN) + vt_ref[4:5, :]
    x2_ref[...] = x2
    c, r = norm_stats(x2)
    h = (c * r * vt_ref[5:6, :] + vt_ref[6:7, :]).astype(BF)
    y = x2 + vt_ref[7:8, :]

    @pl.when(pl.program_id(0) == 0)
    def _():
        wait_mlp(w2_ref, sem.at[1])

    for f in range(0, ff, fc):
        u = dg(h, w1_ref[:, d + f : d + f + fc], NN) + bu_ref[:, f : f + fc]
        g, gp = gelu_both(u)
        g = g.astype(BF)
        gl_ref[:, f : f + fc] = g
        gp_ref[:, f : f + fc] = gp.astype(BF)
        y = y + dg(g, w2_ref[f : f + fc, :], NN)
    y_ref[...] = y.astype(BF)


def mlp(idx, x, o, vt, bu, pieces, tb=256, fc=768):
    t, d = x.shape
    ff = bu.shape[1]
    return pl.pallas_call(
        functools.partial(mlp_kernel, fc=fc),
        grid_spec=pltpu.PrefetchScalarGridSpec(
            num_scalar_prefetch=1,
            grid=(t // tb,),
            in_specs=[rows_of(tb, d)] * 2 + [whole(vt.shape), whole(bu.shape)] + [ANY] * 8,
            out_specs=[rows_of(tb, d), rows_of(tb, ff), rows_of(tb, ff), rows_of(tb, d)],
            scratch_shapes=[
                pltpu.VMEM((d, d + ff), BF),
                pltpu.VMEM((ff, d), BF),
                pltpu.SemaphoreType.DMA((2,)),
            ],
        ),
        out_shape=[SDS((t, d), F32), SDS((t, ff), BF), SDS((t, ff), BF), SDS((t, d), BF)],
        compiler_params=params(),
        cost_estimate=cost(4 * t * d * (d + 2 * ff), t * (10 * d + 4 * ff) + 4 * d * ff, 2 * t * ff),
        name="mlp",
    )(idx, x, o, vt, bu, *pieces)


def permute_kernel(ord_ref, y_ref, o_ref):
    jb = o_ref.shape[0]
    t = y_ref.shape[0]
    order = jnp.broadcast_to(ord_ref[...].astype(F32), (8, jb)).T[:, 0:1]
    hot = jnp.where(order == lax.broadcasted_iota(jnp.int32, (jb, t), 1).astype(F32), 1.0, 0.0)
    o_ref[...] = dg(hot.astype(BF), y_ref[...], NN).astype(BF)


def permute(order, y, jb=512):
    t, d = y.shape
    return pl.pallas_call(
        permute_kernel,
        grid=(t // jb,),
        in_specs=[pl.BlockSpec((1, jb), lambda i: (0, i)), whole((t, d))],
        out_specs=rows_of(jb, d),
        out_shape=pltpu.HBM((t, d), BF),
        compiler_params=params(),
        cost_estimate=cost(2 * t * t * d, t * d * 4),
        name="permute",
    )(order, y)


def split_halves(c, r, mine_ref, theirs_ref):
    h = r.shape[1] // 2
    left, right = r[:, :h], r[:, h:]
    mine_ref[...] = jnp.where(c == 0, left, right)
    theirs_ref[...] = jnp.where(c == 0, right, left)


def mlp_back_kernel(idx_ref, ord_ref, ret_ref, gp_ref, x2_ref, o_ref, vt_ref, *refs, fc):
    pieces = refs[:8]
    (dm_ref, du_ref, dx2_ref, do_ref, h2_ref, sums_ref, gbu_ref, mine_ref, theirs_ref) = refs[8:17]
    w1_ref, w2_ref, acc_ref, sem = refs[17:]
    i = pl.program_id(0)
    tb, ff = gp_ref.shape
    t, d = ret_ref.shape

    @pl.when(i == 0)
    def _():
        load_mlp(idx_ref, pieces, w1_ref, w2_ref, sem)
        sums_ref[...] = jnp.zeros_like(sums_ref)
        gbu_ref[...] = jnp.zeros_like(gbu_ref)
        acc_ref[...] = jnp.zeros_like(acc_ref)
        wait_mlp(w2_ref, sem.at[1])
        wait_mlp(w1_ref, sem.at[0])

    at = lax.broadcasted_iota(jnp.int32, (tb, t), 0) + i * tb
    hot = jnp.where(ord_ref[...] == at, 1.0, 0.0).astype(BF)
    dy = dg(hot, ret_ref[...], NN)
    dm = dy.astype(BF)
    dm_ref[...] = dm
    sums_ref[0:1, :] += jnp.sum(dy, axis=0, keepdims=True)
    dh = jnp.zeros((tb, d), F32)
    ahead = dg(dm, w2_ref[:fc, :], NT)
    for f in range(0, ff, fc):
        du = ahead * gp_ref[:, f : f + fc].astype(F32)
        if f + fc < ff:
            ahead = dg(dm, w2_ref[f + fc : f + 2 * fc, :], NT)
        gbu_ref[:, f : f + fc] += jnp.sum(du, axis=0, keepdims=True)
        du = du.astype(BF)
        du_ref[:, f : f + fc] = du
        dh = dh + dg(du, w1_ref[:, d + f : d + f + fc], NT)
    c, r = norm_stats(x2_ref[...])
    xh = c * r
    gain = vt_ref[5:6, :]
    h2_ref[...] = (xh * gain + vt_ref[6:7, :]).astype(BF)
    sums_ref[1:2, :] += jnp.sum(dh * xh, axis=0, keepdims=True)
    sums_ref[2:3, :] += jnp.sum(dh, axis=0, keepdims=True)
    dz = dh * gain
    m1 = jnp.sum(dz, axis=-1, keepdims=True) * (1.0 / d)
    m2 = jnp.sum(dz * xh, axis=-1, keepdims=True) * (1.0 / d)
    dx2 = dy + r * (dz - m1 - xh * m2)
    dx2_ref[...] = dx2
    da = dx2.astype(BF)
    sums_ref[3:4, :] += jnp.sum(da.astype(F32), axis=0, keepdims=True)
    do_ref[...] = dg(da, w1_ref[:, :d], NT).astype(BF)
    acc_ref[...] += dg(o_ref[...], da, TN)

    @pl.when(i == pl.num_programs(0) - 1)
    def _():
        split_halves(idx_ref[1], acc_ref[...].astype(BF), mine_ref, theirs_ref)


def mlp_back(idx, order_row, ret, gp, x2, o, vt, pieces, tb=256, fc=768):
    t, d = x2.shape
    ff = gp.shape[1]
    return pl.pallas_call(
        functools.partial(mlp_back_kernel, fc=fc),
        grid_spec=pltpu.PrefetchScalarGridSpec(
            num_scalar_prefetch=1,
            grid=(t // tb,),
            in_specs=[whole((1, t)), whole((t, d)), rows_of(tb, ff), rows_of(tb, d), rows_of(tb, d), whole(vt.shape)]
            + [ANY] * 8,
            out_specs=[rows_of(tb, d), rows_of(tb, ff)]
            + [rows_of(tb, d)] * 3
            + [fixed((8, d)), fixed((1, ff))]
            + [fixed((d, d // 2))] * 2,
            scratch_shapes=[
                pltpu.VMEM((d, d + ff), BF),
                pltpu.VMEM((ff, d), BF),
                pltpu.VMEM((d, d), F32),
                pltpu.SemaphoreType.DMA((2,)),
            ],
        ),
        out_shape=[
            SDS((t, d), BF),
            SDS((t, ff), BF),
            SDS((t, d), F32),
            SDS((t, d), BF),
            SDS((t, d), BF),
            SDS((8, d), F32),
            SDS((1, ff), F32),
            pltpu.HBM((d, d // 2), BF),
            pltpu.HBM((d, d // 2), BF),
        ],
        compiler_params=params(),
        cost_estimate=cost(2 * t * d * (d + 2 * ff + t) * 1.5, t * (20 * d + 4 * ff)),
        name="mlp_back",
    )(idx, order_row, ret, gp, x2, o, vt, *pieces)


def grad_mlp_kernel(
    idx_ref, g_ref, dm_ref, h2_any, du_ref, down_own, down_other, up_own, up_other, h2_ref, sem
):
    i = pl.program_id(0)
    steps = pl.num_programs(0) // 2

    @pl.when(i == 0)
    def _():
        pltpu.make_async_copy(h2_any, h2_ref, sem).start()

    @pl.when(i == steps)
    def _():
        pltpu.make_async_copy(h2_any, h2_ref, sem).wait()

    @pl.when(i < steps)
    def _():
        split_halves(idx_ref[1], dg(g_ref[...], dm_ref[...], TN).astype(BF), down_own, down_other)

    @pl.when(i >= steps)
    def _():
        split_halves(idx_ref[1], dg(h2_ref[...], du_ref[...], TN).astype(BF), up_own, up_other)


def grad_mlp(idx, g, dm, h2, du):
    t, ff = g.shape
    d = dm.shape[1]
    steps = ff // d

    def down(i):
        return jnp.minimum(i, steps - 1)

    def up(i):
        return jnp.maximum(i - steps, 0)

    return pl.pallas_call(
        grad_mlp_kernel,
        grid_spec=pltpu.PrefetchScalarGridSpec(
            num_scalar_prefetch=1,
            grid=(2 * steps,),
            in_specs=[
                pl.BlockSpec((t, d), lambda i, _: (0, down(i))),
                whole((t, d)),
                ANY,
                pl.BlockSpec((t, d), lambda i, _: (0, up(i))),
            ],
            out_specs=[pl.BlockSpec((d, d // 2), lambda i, _: (down(i), 0))] * 2
            + [pl.BlockSpec((d, d // 2), lambda i, _: (0, up(i)))] * 2,
            scratch_shapes=[pltpu.VMEM((t, d), BF), pltpu.SemaphoreType.DMA],
        ),
        out_shape=[pltpu.HBM((ff, d // 2), BF)] * 2 + [pltpu.HBM((d, ff // 2), BF)] * 2,
        compiler_params=params(),
        cost_estimate=cost(6 * t * ff * d, 4 * t * (ff + d) + 4 * ff * d),
        name="grad_mlp",
    )(idx, g, dm, h2, du)


def attend_back_kernel(
    tag_ref, q_ref, k_ref, v_ref, do_ref, o_ref, l_ref, *refs, kb, qb
):
    dq_ref, dk_ref, dv_ref, dl_ref, dqt_ref = refs[-5:]
    r = pl.program_id(0)
    length = q_ref.shape[0]
    low = lax.broadcasted_iota(jnp.int32, (1, 128), 1) < 64
    prod = (do_ref[...].astype(F32) * o_ref[...].astype(F32)).T
    dl_ref[0:1, :] = jnp.sum(prod[0:64], axis=0, keepdims=True)
    dl_ref[1:2, :] = jnp.sum(prod[64:128], axis=0, keepdims=True)

    def block(ks, kn, qs, qn):
        k = k_ref[pl.ds(ks, kn), :]
        v = v_ref[pl.ds(ks, kn), :]
        q = q_ref[pl.ds(qs, qn), :]
        do = do_ref[pl.ds(qs, qn), :]
        dks = []
        dvs = []
        dqs = []
        for h in range(2):
            sel = low if h == 0 else jnp.logical_not(low)
            km = jnp.where(sel, k, jnp.asarray(0, BF))
            vm = jnp.where(sel, v, jnp.asarray(0, BF))
            pt = jnp.exp2(dg(km, q, NT) - l_ref[0, 0, h : h + 1, pl.ds(qs, qn)])
            dst = (pt * (dg(vm, do, NT) - dl_ref[h : h + 1, pl.ds(qs, qn)])).astype(BF)
            dvs.append(dg(pt.astype(BF), do, NN))
            dks.append(dg(dst, q, NN))
            dqs.append(dg(km.T, dst, NN))
        return jnp.where(low, dks[0], dks[1]), jnp.where(low, dvs[0], dvs[1]), dqs[0] + dqs[1]

    def run(kn, qn, plan):
        seen = set()
        for ks, starts in plan:
            dk = dv = None
            for qs in starts:
                a, b, dq = block(ks, kn, qs, qn)
                dk = a if dk is None else dk + a
                dv = b if dv is None else dv + b
                if qs in seen:
                    dqt_ref[:, pl.ds(qs, qn)] += dq
                else:
                    dqt_ref[:, pl.ds(qs, qn)] = dq
                seen.add(qs)
            dk_ref[pl.ds(ks, kn), :] = (dk * LN2).astype(BF)
            dv_ref[pl.ds(ks, kn), :] = dv.astype(BF)
        dq_ref[...] = (dqt_ref[...].T * 0.125).astype(BF)

    @pl.when(tag_ref[r] == 0)
    def _():
        run(kb, qb, [(ks, range(0, length, qb)) for ks in range(0, length, kb)])

    @pl.when(tag_ref[r] != 0)
    def _():
        c = length // 4
        run(c, c, [(ks, [ks]) for ks in range(0, length, c)])


def attend_back(tag, q, k, v, do, o, lse, first, pairs, before=(), kb=512, qb=512):
    t, d = q.shape
    rows = tag.shape[0]
    length = t // rows
    blk = pl.BlockSpec((length, 128), lambda r, p, _: (r, p + first))
    lse_spec = pl.BlockSpec((1, 1, 2, length), lambda r, p, _: (r, p + first, 0, 0))
    return pl.pallas_call(
        functools.partial(attend_back_kernel, kb=kb, qb=qb),
        grid_spec=pltpu.PrefetchScalarGridSpec(
            num_scalar_prefetch=1,
            grid=(rows, pairs),
            in_specs=[blk] * 5 + [lse_spec] + [ANY] * len(before),
            out_specs=[blk] * 3,
            scratch_shapes=[pltpu.VMEM((2, length), F32), pltpu.VMEM((128, length), F32)],
        ),
        out_shape=[SDS((t, d), BF)] * 3,
        input_output_aliases={7: 0, 8: 1, 9: 2} if before else {},
        compiler_params=params(2),
        cost_estimate=cost(5120 * t * length * pairs, t * d * 16, t * length * 12),
        name="attend_back",
    )(tag, q, k, v, do, o, lse, *before)


def grad_qkv_kernel(idx_ref, h_any, dq_any, dk_any, dv_any, *refs, rows):
    h_ref, d_ref, sem = refs[-3:]
    w = d_ref.shape[2]
    half = idx_ref[1] if rows is not None else 1 - idx_ref[1]
    cols = pl.ds(pl.multiple_of(half * w, 128), w)
    going = [pltpu.make_async_copy(h_any, h_ref, sem.at[3])]
    for m, ref in enumerate((dq_any, dk_any, dv_any)):
        going.append(pltpu.make_async_copy(ref.at[:, cols], d_ref.at[m], sem.at[m]))
    for cp in going:
        cp.start()
    going[0].wait()
    for m in range(3):
        at = slice(m * w, (m + 1) * w)
        going[1 + m].wait()
        part = dg(h_ref[...], d_ref[m], TN)
        if rows is None:
            refs[0][:, at] = part.astype(BF)
        else:
            outs, sum_ref = refs[1:-4], refs[-4]
            q = len(outs)
            sum_ref[...] = part + refs[0][:, at].astype(F32)
            for e in range(q):
                for z in range(4):
                    s = z * q + lax.bitwise_xor(idx_ref[0] % q, jnp.int32(e))
                    outs[e][z, :, at] = sum_ref[pl.ds(pl.multiple_of(s * rows, 8), rows), :].astype(BF)


def grad_qkv(idx, h1, dq, dk, dv, recv=None, n=None):
    t, d = h1.shape
    w = d // 2
    own = recv is not None
    outs = [(4, d // n, 3 * w)] * (n // 4) if own else [(d, 3 * w)]
    return pl.pallas_call(
        functools.partial(grad_qkv_kernel, rows=d // n if own else None),
        grid_spec=pltpu.PrefetchScalarGridSpec(
            num_scalar_prefetch=1,
            grid=(1,),
            in_specs=[ANY] * 4 + [whole((d, 3 * w))] * own,
            out_specs=[fixed(o) for o in outs],
            scratch_shapes=[pltpu.VMEM((d, w), F32)] * own
            + [pltpu.VMEM((t, d), BF), pltpu.VMEM((3, t, w), BF), pltpu.SemaphoreType.DMA((4,))],
        ),
        out_shape=[pltpu.HBM(o, BF) for o in outs],
        compiler_params=params(),
        cost_estimate=cost(6 * t * d * w, t * d * 6),
        name="grad_qkv_own" if own else "grad_qkv_other",
    )(idx, h1, dq, dk, dv, *([recv] * own))


def tokens_back_kernel(idx_ref, x_ref, vt_ref, dx2_ref, dq_ref, dk_ref, dv_ref, *refs):
    pieces = refs[:-4]
    tg_ref, s_ref, w_ref, sem = refs[-4:]
    d = x_ref.shape[1]

    @pl.when(pl.program_id(0) == 0)
    def _():
        going = load_qkv(idx_ref, pieces, w_ref, sem)
        s_ref[...] = jnp.zeros_like(s_ref)
        for cp in going:
            cp.wait()

    dh = dg(dq_ref[...], w_ref[:, :d], NT)
    dh = dh + dg(dk_ref[...], w_ref[:, d : 2 * d], NT)
    dh = dh + dg(dv_ref[...], w_ref[:, 2 * d :], NT)
    ones = jnp.ones((8, x_ref.shape[0]), BF)
    s_ref[2:3, :] += dg(ones, dq_ref[...], NN)[0:1]
    s_ref[3:4, :] += dg(ones, dv_ref[...], NN)[0:1]
    c, r = norm_stats(x_ref[...].astype(F32))
    xh = c * r
    s_ref[0:1, :] += jnp.sum(dh * xh, axis=0, keepdims=True)
    s_ref[1:2, :] += jnp.sum(dh, axis=0, keepdims=True)
    dz = dh * vt_ref[0:1, :]
    m1 = jnp.sum(dz, axis=-1, keepdims=True) * (1.0 / d)
    m2 = jnp.sum(dz * xh, axis=-1, keepdims=True) * (1.0 / d)
    tg_ref[...] = dx2_ref[...] + r * (dz - m1 - xh * m2)


def tokens_back(idx, dq, dk, dv, x, vt, dx2, pieces, tb=512):
    t, d = x.shape
    return pl.pallas_call(
        tokens_back_kernel,
        grid_spec=pltpu.PrefetchScalarGridSpec(
            num_scalar_prefetch=1,
            grid=(t // tb,),
            in_specs=[rows_of(tb, d), whole(vt.shape)] + [rows_of(tb, d)] * 4 + [ANY] * len(pieces),
            out_specs=[rows_of(tb, d), fixed((8, d))],
            scratch_shapes=[pltpu.VMEM((d, 3 * d), BF), pltpu.SemaphoreType.DMA],
        ),
        out_shape=[SDS((t, d), F32), SDS((8, d), F32)],
        compiler_params=params(),
        cost_estimate=cost(9 * t * d * d, t * d * 16 + d * d * 6),
        name="tokens_back",
    )(idx, x, vt, dx2, dq, dk, dv, *pieces)


def hop(x, groups):
    return lax.all_to_all(x, "fsdp", split_axis=0, concat_axis=0, tiled=True, axis_index_groups=groups)


def sum_cores_kernel(idx_ref, *refs, q):
    outs = refs[-q:]
    rows = outs[0].shape[1]
    for e in range(q):
        at = lax.bitwise_xor(idx_ref[0] % q, jnp.int32(e))
        start = 0
        for a_ref, b_ref in zip(refs[:-q:2], refs[1:-q:2], strict=True):
            total = a_ref[at] + b_ref[at]
            w = total.shape[1]
            for j in range(total.shape[0] // rows):
                outs[e][0, :, start : start + w] = total[j * rows : (j + 1) * rows]
                start += w


def sum_cores(idx, pairs, rows, n):
    q = n // 4
    ops, specs, width = [], [], 0
    for pair in pairs:
        shape = (pair[0].shape[0] // n, pair[0].shape[1])
        width += shape[0] // rows * shape[1]
        ops += [x.reshape((n,) + shape) for x in pair]
        specs += [pl.BlockSpec((q,) + shape, lambda z, _: (z, 0, 0))] * 2
    return pl.pallas_call(
        functools.partial(sum_cores_kernel, q=q),
        grid_spec=pltpu.PrefetchScalarGridSpec(
            num_scalar_prefetch=1,
            grid=(4,),
            in_specs=specs,
            out_specs=[pl.BlockSpec((1, rows, width), lambda z, _: (z, 0, 0))] * q,
        ),
        out_shape=[pltpu.HBM((4, rows, width), BF)] * q,
        compiler_params=params(),
        cost_estimate=cost(n * rows * width, n * rows * width * 6),
        name="sum_cores",
    )(idx, *ops)


def spread(parts, n):
    return [parts[0]] + [xor_pp(parts[e], e, n) for e in range(1, n // 4)]


def sum_parts_kernel(*refs):
    total = refs[0][...].astype(F32)
    for x in refs[1:-1]:
        total = total + x[...].astype(F32)
    refs[-1][...] = total.astype(BF)


def sum_parts(parts):
    shape = (1,) + parts[0].shape[1:]
    spec = pl.BlockSpec(shape, lambda i: (i, 0, 0))
    return pl.pallas_call(
        sum_parts_kernel,
        grid=(4,),
        in_specs=[spec] * len(parts),
        out_specs=spec,
        out_shape=pltpu.HBM(parts[0].shape, BF),
        compiler_params=params(),
        cost_estimate=cost(4 * len(parts) * math.prod(shape), 8 * len(parts) * math.prod(shape)),
        name="sum_parts",
    )(*parts)


def sum_qkv_kernel(idx_ref, *refs, q):
    for d in range(4):
        at = lax.bitwise_xor(idx_ref[0] // q, jnp.int32(d))
        start = 0
        for parts in (refs[:q], refs[q : 2 * q]):
            total = parts[0][at].astype(F32)
            for x in parts[1:]:
                total = total + x[at].astype(F32)
            w = total.shape[1]
            refs[2 * q + d][:, start : start + w] = total.astype(BF)
            start += w


def sum_qkv(idx, far, vecs, n):
    _, rows, w = far[0].shape
    width = w + vecs[0].shape[2]
    ops = list(far) + list(vecs)
    near = pl.pallas_call(
        functools.partial(sum_qkv_kernel, q=n // 4),
        grid_spec=pltpu.PrefetchScalarGridSpec(
            num_scalar_prefetch=1,
            grid=(1,),
            in_specs=[whole(x.shape) for x in ops],
            out_specs=[fixed((rows, width))] * 4,
        ),
        out_shape=[pltpu.HBM((rows, width), BF)] * 4,
        compiler_params=params(),
        cost_estimate=cost(n * rows * width, n * rows * width * 3),
        name="sum_qkv",
    )(idx, *ops)
    return near


def reduce_last(near, n, m):
    total = near[0].astype(F32)
    for x in near[1:]:
        total = total + x.astype(F32)
    return over_pairs(total, m)


def over_pairs(total, m):
    b = 2
    while b < m:
        total = total + lax.ppermute(total.astype(BF), "dp", [(i, i ^ b) for i in range(m)]).astype(F32)
        b *= 2
    return total


def vec_table_kernel(idx_ref, a, c, u, *refs, q):
    table_ref = refs[q]
    d = a.shape[1]
    rows = refs[0].shape[1]
    wide = u.shape[1] // d
    bias = [
        jnp.concatenate(
            [u[:, (s * wide + j) * rows : (s * wide + j + 1) * rows] for s in range(4 * q)], axis=1
        )
        for j in range(wide)
    ]
    lines = [c[0:4, :], a[3:4, :], a[1:3, :], a[0:1, :]] + bias + [jnp.zeros((120 - wide, d), F32)]
    table_ref[...] = jnp.concatenate(lines, axis=0).T
    for e in range(q):
        for z in range(4):
            s = z * q + lax.bitwise_xor(idx_ref[0] % q, jnp.int32(e))
            refs[e][z] = table_ref[pl.ds(pl.multiple_of(s * rows, 8), rows), :].astype(BF)


def vec_table(idx, s_mlp, s_tok, gbu, n):
    d = s_mlp.shape[1]
    q = n // 4
    return pl.pallas_call(
        functools.partial(vec_table_kernel, q=q),
        grid_spec=pltpu.PrefetchScalarGridSpec(
            num_scalar_prefetch=1,
            grid=(1,),
            in_specs=[whole(s_mlp.shape), whole(s_tok.shape), whole(gbu.shape)],
            out_specs=[fixed((4, d // n, 128))] * q,
            scratch_shapes=[pltpu.VMEM((d, 128), F32)],
        ),
        out_shape=[SDS((4, d // n, 128), BF)] * q,
        compiler_params=params(),
        cost_estimate=cost(d * 128, d * 1024),
        name="vec_table",
    )(idx, s_mlp, s_tok, gbu)


def local(
    tokens,
    sensor_tag,
    owner_order,
    ln1_gain,
    ln1_bias,
    w_qkv,
    b_query,
    b_value,
    w_out,
    b_out,
    ln2_gain,
    ln2_bias,
    w_up,
    b_up,
    w_down,
    b_down,
    out_grad,
    *,
    n,
    m,
):
    t, d = tokens.shape
    ff = w_up.shape[1]
    rows = d // n
    wide = ff // d
    f = lax.axis_index("fsdp")
    c = lax.axis_index("dp") % 2
    idx = jnp.stack([f, c]).astype(jnp.int32)
    use = idx if fits(rows, n) else jnp.zeros_like(idx)

    def core_half(x):
        h = x.shape[1] // 2
        return jnp.where(c == 0, x[:, :h], x[:, h:])

    vec = jnp.stack([ln1_gain, ln1_bias, b_query, b_value, b_out, ln2_gain, ln2_bias, b_down], axis=1)
    vec = jnp.concatenate([vec, b_up.reshape(wide, rows).T], axis=1)
    vec = jnp.pad(vec, ((0, 0), (0, 128 - vec.shape[1])))
    shard_a = jnp.concatenate([core_half(w_qkv), vec], axis=1)
    shard_b = jnp.concatenate(
        [core_half(jnp.concatenate([w_out, w_up], axis=1))]
        + [core_half(w_down[j * rows : (j + 1) * rows]) for j in range(wide)],
        axis=1,
    )
    q = n // 4
    everyone = jnp.arange(n)

    near_a = gather_near(shard_a, n)
    near_b = hop(jnp.broadcast_to(after(shard_b, near_a)[None], (4,) + shard_b.shape), tops(n))
    own_a = gather_far(near_a, n)
    cast = after(out_grad, near_a).astype(BF)
    own_a[1:] = after(own_a[1:], cast)
    swap_a = [core_swap(near_a, m), core_swap(jnp.stack(own_a[1:]), m)]
    if fits(rows, n):
        pieces_a = own_a + swap_a
    else:
        pieces_a = settle(own_a + swap_a[:1] + [swap_a[1][e] for e in range(q - 1)], f ^ everyone, c, n)
    near_b = after(near_b, own_a[1:])
    qh, kh, vh, h1, vt, bu = qkv(use, after(tokens, near_b), pieces_a)
    pairs = d // 128
    early = pairs * 2 // 3
    if fits(rows, n):
        first = [near_b[..., : (d + ff) // 2], near_b[..., (d + ff) // 2 :]]
        bits = (1, 2)
        second = [xor_pp(x, b, n) for x, b in zip(first, bits, strict=True)]
        both_b = [jnp.stack([x, y]) for x, y in zip(first, after(second, vt), strict=True)]
        far_b = [xor_pp(x, b, n) for x, b in zip(both_b, bits[::-1], strict=True)]
        part = attend(sensor_tag, after(qh, both_b), kh, vh, 0, early)
        far_b = after(far_b, part[0])
        pieces_b = []
        for x, y in zip(both_b, far_b, strict=True):
            pieces_b += [x, y, core_swap(x, m), core_swap(y, m)]
    else:
        far_b = gather_far(near_b, n)
        side = settle(
            far_b + [core_swap(x, m) for x in far_b], everyone // q * q + (everyone ^ f) % q, c, n, wide
        )
        part = attend(sensor_tag, qh, kh, vh, 0, early)
        cut = (d + ff) // 2
        one = [x[..., :cut] for x in side]
        two = [x[..., cut:] for x in side]
        pieces_b = [jnp.stack(one[i : i + 2]) for i in (0, 2, 4, 6)]
        pieces_b += [jnp.stack([two[i], two[i + 2]]) for i in (0, 1, 4, 5)]
    returned = lax.all_to_all(after(cast, far_b), "fsdp", split_axis=0, concat_axis=0, tiled=True)
    mixed, lse = attend(sensor_tag, qh, kh, vh, early, pairs - early, part)

    x2, active, slope, y = mlp(use, tokens, mixed, vt, bu, pieces_b)
    sent = permute(owner_order, y)
    encoded = lax.all_to_all(sent, "fsdp", split_axis=0, concat_axis=0, tiled=True)

    returned = after(returned, sent)
    dm, du, dx2, do, h2, s_mlp, gbu, out_own, out_other = mlp_back(
        use, owner_order, returned, slope, x2, mixed, vt, pieces_b
    )
    out_recv = core_swap(out_other, m)
    down_own, down_other, up_own, up_other = grad_mlp(idx, active, dm, h2, du)
    down_recv = core_swap(down_other, m)
    up_recv = core_swap(up_other, m)
    part = attend_back(sensor_tag, qh, kh, vh, after(do, up_own, encoded), mixed, lse, 0, 1)
    out_recv, down_recv, up_recv = after((out_recv, down_recv, up_recv), part[0])
    pairs_b = [(up_own, up_recv), (out_own, out_recv), (down_own, down_recv)]
    far_b = sum_cores(idx, pairs_b, rows, n)
    do = after(do, far_b[0])
    far_b = spread(far_b, n)
    dj = attend_back(sensor_tag, qh, kh, vh, do, mixed, lse, 1, pairs - 1, part)
    (qkv_other,) = grad_qkv(idx, h1, *dj)
    qkv_recv = core_swap(qkv_other, m)
    far_b = after(far_b, dj[0])
    near_b = sum_parts([after(far_b[0], qkv_other)] + far_b[1:])
    total_b = hop(near_b, tops(n))
    far_a = grad_qkv(idx, after(h1, near_b), *dj, qkv_recv, n)
    dj = after(dj, far_a[0])
    far_a = spread(far_a, n)
    tokens_grad, s_tok = tokens_back(use, *dj, tokens, vt, dx2, pieces_a)
    far_a, total_b = after((far_a, total_b), tokens_grad)
    total_b = over_pairs(jnp.sum(total_b.astype(F32), axis=0), m).astype(BF)
    other_b = core_swap(total_b, m)
    far_v = spread(vec_table(idx, s_mlp, s_tok, after(gbu, far_a), n), n)

    near_a = sum_qkv(idx, after(far_a, total_b), far_v, n)
    encoded = after(encoded, near_a[0]).astype(F32)
    near_a = [near_a[0]] + [xor_pp(near_a[i], i * q, n) for i in range(1, 4)]
    def both(mine, other):
        first = c == 0
        return jnp.where(first, mine, other).astype(F32), jnp.where(first, other, mine).astype(F32)

    def join(pair, start, width, parts, axis=1):
        out = []
        for p in range(parts):
            at = slice(start + p * width, start + (p + 1) * width)
            out.append(jnp.concatenate([pair[0][:, at], pair[1][:, at]], axis=1))
        return jnp.concatenate(out, axis=axis)

    h = d // 2
    g_mlp = both(total_b, other_b)
    grad_up_out = join(g_mlp, 0, h, wide)
    grad_out_out = join(g_mlp, ff // 2, h, 1)
    grad_down_out = join(g_mlp, (d + ff) // 2, h, wide, 0)
    near_a = after(near_a, grad_up_out, grad_out_out, grad_down_out, encoded)
    total_a = reduce_last(near_a, n, m)
    other_a = core_swap(total_a.astype(BF), m)
    cut = 3 * d // 2
    vecs = (total_a[:, cut:] + other_a[:, cut:].astype(F32)).T
    total_a, other_a = total_a[:, :cut].astype(BF), other_a[:, :cut]

    grad_qkv_out = join(both(total_a, other_a), 0, h, 3)
    return (
        encoded,
        tokens_grad,
        vecs[0],
        vecs[1],
        grad_qkv_out,
        vecs[2],
        vecs[3],
        grad_out_out,
        vecs[4],
        vecs[5],
        vecs[6],
        grad_up_out,
        vecs[8 : 8 + wide].reshape(ff // n),
        grad_down_out,
        vecs[7],
    )


def solution(mesh):
    n = mesh.shape["fsdp"]
    m = mesh.shape["dp"]
    both = P(("dp", "fsdp"), None)
    vec = P("fsdp")
    mat = P("fsdp", None)
    in_specs = (both, P(("dp", "fsdp")), both, vec, vec, mat, vec, vec, mat, vec, vec, vec, mat, vec, mat, vec, both)
    out_specs = (both, both, vec, vec, mat, vec, vec, mat, vec, vec, vec, mat, vec, mat, vec)
    return jax.shard_map(
        functools.partial(local, n=n, m=m), mesh=mesh, in_specs=in_specs, out_specs=out_specs, check_vma=False
    )
```

```python
import functools
import math

import jax
import jax.numpy as jnp
from jax import lax
from jax.experimental import pallas as pl
from jax.experimental.pallas import tpu as pltpu
from jax.sharding import PartitionSpec as P

F32 = jnp.float32
BF = jnp.bfloat16
EPS = 1e-6
LOG2E = math.log2(math.e)
LN2 = math.log(2.0)
NT = (((1,), (1,)), ((), ()))
TN = (((0,), (0,)), ((), ()))
NN = (((1,), (0,)), ((), ()))
ANY = pl.BlockSpec(memory_space=pl.ANY)
VECS = 16
SDS = jax.ShapeDtypeStruct


def dg(a, b, dims):
    return lax.dot_general(a, b, dims, preferred_element_type=F32)


def params(axes=1):
    return pltpu.CompilerParams(
        vmem_limit_bytes=58 * 2**20, dimension_semantics=("arbitrary",) * axes
    )


def cost(flops, nbytes, trans=0):
    return pl.CostEstimate(flops=int(flops) >> 10, bytes_accessed=int(nbytes) >> 10, transcendentals=int(trans) >> 10)


def rows_of(height, width):
    return pl.BlockSpec((height, width), lambda i, *_: (i, 0))


def whole(shape):
    zeros = (0,) * len(shape)
    return pl.BlockSpec(shape, lambda *_: zeros, pipeline_mode=pl.Buffered(1))


def fixed(shape):
    zeros = (0,) * len(shape)
    return pl.BlockSpec(shape, lambda *_: zeros)


def norm_stats(x):
    n = x.shape[-1]
    c = x - jnp.sum(x, axis=-1, keepdims=True) * (1.0 / n)
    var = jnp.sum(c * c, axis=-1, keepdims=True) * (1.0 / n)
    return c, lax.rsqrt(var + EPS)


def after(x, *deps):
    return lax.optimization_barrier((x,) + deps)[0]


def xor_pp(x, b, n):
    return lax.ppermute(x, "fsdp", [(i, i ^ b) for i in range(n)])


def core_swap(x, m):
    return lax.ppermute(x, "dp", [(i, i ^ 1) for i in range(m)])


def gather_near(x, n):
    q = n // 4
    return jnp.stack([x] + [xor_pp(x, d * q, n) for d in (1, 2, 3)])


def tops(n):
    q = n // 4
    return [[low + z * q for z in range(4)] for low in range(q)]


def gather_far(s, n):
    return [s] + [xor_pp(s, e, n) for e in range(1, n // 4)]


def fits(rows, n):
    return rows % 16 == 0 and n == 16


def settle(pieces, order, c, n, wide=None):
    q = n // 4
    rows, width = pieces[0].shape[1:]
    if fits(rows, n):
        return pieces
    height = n * rows // 16
    halves = []
    for side in (pieces[:q], pieces[q:]):
        rel = jnp.stack(side, axis=1).reshape((n, rows, width))
        whole_side = jnp.take(rel, order, axis=0)
        flat = whole_side.reshape(16, height, width)
        if wide is not None:
            cut = width * (wide + 1) // (2 * wide + 1)
            low = whole_side[..., cut:].reshape(n, rows, wide, -1).transpose(0, 2, 1, 3)
            low = low.reshape(16, wide, height, -1).transpose(0, 2, 1, 3).reshape(16, height, -1)
            flat = jnp.concatenate([flat[..., :cut], low], axis=2)
        halves.append(flat.reshape(4, 4, height, width))
    left, right = jnp.where(c == 0, halves[0], halves[1]), jnp.where(c == 0, halves[1], halves[0])
    return [side[:, e] for side in (left, right) for e in range(4)]


def load_pieces(idx_ref, plan, sem):
    c = idx_ref[1]
    started = []
    for find, shard, start, skip, width, dst, height, first in plan:
        for e in range(4):
            for d in range(4):
                for block, h in zip(find(e, d), (c, 1 - c), strict=False):
                    rows = block.shape[0]
                    at = pl.ds(pl.multiple_of(shard(e, d) * height + first, 16), rows)
                    cols = pl.ds(pl.multiple_of(h * width, 128), width) if dst.shape[1] > width else slice(None)
                    src = block.at[:, pl.ds(start if e else start + skip, width)]
                    started.append(pltpu.make_async_copy(src, dst.at[at, cols], sem))
    for cp in started:
        cp.start()
    return started


def relative(idx_ref):
    return lambda e, d: lax.bitwise_xor(idx_ref[0], jnp.int32(d * 4 + e))


def by_top(idx_ref):
    return lambda e, d: lax.bitwise_xor(idx_ref[0] % 4, jnp.int32(e)) + d * 4


def load_qkv(idx_ref, pieces, w_ref, sem, vec_ref=None):
    def find(e, d):
        if len(pieces) == 8:
            return pieces[e].at[d], pieces[4 + e].at[d]
        return pieces[e].at[d], pieces[5].at[e - 1, d] if e else pieces[4].at[d]

    where = relative(idx_ref)
    rows, half = pieces[0].shape[1], w_ref.shape[1] // 2
    if vec_ref is not None:
        return load_pieces(idx_ref, [(lambda e, d: find(e, d)[:1], where, half, 0, 128, vec_ref, rows, 0)], sem)
    return load_pieces(idx_ref, [(find, where, 0, 0, half, w_ref, rows, 0)], sem)


def load_mlp(idx_ref, pieces, w1_ref, w2_ref, sem):
    where = by_top(idx_ref)

    def find1(e, d):
        return pieces[2 * e].at[d], pieces[2 * e + 1].at[d]

    def find2(e, d):
        at = 6 + 2 * e if e else 0
        return pieces[at].at[d], pieces[at + 1].at[d]

    rows = pieces[0].shape[1]
    half = w1_ref.shape[1] // 2
    w = w2_ref.shape[1] // 2
    one = [(find1, where, 0, 0, half, w1_ref, rows, 0)]
    two = [(find2, where, j * w, half, w, w2_ref, 4 * rows, j * rows) for j in range(4)]
    return load_pieces(idx_ref, one, sem.at[0]), load_pieces(idx_ref, two, sem.at[1])


def wait_mlp(w_ref, sem):
    pltpu.make_async_copy(w_ref, w_ref, sem).wait()


def qkv_kernel(idx_ref, x_ref, *refs):
    pieces = refs[:-9]
    q_ref, k_ref, v_ref, h_ref, vt_ref, bu_ref, w_ref, vec_ref, sem = refs[-9:]
    d = x_ref.shape[1]

    @pl.when(pl.program_id(0) == 0)
    def _():
        rows = pieces[0].shape[1]
        vecs = load_qkv(idx_ref, pieces, w_ref, sem.at[1], vec_ref)
        going = load_qkv(idx_ref, pieces, w_ref, sem.at[0])
        for cp in vecs:
            cp.wait()
        table = vec_ref[...].astype(F32).T[:VECS]
        vt_ref[...] = table
        bu_ref[...] = jnp.concatenate(
            [table[8 + j : 9 + j, s * rows : (s + 1) * rows] for s in range(d // rows) for j in range(4)], axis=1
        )
        for cp in going:
            cp.wait()

    c, r = norm_stats(x_ref[...].astype(F32))
    h = (c * r * vt_ref[0:1, :] + vt_ref[1:2, :]).astype(BF)
    h_ref[...] = h
    q = dg(h, w_ref[:, :d], NN)
    q_ref[...] = ((q + vt_ref[2:3, :]) * (0.125 * LOG2E)).astype(BF)
    k_ref[...] = dg(h, w_ref[:, d : 2 * d], NN).astype(BF)
    v_ref[...] = (dg(h, w_ref[:, 2 * d :], NN) + vt_ref[3:4, :]).astype(BF)


def qkv(idx, x, pieces, tb=512):
    t, d = x.shape
    return pl.pallas_call(
        qkv_kernel,
        grid_spec=pltpu.PrefetchScalarGridSpec(
            num_scalar_prefetch=1,
            grid=(t // tb,),
            in_specs=[rows_of(tb, d)] + [ANY] * len(pieces),
            out_specs=[rows_of(tb, d)] * 4 + [fixed((VECS, d)), fixed((1, 4 * d))],
            scratch_shapes=[
                pltpu.VMEM((d, 3 * d), BF),
                pltpu.VMEM((d, 128), BF),
                pltpu.SemaphoreType.DMA((2,)),
            ],
        ),
        out_shape=[SDS((t, d), BF)] * 4 + [SDS((VECS, d), F32), SDS((1, 4 * d), F32)],
        compiler_params=params(),
        cost_estimate=cost(6 * t * d * d, t * d * 8 + d * d * 6),
        name="qkv",
    )(idx, x, *pieces)


def attend_kernel(tag_ref, q_ref, k_ref, v_ref, *refs, qb):
    o_ref, l_ref = refs[-2:]
    r = pl.program_id(0)
    length = q_ref.shape[0]
    low = lax.broadcasted_iota(jnp.int32, (1, 128), 1) < 64

    def block(qs, qn, ks, kn):
        q = q_ref[pl.ds(qs, qn), :]
        k = k_ref[pl.ds(ks, kn), :]
        v = v_ref[pl.ds(ks, kn), :]
        outs = []
        for h in range(2):
            sel = low if h == 0 else jnp.logical_not(low)
            qm = jnp.where(sel, q, jnp.asarray(0, BF))
            vm = jnp.where(sel, v, jnp.asarray(1, BF))
            s = dg(qm, k, NT)
            m = jnp.max(s, axis=1, keepdims=True)
            outs.append((dg(jnp.exp2(s - m).astype(BF), vm, NN), m))
        (a, ma), (b, mb) = outs
        acc = jnp.where(low, a, b)
        total = pltpu.roll(jnp.where(low, b, a), 64, 1)
        o_ref[pl.ds(qs, qn), :] = (acc / total).astype(o_ref.dtype)
        lse = (jnp.where(low, ma, mb) + jnp.log2(total)).T
        l_ref[0, 0, 0:1, pl.ds(qs, qn)] = lse[0:1]
        l_ref[0, 0, 1:2, pl.ds(qs, qn)] = lse[64:65]

    @pl.when(tag_ref[r] == 0)
    def _():
        for i in range(length // qb):
            block(i * qb, qb, 0, length)

    @pl.when(tag_ref[r] != 0)
    def _():
        c = length // 4
        for i in range(4):
            block(i * c, c, i * c, c)


def attend(tag, q, k, v, first, pairs, before=(), qb=512):
    t, d = q.shape
    rows = tag.shape[0]
    length = t // rows
    blk = pl.BlockSpec((length, 128), lambda r, p, _: (r, p + first))
    lse = pl.BlockSpec((1, 1, 2, length), lambda r, p, _: (r, p + first, 0, 0))
    return pl.pallas_call(
        functools.partial(attend_kernel, qb=qb),
        grid_spec=pltpu.PrefetchScalarGridSpec(
            num_scalar_prefetch=1,
            grid=(rows, pairs),
            in_specs=[blk] * 3 + [ANY] * len(before),
            out_specs=[blk, lse],
        ),
        out_shape=[SDS((t, d), BF), SDS((rows, d // 128, 2, length), F32)],
        input_output_aliases={4: 0, 5: 1} if before else {},
        compiler_params=params(2),
        cost_estimate=cost(2048 * t * length * pairs, t * d * 8, t * length * 12),
        name="attend",
    )(tag, q, k, v, *before)


ODDS = (2.3021649, 1.05007451e-1, -2.545477e-4, -1.0560537e-4, 4.093017e-6)


def gelu_both(u):
    z = u * u
    odds = ODDS[3] + z * ODDS[4]
    odds = ODDS[2] + z * odds
    odds = ODDS[1] + z * odds
    odds = ODDS[0] + z * odds
    phi = pltpu.reciprocal(1.0 + jnp.exp2(-u * odds), approx=True)
    density = jnp.exp2(z * (-0.5 * LOG2E) - 0.5 * math.log2(2.0 * math.pi))
    return u * phi, phi + u * density


def mlp_kernel(idx_ref, x_ref, o_ref, vt_ref, bu_ref, *refs, fc):
    pieces = refs[:14]
    x2_ref, gl_ref, gp_ref, y_ref, w1_ref, w2_ref, sem = refs[14:]
    d = x_ref.shape[1]
    ff = w2_ref.shape[0]

    @pl.when(pl.program_id(0) == 0)
    def _():
        going, _ = load_mlp(idx_ref, pieces, w1_ref, w2_ref, sem)
        for cp in going:
            cp.wait()

    x2 = x_ref[...].astype(F32) + dg(o_ref[...], w1_ref[:, :d], NN) + vt_ref[4:5, :]
    x2_ref[...] = x2
    c, r = norm_stats(x2)
    h = (c * r * vt_ref[5:6, :] + vt_ref[6:7, :]).astype(BF)
    y = x2 + vt_ref[7:8, :]

    @pl.when(pl.program_id(0) == 0)
    def _():
        wait_mlp(w2_ref, sem.at[1])

    for f in range(0, ff, fc):
        u = dg(h, w1_ref[:, d + f : d + f + fc], NN) + bu_ref[:, f : f + fc]
        g, gp = gelu_both(u)
        g = g.astype(BF)
        gl_ref[:, f : f + fc] = g
        gp_ref[:, f : f + fc] = gp.astype(BF)
        y = y + dg(g, w2_ref[f : f + fc, :], NN)
    y_ref[...] = y.astype(BF)


def mlp(idx, x, o, vt, bu, pieces, tb=256, fc=768):
    t, d = x.shape
    ff = bu.shape[1]
    return pl.pallas_call(
        functools.partial(mlp_kernel, fc=fc),
        grid_spec=pltpu.PrefetchScalarGridSpec(
            num_scalar_prefetch=1,
            grid=(t // tb,),
            in_specs=[rows_of(tb, d)] * 2 + [whole(vt.shape), whole(bu.shape)] + [ANY] * 14,
            out_specs=[rows_of(tb, d), rows_of(tb, ff), rows_of(tb, ff), rows_of(tb, d)],
            scratch_shapes=[
                pltpu.VMEM((d, d + ff), BF),
                pltpu.VMEM((ff, d), BF),
                pltpu.SemaphoreType.DMA((2,)),
            ],
        ),
        out_shape=[SDS((t, d), F32), SDS((t, ff), BF), SDS((t, ff), BF), SDS((t, d), BF)],
        compiler_params=params(),
        cost_estimate=cost(4 * t * d * (d + 2 * ff), t * (10 * d + 4 * ff) + 4 * d * ff, 2 * t * ff),
        name="mlp",
    )(idx, x, o, vt, bu, *pieces)


def permute_kernel(ord_ref, y_ref, o_ref):
    jb = o_ref.shape[0]
    t = y_ref.shape[0]
    order = jnp.broadcast_to(ord_ref[...].astype(F32), (8, jb)).T[:, 0:1]
    hot = jnp.where(order == lax.broadcasted_iota(jnp.int32, (jb, t), 1).astype(F32), 1.0, 0.0)
    o_ref[...] = dg(hot.astype(BF), y_ref[...], NN).astype(BF)


def permute(order, y, jb=512):
    t, d = y.shape
    return pl.pallas_call(
        permute_kernel,
        grid=(t // jb,),
        in_specs=[pl.BlockSpec((1, jb), lambda i: (0, i)), whole((t, d))],
        out_specs=rows_of(jb, d),
        out_shape=pltpu.HBM((t, d), BF),
        compiler_params=params(),
        cost_estimate=cost(2 * t * t * d, t * d * 4),
        name="permute",
    )(order, y)


def split_halves(c, r, mine_ref, theirs_ref):
    h = r.shape[1] // 2
    left, right = r[:, :h], r[:, h:]
    mine_ref[...] = jnp.where(c == 0, left, right)
    theirs_ref[...] = jnp.where(c == 0, right, left)


def mlp_back_kernel(idx_ref, ord_ref, ret_ref, gp_ref, x2_ref, o_ref, vt_ref, *refs, fc):
    pieces = refs[:14]
    (dm_ref, du_ref, dx2_ref, do_ref, h2_ref, sums_ref, gbu_ref, mine_ref, theirs_ref) = refs[14:23]
    w1_ref, w2_ref, acc_ref, sem = refs[23:]
    i = pl.program_id(0)
    tb, ff = gp_ref.shape
    t, d = ret_ref.shape

    @pl.when(i == 0)
    def _():
        load_mlp(idx_ref, pieces, w1_ref, w2_ref, sem)
        sums_ref[...] = jnp.zeros_like(sums_ref)
        gbu_ref[...] = jnp.zeros_like(gbu_ref)
        acc_ref[...] = jnp.zeros_like(acc_ref)
        wait_mlp(w2_ref, sem.at[1])
        wait_mlp(w1_ref, sem.at[0])

    at = lax.broadcasted_iota(jnp.int32, (tb, t), 0) + i * tb
    hot = jnp.where(ord_ref[...] == at, 1.0, 0.0).astype(BF)
    dy = dg(hot, ret_ref[...], NN)
    dm = dy.astype(BF)
    dm_ref[...] = dm
    sums_ref[0:1, :] += jnp.sum(dy, axis=0, keepdims=True)
    dh = jnp.zeros((tb, d), F32)
    ahead = dg(dm, w2_ref[:fc, :], NT)
    for f in range(0, ff, fc):
        du = ahead * gp_ref[:, f : f + fc].astype(F32)
        if f + fc < ff:
            ahead = dg(dm, w2_ref[f + fc : f + 2 * fc, :], NT)
        gbu_ref[:, f : f + fc] += jnp.sum(du, axis=0, keepdims=True)
        du = du.astype(BF)
        du_ref[:, f : f + fc] = du
        dh = dh + dg(du, w1_ref[:, d + f : d + f + fc], NT)
    c, r = norm_stats(x2_ref[...])
    xh = c * r
    gain = vt_ref[5:6, :]
    h2_ref[...] = (xh * gain + vt_ref[6:7, :]).astype(BF)
    sums_ref[1:2, :] += jnp.sum(dh * xh, axis=0, keepdims=True)
    sums_ref[2:3, :] += jnp.sum(dh, axis=0, keepdims=True)
    dz = dh * gain
    m1 = jnp.sum(dz, axis=-1, keepdims=True) * (1.0 / d)
    m2 = jnp.sum(dz * xh, axis=-1, keepdims=True) * (1.0 / d)
    dx2 = dy + r * (dz - m1 - xh * m2)
    dx2_ref[...] = dx2
    da = dx2.astype(BF)
    sums_ref[3:4, :] += jnp.sum(da.astype(F32), axis=0, keepdims=True)
    do_ref[...] = dg(da, w1_ref[:, :d], NT).astype(BF)
    acc_ref[...] += dg(o_ref[...], da, TN)

    @pl.when(i == pl.num_programs(0) - 1)
    def _():
        split_halves(idx_ref[1], acc_ref[...].astype(BF), mine_ref, theirs_ref)


def mlp_back(idx, order_row, ret, gp, x2, o, vt, pieces, tb=256, fc=768):
    t, d = x2.shape
    ff = gp.shape[1]
    return pl.pallas_call(
        functools.partial(mlp_back_kernel, fc=fc),
        grid_spec=pltpu.PrefetchScalarGridSpec(
            num_scalar_prefetch=1,
            grid=(t // tb,),
            in_specs=[whole((1, t)), whole((t, d)), rows_of(tb, ff), rows_of(tb, d), rows_of(tb, d), whole(vt.shape)]
            + [ANY] * 14,
            out_specs=[rows_of(tb, d), rows_of(tb, ff)]
            + [rows_of(tb, d)] * 3
            + [fixed((8, d)), fixed((1, ff))]
            + [fixed((d, d // 2))] * 2,
            scratch_shapes=[
                pltpu.VMEM((d, d + ff), BF),
                pltpu.VMEM((ff, d), BF),
                pltpu.VMEM((d, d), F32),
                pltpu.SemaphoreType.DMA((2,)),
            ],
        ),
        out_shape=[
            SDS((t, d), BF),
            SDS((t, ff), BF),
            SDS((t, d), F32),
            SDS((t, d), BF),
            SDS((t, d), BF),
            SDS((8, d), F32),
            SDS((1, ff), F32),
            pltpu.HBM((d, d // 2), BF),
            pltpu.HBM((d, d // 2), BF),
        ],
        compiler_params=params(),
        cost_estimate=cost(2 * t * d * (d + 2 * ff + t) * 1.5, t * (20 * d + 4 * ff)),
        name="mlp_back",
    )(idx, order_row, ret, gp, x2, o, vt, *pieces)


def grad_mlp_kernel(
    idx_ref, g_ref, dm_ref, h2_any, du_ref, down_own, down_other, up_own, up_other, h2_ref, sem
):
    i = pl.program_id(0)
    steps = pl.num_programs(0) // 2

    @pl.when(i == 0)
    def _():
        pltpu.make_async_copy(h2_any, h2_ref, sem).start()

    @pl.when(i == steps)
    def _():
        pltpu.make_async_copy(h2_any, h2_ref, sem).wait()

    @pl.when(i < steps)
    def _():
        split_halves(idx_ref[1], dg(g_ref[...], dm_ref[...], TN).astype(BF), down_own, down_other)

    @pl.when(i >= steps)
    def _():
        split_halves(idx_ref[1], dg(h2_ref[...], du_ref[...], TN).astype(BF), up_own, up_other)


def grad_mlp(idx, g, dm, h2, du):
    t, ff = g.shape
    d = dm.shape[1]
    steps = ff // d

    def down(i):
        return jnp.minimum(i, steps - 1)

    def up(i):
        return jnp.maximum(i - steps, 0)

    return pl.pallas_call(
        grad_mlp_kernel,
        grid_spec=pltpu.PrefetchScalarGridSpec(
            num_scalar_prefetch=1,
            grid=(2 * steps,),
            in_specs=[
                pl.BlockSpec((t, d), lambda i, _: (0, down(i))),
                whole((t, d)),
                ANY,
                pl.BlockSpec((t, d), lambda i, _: (0, up(i))),
            ],
            out_specs=[pl.BlockSpec((d, d // 2), lambda i, _: (down(i), 0))] * 2
            + [pl.BlockSpec((d, d // 2), lambda i, _: (0, up(i)))] * 2,
            scratch_shapes=[pltpu.VMEM((t, d), BF), pltpu.SemaphoreType.DMA],
        ),
        out_shape=[pltpu.HBM((ff, d // 2), BF)] * 2 + [pltpu.HBM((d, ff // 2), BF)] * 2,
        compiler_params=params(),
        cost_estimate=cost(6 * t * ff * d, 4 * t * (ff + d) + 4 * ff * d),
        name="grad_mlp",
    )(idx, g, dm, h2, du)


def attend_back_kernel(
    tag_ref, q_ref, k_ref, v_ref, do_ref, o_ref, l_ref, *refs, kb, qb
):
    dq_ref, dk_ref, dv_ref, dl_ref, dqt_ref = refs[-5:]
    r = pl.program_id(0)
    length = q_ref.shape[0]
    low = lax.broadcasted_iota(jnp.int32, (1, 128), 1) < 64
    prod = (do_ref[...].astype(F32) * o_ref[...].astype(F32)).T
    dl_ref[0:1, :] = jnp.sum(prod[0:64], axis=0, keepdims=True)
    dl_ref[1:2, :] = jnp.sum(prod[64:128], axis=0, keepdims=True)

    def block(ks, kn, qs, qn):
        k = k_ref[pl.ds(ks, kn), :]
        v = v_ref[pl.ds(ks, kn), :]
        q = q_ref[pl.ds(qs, qn), :]
        do = do_ref[pl.ds(qs, qn), :]
        dks = []
        dvs = []
        dqs = []
        for h in range(2):
            sel = low if h == 0 else jnp.logical_not(low)
            km = jnp.where(sel, k, jnp.asarray(0, BF))
            vm = jnp.where(sel, v, jnp.asarray(0, BF))
            pt = jnp.exp2(dg(km, q, NT) - l_ref[0, 0, h : h + 1, pl.ds(qs, qn)])
            dst = (pt * (dg(vm, do, NT) - dl_ref[h : h + 1, pl.ds(qs, qn)])).astype(BF)
            dvs.append(dg(pt.astype(BF), do, NN))
            dks.append(dg(dst, q, NN))
            dqs.append(dg(km.T, dst, NN))
        return jnp.where(low, dks[0], dks[1]), jnp.where(low, dvs[0], dvs[1]), dqs[0] + dqs[1]

    def run(kn, qn, plan):
        seen = set()
        for ks, starts in plan:
            dk = dv = None
            for qs in starts:
                a, b, dq = block(ks, kn, qs, qn)
                dk = a if dk is None else dk + a
                dv = b if dv is None else dv + b
                if qs in seen:
                    dqt_ref[:, pl.ds(qs, qn)] += dq
                else:
                    dqt_ref[:, pl.ds(qs, qn)] = dq
                seen.add(qs)
            dk_ref[pl.ds(ks, kn), :] = (dk * LN2).astype(BF)
            dv_ref[pl.ds(ks, kn), :] = dv.astype(BF)
        dq_ref[...] = (dqt_ref[...].T * 0.125).astype(BF)

    @pl.when(tag_ref[r] == 0)
    def _():
        run(kb, qb, [(ks, range(0, length, qb)) for ks in range(0, length, kb)])

    @pl.when(tag_ref[r] != 0)
    def _():
        c = length // 4
        run(c, c, [(ks, [ks]) for ks in range(0, length, c)])


def attend_back(tag, q, k, v, do, o, lse, first, pairs, before=(), kb=512, qb=512):
    t, d = q.shape
    rows = tag.shape[0]
    length = t // rows
    blk = pl.BlockSpec((length, 128), lambda r, p, _: (r, p + first))
    lse_spec = pl.BlockSpec((1, 1, 2, length), lambda r, p, _: (r, p + first, 0, 0))
    return pl.pallas_call(
        functools.partial(attend_back_kernel, kb=kb, qb=qb),
        grid_spec=pltpu.PrefetchScalarGridSpec(
            num_scalar_prefetch=1,
            grid=(rows, pairs),
            in_specs=[blk] * 5 + [lse_spec] + [ANY] * len(before),
            out_specs=[blk] * 3,
            scratch_shapes=[pltpu.VMEM((2, length), F32), pltpu.VMEM((128, length), F32)],
        ),
        out_shape=[SDS((t, d), BF)] * 3,
        input_output_aliases={7: 0, 8: 1, 9: 2} if before else {},
        compiler_params=params(2),
        cost_estimate=cost(5120 * t * length * pairs, t * d * 16, t * length * 12),
        name="attend_back",
    )(tag, q, k, v, do, o, lse, *before)


def grad_qkv_kernel(idx_ref, h_any, dq_any, dk_any, dv_any, *refs, rows):
    h_ref, d_ref, sem = refs[-3:]
    w = d_ref.shape[2]
    half = idx_ref[1] if rows is not None else 1 - idx_ref[1]
    cols = pl.ds(pl.multiple_of(half * w, 128), w)
    going = [pltpu.make_async_copy(h_any, h_ref, sem.at[3])]
    for m, ref in enumerate((dq_any, dk_any, dv_any)):
        going.append(pltpu.make_async_copy(ref.at[:, cols], d_ref.at[m], sem.at[m]))
    for cp in going:
        cp.start()
    going[0].wait()
    for m in range(3):
        at = slice(m * w, (m + 1) * w)
        going[1 + m].wait()
        part = dg(h_ref[...], d_ref[m], TN)
        if rows is None:
            refs[0][:, at] = part.astype(BF)
        else:
            outs, sum_ref = refs[1:-4], refs[-4]
            q = len(outs)
            sum_ref[...] = part + refs[0][:, at].astype(F32)
            for e in range(q):
                for z in range(4):
                    s = z * q + lax.bitwise_xor(idx_ref[0] % q, jnp.int32(e))
                    outs[e][z, :, at] = sum_ref[pl.ds(pl.multiple_of(s * rows, 8), rows), :].astype(BF)


def grad_qkv(idx, h1, dq, dk, dv, recv=None, n=None):
    t, d = h1.shape
    w = d // 2
    own = recv is not None
    outs = [(4, d // n, 3 * w)] * (n // 4) if own else [(d, 3 * w)]
    return pl.pallas_call(
        functools.partial(grad_qkv_kernel, rows=d // n if own else None),
        grid_spec=pltpu.PrefetchScalarGridSpec(
            num_scalar_prefetch=1,
            grid=(1,),
            in_specs=[ANY] * 4 + [whole((d, 3 * w))] * own,
            out_specs=[fixed(o) for o in outs],
            scratch_shapes=[pltpu.VMEM((d, w), F32)] * own
            + [pltpu.VMEM((t, d), BF), pltpu.VMEM((3, t, w), BF), pltpu.SemaphoreType.DMA((4,))],
        ),
        out_shape=[pltpu.HBM(o, BF) for o in outs],
        compiler_params=params(),
        cost_estimate=cost(6 * t * d * w, t * d * 6),
        name="grad_qkv_own" if own else "grad_qkv_other",
    )(idx, h1, dq, dk, dv, *([recv] * own))


def tokens_back_kernel(idx_ref, x_ref, vt_ref, dx2_ref, dq_ref, dk_ref, dv_ref, *refs):
    pieces = refs[:-4]
    tg_ref, s_ref, w_ref, sem = refs[-4:]
    d = x_ref.shape[1]

    @pl.when(pl.program_id(0) == 0)
    def _():
        going = load_qkv(idx_ref, pieces, w_ref, sem)
        s_ref[...] = jnp.zeros_like(s_ref)
        for cp in going:
            cp.wait()

    dh = dg(dq_ref[...], w_ref[:, :d], NT)
    dh = dh + dg(dk_ref[...], w_ref[:, d : 2 * d], NT)
    dh = dh + dg(dv_ref[...], w_ref[:, 2 * d :], NT)
    ones = jnp.ones((8, x_ref.shape[0]), BF)
    s_ref[2:3, :] += dg(ones, dq_ref[...], NN)[0:1]
    s_ref[3:4, :] += dg(ones, dv_ref[...], NN)[0:1]
    c, r = norm_stats(x_ref[...].astype(F32))
    xh = c * r
    s_ref[0:1, :] += jnp.sum(dh * xh, axis=0, keepdims=True)
    s_ref[1:2, :] += jnp.sum(dh, axis=0, keepdims=True)
    dz = dh * vt_ref[0:1, :]
    m1 = jnp.sum(dz, axis=-1, keepdims=True) * (1.0 / d)
    m2 = jnp.sum(dz * xh, axis=-1, keepdims=True) * (1.0 / d)
    tg_ref[...] = dx2_ref[...] + r * (dz - m1 - xh * m2)


def tokens_back(idx, dq, dk, dv, x, vt, dx2, pieces, tb=512):
    t, d = x.shape
    return pl.pallas_call(
        tokens_back_kernel,
        grid_spec=pltpu.PrefetchScalarGridSpec(
            num_scalar_prefetch=1,
            grid=(t // tb,),
            in_specs=[rows_of(tb, d), whole(vt.shape)] + [rows_of(tb, d)] * 4 + [ANY] * len(pieces),
            out_specs=[rows_of(tb, d), fixed((8, d))],
            scratch_shapes=[pltpu.VMEM((d, 3 * d), BF), pltpu.SemaphoreType.DMA],
        ),
        out_shape=[SDS((t, d), F32), SDS((8, d), F32)],
        compiler_params=params(),
        cost_estimate=cost(9 * t * d * d, t * d * 16 + d * d * 6),
        name="tokens_back",
    )(idx, x, vt, dx2, dq, dk, dv, *pieces)


def hop(x, groups):
    return lax.all_to_all(x, "fsdp", split_axis=0, concat_axis=0, tiled=True, axis_index_groups=groups)


def sum_cores_kernel(idx_ref, *refs, q):
    outs = refs[-q:]
    rows = outs[0].shape[1]
    for e in range(q):
        at = lax.bitwise_xor(idx_ref[0] % q, jnp.int32(e))
        start = 0
        for a_ref, b_ref in zip(refs[:-q:2], refs[1:-q:2], strict=True):
            total = a_ref[at] + b_ref[at]
            w = total.shape[1]
            for j in range(total.shape[0] // rows):
                outs[e][0, :, start : start + w] = total[j * rows : (j + 1) * rows]
                start += w


def sum_cores(idx, pairs, rows, n):
    q = n // 4
    ops, specs, width = [], [], 0
    for pair in pairs:
        shape = (pair[0].shape[0] // n, pair[0].shape[1])
        width += shape[0] // rows * shape[1]
        ops += [x.reshape((n,) + shape) for x in pair]
        specs += [pl.BlockSpec((q,) + shape, lambda z, _: (z, 0, 0))] * 2
    return pl.pallas_call(
        functools.partial(sum_cores_kernel, q=q),
        grid_spec=pltpu.PrefetchScalarGridSpec(
            num_scalar_prefetch=1,
            grid=(4,),
            in_specs=specs,
            out_specs=[pl.BlockSpec((1, rows, width), lambda z, _: (z, 0, 0))] * q,
        ),
        out_shape=[pltpu.HBM((4, rows, width), BF)] * q,
        compiler_params=params(),
        cost_estimate=cost(n * rows * width, n * rows * width * 6),
        name="sum_cores",
    )(idx, *ops)


def spread(parts, n):
    return [parts[0]] + [xor_pp(parts[e], e, n) for e in range(1, n // 4)]


def sum_parts_kernel(*refs):
    total = refs[0][...].astype(F32)
    for x in refs[1:-1]:
        total = total + x[...].astype(F32)
    refs[-1][...] = total.astype(BF)


def sum_parts(parts):
    shape = (1,) + parts[0].shape[1:]
    spec = pl.BlockSpec(shape, lambda i: (i, 0, 0))
    return pl.pallas_call(
        sum_parts_kernel,
        grid=(4,),
        in_specs=[spec] * len(parts),
        out_specs=spec,
        out_shape=pltpu.HBM(parts[0].shape, BF),
        compiler_params=params(),
        cost_estimate=cost(4 * len(parts) * math.prod(shape), 8 * len(parts) * math.prod(shape)),
        name="sum_parts",
    )(*parts)


def sum_qkv_kernel(idx_ref, *refs, q):
    for d in range(4):
        at = lax.bitwise_xor(idx_ref[0] // q, jnp.int32(d))
        start = 0
        for parts in (refs[:q], refs[q : 2 * q]):
            total = parts[0][at].astype(F32)
            for x in parts[1:]:
                total = total + x[at].astype(F32)
            w = total.shape[1]
            refs[2 * q + d][:, start : start + w] = total.astype(BF)
            start += w


def sum_qkv(idx, far, vecs, n):
    _, rows, w = far[0].shape
    width = w + vecs[0].shape[2]
    ops = list(far) + list(vecs)
    near = pl.pallas_call(
        functools.partial(sum_qkv_kernel, q=n // 4),
        grid_spec=pltpu.PrefetchScalarGridSpec(
            num_scalar_prefetch=1,
            grid=(1,),
            in_specs=[whole(x.shape) for x in ops],
            out_specs=[fixed((rows, width))] * 4,
        ),
        out_shape=[pltpu.HBM((rows, width), BF)] * 4,
        compiler_params=params(),
        cost_estimate=cost(n * rows * width, n * rows * width * 3),
        name="sum_qkv",
    )(idx, *ops)
    return near


def reduce_last(near, n, m):
    total = near[0].astype(F32)
    for x in near[1:]:
        total = total + x.astype(F32)
    return over_pairs(total, m)


def over_pairs(total, m):
    b = 2
    while b < m:
        total = total + lax.ppermute(total.astype(BF), "dp", [(i, i ^ b) for i in range(m)]).astype(F32)
        b *= 2
    return total


def vec_table_kernel(idx_ref, a, c, u, *refs, q):
    table_ref = refs[q]
    d = a.shape[1]
    rows = refs[0].shape[1]
    wide = u.shape[1] // d
    bias = [
        jnp.concatenate(
            [u[:, (s * wide + j) * rows : (s * wide + j + 1) * rows] for s in range(4 * q)], axis=1
        )
        for j in range(wide)
    ]
    lines = [c[0:4, :], a[3:4, :], a[1:3, :], a[0:1, :]] + bias + [jnp.zeros((120 - wide, d), F32)]
    table_ref[...] = jnp.concatenate(lines, axis=0).T
    for e in range(q):
        for z in range(4):
            s = z * q + lax.bitwise_xor(idx_ref[0] % q, jnp.int32(e))
            refs[e][z] = table_ref[pl.ds(pl.multiple_of(s * rows, 8), rows), :].astype(BF)


def vec_table(idx, s_mlp, s_tok, gbu, n):
    d = s_mlp.shape[1]
    q = n // 4
    return pl.pallas_call(
        functools.partial(vec_table_kernel, q=q),
        grid_spec=pltpu.PrefetchScalarGridSpec(
            num_scalar_prefetch=1,
            grid=(1,),
            in_specs=[whole(s_mlp.shape), whole(s_tok.shape), whole(gbu.shape)],
            out_specs=[fixed((4, d // n, 128))] * q,
            scratch_shapes=[pltpu.VMEM((d, 128), F32)],
        ),
        out_shape=[SDS((4, d // n, 128), BF)] * q,
        compiler_params=params(),
        cost_estimate=cost(d * 128, d * 1024),
        name="vec_table",
    )(idx, s_mlp, s_tok, gbu)


def local(
    tokens,
    sensor_tag,
    owner_order,
    ln1_gain,
    ln1_bias,
    w_qkv,
    b_query,
    b_value,
    w_out,
    b_out,
    ln2_gain,
    ln2_bias,
    w_up,
    b_up,
    w_down,
    b_down,
    out_grad,
    *,
    n,
    m,
):
    t, d = tokens.shape
    ff = w_up.shape[1]
    rows = d // n
    wide = ff // d
    f = lax.axis_index("fsdp")
    c = lax.axis_index("dp") % 2
    idx = jnp.stack([f, c]).astype(jnp.int32)
    use = idx if fits(rows, n) else jnp.zeros_like(idx)

    def core_half(x):
        h = x.shape[1] // 2
        return jnp.where(c == 0, x[:, :h], x[:, h:])

    vec = jnp.stack([ln1_gain, ln1_bias, b_query, b_value, b_out, ln2_gain, ln2_bias, b_down], axis=1)
    vec = jnp.concatenate([vec, b_up.reshape(wide, rows).T], axis=1)
    vec = jnp.pad(vec, ((0, 0), (0, 128 - vec.shape[1])))
    shard_a = jnp.concatenate([core_half(w_qkv), vec], axis=1)
    shard_b = jnp.concatenate(
        [core_half(jnp.concatenate([w_out, w_up], axis=1))]
        + [core_half(w_down[j * rows : (j + 1) * rows]) for j in range(wide)],
        axis=1,
    )
    q = n // 4
    everyone = jnp.arange(n)

    near_a = gather_near(shard_a, n)
    near_b = hop(jnp.broadcast_to(after(shard_b, near_a)[None], (4,) + shard_b.shape), tops(n))
    own_a = gather_far(near_a, n)
    cast = after(out_grad, near_a).astype(BF)
    own_a[1:] = after(own_a[1:], cast)
    swap_a = [core_swap(near_a, m), core_swap(jnp.stack(own_a[1:]), m)]
    if fits(rows, n):
        pieces_a = own_a + swap_a
    else:
        pieces_a = settle(own_a + swap_a[:1] + [swap_a[1][e] for e in range(q - 1)], f ^ everyone, c, n)
    near_b = after(near_b, own_a[1:])
    qh, kh, vh, h1, vt, bu = qkv(use, after(tokens, near_b), pieces_a)
    pairs = d // 128
    early = pairs * 2 // 3
    cut = (d + ff) // 2
    if fits(rows, n):
        x, y = near_b[..., :cut], near_b[..., cut:]
        x1, y2 = after((xor_pp(x, 1, n), xor_pp(y, 2, n)), vt)
        x2, y1 = xor_pp(x, 2, n), xor_pp(y, 1, n)
        x3, y3 = xor_pp(x1, 2, n), xor_pp(y2, 1, n)
        part = attend(sensor_tag, after(qh, x1, y2), kh, vh, 0, early)
        side = [near_b] + after([x1, x2, x3, y1, y2, y3], part[0])
        pieces_b = []
        for x in side:
            pieces_b += [x, core_swap(x, m)]
        gate = side[1:]
    else:
        far_b = gather_far(near_b, n)
        side = settle(
            far_b + [core_swap(x, m) for x in far_b], everyone // q * q + (everyone ^ f) % q, c, n, wide
        )
        part = attend(sensor_tag, qh, kh, vh, 0, early)
        pieces_b = [side[0], side[4]]
        for e in range(1, 4):
            pieces_b += [side[e][..., :cut], side[4 + e][..., :cut]]
        for e in range(1, 4):
            pieces_b += [side[e][..., cut:], side[4 + e][..., cut:]]
        gate = far_b
    returned = lax.all_to_all(after(cast, gate), "fsdp", split_axis=0, concat_axis=0, tiled=True)
    mixed, lse = attend(sensor_tag, qh, kh, vh, early, pairs - early, part)

    x2, active, slope, y = mlp(use, tokens, mixed, vt, bu, pieces_b)
    sent = permute(owner_order, y)
    encoded = lax.all_to_all(sent, "fsdp", split_axis=0, concat_axis=0, tiled=True)

    returned = after(returned, sent)
    dm, du, dx2, do, h2, s_mlp, gbu, out_own, out_other = mlp_back(
        use, owner_order, returned, slope, x2, mixed, vt, pieces_b
    )
    out_recv = core_swap(out_other, m)
    down_own, down_other, up_own, up_other = grad_mlp(idx, active, dm, h2, du)
    down_recv = core_swap(down_other, m)
    up_recv = core_swap(up_other, m)
    part = attend_back(sensor_tag, qh, kh, vh, after(do, up_own, encoded), mixed, lse, 0, 1)
    out_recv, down_recv, up_recv = after((out_recv, down_recv, up_recv), part[0])
    pairs_b = [(up_own, up_recv), (out_own, out_recv), (down_own, down_recv)]
    far_b = sum_cores(idx, pairs_b, rows, n)
    do = after(do, far_b[0])
    far_b = spread(far_b, n)
    dj = attend_back(sensor_tag, qh, kh, vh, do, mixed, lse, 1, pairs - 1, part)
    (qkv_other,) = grad_qkv(idx, h1, *dj)
    qkv_recv = core_swap(qkv_other, m)
    far_b = after(far_b, dj[0])
    near_b = sum_parts([after(far_b[0], qkv_other)] + far_b[1:])
    total_b = hop(near_b, tops(n))
    far_a = grad_qkv(idx, after(h1, near_b), *dj, qkv_recv, n)
    dj = after(dj, far_a[0])
    far_a = spread(far_a, n)
    tokens_grad, s_tok = tokens_back(use, *dj, tokens, vt, dx2, pieces_a)
    far_a, total_b = after((far_a, total_b), tokens_grad)
    total_b = over_pairs(jnp.sum(total_b.astype(F32), axis=0), m).astype(BF)
    other_b = core_swap(total_b, m)
    far_v = spread(vec_table(idx, s_mlp, s_tok, after(gbu, far_a), n), n)

    near_a = sum_qkv(idx, after(far_a, total_b), far_v, n)
    encoded = after(encoded, near_a[0]).astype(F32)
    near_a = [near_a[0]] + [xor_pp(near_a[i], i * q, n) for i in range(1, 4)]
    def both(mine, other):
        first = c == 0
        return jnp.where(first, mine, other).astype(F32), jnp.where(first, other, mine).astype(F32)

    def join(pair, start, width, parts, axis=1):
        out = []
        for p in range(parts):
            at = slice(start + p * width, start + (p + 1) * width)
            out.append(jnp.concatenate([pair[0][:, at], pair[1][:, at]], axis=1))
        return jnp.concatenate(out, axis=axis)

    h = d // 2
    g_mlp = both(total_b, other_b)
    grad_up_out = join(g_mlp, 0, h, wide)
    grad_out_out = join(g_mlp, ff // 2, h, 1)
    grad_down_out = join(g_mlp, (d + ff) // 2, h, wide, 0)
    near_a = after(near_a, grad_up_out, grad_out_out, grad_down_out, encoded)
    total_a = reduce_last(near_a, n, m)
    other_a = core_swap(total_a.astype(BF), m)
    cut = 3 * d // 2
    vecs = (total_a[:, cut:] + other_a[:, cut:].astype(F32)).T
    total_a, other_a = total_a[:, :cut].astype(BF), other_a[:, :cut]

    grad_qkv_out = join(both(total_a, other_a), 0, h, 3)
    return (
        encoded,
        tokens_grad,
        vecs[0],
        vecs[1],
        grad_qkv_out,
        vecs[2],
        vecs[3],
        grad_out_out,
        vecs[4],
        vecs[5],
        vecs[6],
        grad_up_out,
        vecs[8 : 8 + wide].reshape(ff // n),
        grad_down_out,
        vecs[7],
    )


def solution(mesh):
    n = mesh.shape["fsdp"]
    m = mesh.shape["dp"]
    both = P(("dp", "fsdp"), None)
    vec = P("fsdp")
    mat = P("fsdp", None)
    in_specs = (both, P(("dp", "fsdp")), both, vec, vec, mat, vec, vec, mat, vec, vec, vec, mat, vec, mat, vec, both)
    out_specs = (both, both, vec, vec, mat, vec, vec, mat, vec, vec, vec, mat, vec, mat, vec)
    return jax.shard_map(
        functools.partial(local, n=n, m=m), mesh=mesh, in_specs=in_specs, out_specs=out_specs, check_vma=False
    )
```

```python
import functools
import math

import jax
import jax.numpy as jnp
from jax import lax
from jax.experimental import pallas as pl
from jax.experimental.pallas import tpu as pltpu
from jax.sharding import PartitionSpec as P

F32 = jnp.float32
BF = jnp.bfloat16
EPS = 1e-6
LOG2E = math.log2(math.e)
LN2 = math.log(2.0)
NT = (((1,), (1,)), ((), ()))
TN = (((0,), (0,)), ((), ()))
NN = (((1,), (0,)), ((), ()))
ANY = pl.BlockSpec(memory_space=pl.ANY)
SAFE_SCORE = 90.0
VECS = 16
SDS = jax.ShapeDtypeStruct


def dg(a, b, dims):
    return lax.dot_general(a, b, dims, preferred_element_type=F32)


def params(axes=1):
    return pltpu.CompilerParams(
        vmem_limit_bytes=58 * 2**20, dimension_semantics=("arbitrary",) * axes
    )


def cost(flops, nbytes, trans=0):
    return pl.CostEstimate(flops=int(flops) >> 10, bytes_accessed=int(nbytes) >> 10, transcendentals=int(trans) >> 10)


def rows_of(height, width):
    return pl.BlockSpec((height, width), lambda i, *_: (i, 0))


def whole(shape):
    zeros = (0,) * len(shape)
    return pl.BlockSpec(shape, lambda *_: zeros, pipeline_mode=pl.Buffered(1))


def fixed(shape):
    zeros = (0,) * len(shape)
    return pl.BlockSpec(shape, lambda *_: zeros)


def norm_stats(x):
    n = x.shape[-1]
    c = x - jnp.sum(x, axis=-1, keepdims=True) * (1.0 / n)
    var = jnp.sum(c * c, axis=-1, keepdims=True) * (1.0 / n)
    return c, lax.rsqrt(var + EPS)


def after(x, *deps):
    return lax.optimization_barrier((x,) + deps)[0]


def xor_pp(x, b, n):
    return lax.ppermute(x, "fsdp", [(i, i ^ b) for i in range(n)])


def core_swap(x, m):
    return lax.ppermute(x, "dp", [(i, i ^ 1) for i in range(m)])


def gather_near(x, n):
    q = n // 4
    return jnp.stack([x] + [xor_pp(x, d * q, n) for d in (1, 2, 3)])


def tops(n):
    q = n // 4
    return [[low + z * q for z in range(4)] for low in range(q)]


def gather_far(s, n):
    return [s] + [xor_pp(s, e, n) for e in range(1, n // 4)]


def fits(rows, n):
    return rows % 16 == 0 and n == 16


def settle(pieces, order, c, n, wide=None):
    q = n // 4
    rows, width = pieces[0].shape[1:]
    if fits(rows, n):
        return pieces
    height = n * rows // 16
    halves = []
    for side in (pieces[:q], pieces[q:]):
        rel = jnp.stack(side, axis=1).reshape((n, rows, width))
        whole_side = jnp.take(rel, order, axis=0)
        flat = whole_side.reshape(16, height, width)
        if wide is not None:
            cut = width * (wide + 1) // (2 * wide + 1)
            low = whole_side[..., cut:].reshape(n, rows, wide, -1).transpose(0, 2, 1, 3)
            low = low.reshape(16, wide, height, -1).transpose(0, 2, 1, 3).reshape(16, height, -1)
            flat = jnp.concatenate([flat[..., :cut], low], axis=2)
        halves.append(flat.reshape(4, 4, height, width))
    left, right = jnp.where(c == 0, halves[0], halves[1]), jnp.where(c == 0, halves[1], halves[0])
    return [side[:, e] for side in (left, right) for e in range(4)]


def load_pieces(idx_ref, plan, sem):
    c = idx_ref[1]
    started = []
    for find, shard, start, skip, width, dst, height, first in plan:
        for e in range(4):
            for d in range(4):
                for block, h in zip(find(e, d), (c, 1 - c), strict=False):
                    rows = block.shape[0]
                    at = pl.ds(pl.multiple_of(shard(e, d) * height + first, 16), rows)
                    cols = pl.ds(pl.multiple_of(h * width, 128), width) if dst.shape[1] > width else slice(None)
                    src = block.at[:, pl.ds(start if e else start + skip, width)]
                    started.append(pltpu.make_async_copy(src, dst.at[at, cols], sem))
    for cp in started:
        cp.start()
    return started


def relative(idx_ref):
    return lambda e, d: lax.bitwise_xor(idx_ref[0], jnp.int32(d * 4 + e))


def by_top(idx_ref):
    return lambda e, d: lax.bitwise_xor(idx_ref[0] % 4, jnp.int32(e)) + d * 4


def load_qkv(idx_ref, pieces, w_ref, sem, vec_ref=None):
    def find(e, d):
        if len(pieces) == 8:
            return pieces[e].at[d], pieces[4 + e].at[d]
        return pieces[e].at[d], pieces[5].at[e - 1, d] if e else pieces[4].at[d]

    where = relative(idx_ref)
    rows, half = pieces[0].shape[1], w_ref.shape[1] // 2
    if vec_ref is not None:
        return load_pieces(idx_ref, [(lambda e, d: find(e, d)[:1], where, half, 0, 128, vec_ref, rows, 0)], sem)
    return load_pieces(idx_ref, [(find, where, 0, 0, half, w_ref, rows, 0)], sem)


def load_mlp(idx_ref, pieces, w1_ref, w2_ref, sem):
    where = by_top(idx_ref)

    def find1(e, d):
        return pieces[2 * e].at[d], pieces[2 * e + 1].at[d]

    def find2(e, d):
        at = 6 + 2 * e if e else 0
        return pieces[at].at[d], pieces[at + 1].at[d]

    rows = pieces[0].shape[1]
    half = w1_ref.shape[1] // 2
    w = w2_ref.shape[1] // 2
    one = [(find1, where, 0, 0, half, w1_ref, rows, 0)]
    two = [(find2, where, j * w, half, w, w2_ref, 4 * rows, j * rows) for j in range(4)]
    return load_pieces(idx_ref, one, sem.at[0]), load_pieces(idx_ref, two, sem.at[1])


def wait_mlp(w_ref, sem):
    pltpu.make_async_copy(w_ref, w_ref, sem).wait()


def qkv_kernel(idx_ref, x_ref, *refs):
    pieces = refs[:-11]
    q_ref, k_ref, v_ref, h_ref, vt_ref, bu_ref, qn_ref, kn_ref, w_ref, vec_ref, sem = refs[-11:]
    d = x_ref.shape[1]

    @pl.when(pl.program_id(0) == 0)
    def _():
        rows = pieces[0].shape[1]
        vecs = load_qkv(idx_ref, pieces, w_ref, sem.at[1], vec_ref)
        going = load_qkv(idx_ref, pieces, w_ref, sem.at[0])
        for cp in vecs:
            cp.wait()
        table = vec_ref[...].astype(F32).T[:VECS]
        vt_ref[...] = table
        bu_ref[...] = jnp.concatenate(
            [table[8 + j : 9 + j, s * rows : (s + 1) * rows] for s in range(d // rows) for j in range(4)], axis=1
        )
        for cp in going:
            cp.wait()

    c, r = norm_stats(x_ref[...].astype(F32))
    h = (c * r * vt_ref[0:1, :] + vt_ref[1:2, :]).astype(BF)
    h_ref[...] = h
    q = (dg(h, w_ref[:, :d], NN) + vt_ref[2:3, :]) * (0.125 * LOG2E)
    q_ref[...] = q.astype(BF)
    k = dg(h, w_ref[:, d : 2 * d], NN)
    k_ref[...] = k.astype(BF)
    lane = lax.broadcasted_iota(jnp.int32, (d, 128), 0)
    head = lax.broadcasted_iota(jnp.int32, (d, 128), 1) * 64
    of_head = jnp.where((lane >= head) & (lane < head + 64), 1.0, 0.0).astype(BF)
    for x, n_ref in ((q, qn_ref), (k, kn_ref)):
        n_ref[0] = jnp.max(dg((x * x).astype(BF), of_head, NN), axis=0, keepdims=True)
    v_ref[...] = (dg(h, w_ref[:, 2 * d :], NN) + vt_ref[3:4, :]).astype(BF)


def qkv(idx, x, pieces, tb=512):
    t, d = x.shape
    return pl.pallas_call(
        qkv_kernel,
        grid_spec=pltpu.PrefetchScalarGridSpec(
            num_scalar_prefetch=1,
            grid=(t // tb,),
            in_specs=[rows_of(tb, d)] + [ANY] * len(pieces),
            out_specs=[rows_of(tb, d)] * 4
            + [fixed((VECS, d)), fixed((1, 4 * d))]
            + [pl.BlockSpec((1, 1, 128), lambda i, _: (i, 0, 0))] * 2,
            scratch_shapes=[
                pltpu.VMEM((d, 3 * d), BF),
                pltpu.VMEM((d, 128), BF),
                pltpu.SemaphoreType.DMA((2,)),
            ],
        ),
        out_shape=[SDS((t, d), BF)] * 4
        + [SDS((VECS, d), F32), SDS((1, 4 * d), F32)]
        + [SDS((t // tb, 1, 128), F32)] * 2,
        compiler_params=params(),
        cost_estimate=cost(6 * t * d * d, t * d * 8 + d * d * 6),
        name="qkv",
    )(idx, x, *pieces)


def attend_kernel(tag_ref, qn_ref, kn_ref, q_ref, k_ref, v_ref, *refs, qb, first):
    o_ref, l_ref = refs[-2:]
    r = pl.program_id(0)
    length = q_ref.shape[0]
    low = lax.broadcasted_iota(jnp.int32, (1, 128), 1) < 64

    steps = qn_ref.shape[0] // tag_ref.shape[0]
    safe = True
    for h in range(2):
        head = 2 * (pl.program_id(1) + first) + h
        top = []
        for n_ref in (qn_ref, kn_ref):
            most = n_ref[r * steps, 0, head]
            for i in range(1, steps):
                most = jnp.maximum(most, n_ref[r * steps + i, 0, head])
            top.append(most)
        safe = jnp.logical_and(safe, top[0] * top[1] <= SAFE_SCORE**2)

    def block(qs, qn, ks, kn, plain):
        q = q_ref[pl.ds(qs, qn), :]
        k = k_ref[pl.ds(ks, kn), :]
        v = v_ref[pl.ds(ks, kn), :]
        outs = []
        for h in range(2):
            sel = low if h == 0 else jnp.logical_not(low)
            qm = jnp.where(sel, q, jnp.asarray(0, BF))
            vm = jnp.where(sel, v, jnp.asarray(1, BF))
            s = dg(qm, k, NT)
            if plain:
                outs.append((dg(jnp.exp2(s).astype(BF), vm, NN), 0.0))
            else:
                m = jnp.max(s, axis=1, keepdims=True)
                outs.append((dg(jnp.exp2(s - m).astype(BF), vm, NN), m))
        (a, ma), (b, mb) = outs
        acc = jnp.where(low, a, b)
        total = pltpu.roll(jnp.where(low, b, a), 64, 1)
        o_ref[pl.ds(qs, qn), :] = (acc / total).astype(o_ref.dtype)
        lse = jnp.log2(total) if plain else jnp.where(low, ma, mb) + jnp.log2(total)
        lse = lse.T
        l_ref[0, 0, 0:1, pl.ds(qs, qn)] = lse[0:1]
        l_ref[0, 0, 1:2, pl.ds(qs, qn)] = lse[64:65]

    for plain in (True, False):
        chosen = safe if plain else jnp.logical_not(safe)

        @pl.when(jnp.logical_and(tag_ref[r] == 0, chosen))
        def _(plain=plain):
            for i in range(length // qb):
                block(i * qb, qb, 0, length, plain)

        @pl.when(jnp.logical_and(tag_ref[r] != 0, chosen))
        def _(plain=plain):
            c = length // 4
            for i in range(4):
                block(i * c, c, i * c, c, plain)


def attend(tag, qn, kn, q, k, v, first, pairs, before=(), qb=512):
    t, d = q.shape
    rows = tag.shape[0]
    length = t // rows
    blk = pl.BlockSpec((length, 128), lambda r, p, _: (r, p + first))
    lse = pl.BlockSpec((1, 1, 2, length), lambda r, p, _: (r, p + first, 0, 0))
    return pl.pallas_call(
        functools.partial(attend_kernel, qb=qb, first=first),
        grid_spec=pltpu.PrefetchScalarGridSpec(
            num_scalar_prefetch=1,
            grid=(rows, pairs),
            in_specs=[pl.BlockSpec(memory_space=pltpu.SMEM)] * 2 + [blk] * 3 + [ANY] * len(before),
            out_specs=[blk, lse],
        ),
        out_shape=[SDS((t, d), BF), SDS((rows, d // 128, 2, length), F32)],
        input_output_aliases={6: 0, 7: 1} if before else {},
        compiler_params=params(2),
        cost_estimate=cost(2048 * t * length * pairs, t * d * 8, t * length * 12),
        name="attend",
    )(tag, qn, kn, q, k, v, *before)


ODDS = (2.3021649, 1.05007451e-1, -2.545477e-4, -1.0560537e-4, 4.093017e-6)


def gelu_both(u):
    z = u * u
    odds = ODDS[3] + z * ODDS[4]
    odds = ODDS[2] + z * odds
    odds = ODDS[1] + z * odds
    odds = ODDS[0] + z * odds
    phi = pltpu.reciprocal(1.0 + jnp.exp2(-u * odds), approx=True)
    density = jnp.exp2(z * (-0.5 * LOG2E) - 0.5 * math.log2(2.0 * math.pi))
    return u * phi, phi + u * density


def mlp_kernel(idx_ref, x_ref, o_ref, vt_ref, bu_ref, *refs, fc):
    pieces = refs[:14]
    x2_ref, gl_ref, gp_ref, y_ref, w1_ref, w2_ref, sem = refs[14:]
    d = x_ref.shape[1]
    ff = w2_ref.shape[0]

    @pl.when(pl.program_id(0) == 0)
    def _():
        going, _ = load_mlp(idx_ref, pieces, w1_ref, w2_ref, sem)
        for cp in going:
            cp.wait()

    x2 = x_ref[...].astype(F32) + dg(o_ref[...], w1_ref[:, :d], NN) + vt_ref[4:5, :]
    x2_ref[...] = x2
    c, r = norm_stats(x2)
    h = (c * r * vt_ref[5:6, :] + vt_ref[6:7, :]).astype(BF)
    y = x2 + vt_ref[7:8, :]

    @pl.when(pl.program_id(0) == 0)
    def _():
        wait_mlp(w2_ref, sem.at[1])

    for f in range(0, ff, fc):
        u = dg(h, w1_ref[:, d + f : d + f + fc], NN) + bu_ref[:, f : f + fc]
        g, gp = gelu_both(u)
        g = g.astype(BF)
        gl_ref[:, f : f + fc] = g
        gp_ref[:, f : f + fc] = gp.astype(BF)
        y = y + dg(g, w2_ref[f : f + fc, :], NN)
    y_ref[...] = y.astype(BF)


def mlp(idx, x, o, vt, bu, pieces, tb=256, fc=768):
    t, d = x.shape
    ff = bu.shape[1]
    return pl.pallas_call(
        functools.partial(mlp_kernel, fc=fc),
        grid_spec=pltpu.PrefetchScalarGridSpec(
            num_scalar_prefetch=1,
            grid=(t // tb,),
            in_specs=[rows_of(tb, d)] * 2 + [whole(vt.shape), whole(bu.shape)] + [ANY] * 14,
            out_specs=[rows_of(tb, d), rows_of(tb, ff), rows_of(tb, ff), rows_of(tb, d)],
            scratch_shapes=[
                pltpu.VMEM((d, d + ff), BF),
                pltpu.VMEM((ff, d), BF),
                pltpu.SemaphoreType.DMA((2,)),
            ],
        ),
        out_shape=[SDS((t, d), F32), SDS((t, ff), BF), SDS((t, ff), BF), SDS((t, d), BF)],
        compiler_params=params(),
        cost_estimate=cost(4 * t * d * (d + 2 * ff), t * (10 * d + 4 * ff) + 4 * d * ff, 2 * t * ff),
        name="mlp",
    )(idx, x, o, vt, bu, *pieces)


def permute_kernel(ord_ref, y_ref, o_ref):
    jb = o_ref.shape[0]
    t = y_ref.shape[0]
    order = jnp.broadcast_to(ord_ref[...].astype(F32), (8, jb)).T[:, 0:1]
    hot = jnp.where(order == lax.broadcasted_iota(jnp.int32, (jb, t), 1).astype(F32), 1.0, 0.0)
    o_ref[...] = dg(hot.astype(BF), y_ref[...], NN).astype(BF)


def permute(order, y, jb=512):
    t, d = y.shape
    return pl.pallas_call(
        permute_kernel,
        grid=(t // jb,),
        in_specs=[pl.BlockSpec((1, jb), lambda i: (0, i)), whole((t, d))],
        out_specs=rows_of(jb, d),
        out_shape=pltpu.HBM((t, d), BF),
        compiler_params=params(),
        cost_estimate=cost(2 * t * t * d, t * d * 4),
        name="permute",
    )(order, y)


def split_halves(c, r, mine_ref, theirs_ref):
    h = r.shape[1] // 2
    left, right = r[:, :h], r[:, h:]
    mine_ref[...] = jnp.where(c == 0, left, right)
    theirs_ref[...] = jnp.where(c == 0, right, left)


def mlp_back_kernel(idx_ref, ord_ref, ret_ref, gp_ref, x2_ref, o_ref, vt_ref, *refs, fc):
    pieces = refs[:14]
    (dm_ref, du_ref, dx2_ref, do_ref, h2_ref, sums_ref, gbu_ref, mine_ref, theirs_ref) = refs[14:23]
    w1_ref, w2_ref, acc_ref, sem = refs[23:]
    i = pl.program_id(0)
    tb, ff = gp_ref.shape
    t, d = ret_ref.shape

    @pl.when(i == 0)
    def _():
        load_mlp(idx_ref, pieces, w1_ref, w2_ref, sem)
        sums_ref[...] = jnp.zeros_like(sums_ref)
        gbu_ref[...] = jnp.zeros_like(gbu_ref)
        acc_ref[...] = jnp.zeros_like(acc_ref)
        wait_mlp(w2_ref, sem.at[1])
        wait_mlp(w1_ref, sem.at[0])

    at = lax.broadcasted_iota(jnp.int32, (tb, t), 0) + i * tb
    hot = jnp.where(ord_ref[...] == at, 1.0, 0.0).astype(BF)
    dy = dg(hot, ret_ref[...], NN)
    dm = dy.astype(BF)
    dm_ref[...] = dm
    sums_ref[0:1, :] += jnp.sum(dy, axis=0, keepdims=True)
    dh = jnp.zeros((tb, d), F32)
    ahead = dg(dm, w2_ref[:fc, :], NT)
    for f in range(0, ff, fc):
        du = ahead * gp_ref[:, f : f + fc].astype(F32)
        if f + fc < ff:
            ahead = dg(dm, w2_ref[f + fc : f + 2 * fc, :], NT)
        gbu_ref[:, f : f + fc] += jnp.sum(du, axis=0, keepdims=True)
        du = du.astype(BF)
        du_ref[:, f : f + fc] = du
        dh = dh + dg(du, w1_ref[:, d + f : d + f + fc], NT)
    c, r = norm_stats(x2_ref[...])
    xh = c * r
    gain = vt_ref[5:6, :]
    h2_ref[...] = (xh * gain + vt_ref[6:7, :]).astype(BF)
    sums_ref[1:2, :] += jnp.sum(dh * xh, axis=0, keepdims=True)
    sums_ref[2:3, :] += jnp.sum(dh, axis=0, keepdims=True)
    dz = dh * gain
    m1 = jnp.sum(dz, axis=-1, keepdims=True) * (1.0 / d)
    m2 = jnp.sum(dz * xh, axis=-1, keepdims=True) * (1.0 / d)
    dx2 = dy + r * (dz - m1 - xh * m2)
    dx2_ref[...] = dx2
    da = dx2.astype(BF)
    sums_ref[3:4, :] += jnp.sum(da.astype(F32), axis=0, keepdims=True)
    do_ref[...] = dg(da, w1_ref[:, :d], NT).astype(BF)
    acc_ref[...] += dg(o_ref[...], da, TN)

    @pl.when(i == pl.num_programs(0) - 1)
    def _():
        split_halves(idx_ref[1], acc_ref[...].astype(BF), mine_ref, theirs_ref)


def mlp_back(idx, order_row, ret, gp, x2, o, vt, pieces, tb=256, fc=768):
    t, d = x2.shape
    ff = gp.shape[1]
    return pl.pallas_call(
        functools.partial(mlp_back_kernel, fc=fc),
        grid_spec=pltpu.PrefetchScalarGridSpec(
            num_scalar_prefetch=1,
            grid=(t // tb,),
            in_specs=[whole((1, t)), whole((t, d)), rows_of(tb, ff), rows_of(tb, d), rows_of(tb, d), whole(vt.shape)]
            + [ANY] * 14,
            out_specs=[rows_of(tb, d), rows_of(tb, ff)]
            + [rows_of(tb, d)] * 3
            + [fixed((8, d)), fixed((1, ff))]
            + [fixed((d, d // 2))] * 2,
            scratch_shapes=[
                pltpu.VMEM((d, d + ff), BF),
                pltpu.VMEM((ff, d), BF),
                pltpu.VMEM((d, d), F32),
                pltpu.SemaphoreType.DMA((2,)),
            ],
        ),
        out_shape=[
            SDS((t, d), BF),
            SDS((t, ff), BF),
            SDS((t, d), F32),
            SDS((t, d), BF),
            SDS((t, d), BF),
            SDS((8, d), F32),
            SDS((1, ff), F32),
            pltpu.HBM((d, d // 2), BF),
            pltpu.HBM((d, d // 2), BF),
        ],
        compiler_params=params(),
        cost_estimate=cost(2 * t * d * (d + 2 * ff + t) * 1.5, t * (20 * d + 4 * ff)),
        name="mlp_back",
    )(idx, order_row, ret, gp, x2, o, vt, *pieces)


def grad_mlp_kernel(
    idx_ref, g_ref, dm_ref, h2_any, du_ref, u, down_own, down_other, up_own, up_other, bias_ref, h2_ref, sem, *, rows
):
    i = pl.program_id(0)
    steps = pl.num_programs(0) // 2

    @pl.when(i == 0)
    def _():
        pltpu.make_async_copy(h2_any, h2_ref, sem).start()

    @pl.when(i == steps)
    def _():
        pltpu.make_async_copy(h2_any, h2_ref, sem).wait()

    @pl.when(i < steps)
    def _():
        split_halves(idx_ref[1], dg(g_ref[...], dm_ref[...], TN).astype(BF), down_own, down_other)
        d = dm_ref.shape[1]
        wide = u.shape[1] // d
        for j in range(wide):
            parts = [u[:, (s * wide + j) * rows : (s * wide + j + 1) * rows] for s in range(d // rows)]
            bias_ref[j : j + 1, :] = jnp.concatenate(parts, axis=1)

    @pl.when(i >= steps)
    def _():
        split_halves(idx_ref[1], dg(h2_ref[...], du_ref[...], TN).astype(BF), up_own, up_other)


def grad_mlp(idx, g, dm, h2, du, gbu, rows):
    t, ff = g.shape
    d = dm.shape[1]
    steps = ff // d

    def down(i):
        return jnp.minimum(i, steps - 1)

    def up(i):
        return jnp.maximum(i - steps, 0)

    return pl.pallas_call(
        functools.partial(grad_mlp_kernel, rows=rows),
        grid_spec=pltpu.PrefetchScalarGridSpec(
            num_scalar_prefetch=1,
            grid=(2 * steps,),
            in_specs=[
                pl.BlockSpec((t, d), lambda i, _: (0, down(i))),
                whole((t, d)),
                ANY,
                pl.BlockSpec((t, d), lambda i, _: (0, up(i))),
                whole(gbu.shape),
            ],
            out_specs=[pl.BlockSpec((d, d // 2), lambda i, _: (down(i), 0))] * 2
            + [pl.BlockSpec((d, d // 2), lambda i, _: (0, up(i)))] * 2
            + [fixed((steps, d))],
            scratch_shapes=[pltpu.VMEM((t, d), BF), pltpu.SemaphoreType.DMA],
        ),
        out_shape=[pltpu.HBM((ff, d // 2), BF)] * 2
        + [pltpu.HBM((d, ff // 2), BF)] * 2
        + [SDS((steps, d), F32)],
        compiler_params=params(),
        cost_estimate=cost(6 * t * ff * d, 4 * t * (ff + d) + 4 * ff * d),
        name="grad_mlp",
    )(idx, g, dm, h2, du, gbu)


def attend_back_kernel(
    tag_ref, q_ref, k_ref, v_ref, do_ref, o_ref, l_ref, *refs, kb, qb
):
    dq_ref, dk_ref, dv_ref, dl_ref, dqt_ref = refs[-5:]
    r = pl.program_id(0)
    length = q_ref.shape[0]
    low = lax.broadcasted_iota(jnp.int32, (1, 128), 1) < 64
    prod = (do_ref[...].astype(F32) * o_ref[...].astype(F32)).T
    dl_ref[0:1, :] = jnp.sum(prod[0:64], axis=0, keepdims=True)
    dl_ref[1:2, :] = jnp.sum(prod[64:128], axis=0, keepdims=True)

    def block(ks, kn, qs, qn):
        k = k_ref[pl.ds(ks, kn), :]
        v = v_ref[pl.ds(ks, kn), :]
        q = q_ref[pl.ds(qs, qn), :]
        do = do_ref[pl.ds(qs, qn), :]
        dks = []
        dvs = []
        dqs = []
        for h in range(2):
            sel = low if h == 0 else jnp.logical_not(low)
            km = jnp.where(sel, k, jnp.asarray(0, BF))
            vm = jnp.where(sel, v, jnp.asarray(0, BF))
            pt = jnp.exp2(dg(km, q, NT) - l_ref[0, 0, h : h + 1, pl.ds(qs, qn)])
            dst = (pt * (dg(vm, do, NT) - dl_ref[h : h + 1, pl.ds(qs, qn)])).astype(BF)
            dvs.append(dg(pt.astype(BF), do, NN))
            dks.append(dg(dst, q, NN))
            dqs.append(dg(km.T, dst, NN))
        return jnp.where(low, dks[0], dks[1]), jnp.where(low, dvs[0], dvs[1]), dqs[0] + dqs[1]

    def run(kn, qn, plan):
        seen = set()
        for ks, starts in plan:
            dk = dv = None
            for qs in starts:
                a, b, dq = block(ks, kn, qs, qn)
                dk = a if dk is None else dk + a
                dv = b if dv is None else dv + b
                if qs in seen:
                    dqt_ref[:, pl.ds(qs, qn)] += dq
                else:
                    dqt_ref[:, pl.ds(qs, qn)] = dq
                seen.add(qs)
            dk_ref[pl.ds(ks, kn), :] = (dk * LN2).astype(BF)
            dv_ref[pl.ds(ks, kn), :] = dv.astype(BF)
        dq_ref[...] = (dqt_ref[...].T * 0.125).astype(BF)

    @pl.when(tag_ref[r] == 0)
    def _():
        run(kb, qb, [(ks, range(0, length, qb)) for ks in range(0, length, kb)])

    @pl.when(tag_ref[r] != 0)
    def _():
        c = length // 4
        run(c, c, [(ks, [ks]) for ks in range(0, length, c)])


def attend_back(tag, q, k, v, do, o, lse, first, pairs, before=(), kb=512, qb=512):
    t, d = q.shape
    rows = tag.shape[0]
    length = t // rows
    blk = pl.BlockSpec((length, 128), lambda r, p, _: (r, p + first))
    lse_spec = pl.BlockSpec((1, 1, 2, length), lambda r, p, _: (r, p + first, 0, 0))
    return pl.pallas_call(
        functools.partial(attend_back_kernel, kb=kb, qb=qb),
        grid_spec=pltpu.PrefetchScalarGridSpec(
            num_scalar_prefetch=1,
            grid=(rows, pairs),
            in_specs=[blk] * 5 + [lse_spec] + [ANY] * len(before),
            out_specs=[blk] * 3,
            scratch_shapes=[pltpu.VMEM((2, length), F32), pltpu.VMEM((128, length), F32)],
        ),
        out_shape=[SDS((t, d), BF)] * 3,
        input_output_aliases={7: 0, 8: 1, 9: 2} if before else {},
        compiler_params=params(2),
        cost_estimate=cost(5120 * t * length * pairs, t * d * 16, t * length * 12),
        name="attend_back",
    )(tag, q, k, v, do, o, lse, *before)


def grad_qkv_kernel(idx_ref, h_any, dq_any, dk_any, dv_any, *refs, rows):
    h_ref, d_ref, sem = refs[-3:]
    w = d_ref.shape[2]
    half = idx_ref[1] if rows is not None else 1 - idx_ref[1]
    cols = pl.ds(pl.multiple_of(half * w, 128), w)
    going = [pltpu.make_async_copy(h_any, h_ref, sem.at[3])]
    for m, ref in enumerate((dq_any, dk_any, dv_any)):
        going.append(pltpu.make_async_copy(ref.at[:, cols], d_ref.at[m], sem.at[m]))
    for cp in going:
        cp.start()
    going[0].wait()
    for m in range(3):
        at = slice(m * w, (m + 1) * w)
        going[1 + m].wait()
        part = dg(h_ref[...], d_ref[m], TN)
        if rows is None:
            refs[0][:, at] = part.astype(BF)
        else:
            outs, sum_ref = refs[1:-4], refs[-4]
            q = len(outs)
            sum_ref[...] = part + refs[0][:, at].astype(F32)
            for e in range(q):
                for z in range(4):
                    s = z * q + lax.bitwise_xor(idx_ref[0] % q, jnp.int32(e))
                    outs[e][z, :, at] = sum_ref[pl.ds(pl.multiple_of(s * rows, 8), rows), :].astype(BF)


def grad_qkv(idx, h1, dq, dk, dv, recv=None, n=None):
    t, d = h1.shape
    w = d // 2
    own = recv is not None
    outs = [(4, d // n, 3 * w)] * (n // 4) if own else [(d, 3 * w)]
    return pl.pallas_call(
        functools.partial(grad_qkv_kernel, rows=d // n if own else None),
        grid_spec=pltpu.PrefetchScalarGridSpec(
            num_scalar_prefetch=1,
            grid=(1,),
            in_specs=[ANY] * 4 + [whole((d, 3 * w))] * own,
            out_specs=[fixed(o) for o in outs],
            scratch_shapes=[pltpu.VMEM((d, w), F32)] * own
            + [pltpu.VMEM((t, d), BF), pltpu.VMEM((3, t, w), BF), pltpu.SemaphoreType.DMA((4,))],
        ),
        out_shape=[pltpu.HBM(o, BF) for o in outs],
        compiler_params=params(),
        cost_estimate=cost(6 * t * d * w, t * d * 6),
        name="grad_qkv_own" if own else "grad_qkv_other",
    )(idx, h1, dq, dk, dv, *([recv] * own))


def tokens_back_kernel(idx_ref, me_ref, x_ref, vt_ref, dx2_ref, dq_ref, dk_ref, dv_ref, a_ref, u_ref, *refs, q):
    pieces = refs[: -5 - q]
    tg_ref, *outs, s_ref, table_ref, w_ref, sem = refs[-5 - q :]
    d = x_ref.shape[1]

    @pl.when(pl.program_id(0) == 0)
    def _():
        going = load_qkv(idx_ref, pieces, w_ref, sem)
        s_ref[...] = jnp.zeros_like(s_ref)
        for cp in going:
            cp.wait()

    dh = dg(dq_ref[...], w_ref[:, :d], NT)
    dh = dh + dg(dk_ref[...], w_ref[:, d : 2 * d], NT)
    dh = dh + dg(dv_ref[...], w_ref[:, 2 * d :], NT)
    ones = jnp.ones((8, x_ref.shape[0]), BF)
    s_ref[2:3, :] += dg(ones, dq_ref[...], NN)[0:1]
    s_ref[3:4, :] += dg(ones, dv_ref[...], NN)[0:1]
    c, r = norm_stats(x_ref[...].astype(F32))
    xh = c * r
    s_ref[0:1, :] += jnp.sum(dh * xh, axis=0, keepdims=True)
    s_ref[1:2, :] += jnp.sum(dh, axis=0, keepdims=True)
    dz = dh * vt_ref[0:1, :]
    m1 = jnp.sum(dz, axis=-1, keepdims=True) * (1.0 / d)
    m2 = jnp.sum(dz * xh, axis=-1, keepdims=True) * (1.0 / d)
    tg_ref[...] = dx2_ref[...] + r * (dz - m1 - xh * m2)

    @pl.when(pl.program_id(0) == pl.num_programs(0) - 1)
    def _():
        rows = outs[0].shape[1]
        wide = u_ref.shape[0]
        lines = [s_ref[0:4, :], a_ref[3:4, :], a_ref[1:3, :], a_ref[0:1, :], u_ref[...]]
        table_ref[...] = jnp.concatenate(lines + [jnp.zeros((120 - wide, d), F32)], axis=0).T
        for e in range(q):
            for z in range(4):
                s = z * q + lax.bitwise_xor(me_ref[0] % q, jnp.int32(e))
                outs[e][z] = table_ref[pl.ds(pl.multiple_of(s * rows, 8), rows), :].astype(BF)


def tokens_back(idx, me, dq, dk, dv, x, vt, dx2, s_mlp, bias, pieces, n, tb=512):
    t, d = x.shape
    q = n // 4
    return pl.pallas_call(
        functools.partial(tokens_back_kernel, q=q),
        grid_spec=pltpu.PrefetchScalarGridSpec(
            num_scalar_prefetch=2,
            grid=(t // tb,),
            in_specs=[rows_of(tb, d), whole(vt.shape)]
            + [rows_of(tb, d)] * 4
            + [whole(s_mlp.shape), whole(bias.shape)]
            + [ANY] * len(pieces),
            out_specs=[rows_of(tb, d)] + [fixed((4, d // n, 128))] * q,
            scratch_shapes=[
                pltpu.VMEM((8, d), F32),
                pltpu.VMEM((d, 128), F32),
                pltpu.VMEM((d, 3 * d), BF),
                pltpu.SemaphoreType.DMA,
            ],
        ),
        out_shape=[SDS((t, d), F32)] + [pltpu.HBM((4, d // n, 128), BF)] * q,
        compiler_params=params(),
        cost_estimate=cost(9 * t * d * d, t * d * 16 + d * d * 6),
        name="tokens_back",
    )(idx, me, x, vt, dx2, dq, dk, dv, s_mlp, bias, *pieces)


def hop(x, groups):
    return lax.all_to_all(x, "fsdp", split_axis=0, concat_axis=0, tiled=True, axis_index_groups=groups)


def sum_cores_kernel(idx_ref, *refs, q):
    outs = refs[-q:]
    rows = outs[0].shape[1]
    for e in range(q):
        at = lax.bitwise_xor(idx_ref[0] % q, jnp.int32(e))
        start = 0
        for a_ref, b_ref in zip(refs[:-q:2], refs[1:-q:2], strict=True):
            total = a_ref[at] + b_ref[at]
            w = total.shape[1]
            for j in range(total.shape[0] // rows):
                outs[e][0, :, start : start + w] = total[j * rows : (j + 1) * rows]
                start += w


def sum_cores(idx, pairs, rows, n):
    q = n // 4
    ops, specs, width = [], [], 0
    for pair in pairs:
        shape = (pair[0].shape[0] // n, pair[0].shape[1])
        width += shape[0] // rows * shape[1]
        ops += [x.reshape((n,) + shape) for x in pair]
        specs += [pl.BlockSpec((q,) + shape, lambda z, _: (z, 0, 0))] * 2
    return pl.pallas_call(
        functools.partial(sum_cores_kernel, q=q),
        grid_spec=pltpu.PrefetchScalarGridSpec(
            num_scalar_prefetch=1,
            grid=(4,),
            in_specs=specs,
            out_specs=[pl.BlockSpec((1, rows, width), lambda z, _: (z, 0, 0))] * q,
        ),
        out_shape=[pltpu.HBM((4, rows, width), BF)] * q,
        compiler_params=params(),
        cost_estimate=cost(n * rows * width, n * rows * width * 6),
        name="sum_cores",
    )(idx, *ops)


def spread(parts, n):
    return [parts[0]] + [xor_pp(parts[e], e, n) for e in range(1, n // 4)]


def sum_parts_kernel(*refs):
    total = refs[0][...].astype(F32)
    for x in refs[1:-1]:
        total = total + x[...].astype(F32)
    refs[-1][...] = total.astype(BF)


def sum_parts(parts):
    shape = (1,) + parts[0].shape[1:]
    spec = pl.BlockSpec(shape, lambda i: (i, 0, 0))
    return pl.pallas_call(
        sum_parts_kernel,
        grid=(4,),
        in_specs=[spec] * len(parts),
        out_specs=spec,
        out_shape=pltpu.HBM(parts[0].shape, BF),
        compiler_params=params(),
        cost_estimate=cost(4 * len(parts) * math.prod(shape), 8 * len(parts) * math.prod(shape)),
        name="sum_parts",
    )(*parts)


def sum_qkv_kernel(idx_ref, *refs, q):
    outs = refs[2 * q + 1 :]
    for d in range(4):
        at = lax.bitwise_xor(idx_ref[0] // q, jnp.int32(d))
        start = 0
        for parts in (refs[:q], refs[q : 2 * q]):
            total = parts[0][at].astype(F32)
            for x in parts[1:]:
                total = total + x[at].astype(F32)
            w = total.shape[1]
            outs[d][:, start : start + w] = total.astype(BF)
            start += w
    last = refs[2 * q]
    outs[4][...] = (
        last[0].astype(F32) + last[1].astype(F32) + last[2].astype(F32) + last[3].astype(F32)
    ).astype(BF)


def sum_qkv(idx, far, vecs, last, n):
    _, rows, w = far[0].shape
    width = w + vecs[0].shape[2]
    ops = list(far) + list(vecs) + [last]
    *near, total = pl.pallas_call(
        functools.partial(sum_qkv_kernel, q=n // 4),
        grid_spec=pltpu.PrefetchScalarGridSpec(
            num_scalar_prefetch=1,
            grid=(1,),
            in_specs=[whole(x.shape) for x in ops],
            out_specs=[fixed((rows, width))] * 4 + [fixed(last.shape[1:])],
        ),
        out_shape=[pltpu.HBM((rows, width), BF)] * 4 + [pltpu.HBM(last.shape[1:], BF)],
        compiler_params=params(),
        cost_estimate=cost(n * rows * width, n * rows * width * 3),
        name="sum_qkv",
    )(idx, *ops)
    return near, total


def reduce_last(near, n, m):
    total = near[0].astype(F32)
    for x in near[1:]:
        total = total + x.astype(F32)
    return over_pairs(total, m)


def over_pairs(total, m):
    b = 2
    while b < m:
        total = total + lax.ppermute(total.astype(BF), "dp", [(i, i ^ b) for i in range(m)]).astype(F32)
        b *= 2
    return total


def local(
    tokens,
    sensor_tag,
    owner_order,
    ln1_gain,
    ln1_bias,
    w_qkv,
    b_query,
    b_value,
    w_out,
    b_out,
    ln2_gain,
    ln2_bias,
    w_up,
    b_up,
    w_down,
    b_down,
    out_grad,
    *,
    n,
    m,
):
    t, d = tokens.shape
    ff = w_up.shape[1]
    rows = d // n
    wide = ff // d
    f = lax.axis_index("fsdp")
    c = lax.axis_index("dp") % 2
    idx = jnp.stack([f, c]).astype(jnp.int32)
    use = idx if fits(rows, n) else jnp.zeros_like(idx)

    def core_half(x):
        h = x.shape[1] // 2
        return jnp.where(c == 0, x[:, :h], x[:, h:])

    vec = jnp.stack([ln1_gain, ln1_bias, b_query, b_value, b_out, ln2_gain, ln2_bias, b_down], axis=1)
    vec = jnp.concatenate([vec, b_up.reshape(wide, rows).T], axis=1)
    vec = jnp.pad(vec, ((0, 0), (0, 128 - vec.shape[1])))
    shard_a = jnp.concatenate([core_half(w_qkv), vec], axis=1)
    shard_b = jnp.concatenate(
        [core_half(jnp.concatenate([w_out, w_up], axis=1))]
        + [core_half(w_down[j * rows : (j + 1) * rows]) for j in range(wide)],
        axis=1,
    )
    q = n // 4
    everyone = jnp.arange(n)

    near_a = gather_near(shard_a, n)
    near_b = hop(jnp.broadcast_to(after(shard_b, near_a)[None], (4,) + shard_b.shape), tops(n))
    own_a = gather_far(near_a, n)
    cast = after(out_grad, near_a).astype(BF)
    own_a[1:] = after(own_a[1:], cast)
    swap_a = [core_swap(near_a, m), core_swap(jnp.stack(own_a[1:]), m)]
    if fits(rows, n):
        pieces_a = own_a + swap_a
    else:
        pieces_a = settle(own_a + swap_a[:1] + [swap_a[1][e] for e in range(q - 1)], f ^ everyone, c, n)
    near_b = after(near_b, own_a[1:])
    qh, kh, vh, h1, vt, bu, qn, kn = qkv(use, after(tokens, near_b), pieces_a)
    pairs = d // 128
    early = pairs * 2 // 3
    cut = (d + ff) // 2
    if fits(rows, n):
        x, y = near_b[..., :cut], near_b[..., cut:]
        x1, y2 = after((xor_pp(x, 1, n), xor_pp(y, 2, n)), vt)
        x2, y1 = xor_pp(x, 2, n), xor_pp(y, 1, n)
        x3, y3 = xor_pp(x1, 2, n), xor_pp(y2, 1, n)
        part = attend(sensor_tag, qn, kn, after(qh, x1, y2), kh, vh, 0, early)
        side = [near_b] + after([x1, x2, x3, y1, y2, y3], part[0])
        pieces_b = []
        for x in side:
            pieces_b += [x, core_swap(x, m)]
        gate = side[1:]
    else:
        far_b = gather_far(near_b, n)
        side = settle(
            far_b + [core_swap(x, m) for x in far_b], everyone // q * q + (everyone ^ f) % q, c, n, wide
        )
        part = attend(sensor_tag, qn, kn, qh, kh, vh, 0, early)
        pieces_b = [side[0], side[4]]
        for e in range(1, 4):
            pieces_b += [side[e][..., :cut], side[4 + e][..., :cut]]
        for e in range(1, 4):
            pieces_b += [side[e][..., cut:], side[4 + e][..., cut:]]
        gate = far_b
    returned = lax.all_to_all(after(cast, gate), "fsdp", split_axis=0, concat_axis=0, tiled=True)
    mixed, lse = attend(sensor_tag, qn, kn, qh, kh, vh, early, pairs - early, part)

    x2, active, slope, y = mlp(use, tokens, mixed, vt, bu, pieces_b)
    sent = permute(owner_order, y)
    encoded = lax.all_to_all(sent, "fsdp", split_axis=0, concat_axis=0, tiled=True)

    returned = after(returned, sent)
    dm, du, dx2, do, h2, s_mlp, gbu, out_own, out_other = mlp_back(
        use, owner_order, returned, slope, x2, mixed, vt, pieces_b
    )
    out_recv = core_swap(out_other, m)
    down_own, down_other, up_own, up_other, bias = grad_mlp(idx, active, dm, h2, du, gbu, rows)
    down_recv = core_swap(down_other, m)
    up_recv = core_swap(up_other, m)
    part = attend_back(sensor_tag, qh, kh, vh, after(do, up_own, encoded), mixed, lse, 0, 1)
    out_recv, down_recv, up_recv = after((out_recv, down_recv, up_recv), part[0])
    pairs_b = [(up_own, up_recv), (out_own, out_recv), (down_own, down_recv)]
    far_b = sum_cores(idx, pairs_b, rows, n)
    do = after(do, far_b[0])
    far_b = spread(far_b, n)
    dj = attend_back(sensor_tag, qh, kh, vh, do, mixed, lse, 1, pairs - 1, part)
    (qkv_other,) = grad_qkv(idx, h1, *dj)
    qkv_recv = core_swap(qkv_other, m)
    far_b = after(far_b, dj[0])
    near_b = sum_parts([after(far_b[0], qkv_other)] + far_b[1:])
    total_b = hop(near_b, tops(n))
    far_a = grad_qkv(idx, after(h1, near_b), *dj, qkv_recv, n)
    dj = after(dj, far_a[0])
    far_a = spread(far_a, n)
    tokens_grad, *far_v = tokens_back(use, idx, *dj, tokens, vt, dx2, s_mlp, bias, pieces_a, n)
    far_a, total_b = after((far_a, total_b), tokens_grad)
    far_v = spread([far_v[0]] + after(far_v[1:], far_a), n)

    near_a, total_b = sum_qkv(idx, far_a, far_v, total_b, n)
    if m > 2:
        total_b = over_pairs(total_b.astype(F32), m).astype(BF)
    other_b = core_swap(total_b, m)
    encoded = after(encoded, near_a[0]).astype(F32)
    near_a = [near_a[0]] + [xor_pp(near_a[i], i * q, n) for i in range(1, 4)]
    def both(mine, other):
        first = c == 0
        return jnp.where(first, mine, other).astype(F32), jnp.where(first, other, mine).astype(F32)

    def join(pair, start, width, parts, axis=1):
        out = []
        for p in range(parts):
            at = slice(start + p * width, start + (p + 1) * width)
            out.append(jnp.concatenate([pair[0][:, at], pair[1][:, at]], axis=1))
        return jnp.concatenate(out, axis=axis)

    h = d // 2
    g_mlp = both(total_b, other_b)
    grad_up_out = join(g_mlp, 0, h, wide)
    grad_out_out = join(g_mlp, ff // 2, h, 1)
    grad_down_out = join(g_mlp, (d + ff) // 2, h, wide, 0)
    near_a = after(near_a, grad_up_out, grad_out_out, grad_down_out, encoded)
    total_a = reduce_last(near_a, n, m)
    other_a = core_swap(total_a.astype(BF), m)
    cut = 3 * d // 2
    vecs = (total_a[:, cut:] + other_a[:, cut:].astype(F32)).T
    total_a, other_a = total_a[:, :cut].astype(BF), other_a[:, :cut]

    grad_qkv_out = join(both(total_a, other_a), 0, h, 3)
    return (
        encoded,
        tokens_grad,
        vecs[0],
        vecs[1],
        grad_qkv_out,
        vecs[2],
        vecs[3],
        grad_out_out,
        vecs[4],
        vecs[5],
        vecs[6],
        grad_up_out,
        vecs[8 : 8 + wide].reshape(ff // n),
        grad_down_out,
        vecs[7],
    )


def solution(mesh):
    n = mesh.shape["fsdp"]
    m = mesh.shape["dp"]
    both = P(("dp", "fsdp"), None)
    vec = P("fsdp")
    mat = P("fsdp", None)
    in_specs = (both, P(("dp", "fsdp")), both, vec, vec, mat, vec, vec, mat, vec, vec, vec, mat, vec, mat, vec, both)
    out_specs = (both, both, vec, vec, mat, vec, vec, mat, vec, vec, vec, mat, vec, mat, vec)
    return jax.shard_map(
        functools.partial(local, n=n, m=m), mesh=mesh, in_specs=in_specs, out_specs=out_specs, check_vma=False
    )
```

```python
import functools
import math

import jax
import jax.numpy as jnp
from jax import lax
from jax.experimental import pallas as pl
from jax.experimental.pallas import tpu as pltpu
from jax.sharding import PartitionSpec as P

F32 = jnp.float32
BF = jnp.bfloat16
EPS = 1e-6
LOG2E = math.log2(math.e)
LN2 = math.log(2.0)
NT = (((1,), (1,)), ((), ()))
TN = (((0,), (0,)), ((), ()))
NN = (((1,), (0,)), ((), ()))
ANY = pl.BlockSpec(memory_space=pl.ANY)
SAFE_SCORE = 90.0
VECS = 16
SDS = jax.ShapeDtypeStruct


def dg(a, b, dims):
    return lax.dot_general(a, b, dims, preferred_element_type=F32)


def params(axes=1):
    return pltpu.CompilerParams(
        vmem_limit_bytes=58 * 2**20, dimension_semantics=("arbitrary",) * axes
    )


def cost(flops, nbytes, trans=0):
    return pl.CostEstimate(flops=int(flops) >> 10, bytes_accessed=int(nbytes) >> 10, transcendentals=int(trans) >> 10)


def rows_of(height, width):
    return pl.BlockSpec((height, width), lambda i, *_: (i, 0))


def whole(shape):
    zeros = (0,) * len(shape)
    return pl.BlockSpec(shape, lambda *_: zeros, pipeline_mode=pl.Buffered(1))


def fixed(shape):
    zeros = (0,) * len(shape)
    return pl.BlockSpec(shape, lambda *_: zeros)


def norm_stats(x):
    n = x.shape[-1]
    c = x - jnp.sum(x, axis=-1, keepdims=True) * (1.0 / n)
    var = jnp.sum(c * c, axis=-1, keepdims=True) * (1.0 / n)
    return c, lax.rsqrt(var + EPS)


def after(x, *deps):
    return lax.optimization_barrier((x,) + deps)[0]


def xor_pp(x, b, n):
    return lax.ppermute(x, "fsdp", [(i, i ^ b) for i in range(n)])


def core_swap(x, m):
    return lax.ppermute(x, "dp", [(i, i ^ 1) for i in range(m)])


def gather_near(x, n):
    q = n // 4
    return jnp.stack([x] + [xor_pp(x, d * q, n) for d in (1, 2, 3)])


def tops(n):
    q = n // 4
    return [[low + z * q for z in range(4)] for low in range(q)]


def gather_far(s, n):
    return [s] + [xor_pp(s, e, n) for e in range(1, n // 4)]


def fits(rows, n):
    return rows % 16 == 0 and n == 16


def settle(pieces, order, c, n, wide=None):
    q = n // 4
    rows, width = pieces[0].shape[1:]
    if fits(rows, n):
        return pieces
    height = n * rows // 16
    halves = []
    for side in (pieces[:q], pieces[q:]):
        rel = jnp.stack(side, axis=1).reshape((n, rows, width))
        whole_side = jnp.take(rel, order, axis=0)
        flat = whole_side.reshape(16, height, width)
        if wide is not None:
            cut = width * (wide + 1) // (2 * wide + 1)
            low = whole_side[..., cut:].reshape(n, rows, wide, -1).transpose(0, 2, 1, 3)
            low = low.reshape(16, wide, height, -1).transpose(0, 2, 1, 3).reshape(16, height, -1)
            flat = jnp.concatenate([flat[..., :cut], low], axis=2)
        halves.append(flat.reshape(4, 4, height, width))
    left, right = jnp.where(c == 0, halves[0], halves[1]), jnp.where(c == 0, halves[1], halves[0])
    return [side[:, e] for side in (left, right) for e in range(4)]


def load_pieces(idx_ref, plan, sem):
    c = idx_ref[1]
    started = []
    for find, shard, start, skip, width, dst, height, first in plan:
        for e in range(4):
            for d in range(4):
                for block, h in zip(find(e, d), (c, 1 - c), strict=False):
                    rows = block.shape[0]
                    at = pl.ds(pl.multiple_of(shard(e, d) * height + first, 16), rows)
                    cols = pl.ds(pl.multiple_of(h * width, 128), width) if dst.shape[1] > width else slice(None)
                    src = block.at[:, pl.ds(start if e else start + skip, width)]
                    started.append(pltpu.make_async_copy(src, dst.at[at, cols], sem))
    for cp in started:
        cp.start()
    return started


def relative(idx_ref):
    return lambda e, d: lax.bitwise_xor(idx_ref[0], jnp.int32(d * 4 + e))


def by_top(idx_ref):
    return lambda e, d: lax.bitwise_xor(idx_ref[0] % 4, jnp.int32(e)) + d * 4


def load_qkv(idx_ref, pieces, w_ref, sem, vec_ref=None):
    def find(e, d):
        if len(pieces) == 8:
            return pieces[e].at[d], pieces[4 + e].at[d]
        return pieces[e].at[d], pieces[5].at[e - 1, d] if e else pieces[4].at[d]

    where = relative(idx_ref)
    rows, half = pieces[0].shape[1], w_ref.shape[1] // 2
    if vec_ref is not None:
        return load_pieces(idx_ref, [(lambda e, d: find(e, d)[:1], where, half, 0, 128, vec_ref, rows, 0)], sem)
    return load_pieces(idx_ref, [(find, where, 0, 0, half, w_ref, rows, 0)], sem)


def load_mlp(idx_ref, pieces, w1_ref, w2_ref, sem):
    where = by_top(idx_ref)

    def find1(e, d):
        return pieces[2 * e].at[d], pieces[2 * e + 1].at[d]

    def find2(e, d):
        at = 6 + 2 * e if e else 0
        return pieces[at].at[d], pieces[at + 1].at[d]

    rows = pieces[0].shape[1]
    half = w1_ref.shape[1] // 2
    w = w2_ref.shape[1] // 2
    one = [(find1, where, 0, 0, half, w1_ref, rows, 0)]
    two = [(find2, where, j * w, half, w, w2_ref, 4 * rows, j * rows) for j in range(4)]
    return load_pieces(idx_ref, one, sem.at[0]), load_pieces(idx_ref, two, sem.at[1])


def wait_mlp(w_ref, sem):
    pltpu.make_async_copy(w_ref, w_ref, sem).wait()


def qkv_kernel(idx_ref, x_ref, *refs):
    pieces = refs[:-11]
    q_ref, k_ref, v_ref, h_ref, vt_ref, bu_ref, qn_ref, kn_ref, w_ref, vec_ref, sem = refs[-11:]
    d = x_ref.shape[1]

    @pl.when(pl.program_id(0) == 0)
    def _():
        rows = pieces[0].shape[1]
        vecs = load_qkv(idx_ref, pieces, w_ref, sem.at[1], vec_ref)
        going = load_qkv(idx_ref, pieces, w_ref, sem.at[0])
        for cp in vecs:
            cp.wait()
        table = vec_ref[...].astype(F32).T[:VECS]
        vt_ref[...] = table
        bu_ref[...] = jnp.concatenate(
            [table[8 + j : 9 + j, s * rows : (s + 1) * rows] for s in range(d // rows) for j in range(4)], axis=1
        )
        for cp in going:
            cp.wait()

    c, r = norm_stats(x_ref[...].astype(F32))
    h = (c * r * vt_ref[0:1, :] + vt_ref[1:2, :]).astype(BF)
    h_ref[...] = h
    q = (dg(h, w_ref[:, :d], NN) + vt_ref[2:3, :]) * (0.125 * LOG2E)
    q_ref[...] = q.astype(BF)
    k = dg(h, w_ref[:, d : 2 * d], NN)
    k_ref[...] = k.astype(BF)
    lane = lax.broadcasted_iota(jnp.int32, (d, 128), 0)
    head = lax.broadcasted_iota(jnp.int32, (d, 128), 1) * 64
    of_head = jnp.where((lane >= head) & (lane < head + 64), 1.0, 0.0).astype(BF)
    for x, n_ref in ((q, qn_ref), (k, kn_ref)):
        n_ref[0] = jnp.max(dg((x * x).astype(BF), of_head, NN), axis=0, keepdims=True)
    v_ref[...] = (dg(h, w_ref[:, 2 * d :], NN) + vt_ref[3:4, :]).astype(BF)


def qkv(idx, x, pieces, tb=512):
    t, d = x.shape
    return pl.pallas_call(
        qkv_kernel,
        grid_spec=pltpu.PrefetchScalarGridSpec(
            num_scalar_prefetch=1,
            grid=(t // tb,),
            in_specs=[rows_of(tb, d)] + [ANY] * len(pieces),
            out_specs=[rows_of(tb, d)] * 4
            + [fixed((VECS, d)), fixed((1, 4 * d))]
            + [pl.BlockSpec((1, 1, 128), lambda i, _: (i, 0, 0))] * 2,
            scratch_shapes=[
                pltpu.VMEM((d, 3 * d), BF),
                pltpu.VMEM((d, 128), BF),
                pltpu.SemaphoreType.DMA((2,)),
            ],
        ),
        out_shape=[SDS((t, d), BF)] * 4
        + [SDS((VECS, d), F32), SDS((1, 4 * d), F32)]
        + [SDS((t // tb, 1, 128), F32)] * 2,
        compiler_params=params(),
        cost_estimate=cost(6 * t * d * d, t * d * 8 + d * d * 6),
        name="qkv",
    )(idx, x, *pieces)


def attend_kernel(tag_ref, qn_ref, kn_ref, q_ref, k_ref, v_ref, *refs, qb, first):
    o_ref, l_ref = refs[-2:]
    r = pl.program_id(0)
    length = q_ref.shape[0]
    low = lax.broadcasted_iota(jnp.int32, (1, 128), 1) < 64

    steps = qn_ref.shape[0] // tag_ref.shape[0]
    safe = True
    for h in range(2):
        head = 2 * (pl.program_id(1) + first) + h
        top = []
        for n_ref in (qn_ref, kn_ref):
            most = n_ref[r * steps, 0, head]
            for i in range(1, steps):
                most = jnp.maximum(most, n_ref[r * steps + i, 0, head])
            top.append(most)
        safe = jnp.logical_and(safe, top[0] * top[1] <= SAFE_SCORE**2)

    def block(qs, qn, ks, kn, plain):
        q = q_ref[pl.ds(qs, qn), :]
        k = k_ref[pl.ds(ks, kn), :]
        v = v_ref[pl.ds(ks, kn), :]
        outs = []
        for h in range(2):
            sel = low if h == 0 else jnp.logical_not(low)
            qm = jnp.where(sel, q, jnp.asarray(0, BF))
            vm = jnp.where(sel, v, jnp.asarray(1, BF))
            s = dg(qm, k, NT)
            if plain:
                outs.append((dg(jnp.exp2(s).astype(BF), vm, NN), 0.0))
            else:
                m = jnp.max(s, axis=1, keepdims=True)
                outs.append((dg(jnp.exp2(s - m).astype(BF), vm, NN), m))
        (a, ma), (b, mb) = outs
        acc = jnp.where(low, a, b)
        total = pltpu.roll(jnp.where(low, b, a), 64, 1)
        o_ref[pl.ds(qs, qn), :] = (acc / total).astype(o_ref.dtype)
        lse = jnp.log2(total) if plain else jnp.where(low, ma, mb) + jnp.log2(total)
        lse = lse.T
        l_ref[0, 0, 0:1, pl.ds(qs, qn)] = lse[0:1]
        l_ref[0, 0, 1:2, pl.ds(qs, qn)] = lse[64:65]

    for plain in (True, False):
        chosen = safe if plain else jnp.logical_not(safe)

        @pl.when(jnp.logical_and(tag_ref[r] == 0, chosen))
        def _(plain=plain):
            for i in range(length // qb):
                block(i * qb, qb, 0, length, plain)

        @pl.when(jnp.logical_and(tag_ref[r] != 0, chosen))
        def _(plain=plain):
            c = length // 4
            for i in range(4):
                block(i * c, c, i * c, c, plain)


def attend(tag, qn, kn, q, k, v, first, pairs, before=(), qb=512):
    t, d = q.shape
    rows = tag.shape[0]
    length = t // rows
    blk = pl.BlockSpec((length, 128), lambda r, p, _: (r, p + first))
    lse = pl.BlockSpec((1, 1, 2, length), lambda r, p, _: (r, p + first, 0, 0))
    return pl.pallas_call(
        functools.partial(attend_kernel, qb=qb, first=first),
        grid_spec=pltpu.PrefetchScalarGridSpec(
            num_scalar_prefetch=1,
            grid=(rows, pairs),
            in_specs=[pl.BlockSpec(memory_space=pltpu.SMEM)] * 2 + [blk] * 3 + [ANY] * len(before),
            out_specs=[blk, lse],
        ),
        out_shape=[SDS((t, d), BF), SDS((rows, d // 128, 2, length), F32)],
        input_output_aliases={6: 0, 7: 1} if before else {},
        compiler_params=params(2),
        cost_estimate=cost(2048 * t * length * pairs, t * d * 8, t * length * 12),
        name="attend",
    )(tag, qn, kn, q, k, v, *before)


ODDS = (2.3021649, 1.05007451e-1, -2.545477e-4, -1.0560537e-4, 4.093017e-6)


def gelu_both(u):
    z = u * u
    odds = ODDS[3] + z * ODDS[4]
    odds = ODDS[2] + z * odds
    odds = ODDS[1] + z * odds
    odds = ODDS[0] + z * odds
    phi = pltpu.reciprocal(1.0 + jnp.exp2(-u * odds), approx=True)
    density = jnp.exp2(z * (-0.5 * LOG2E) - 0.5 * math.log2(2.0 * math.pi))
    return u * phi, phi + u * density


def mlp_kernel(idx_ref, x_ref, o_ref, vt_ref, bu_ref, ord_ref, *refs, fc, steps):
    pieces = refs[:14]
    x2_ref, gl_ref, gp_ref, sent_ref, y_ref, w1_ref, w2_ref, sem = refs[14:]
    d = x_ref.shape[1]
    ff = w2_ref.shape[0]

    i = pl.program_id(0)
    tb = x_ref.shape[0]

    @pl.when(pl.program_id(0) == 0)
    def _():
        going, _ = load_mlp(idx_ref, pieces, w1_ref, w2_ref, sem)
        for cp in going:
            cp.wait()

    @pl.when(i < steps)
    def _():
        x2 = x_ref[...].astype(F32) + dg(o_ref[...], w1_ref[:, :d], NN) + vt_ref[4:5, :]
        x2_ref[...] = x2
        c, r = norm_stats(x2)
        h = (c * r * vt_ref[5:6, :] + vt_ref[6:7, :]).astype(BF)
        y = x2 + vt_ref[7:8, :]

        @pl.when(pl.program_id(0) == 0)
        def _():
            wait_mlp(w2_ref, sem.at[1])

        for f in range(0, ff, fc):
            u = dg(h, w1_ref[:, d + f : d + f + fc], NN) + bu_ref[:, f : f + fc]
            g, gp = gelu_both(u)
            g = g.astype(BF)
            gl_ref[:, f : f + fc] = g
            gp_ref[:, f : f + fc] = gp.astype(BF)
            y = y + dg(g, w2_ref[f : f + fc, :], NN)
        y_ref[pl.ds(pl.multiple_of(i * tb, tb), tb), :] = y.astype(BF)

    @pl.when(i >= steps)
    def _():
        pb, t = sent_ref.shape[0], y_ref.shape[0]
        order = jnp.broadcast_to(ord_ref[...].astype(F32), (8, pb)).T[:, 0:1]
        hot = jnp.where(order == lax.broadcasted_iota(jnp.int32, (pb, t), 1).astype(F32), 1.0, 0.0)
        sent_ref[...] = dg(hot.astype(BF), y_ref[...], NN).astype(BF)


def mlp(idx, x, o, vt, bu, order, pieces, tb=256, fc=768, pb=512):
    t, d = x.shape
    ff = bu.shape[1]
    steps = t // tb

    def rows(height, width):
        return pl.BlockSpec((height, width), lambda i, _: (jnp.minimum(i, steps - 1), 0))

    def late(i):
        return jnp.maximum(i - steps, 0)

    return pl.pallas_call(
        functools.partial(mlp_kernel, fc=fc, steps=steps),
        grid_spec=pltpu.PrefetchScalarGridSpec(
            num_scalar_prefetch=1,
            grid=(steps + t // pb,),
            in_specs=[rows(tb, d)] * 2
            + [whole(vt.shape), whole(bu.shape), pl.BlockSpec((1, pb), lambda i, _: (0, late(i)))]
            + [ANY] * 14,
            out_specs=[rows(tb, d), rows(tb, ff), rows(tb, ff), pl.BlockSpec((pb, d), lambda i, _: (late(i), 0))],
            scratch_shapes=[
                pltpu.VMEM((t, d), BF),
                pltpu.VMEM((d, d + ff), BF),
                pltpu.VMEM((ff, d), BF),
                pltpu.SemaphoreType.DMA((2,)),
            ],
        ),
        out_shape=[SDS((t, d), F32), SDS((t, ff), BF), SDS((t, ff), BF), pltpu.HBM((t, d), BF)],
        compiler_params=params(),
        cost_estimate=cost(4 * t * d * (d + 2 * ff), t * (10 * d + 4 * ff) + 4 * d * ff, 2 * t * ff),
        name="mlp",
    )(idx, x, o, vt, bu, order, *pieces)


def split_halves(c, r, mine_ref, theirs_ref):
    h = r.shape[1] // 2
    left, right = r[:, :h], r[:, h:]
    mine_ref[...] = jnp.where(c == 0, left, right)
    theirs_ref[...] = jnp.where(c == 0, right, left)


def mlp_back_kernel(idx_ref, ord_ref, ret_ref, gp_ref, x2_ref, o_ref, vt_ref, *refs, fc):
    pieces = refs[:14]
    (dm_ref, du_ref, dx2_ref, do_ref, h2_ref, sums_ref, gbu_ref, mine_ref, theirs_ref) = refs[14:23]
    w1_ref, w2_ref, acc_ref, sem = refs[23:]
    i = pl.program_id(0)
    tb, ff = gp_ref.shape
    t, d = ret_ref.shape

    @pl.when(i == 0)
    def _():
        load_mlp(idx_ref, pieces, w1_ref, w2_ref, sem)
        sums_ref[...] = jnp.zeros_like(sums_ref)
        gbu_ref[...] = jnp.zeros_like(gbu_ref)
        acc_ref[...] = jnp.zeros_like(acc_ref)
        wait_mlp(w2_ref, sem.at[1])
        wait_mlp(w1_ref, sem.at[0])

    at = lax.broadcasted_iota(jnp.int32, (tb, t), 0) + i * tb
    hot = jnp.where(ord_ref[...] == at, 1.0, 0.0).astype(BF)
    dy = dg(hot, ret_ref[...], NN)
    dm = dy.astype(BF)
    dm_ref[...] = dm
    sums_ref[0:1, :] += jnp.sum(dy, axis=0, keepdims=True)
    dh = jnp.zeros((tb, d), F32)
    ahead = dg(dm, w2_ref[:fc, :], NT)
    for f in range(0, ff, fc):
        du = ahead * gp_ref[:, f : f + fc].astype(F32)
        if f + fc < ff:
            ahead = dg(dm, w2_ref[f + fc : f + 2 * fc, :], NT)
        gbu_ref[:, f : f + fc] += jnp.sum(du, axis=0, keepdims=True)
        du = du.astype(BF)
        du_ref[:, f : f + fc] = du
        dh = dh + dg(du, w1_ref[:, d + f : d + f + fc], NT)
    c, r = norm_stats(x2_ref[...])
    xh = c * r
    gain = vt_ref[5:6, :]
    h2_ref[...] = (xh * gain + vt_ref[6:7, :]).astype(BF)
    sums_ref[1:2, :] += jnp.sum(dh * xh, axis=0, keepdims=True)
    sums_ref[2:3, :] += jnp.sum(dh, axis=0, keepdims=True)
    dz = dh * gain
    m1 = jnp.sum(dz, axis=-1, keepdims=True) * (1.0 / d)
    m2 = jnp.sum(dz * xh, axis=-1, keepdims=True) * (1.0 / d)
    dx2 = dy + r * (dz - m1 - xh * m2)
    dx2_ref[...] = dx2
    da = dx2.astype(BF)
    sums_ref[3:4, :] += jnp.sum(da.astype(F32), axis=0, keepdims=True)
    do_ref[...] = dg(da, w1_ref[:, :d], NT).astype(BF)
    acc_ref[...] += dg(o_ref[...], da, TN)

    @pl.when(i == pl.num_programs(0) - 1)
    def _():
        split_halves(idx_ref[1], acc_ref[...].astype(BF), mine_ref, theirs_ref)


def mlp_back(idx, order_row, ret, gp, x2, o, vt, pieces, tb=256, fc=768):
    t, d = x2.shape
    ff = gp.shape[1]
    return pl.pallas_call(
        functools.partial(mlp_back_kernel, fc=fc),
        grid_spec=pltpu.PrefetchScalarGridSpec(
            num_scalar_prefetch=1,
            grid=(t // tb,),
            in_specs=[whole((1, t)), whole((t, d)), rows_of(tb, ff), rows_of(tb, d), rows_of(tb, d), whole(vt.shape)]
            + [ANY] * 14,
            out_specs=[rows_of(tb, d), rows_of(tb, ff)]
            + [rows_of(tb, d)] * 3
            + [fixed((8, d)), fixed((1, ff))]
            + [fixed((d, d // 2))] * 2,
            scratch_shapes=[
                pltpu.VMEM((d, d + ff), BF),
                pltpu.VMEM((ff, d), BF),
                pltpu.VMEM((d, d), F32),
                pltpu.SemaphoreType.DMA((2,)),
            ],
        ),
        out_shape=[
            SDS((t, d), BF),
            SDS((t, ff), BF),
            SDS((t, d), F32),
            SDS((t, d), BF),
            SDS((t, d), BF),
            SDS((8, d), F32),
            SDS((1, ff), F32),
            pltpu.HBM((d, d // 2), BF),
            pltpu.HBM((d, d // 2), BF),
        ],
        compiler_params=params(),
        cost_estimate=cost(2 * t * d * (d + 2 * ff + t) * 1.5, t * (20 * d + 4 * ff)),
        name="mlp_back",
    )(idx, order_row, ret, gp, x2, o, vt, *pieces)


def grad_mlp_kernel(
    idx_ref, g_ref, dm_ref, h2_any, du_ref, u, down_own, down_other, up_own, up_other, bias_ref, h2_ref, sem, *, rows
):
    i = pl.program_id(0)
    steps = pl.num_programs(0) // 2

    @pl.when(i == 0)
    def _():
        pltpu.make_async_copy(h2_any, h2_ref, sem).start()

    @pl.when(i == steps)
    def _():
        pltpu.make_async_copy(h2_any, h2_ref, sem).wait()

    @pl.when(i < steps)
    def _():
        split_halves(idx_ref[1], dg(g_ref[...], dm_ref[...], TN).astype(BF), down_own, down_other)
        d = dm_ref.shape[1]
        wide = u.shape[1] // d
        for j in range(wide):
            parts = [u[:, (s * wide + j) * rows : (s * wide + j + 1) * rows] for s in range(d // rows)]
            bias_ref[j : j + 1, :] = jnp.concatenate(parts, axis=1)

    @pl.when(i >= steps)
    def _():
        split_halves(idx_ref[1], dg(h2_ref[...], du_ref[...], TN).astype(BF), up_own, up_other)


def grad_mlp(idx, g, dm, h2, du, gbu, rows):
    t, ff = g.shape
    d = dm.shape[1]
    steps = ff // d

    def down(i):
        return jnp.minimum(i, steps - 1)

    def up(i):
        return jnp.maximum(i - steps, 0)

    return pl.pallas_call(
        functools.partial(grad_mlp_kernel, rows=rows),
        grid_spec=pltpu.PrefetchScalarGridSpec(
            num_scalar_prefetch=1,
            grid=(2 * steps,),
            in_specs=[
                pl.BlockSpec((t, d), lambda i, _: (0, down(i))),
                whole((t, d)),
                ANY,
                pl.BlockSpec((t, d), lambda i, _: (0, up(i))),
                whole(gbu.shape),
            ],
            out_specs=[pl.BlockSpec((d, d // 2), lambda i, _: (down(i), 0))] * 2
            + [pl.BlockSpec((d, d // 2), lambda i, _: (0, up(i)))] * 2
            + [fixed((steps, d))],
            scratch_shapes=[pltpu.VMEM((t, d), BF), pltpu.SemaphoreType.DMA],
        ),
        out_shape=[pltpu.HBM((ff, d // 2), BF)] * 2
        + [pltpu.HBM((d, ff // 2), BF)] * 2
        + [SDS((steps, d), F32)],
        compiler_params=params(),
        cost_estimate=cost(6 * t * ff * d, 4 * t * (ff + d) + 4 * ff * d),
        name="grad_mlp",
    )(idx, g, dm, h2, du, gbu)


def attend_back_kernel(
    tag_ref, q_ref, k_ref, v_ref, do_ref, o_ref, l_ref, *refs, kb, qb
):
    dq_ref, dk_ref, dv_ref, dl_ref, dqt_ref = refs[-5:]
    r = pl.program_id(0)
    length = q_ref.shape[0]
    low = lax.broadcasted_iota(jnp.int32, (1, 128), 1) < 64
    prod = (do_ref[...].astype(F32) * o_ref[...].astype(F32)).T
    dl_ref[0:1, :] = jnp.sum(prod[0:64], axis=0, keepdims=True)
    dl_ref[1:2, :] = jnp.sum(prod[64:128], axis=0, keepdims=True)

    def block(ks, kn, qs, qn):
        k = k_ref[pl.ds(ks, kn), :]
        v = v_ref[pl.ds(ks, kn), :]
        q = q_ref[pl.ds(qs, qn), :]
        do = do_ref[pl.ds(qs, qn), :]
        dks = []
        dvs = []
        dqs = []
        for h in range(2):
            sel = low if h == 0 else jnp.logical_not(low)
            km = jnp.where(sel, k, jnp.asarray(0, BF))
            vm = jnp.where(sel, v, jnp.asarray(0, BF))
            pt = jnp.exp2(dg(km, q, NT) - l_ref[0, 0, h : h + 1, pl.ds(qs, qn)])
            dst = (pt * (dg(vm, do, NT) - dl_ref[h : h + 1, pl.ds(qs, qn)])).astype(BF)
            dvs.append(dg(pt.astype(BF), do, NN))
            dks.append(dg(dst, q, NN))
            dqs.append(dg(km.T, dst, NN))
        return jnp.where(low, dks[0], dks[1]), jnp.where(low, dvs[0], dvs[1]), dqs[0] + dqs[1]

    def run(kn, qn, plan):
        seen = set()
        for ks, starts in plan:
            dk = dv = None
            for qs in starts:
                a, b, dq = block(ks, kn, qs, qn)
                dk = a if dk is None else dk + a
                dv = b if dv is None else dv + b
                if qs in seen:
                    dqt_ref[:, pl.ds(qs, qn)] += dq
                else:
                    dqt_ref[:, pl.ds(qs, qn)] = dq
                seen.add(qs)
            dk_ref[pl.ds(ks, kn), :] = (dk * LN2).astype(BF)
            dv_ref[pl.ds(ks, kn), :] = dv.astype(BF)
        dq_ref[...] = (dqt_ref[...].T * 0.125).astype(BF)

    @pl.when(tag_ref[r] == 0)
    def _():
        run(kb, qb, [(ks, range(0, length, qb)) for ks in range(0, length, kb)])

    @pl.when(tag_ref[r] != 0)
    def _():
        c = length // 4
        run(c, c, [(ks, [ks]) for ks in range(0, length, c)])


def attend_back(tag, q, k, v, do, o, lse, first, pairs, before=(), kb=512, qb=512):
    t, d = q.shape
    rows = tag.shape[0]
    length = t // rows
    blk = pl.BlockSpec((length, 128), lambda r, p, _: (r, p + first))
    lse_spec = pl.BlockSpec((1, 1, 2, length), lambda r, p, _: (r, p + first, 0, 0))
    return pl.pallas_call(
        functools.partial(attend_back_kernel, kb=kb, qb=qb),
        grid_spec=pltpu.PrefetchScalarGridSpec(
            num_scalar_prefetch=1,
            grid=(rows, pairs),
            in_specs=[blk] * 5 + [lse_spec] + [ANY] * len(before),
            out_specs=[blk] * 3,
            scratch_shapes=[pltpu.VMEM((2, length), F32), pltpu.VMEM((128, length), F32)],
        ),
        out_shape=[SDS((t, d), BF)] * 3,
        input_output_aliases={7: 0, 8: 1, 9: 2} if before else {},
        compiler_params=params(2),
        cost_estimate=cost(5120 * t * length * pairs, t * d * 16, t * length * 12),
        name="attend_back",
    )(tag, q, k, v, do, o, lse, *before)


def grad_qkv_kernel(idx_ref, h_any, dq_any, dk_any, dv_any, *refs, rows):
    h_ref, d_ref, sem = refs[-3:]
    w = d_ref.shape[2]
    half = idx_ref[1] if rows is not None else 1 - idx_ref[1]
    cols = pl.ds(pl.multiple_of(half * w, 128), w)
    going = [pltpu.make_async_copy(h_any, h_ref, sem.at[3])]
    for m, ref in enumerate((dq_any, dk_any, dv_any)):
        going.append(pltpu.make_async_copy(ref.at[:, cols], d_ref.at[m], sem.at[m]))
    for cp in going:
        cp.start()
    going[0].wait()
    for m in range(3):
        at = slice(m * w, (m + 1) * w)
        going[1 + m].wait()
        part = dg(h_ref[...], d_ref[m], TN)
        if rows is None:
            refs[0][:, at] = part.astype(BF)
        else:
            outs, sum_ref = refs[1:-4], refs[-4]
            q = len(outs)
            sum_ref[...] = part + refs[0][:, at].astype(F32)
            for e in range(q):
                for z in range(4):
                    s = z * q + lax.bitwise_xor(idx_ref[0] % q, jnp.int32(e))
                    outs[e][z, :, at] = sum_ref[pl.ds(pl.multiple_of(s * rows, 8), rows), :].astype(BF)


def grad_qkv(idx, h1, dq, dk, dv, recv=None, n=None):
    t, d = h1.shape
    w = d // 2
    own = recv is not None
    outs = [(4, d // n, 3 * w)] * (n // 4) if own else [(d, 3 * w)]
    return pl.pallas_call(
        functools.partial(grad_qkv_kernel, rows=d // n if own else None),
        grid_spec=pltpu.PrefetchScalarGridSpec(
            num_scalar_prefetch=1,
            grid=(1,),
            in_specs=[ANY] * 4 + [whole((d, 3 * w))] * own,
            out_specs=[fixed(o) for o in outs],
            scratch_shapes=[pltpu.VMEM((d, w), F32)] * own
            + [pltpu.VMEM((t, d), BF), pltpu.VMEM((3, t, w), BF), pltpu.SemaphoreType.DMA((4,))],
        ),
        out_shape=[pltpu.HBM(o, BF) for o in outs],
        compiler_params=params(),
        cost_estimate=cost(6 * t * d * w, t * d * 6),
        name="grad_qkv_own" if own else "grad_qkv_other",
    )(idx, h1, dq, dk, dv, *([recv] * own))


def tokens_back_kernel(idx_ref, me_ref, x_ref, vt_ref, dx2_ref, dq_ref, dk_ref, dv_ref, a_ref, u_ref, *refs, q):
    pieces = refs[: -5 - q]
    tg_ref, *outs, s_ref, table_ref, w_ref, sem = refs[-5 - q :]
    d = x_ref.shape[1]

    @pl.when(pl.program_id(0) == 0)
    def _():
        going = load_qkv(idx_ref, pieces, w_ref, sem)
        s_ref[...] = jnp.zeros_like(s_ref)
        for cp in going:
            cp.wait()

    dh = dg(dq_ref[...], w_ref[:, :d], NT)
    dh = dh + dg(dk_ref[...], w_ref[:, d : 2 * d], NT)
    dh = dh + dg(dv_ref[...], w_ref[:, 2 * d :], NT)
    ones = jnp.ones((8, x_ref.shape[0]), BF)
    s_ref[2:3, :] += dg(ones, dq_ref[...], NN)[0:1]
    s_ref[3:4, :] += dg(ones, dv_ref[...], NN)[0:1]
    c, r = norm_stats(x_ref[...].astype(F32))
    xh = c * r
    s_ref[0:1, :] += jnp.sum(dh * xh, axis=0, keepdims=True)
    s_ref[1:2, :] += jnp.sum(dh, axis=0, keepdims=True)
    dz = dh * vt_ref[0:1, :]
    m1 = jnp.sum(dz, axis=-1, keepdims=True) * (1.0 / d)
    m2 = jnp.sum(dz * xh, axis=-1, keepdims=True) * (1.0 / d)
    tg_ref[...] = dx2_ref[...] + r * (dz - m1 - xh * m2)

    @pl.when(pl.program_id(0) == pl.num_programs(0) - 1)
    def _():
        rows = outs[0].shape[1]
        wide = u_ref.shape[0]
        lines = [s_ref[0:4, :], a_ref[3:4, :], a_ref[1:3, :], a_ref[0:1, :], u_ref[...]]
        table_ref[...] = jnp.concatenate(lines + [jnp.zeros((120 - wide, d), F32)], axis=0).T
        for e in range(q):
            for z in range(4):
                s = z * q + lax.bitwise_xor(me_ref[0] % q, jnp.int32(e))
                outs[e][z] = table_ref[pl.ds(pl.multiple_of(s * rows, 8), rows), :].astype(BF)


def tokens_back(idx, me, dq, dk, dv, x, vt, dx2, s_mlp, bias, pieces, n, tb=512):
    t, d = x.shape
    q = n // 4
    return pl.pallas_call(
        functools.partial(tokens_back_kernel, q=q),
        grid_spec=pltpu.PrefetchScalarGridSpec(
            num_scalar_prefetch=2,
            grid=(t // tb,),
            in_specs=[rows_of(tb, d), whole(vt.shape)]
            + [rows_of(tb, d)] * 4
            + [whole(s_mlp.shape), whole(bias.shape)]
            + [ANY] * len(pieces),
            out_specs=[rows_of(tb, d)] + [fixed((4, d // n, 128))] * q,
            scratch_shapes=[
                pltpu.VMEM((8, d), F32),
                pltpu.VMEM((d, 128), F32),
                pltpu.VMEM((d, 3 * d), BF),
                pltpu.SemaphoreType.DMA,
            ],
        ),
        out_shape=[SDS((t, d), F32)] + [pltpu.HBM((4, d // n, 128), BF)] * q,
        compiler_params=params(),
        cost_estimate=cost(9 * t * d * d, t * d * 16 + d * d * 6),
        name="tokens_back",
    )(idx, me, x, vt, dx2, dq, dk, dv, s_mlp, bias, *pieces)


def hop(x, groups):
    return lax.all_to_all(x, "fsdp", split_axis=0, concat_axis=0, tiled=True, axis_index_groups=groups)


def sum_cores_kernel(idx_ref, *refs, q):
    outs = refs[-q:]
    rows = outs[0].shape[1]
    for e in range(q):
        at = lax.bitwise_xor(idx_ref[0] % q, jnp.int32(e))
        start = 0
        for a_ref, b_ref in zip(refs[:-q:2], refs[1:-q:2], strict=True):
            total = a_ref[at] + b_ref[at]
            w = total.shape[1]
            for j in range(total.shape[0] // rows):
                outs[e][0, :, start : start + w] = total[j * rows : (j + 1) * rows]
                start += w


def sum_cores(idx, pairs, rows, n):
    q = n // 4
    ops, specs, width = [], [], 0
    for pair in pairs:
        shape = (pair[0].shape[0] // n, pair[0].shape[1])
        width += shape[0] // rows * shape[1]
        ops += [x.reshape((n,) + shape) for x in pair]
        specs += [pl.BlockSpec((q,) + shape, lambda z, _: (z, 0, 0))] * 2
    return pl.pallas_call(
        functools.partial(sum_cores_kernel, q=q),
        grid_spec=pltpu.PrefetchScalarGridSpec(
            num_scalar_prefetch=1,
            grid=(4,),
            in_specs=specs,
            out_specs=[pl.BlockSpec((1, rows, width), lambda z, _: (z, 0, 0))] * q,
        ),
        out_shape=[pltpu.HBM((4, rows, width), BF)] * q,
        compiler_params=params(),
        cost_estimate=cost(n * rows * width, n * rows * width * 6),
        name="sum_cores",
    )(idx, *ops)


def spread(parts, n):
    return [parts[0]] + [xor_pp(parts[e], e, n) for e in range(1, n // 4)]


def sum_parts_kernel(*refs):
    total = refs[0][...].astype(F32)
    for x in refs[1:-1]:
        total = total + x[...].astype(F32)
    refs[-1][...] = total.astype(BF)


def sum_parts(parts):
    shape = (1,) + parts[0].shape[1:]
    spec = pl.BlockSpec(shape, lambda i: (i, 0, 0))
    return pl.pallas_call(
        sum_parts_kernel,
        grid=(4,),
        in_specs=[spec] * len(parts),
        out_specs=spec,
        out_shape=pltpu.HBM(parts[0].shape, BF),
        compiler_params=params(),
        cost_estimate=cost(4 * len(parts) * math.prod(shape), 8 * len(parts) * math.prod(shape)),
        name="sum_parts",
    )(*parts)


def sum_qkv_kernel(idx_ref, *refs, q):
    outs = refs[2 * q + 1 :]
    for d in range(4):
        at = lax.bitwise_xor(idx_ref[0] // q, jnp.int32(d))
        start = 0
        for parts in (refs[:q], refs[q : 2 * q]):
            total = parts[0][at].astype(F32)
            for x in parts[1:]:
                total = total + x[at].astype(F32)
            w = total.shape[1]
            outs[d][:, start : start + w] = total.astype(BF)
            start += w
    last = refs[2 * q]
    outs[4][...] = (
        last[0].astype(F32) + last[1].astype(F32) + last[2].astype(F32) + last[3].astype(F32)
    ).astype(BF)


def sum_qkv(idx, far, vecs, last, n):
    _, rows, w = far[0].shape
    width = w + vecs[0].shape[2]
    ops = list(far) + list(vecs) + [last]
    *near, total = pl.pallas_call(
        functools.partial(sum_qkv_kernel, q=n // 4),
        grid_spec=pltpu.PrefetchScalarGridSpec(
            num_scalar_prefetch=1,
            grid=(1,),
            in_specs=[whole(x.shape) for x in ops],
            out_specs=[fixed((rows, width))] * 4 + [fixed(last.shape[1:])],
        ),
        out_shape=[pltpu.HBM((rows, width), BF)] * 4 + [pltpu.HBM(last.shape[1:], BF)],
        compiler_params=params(),
        cost_estimate=cost(n * rows * width, n * rows * width * 3),
        name="sum_qkv",
    )(idx, *ops)
    return near, total


def reduce_last(near, n, m):
    total = near[0].astype(F32)
    for x in near[1:]:
        total = total + x.astype(F32)
    return over_pairs(total, m)


def over_pairs(total, m):
    b = 2
    while b < m:
        total = total + lax.ppermute(total.astype(BF), "dp", [(i, i ^ b) for i in range(m)]).astype(F32)
        b *= 2
    return total


def local(
    tokens,
    sensor_tag,
    owner_order,
    ln1_gain,
    ln1_bias,
    w_qkv,
    b_query,
    b_value,
    w_out,
    b_out,
    ln2_gain,
    ln2_bias,
    w_up,
    b_up,
    w_down,
    b_down,
    out_grad,
    *,
    n,
    m,
):
    t, d = tokens.shape
    ff = w_up.shape[1]
    rows = d // n
    wide = ff // d
    f = lax.axis_index("fsdp")
    c = lax.axis_index("dp") % 2
    idx = jnp.stack([f, c]).astype(jnp.int32)
    use = idx if fits(rows, n) else jnp.zeros_like(idx)

    def core_half(x):
        h = x.shape[1] // 2
        return jnp.where(c == 0, x[:, :h], x[:, h:])

    vec = jnp.stack([ln1_gain, ln1_bias, b_query, b_value, b_out, ln2_gain, ln2_bias, b_down], axis=1)
    vec = jnp.concatenate([vec, b_up.reshape(wide, rows).T], axis=1)
    vec = jnp.pad(vec, ((0, 0), (0, 128 - vec.shape[1])))
    shard_a = jnp.concatenate([core_half(w_qkv), vec], axis=1)
    shard_b = jnp.concatenate(
        [core_half(jnp.concatenate([w_out, w_up], axis=1))]
        + [core_half(w_down[j * rows : (j + 1) * rows]) for j in range(wide)],
        axis=1,
    )
    q = n // 4
    everyone = jnp.arange(n)

    near_a = gather_near(shard_a, n)
    near_b = hop(jnp.broadcast_to(after(shard_b, near_a)[None], (4,) + shard_b.shape), tops(n))
    own_a = gather_far(near_a, n)
    cast = after(out_grad, near_a).astype(BF)
    own_a[1:] = after(own_a[1:], cast)
    swap_a = [core_swap(near_a, m), core_swap(jnp.stack(own_a[1:]), m)]
    if fits(rows, n):
        pieces_a = own_a + swap_a
    else:
        pieces_a = settle(own_a + swap_a[:1] + [swap_a[1][e] for e in range(q - 1)], f ^ everyone, c, n)
    near_b = after(near_b, own_a[1:])
    qh, kh, vh, h1, vt, bu, qn, kn = qkv(use, after(tokens, near_b), pieces_a)
    pairs = d // 128
    early = pairs * 2 // 3
    cut = (d + ff) // 2
    if fits(rows, n):
        x, y = near_b[..., :cut], near_b[..., cut:]
        x1, y2 = after((xor_pp(x, 1, n), xor_pp(y, 2, n)), vt)
        x2, y1 = xor_pp(x, 2, n), xor_pp(y, 1, n)
        x3, y3 = xor_pp(x1, 2, n), xor_pp(y2, 1, n)
        part = attend(sensor_tag, qn, kn, after(qh, x1, y2), kh, vh, 0, early)
        side = [near_b] + after([x1, x2, x3, y1, y2, y3], part[0])
        pieces_b = []
        for x in side:
            pieces_b += [x, core_swap(x, m)]
        gate = side[1:]
    else:
        far_b = gather_far(near_b, n)
        side = settle(
            far_b + [core_swap(x, m) for x in far_b], everyone // q * q + (everyone ^ f) % q, c, n, wide
        )
        part = attend(sensor_tag, qn, kn, qh, kh, vh, 0, early)
        pieces_b = [side[0], side[4]]
        for e in range(1, 4):
            pieces_b += [side[e][..., :cut], side[4 + e][..., :cut]]
        for e in range(1, 4):
            pieces_b += [side[e][..., cut:], side[4 + e][..., cut:]]
        gate = far_b
    returned = lax.all_to_all(after(cast, gate), "fsdp", split_axis=0, concat_axis=0, tiled=True)
    mixed, lse = attend(sensor_tag, qn, kn, qh, kh, vh, early, pairs - early, part)

    x2, active, slope, sent = mlp(use, tokens, mixed, vt, bu, owner_order, pieces_b)
    encoded = lax.all_to_all(sent, "fsdp", split_axis=0, concat_axis=0, tiled=True)

    returned = after(returned, sent)
    dm, du, dx2, do, h2, s_mlp, gbu, out_own, out_other = mlp_back(
        use, owner_order, returned, slope, x2, mixed, vt, pieces_b
    )
    out_recv = core_swap(out_other, m)
    down_own, down_other, up_own, up_other, bias = grad_mlp(idx, active, dm, h2, du, gbu, rows)
    down_recv = core_swap(down_other, m)
    up_recv = core_swap(up_other, m)
    part = attend_back(sensor_tag, qh, kh, vh, after(do, up_own, encoded), mixed, lse, 0, 1)
    out_recv, down_recv, up_recv = after((out_recv, down_recv, up_recv), part[0])
    pairs_b = [(up_own, up_recv), (out_own, out_recv), (down_own, down_recv)]
    far_b = sum_cores(idx, pairs_b, rows, n)
    do = after(do, far_b[0])
    far_b = spread(far_b, n)
    dj = attend_back(sensor_tag, qh, kh, vh, do, mixed, lse, 1, pairs - 1, part)
    (qkv_other,) = grad_qkv(idx, h1, *dj)
    qkv_recv = core_swap(qkv_other, m)
    far_b = after(far_b, dj[0])
    near_b = sum_parts([after(far_b[0], qkv_other)] + far_b[1:])
    total_b = hop(near_b, tops(n))
    far_a = grad_qkv(idx, after(h1, near_b), *dj, qkv_recv, n)
    dj = after(dj, far_a[0])
    far_a = spread(far_a, n)
    tokens_grad, *far_v = tokens_back(use, idx, *dj, tokens, vt, dx2, s_mlp, bias, pieces_a, n)
    far_a, total_b = after((far_a, total_b), tokens_grad)
    far_v = spread([far_v[0]] + after(far_v[1:], far_a), n)

    near_a, total_b = sum_qkv(idx, far_a, far_v, total_b, n)
    if m > 2:
        total_b = over_pairs(total_b.astype(F32), m).astype(BF)
    other_b = core_swap(total_b, m)
    encoded = after(encoded, near_a[0]).astype(F32)
    near_a = [near_a[0]] + [xor_pp(near_a[i], i * q, n) for i in range(1, 4)]
    def both(mine, other):
        first = c == 0
        return jnp.where(first, mine, other).astype(F32), jnp.where(first, other, mine).astype(F32)

    def join(pair, start, width, parts, axis=1):
        out = []
        for p in range(parts):
            at = slice(start + p * width, start + (p + 1) * width)
            out.append(jnp.concatenate([pair[0][:, at], pair[1][:, at]], axis=1))
        return jnp.concatenate(out, axis=axis)

    h = d // 2
    g_mlp = both(total_b, other_b)
    grad_up_out = join(g_mlp, 0, h, wide)
    grad_out_out = join(g_mlp, ff // 2, h, 1)
    grad_down_out = join(g_mlp, (d + ff) // 2, h, wide, 0)
    near_a = after(near_a, grad_up_out, grad_out_out, grad_down_out, encoded)
    total_a = reduce_last(near_a, n, m)
    other_a = core_swap(total_a.astype(BF), m)
    cut = 3 * d // 2
    vecs = (total_a[:, cut:] + other_a[:, cut:].astype(F32)).T
    total_a, other_a = total_a[:, :cut].astype(BF), other_a[:, :cut]

    grad_qkv_out = join(both(total_a, other_a), 0, h, 3)
    return (
        encoded,
        tokens_grad,
        vecs[0],
        vecs[1],
        grad_qkv_out,
        vecs[2],
        vecs[3],
        grad_out_out,
        vecs[4],
        vecs[5],
        vecs[6],
        grad_up_out,
        vecs[8 : 8 + wide].reshape(ff // n),
        grad_down_out,
        vecs[7],
    )


def solution(mesh):
    n = mesh.shape["fsdp"]
    m = mesh.shape["dp"]
    both = P(("dp", "fsdp"), None)
    vec = P("fsdp")
    mat = P("fsdp", None)
    in_specs = (both, P(("dp", "fsdp")), both, vec, vec, mat, vec, vec, mat, vec, vec, vec, mat, vec, mat, vec, both)
    out_specs = (both, both, vec, vec, mat, vec, vec, mat, vec, vec, vec, mat, vec, mat, vec)
    return jax.shard_map(
        functools.partial(local, n=n, m=m), mesh=mesh, in_specs=in_specs, out_specs=out_specs, check_vma=False
    )
```

```python
import functools
import math

import jax
import jax.numpy as jnp
from jax import lax
from jax.experimental import pallas as pl
from jax.experimental.pallas import tpu as pltpu
from jax.sharding import PartitionSpec as P

F32 = jnp.float32
BF = jnp.bfloat16
EPS = 1e-6
LOG2E = math.log2(math.e)
LN2 = math.log(2.0)
NT = (((1,), (1,)), ((), ()))
TN = (((0,), (0,)), ((), ()))
NN = (((1,), (0,)), ((), ()))
ANY = pl.BlockSpec(memory_space=pl.ANY)
SAFE_SCORE = 90.0
VECS = 16
SDS = jax.ShapeDtypeStruct


def dg(a, b, dims):
    return lax.dot_general(a, b, dims, preferred_element_type=F32)


def params(axes=1):
    return pltpu.CompilerParams(
        vmem_limit_bytes=58 * 2**20, dimension_semantics=("arbitrary",) * axes
    )


def cost(flops, nbytes, trans=0):
    return pl.CostEstimate(flops=int(flops) >> 10, bytes_accessed=int(nbytes) >> 10, transcendentals=int(trans) >> 10)


def rows_of(height, width):
    return pl.BlockSpec((height, width), lambda i, *_: (i, 0))


def whole(shape):
    zeros = (0,) * len(shape)
    return pl.BlockSpec(shape, lambda *_: zeros, pipeline_mode=pl.Buffered(1))


def fixed(shape):
    zeros = (0,) * len(shape)
    return pl.BlockSpec(shape, lambda *_: zeros)


def norm_stats(x):
    n = x.shape[-1]
    c = x - jnp.sum(x, axis=-1, keepdims=True) * (1.0 / n)
    var = jnp.sum(c * c, axis=-1, keepdims=True) * (1.0 / n)
    return c, lax.rsqrt(var + EPS)


def after(x, *deps):
    return lax.optimization_barrier((x,) + deps)[0]


def xor_pp(x, b, n):
    return lax.ppermute(x, "fsdp", [(i, i ^ b) for i in range(n)])


def core_swap(x, m):
    return lax.ppermute(x, "dp", [(i, i ^ 1) for i in range(m)])


def gather_near(x, n):
    q = n // 4
    return jnp.stack([x] + [xor_pp(x, d * q, n) for d in (1, 2, 3)])


def tops(n):
    q = n // 4
    return [[low + z * q for z in range(4)] for low in range(q)]


def gather_far(s, n):
    return [s] + [xor_pp(s, e, n) for e in range(1, n // 4)]


def fits(rows, n):
    return rows % 16 == 0 and n == 16


def settle(pieces, order, c, n, wide=None):
    q = n // 4
    rows, width = pieces[0].shape[1:]
    if fits(rows, n):
        return pieces
    height = n * rows // 16
    halves = []
    for side in (pieces[:q], pieces[q:]):
        rel = jnp.stack(side, axis=1).reshape((n, rows, width))
        whole_side = jnp.take(rel, order, axis=0)
        flat = whole_side.reshape(16, height, width)
        if wide is not None:
            cut = width * (wide + 1) // (2 * wide + 1)
            low = whole_side[..., cut:].reshape(n, rows, wide, -1).transpose(0, 2, 1, 3)
            low = low.reshape(16, wide, height, -1).transpose(0, 2, 1, 3).reshape(16, height, -1)
            flat = jnp.concatenate([flat[..., :cut], low], axis=2)
        halves.append(flat.reshape(4, 4, height, width))
    left, right = jnp.where(c == 0, halves[0], halves[1]), jnp.where(c == 0, halves[1], halves[0])
    return [side[:, e] for side in (left, right) for e in range(4)]


def load_pieces(idx_ref, plan, sem):
    c = idx_ref[1]
    started = []
    for find, shard, start, skip, width, dst, height, first in plan:
        for e in range(4):
            for d in range(4):
                for block, h in zip(find(e, d), (c, 1 - c), strict=False):
                    rows = block.shape[0]
                    at = pl.ds(pl.multiple_of(shard(e, d) * height + first, 16), rows)
                    cols = pl.ds(pl.multiple_of(h * width, 128), width) if dst.shape[1] > width else slice(None)
                    src = block.at[:, pl.ds(start if e else start + skip, width)]
                    started.append(pltpu.make_async_copy(src, dst.at[at, cols], sem))
    for cp in started:
        cp.start()
    return started


def relative(idx_ref):
    return lambda e, d: lax.bitwise_xor(idx_ref[0], jnp.int32(d * 4 + e))


def by_top(idx_ref):
    return lambda e, d: lax.bitwise_xor(idx_ref[0] % 4, jnp.int32(e)) + d * 4


def load_qkv(idx_ref, pieces, w_ref, sem, vec_ref=None):
    def find(e, d):
        if len(pieces) == 8:
            return pieces[e].at[d], pieces[4 + e].at[d]
        return pieces[e].at[d], pieces[5].at[e - 1, d] if e else pieces[4].at[d]

    where = relative(idx_ref)
    rows, half = pieces[0].shape[1], w_ref.shape[1] // 2
    if vec_ref is not None:
        return load_pieces(idx_ref, [(lambda e, d: find(e, d)[:1], where, half, 0, 128, vec_ref, rows, 0)], sem)
    return load_pieces(idx_ref, [(find, where, 0, 0, half, w_ref, rows, 0)], sem)


def load_mlp(idx_ref, pieces, w1_ref, w2_ref, sem):
    where = by_top(idx_ref)

    def find1(e, d):
        return pieces[2 * e].at[d], pieces[2 * e + 1].at[d]

    def find2(e, d):
        at = 6 + 2 * e if e else 0
        return pieces[at].at[d], pieces[at + 1].at[d]

    rows = pieces[0].shape[1]
    half = w1_ref.shape[1] // 2
    w = w2_ref.shape[1] // 2
    one = [(find1, where, 0, 0, half, w1_ref, rows, 0)]
    two = [(find2, where, j * w, half, w, w2_ref, 4 * rows, j * rows) for j in range(4)]
    return load_pieces(idx_ref, one, sem.at[0]), load_pieces(idx_ref, two, sem.at[1])


def wait_mlp(w_ref, sem):
    pltpu.make_async_copy(w_ref, w_ref, sem).wait()


def qkv_kernel(idx_ref, x_ref, *refs):
    pieces = refs[:-11]
    q_ref, k_ref, v_ref, h_ref, vt_ref, bu_ref, qn_ref, kn_ref, w_ref, vec_ref, sem = refs[-11:]
    d = x_ref.shape[1]

    @pl.when(pl.program_id(0) == 0)
    def _():
        rows = pieces[0].shape[1]
        vecs = load_qkv(idx_ref, pieces, w_ref, sem.at[1], vec_ref)
        going = load_qkv(idx_ref, pieces, w_ref, sem.at[0])
        for cp in vecs:
            cp.wait()
        table = vec_ref[...].astype(F32).T[:VECS]
        vt_ref[...] = table
        bu_ref[...] = jnp.concatenate(
            [table[8 + j : 9 + j, s * rows : (s + 1) * rows] for s in range(d // rows) for j in range(4)], axis=1
        )
        for cp in going:
            cp.wait()

    c, r = norm_stats(x_ref[...].astype(F32))
    h = (c * r * vt_ref[0:1, :] + vt_ref[1:2, :]).astype(BF)
    h_ref[...] = h
    q = (dg(h, w_ref[:, :d], NN) + vt_ref[2:3, :]) * (0.125 * LOG2E)
    q_ref[...] = q.astype(BF)
    k = dg(h, w_ref[:, d : 2 * d], NN)
    k_ref[...] = k.astype(BF)
    lane = lax.broadcasted_iota(jnp.int32, (d, 128), 0)
    head = lax.broadcasted_iota(jnp.int32, (d, 128), 1) * 64
    of_head = jnp.where((lane >= head) & (lane < head + 64), 1.0, 0.0).astype(BF)
    for x, n_ref in ((q, qn_ref), (k, kn_ref)):
        n_ref[0] = jnp.max(dg((x * x).astype(BF), of_head, NN), axis=0, keepdims=True)
    v_ref[...] = (dg(h, w_ref[:, 2 * d :], NN) + vt_ref[3:4, :]).astype(BF)


def qkv(idx, x, pieces, tb=512):
    t, d = x.shape
    return pl.pallas_call(
        qkv_kernel,
        grid_spec=pltpu.PrefetchScalarGridSpec(
            num_scalar_prefetch=1,
            grid=(t // tb,),
            in_specs=[rows_of(tb, d)] + [ANY] * len(pieces),
            out_specs=[rows_of(tb, d)] * 4
            + [fixed((VECS, d)), fixed((1, 4 * d))]
            + [pl.BlockSpec((1, 1, 128), lambda i, _: (i, 0, 0))] * 2,
            scratch_shapes=[
                pltpu.VMEM((d, 3 * d), BF),
                pltpu.VMEM((d, 128), BF),
                pltpu.SemaphoreType.DMA((2,)),
            ],
        ),
        out_shape=[SDS((t, d), BF)] * 4
        + [SDS((VECS, d), F32), SDS((1, 4 * d), F32)]
        + [SDS((t // tb, 1, 128), F32)] * 2,
        compiler_params=params(),
        cost_estimate=cost(6 * t * d * d, t * d * 8 + d * d * 6),
        name="qkv",
    )(idx, x, *pieces)


def attend_kernel(tag_ref, qn_ref, kn_ref, q_ref, k_ref, v_ref, *refs, qb, first):
    o_ref, l_ref = refs[-2:]
    r = pl.program_id(0)
    length = q_ref.shape[0]
    low = lax.broadcasted_iota(jnp.int32, (1, 128), 1) < 64

    steps = qn_ref.shape[0] // tag_ref.shape[0]
    safe = True
    for h in range(2):
        head = 2 * (pl.program_id(1) + first) + h
        top = []
        for n_ref in (qn_ref, kn_ref):
            most = n_ref[r * steps, 0, head]
            for i in range(1, steps):
                most = jnp.maximum(most, n_ref[r * steps + i, 0, head])
            top.append(most)
        safe = jnp.logical_and(safe, top[0] * top[1] <= SAFE_SCORE**2)

    def block(qs, qn, ks, kn, plain):
        q = q_ref[pl.ds(qs, qn), :]
        k = k_ref[pl.ds(ks, kn), :]
        v = v_ref[pl.ds(ks, kn), :]
        outs = []
        for h in range(2):
            sel = low if h == 0 else jnp.logical_not(low)
            qm = jnp.where(sel, q, jnp.asarray(0, BF))
            vm = jnp.where(sel, v, jnp.asarray(1, BF))
            s = dg(qm, k, NT)
            if plain:
                outs.append((dg(jnp.exp2(s).astype(BF), vm, NN), 0.0))
            else:
                m = jnp.max(s, axis=1, keepdims=True)
                outs.append((dg(jnp.exp2(s - m).astype(BF), vm, NN), m))
        (a, ma), (b, mb) = outs
        acc = jnp.where(low, a, b)
        total = pltpu.roll(jnp.where(low, b, a), 64, 1)
        o_ref[pl.ds(qs, qn), :] = (acc / total).astype(o_ref.dtype)
        lse = jnp.log2(total) if plain else jnp.where(low, ma, mb) + jnp.log2(total)
        lse = lse.T
        l_ref[0, 0, 0:1, pl.ds(qs, qn)] = lse[0:1]
        l_ref[0, 0, 1:2, pl.ds(qs, qn)] = lse[64:65]

    for plain in (True, False):
        chosen = safe if plain else jnp.logical_not(safe)

        @pl.when(jnp.logical_and(tag_ref[r] == 0, chosen))
        def _(plain=plain):
            n = qb // 2 if plain else qb
            for i in range(length // n):
                block(i * n, n, 0, length, plain)

        @pl.when(jnp.logical_and(tag_ref[r] != 0, chosen))
        def _(plain=plain):
            c = length // 4
            for i in range(4):
                block(i * c, c, i * c, c, plain)


def attend(tag, qn, kn, q, k, v, first, pairs, before=(), qb=512):
    t, d = q.shape
    rows = tag.shape[0]
    length = t // rows
    blk = pl.BlockSpec((length, 128), lambda r, p, _: (r, p + first))
    lse = pl.BlockSpec((1, 1, 2, length), lambda r, p, _: (r, p + first, 0, 0))
    return pl.pallas_call(
        functools.partial(attend_kernel, qb=qb, first=first),
        grid_spec=pltpu.PrefetchScalarGridSpec(
            num_scalar_prefetch=1,
            grid=(rows, pairs),
            in_specs=[pl.BlockSpec(memory_space=pltpu.SMEM)] * 2 + [blk] * 3 + [ANY] * len(before),
            out_specs=[blk, lse],
        ),
        out_shape=[SDS((t, d), BF), SDS((rows, d // 128, 2, length), F32)],
        input_output_aliases={6: 0, 7: 1} if before else {},
        compiler_params=params(2),
        cost_estimate=cost(2048 * t * length * pairs, t * d * 8, t * length * 12),
        name="attend",
    )(tag, qn, kn, q, k, v, *before)


ODDS = (2.3021649, 1.05007451e-1, -2.545477e-4, -1.0560537e-4, 4.093017e-6)


def gelu_both(u):
    z = u * u
    odds = ODDS[3] + z * ODDS[4]
    odds = ODDS[2] + z * odds
    odds = ODDS[1] + z * odds
    odds = ODDS[0] + z * odds
    phi = pltpu.reciprocal(1.0 + jnp.exp2(-u * odds), approx=True)
    density = jnp.exp2(z * (-0.5 * LOG2E) - 0.5 * math.log2(2.0 * math.pi))
    return u * phi, phi + u * density


def mlp_kernel(idx_ref, x_ref, o_ref, vt_ref, bu_ref, ord_ref, *refs, fc, steps):
    pieces = refs[:14]
    x2_ref, gl_ref, gp_ref, sent_ref, y_ref, w1_ref, w2_ref, sem = refs[14:]
    d = x_ref.shape[1]
    ff = w2_ref.shape[0]

    i = pl.program_id(0)
    tb = x_ref.shape[0]

    @pl.when(pl.program_id(0) == 0)
    def _():
        going, _ = load_mlp(idx_ref, pieces, w1_ref, w2_ref, sem)
        for cp in going:
            cp.wait()

    @pl.when(i < steps)
    def _():
        x2 = x_ref[...].astype(F32) + dg(o_ref[...], w1_ref[:, :d], NN) + vt_ref[4:5, :]
        x2_ref[...] = x2
        c, r = norm_stats(x2)
        h = (c * r * vt_ref[5:6, :] + vt_ref[6:7, :]).astype(BF)
        y = x2 + vt_ref[7:8, :]

        @pl.when(pl.program_id(0) == 0)
        def _():
            wait_mlp(w2_ref, sem.at[1])

        for f in range(0, ff, fc):
            u = dg(h, w1_ref[:, d + f : d + f + fc], NN) + bu_ref[:, f : f + fc]
            g, gp = gelu_both(u)
            g = g.astype(BF)
            gl_ref[:, f : f + fc] = g
            gp_ref[:, f : f + fc] = gp.astype(BF)
            y = y + dg(g, w2_ref[f : f + fc, :], NN)
        y_ref[pl.ds(pl.multiple_of(i * tb, tb), tb), :] = y.astype(BF)

    @pl.when(i >= steps)
    def _():
        pb, t = sent_ref.shape[0], y_ref.shape[0]
        order = jnp.broadcast_to(ord_ref[...].astype(F32), (8, pb)).T[:, 0:1]
        hot = jnp.where(order == lax.broadcasted_iota(jnp.int32, (pb, t), 1).astype(F32), 1.0, 0.0)
        sent_ref[...] = dg(hot.astype(BF), y_ref[...], NN).astype(BF)


def mlp(idx, x, o, vt, bu, order, pieces, tb=256, fc=768, pb=512):
    t, d = x.shape
    ff = bu.shape[1]
    steps = t // tb

    def rows(height, width):
        return pl.BlockSpec((height, width), lambda i, _: (jnp.minimum(i, steps - 1), 0))

    def late(i):
        return jnp.maximum(i - steps, 0)

    return pl.pallas_call(
        functools.partial(mlp_kernel, fc=fc, steps=steps),
        grid_spec=pltpu.PrefetchScalarGridSpec(
            num_scalar_prefetch=1,
            grid=(steps + t // pb,),
            in_specs=[rows(tb, d)] * 2
            + [whole(vt.shape), whole(bu.shape), pl.BlockSpec((1, pb), lambda i, _: (0, late(i)))]
            + [ANY] * 14,
            out_specs=[rows(tb, d), rows(tb, ff), rows(tb, ff), pl.BlockSpec((pb, d), lambda i, _: (late(i), 0))],
            scratch_shapes=[
                pltpu.VMEM((t, d), BF),
                pltpu.VMEM((d, d + ff), BF),
                pltpu.VMEM((ff, d), BF),
                pltpu.SemaphoreType.DMA((2,)),
            ],
        ),
        out_shape=[SDS((t, d), F32), SDS((t, ff), BF), SDS((t, ff), BF), pltpu.HBM((t, d), BF)],
        compiler_params=params(),
        cost_estimate=cost(4 * t * d * (d + 2 * ff), t * (10 * d + 4 * ff) + 4 * d * ff, 2 * t * ff),
        name="mlp",
    )(idx, x, o, vt, bu, order, *pieces)


def split_halves(c, r, mine_ref, theirs_ref):
    h = r.shape[1] // 2
    left, right = r[:, :h], r[:, h:]
    mine_ref[...] = jnp.where(c == 0, left, right)
    theirs_ref[...] = jnp.where(c == 0, right, left)


def mlp_back_kernel(idx_ref, ord_ref, ret_ref, gp_ref, x2_ref, o_ref, vt_ref, *refs, fc):
    pieces = refs[:14]
    (dm_ref, du_ref, dx2_ref, do_ref, h2_ref, sums_ref, gbu_ref, mine_ref, theirs_ref) = refs[14:23]
    w1_ref, w2_ref, acc_ref, sem = refs[23:]
    i = pl.program_id(0)
    tb, ff = gp_ref.shape
    t, d = ret_ref.shape

    @pl.when(i == 0)
    def _():
        load_mlp(idx_ref, pieces, w1_ref, w2_ref, sem)
        sums_ref[...] = jnp.zeros_like(sums_ref)
        gbu_ref[...] = jnp.zeros_like(gbu_ref)
        acc_ref[...] = jnp.zeros_like(acc_ref)
        wait_mlp(w2_ref, sem.at[1])
        wait_mlp(w1_ref, sem.at[0])

    at = lax.broadcasted_iota(jnp.int32, (tb, t), 0) + i * tb
    hot = jnp.where(ord_ref[...] == at, 1.0, 0.0).astype(BF)
    dy = dg(hot, ret_ref[...], NN)
    dm = dy.astype(BF)
    dm_ref[...] = dm
    sums_ref[0:1, :] += jnp.sum(dy, axis=0, keepdims=True)
    dh = jnp.zeros((tb, d), F32)
    ahead = dg(dm, w2_ref[:fc, :], NT)
    for f in range(0, ff, fc):
        du = ahead * gp_ref[:, f : f + fc].astype(F32)
        if f + fc < ff:
            ahead = dg(dm, w2_ref[f + fc : f + 2 * fc, :], NT)
        gbu_ref[:, f : f + fc] += jnp.sum(du, axis=0, keepdims=True)
        du = du.astype(BF)
        du_ref[:, f : f + fc] = du
        dh = dh + dg(du, w1_ref[:, d + f : d + f + fc], NT)
    c, r = norm_stats(x2_ref[...])
    xh = c * r
    gain = vt_ref[5:6, :]
    h2_ref[...] = (xh * gain + vt_ref[6:7, :]).astype(BF)
    sums_ref[1:2, :] += jnp.sum(dh * xh, axis=0, keepdims=True)
    sums_ref[2:3, :] += jnp.sum(dh, axis=0, keepdims=True)
    dz = dh * gain
    m1 = jnp.sum(dz, axis=-1, keepdims=True) * (1.0 / d)
    m2 = jnp.sum(dz * xh, axis=-1, keepdims=True) * (1.0 / d)
    dx2 = dy + r * (dz - m1 - xh * m2)
    dx2_ref[...] = dx2
    da = dx2.astype(BF)
    sums_ref[3:4, :] += jnp.sum(da.astype(F32), axis=0, keepdims=True)
    do_ref[...] = dg(da, w1_ref[:, :d], NT).astype(BF)
    acc_ref[...] += dg(o_ref[...], da, TN)

    @pl.when(i == pl.num_programs(0) - 1)
    def _():
        split_halves(idx_ref[1], acc_ref[...].astype(BF), mine_ref, theirs_ref)


def mlp_back(idx, order_row, ret, gp, x2, o, vt, pieces, tb=256, fc=768):
    t, d = x2.shape
    ff = gp.shape[1]
    return pl.pallas_call(
        functools.partial(mlp_back_kernel, fc=fc),
        grid_spec=pltpu.PrefetchScalarGridSpec(
            num_scalar_prefetch=1,
            grid=(t // tb,),
            in_specs=[whole((1, t)), whole((t, d)), rows_of(tb, ff), rows_of(tb, d), rows_of(tb, d), whole(vt.shape)]
            + [ANY] * 14,
            out_specs=[rows_of(tb, d), rows_of(tb, ff)]
            + [rows_of(tb, d)] * 3
            + [fixed((8, d)), fixed((1, ff))]
            + [fixed((d, d // 2))] * 2,
            scratch_shapes=[
                pltpu.VMEM((d, d + ff), BF),
                pltpu.VMEM((ff, d), BF),
                pltpu.VMEM((d, d), F32),
                pltpu.SemaphoreType.DMA((2,)),
            ],
        ),
        out_shape=[
            SDS((t, d), BF),
            SDS((t, ff), BF),
            SDS((t, d), F32),
            SDS((t, d), BF),
            SDS((t, d), BF),
            SDS((8, d), F32),
            SDS((1, ff), F32),
            pltpu.HBM((d, d // 2), BF),
            pltpu.HBM((d, d // 2), BF),
        ],
        compiler_params=params(),
        cost_estimate=cost(2 * t * d * (d + 2 * ff + t) * 1.5, t * (20 * d + 4 * ff)),
        name="mlp_back",
    )(idx, order_row, ret, gp, x2, o, vt, *pieces)


def grad_mlp_kernel(
    idx_ref, g_ref, dm_ref, h2_any, du_ref, u, down_own, down_other, up_own, up_other, bias_ref, h2_ref, sem, *, rows
):
    i = pl.program_id(0)
    steps = pl.num_programs(0) // 2

    @pl.when(i == 0)
    def _():
        pltpu.make_async_copy(h2_any, h2_ref, sem).start()

    @pl.when(i == steps)
    def _():
        pltpu.make_async_copy(h2_any, h2_ref, sem).wait()

    @pl.when(i < steps)
    def _():
        split_halves(idx_ref[1], dg(g_ref[...], dm_ref[...], TN).astype(BF), down_own, down_other)
        d = dm_ref.shape[1]
        wide = u.shape[1] // d
        for j in range(wide):
            parts = [u[:, (s * wide + j) * rows : (s * wide + j + 1) * rows] for s in range(d // rows)]
            bias_ref[j : j + 1, :] = jnp.concatenate(parts, axis=1)

    @pl.when(i >= steps)
    def _():
        split_halves(idx_ref[1], dg(h2_ref[...], du_ref[...], TN).astype(BF), up_own, up_other)


def grad_mlp(idx, g, dm, h2, du, gbu, rows):
    t, ff = g.shape
    d = dm.shape[1]
    steps = ff // d

    def down(i):
        return jnp.minimum(i, steps - 1)

    def up(i):
        return jnp.maximum(i - steps, 0)

    return pl.pallas_call(
        functools.partial(grad_mlp_kernel, rows=rows),
        grid_spec=pltpu.PrefetchScalarGridSpec(
            num_scalar_prefetch=1,
            grid=(2 * steps,),
            in_specs=[
                pl.BlockSpec((t, d), lambda i, _: (0, down(i))),
                whole((t, d)),
                ANY,
                pl.BlockSpec((t, d), lambda i, _: (0, up(i))),
                whole(gbu.shape),
            ],
            out_specs=[pl.BlockSpec((d, d // 2), lambda i, _: (down(i), 0))] * 2
            + [pl.BlockSpec((d, d // 2), lambda i, _: (0, up(i)))] * 2
            + [fixed((steps, d))],
            scratch_shapes=[pltpu.VMEM((t, d), BF), pltpu.SemaphoreType.DMA],
        ),
        out_shape=[pltpu.HBM((ff, d // 2), BF)] * 2
        + [pltpu.HBM((d, ff // 2), BF)] * 2
        + [SDS((steps, d), F32)],
        compiler_params=params(),
        cost_estimate=cost(6 * t * ff * d, 4 * t * (ff + d) + 4 * ff * d),
        name="grad_mlp",
    )(idx, g, dm, h2, du, gbu)


def attend_back_kernel(
    tag_ref, q_ref, k_ref, v_ref, do_ref, o_ref, l_ref, *refs, kb, qb
):
    dq_ref, dk_ref, dv_ref, dl_ref, dqt_ref = refs[-5:]
    r = pl.program_id(0)
    length = q_ref.shape[0]
    low = lax.broadcasted_iota(jnp.int32, (1, 128), 1) < 64
    prod = (do_ref[...].astype(F32) * o_ref[...].astype(F32)).T
    dl_ref[0:1, :] = jnp.sum(prod[0:64], axis=0, keepdims=True)
    dl_ref[1:2, :] = jnp.sum(prod[64:128], axis=0, keepdims=True)

    def block(ks, kn, qs, qn):
        k = k_ref[pl.ds(ks, kn), :]
        v = v_ref[pl.ds(ks, kn), :]
        q = q_ref[pl.ds(qs, qn), :]
        do = do_ref[pl.ds(qs, qn), :]
        dks = []
        dvs = []
        dqs = []
        for h in range(2):
            sel = low if h == 0 else jnp.logical_not(low)
            km = jnp.where(sel, k, jnp.asarray(0, BF))
            vm = jnp.where(sel, v, jnp.asarray(0, BF))
            pt = jnp.exp2(dg(km, q, NT) - l_ref[0, 0, h : h + 1, pl.ds(qs, qn)])
            dst = (pt * (dg(vm, do, NT) - dl_ref[h : h + 1, pl.ds(qs, qn)])).astype(BF)
            dvs.append(dg(pt.astype(BF), do, NN))
            dks.append(dg(dst, q, NN))
            dqs.append(dg(km.T, dst, NN))
        return jnp.where(low, dks[0], dks[1]), jnp.where(low, dvs[0], dvs[1]), dqs[0] + dqs[1]

    def run(kn, qn, plan):
        seen = set()
        for ks, starts in plan:
            dk = dv = None
            for qs in starts:
                a, b, dq = block(ks, kn, qs, qn)
                dk = a if dk is None else dk + a
                dv = b if dv is None else dv + b
                if qs in seen:
                    dqt_ref[:, pl.ds(qs, qn)] += dq
                else:
                    dqt_ref[:, pl.ds(qs, qn)] = dq
                seen.add(qs)
            dk_ref[pl.ds(ks, kn), :] = (dk * LN2).astype(BF)
            dv_ref[pl.ds(ks, kn), :] = dv.astype(BF)
        dq_ref[...] = (dqt_ref[...].T * 0.125).astype(BF)

    @pl.when(tag_ref[r] == 0)
    def _():
        run(kb, qb, [(ks, range(0, length, qb)) for ks in range(0, length, kb)])

    @pl.when(tag_ref[r] != 0)
    def _():
        c = length // 4
        run(c, c, [(ks, [ks]) for ks in range(0, length, c)])


def attend_back(tag, q, k, v, do, o, lse, first, pairs, before=(), kb=512, qb=512):
    t, d = q.shape
    rows = tag.shape[0]
    length = t // rows
    blk = pl.BlockSpec((length, 128), lambda r, p, _: (r, p + first))
    lse_spec = pl.BlockSpec((1, 1, 2, length), lambda r, p, _: (r, p + first, 0, 0))
    return pl.pallas_call(
        functools.partial(attend_back_kernel, kb=kb, qb=qb),
        grid_spec=pltpu.PrefetchScalarGridSpec(
            num_scalar_prefetch=1,
            grid=(rows, pairs),
            in_specs=[blk] * 5 + [lse_spec] + [ANY] * len(before),
            out_specs=[blk] * 3,
            scratch_shapes=[pltpu.VMEM((2, length), F32), pltpu.VMEM((128, length), F32)],
        ),
        out_shape=[SDS((t, d), BF)] * 3,
        input_output_aliases={7: 0, 8: 1, 9: 2} if before else {},
        compiler_params=params(2),
        cost_estimate=cost(5120 * t * length * pairs, t * d * 16, t * length * 12),
        name="attend_back",
    )(tag, q, k, v, do, o, lse, *before)


def grad_qkv_kernel(idx_ref, h_any, dq_any, dk_any, dv_any, *refs, rows):
    h_ref, d_ref, sem = refs[-3:]
    w = d_ref.shape[2]
    half = idx_ref[1] if rows is not None else 1 - idx_ref[1]
    cols = pl.ds(pl.multiple_of(half * w, 128), w)
    going = [pltpu.make_async_copy(h_any, h_ref, sem.at[3])]
    for m, ref in enumerate((dq_any, dk_any, dv_any)):
        going.append(pltpu.make_async_copy(ref.at[:, cols], d_ref.at[m], sem.at[m]))
    for cp in going:
        cp.start()
    going[0].wait()
    for m in range(3):
        at = slice(m * w, (m + 1) * w)
        going[1 + m].wait()
        part = dg(h_ref[...], d_ref[m], TN)
        if rows is None:
            refs[0][:, at] = part.astype(BF)
        else:
            outs, sum_ref = refs[1:-4], refs[-4]
            q = len(outs)
            sum_ref[...] = part + refs[0][:, at].astype(F32)
            for e in range(q):
                for z in range(4):
                    s = z * q + lax.bitwise_xor(idx_ref[0] % q, jnp.int32(e))
                    outs[e][z, :, at] = sum_ref[pl.ds(pl.multiple_of(s * rows, 8), rows), :].astype(BF)


def grad_qkv(idx, h1, dq, dk, dv, recv=None, n=None):
    t, d = h1.shape
    w = d // 2
    own = recv is not None
    outs = [(4, d // n, 3 * w)] * (n // 4) if own else [(d, 3 * w)]
    return pl.pallas_call(
        functools.partial(grad_qkv_kernel, rows=d // n if own else None),
        grid_spec=pltpu.PrefetchScalarGridSpec(
            num_scalar_prefetch=1,
            grid=(1,),
            in_specs=[ANY] * 4 + [whole((d, 3 * w))] * own,
            out_specs=[fixed(o) for o in outs],
            scratch_shapes=[pltpu.VMEM((d, w), F32)] * own
            + [pltpu.VMEM((t, d), BF), pltpu.VMEM((3, t, w), BF), pltpu.SemaphoreType.DMA((4,))],
        ),
        out_shape=[pltpu.HBM(o, BF) for o in outs],
        compiler_params=params(),
        cost_estimate=cost(6 * t * d * w, t * d * 6),
        name="grad_qkv_own" if own else "grad_qkv_other",
    )(idx, h1, dq, dk, dv, *([recv] * own))


def tokens_back_kernel(idx_ref, me_ref, x_ref, vt_ref, dx2_ref, dq_ref, dk_ref, dv_ref, a_ref, u_ref, *refs, q):
    pieces = refs[: -5 - q]
    tg_ref, *outs, s_ref, table_ref, w_ref, sem = refs[-5 - q :]
    d = x_ref.shape[1]

    @pl.when(pl.program_id(0) == 0)
    def _():
        going = load_qkv(idx_ref, pieces, w_ref, sem)
        s_ref[...] = jnp.zeros_like(s_ref)
        for cp in going:
            cp.wait()

    dh = dg(dq_ref[...], w_ref[:, :d], NT)
    dh = dh + dg(dk_ref[...], w_ref[:, d : 2 * d], NT)
    dh = dh + dg(dv_ref[...], w_ref[:, 2 * d :], NT)
    ones = jnp.ones((8, x_ref.shape[0]), BF)
    s_ref[2:3, :] += dg(ones, dq_ref[...], NN)[0:1]
    s_ref[3:4, :] += dg(ones, dv_ref[...], NN)[0:1]
    c, r = norm_stats(x_ref[...].astype(F32))
    xh = c * r
    s_ref[0:1, :] += jnp.sum(dh * xh, axis=0, keepdims=True)
    s_ref[1:2, :] += jnp.sum(dh, axis=0, keepdims=True)
    dz = dh * vt_ref[0:1, :]
    m1 = jnp.sum(dz, axis=-1, keepdims=True) * (1.0 / d)
    m2 = jnp.sum(dz * xh, axis=-1, keepdims=True) * (1.0 / d)
    tg_ref[...] = dx2_ref[...] + r * (dz - m1 - xh * m2)

    @pl.when(pl.program_id(0) == pl.num_programs(0) - 1)
    def _():
        rows = outs[0].shape[1]
        wide = u_ref.shape[0]
        lines = [s_ref[0:4, :], a_ref[3:4, :], a_ref[1:3, :], a_ref[0:1, :], u_ref[...]]
        table_ref[...] = jnp.concatenate(lines + [jnp.zeros((120 - wide, d), F32)], axis=0).T
        for e in range(q):
            for z in range(4):
                s = z * q + lax.bitwise_xor(me_ref[0] % q, jnp.int32(e))
                outs[e][z] = table_ref[pl.ds(pl.multiple_of(s * rows, 8), rows), :].astype(BF)


def tokens_back(idx, me, dq, dk, dv, x, vt, dx2, s_mlp, bias, pieces, n, tb=512):
    t, d = x.shape
    q = n // 4
    return pl.pallas_call(
        functools.partial(tokens_back_kernel, q=q),
        grid_spec=pltpu.PrefetchScalarGridSpec(
            num_scalar_prefetch=2,
            grid=(t // tb,),
            in_specs=[rows_of(tb, d), whole(vt.shape)]
            + [rows_of(tb, d)] * 4
            + [whole(s_mlp.shape), whole(bias.shape)]
            + [ANY] * len(pieces),
            out_specs=[rows_of(tb, d)] + [fixed((4, d // n, 128))] * q,
            scratch_shapes=[
                pltpu.VMEM((8, d), F32),
                pltpu.VMEM((d, 128), F32),
                pltpu.VMEM((d, 3 * d), BF),
                pltpu.SemaphoreType.DMA,
            ],
        ),
        out_shape=[SDS((t, d), F32)] + [pltpu.HBM((4, d // n, 128), BF)] * q,
        compiler_params=params(),
        cost_estimate=cost(9 * t * d * d, t * d * 16 + d * d * 6),
        name="tokens_back",
    )(idx, me, x, vt, dx2, dq, dk, dv, s_mlp, bias, *pieces)


def hop(x, groups):
    return lax.all_to_all(x, "fsdp", split_axis=0, concat_axis=0, tiled=True, axis_index_groups=groups)


def sum_cores_kernel(idx_ref, *refs, q):
    outs = refs[-q:]
    rows = outs[0].shape[1]
    for e in range(q):
        at = lax.bitwise_xor(idx_ref[0] % q, jnp.int32(e))
        start = 0
        for a_ref, b_ref in zip(refs[:-q:2], refs[1:-q:2], strict=True):
            total = a_ref[at] + b_ref[at]
            w = total.shape[1]
            for j in range(total.shape[0] // rows):
                outs[e][0, :, start : start + w] = total[j * rows : (j + 1) * rows]
                start += w


def sum_cores(idx, pairs, rows, n):
    q = n // 4
    ops, specs, width = [], [], 0
    for pair in pairs:
        shape = (pair[0].shape[0] // n, pair[0].shape[1])
        width += shape[0] // rows * shape[1]
        ops += [x.reshape((n,) + shape) for x in pair]
        specs += [pl.BlockSpec((q,) + shape, lambda z, _: (z, 0, 0))] * 2
    return pl.pallas_call(
        functools.partial(sum_cores_kernel, q=q),
        grid_spec=pltpu.PrefetchScalarGridSpec(
            num_scalar_prefetch=1,
            grid=(4,),
            in_specs=specs,
            out_specs=[pl.BlockSpec((1, rows, width), lambda z, _: (z, 0, 0))] * q,
        ),
        out_shape=[pltpu.HBM((4, rows, width), BF)] * q,
        compiler_params=params(),
        cost_estimate=cost(n * rows * width, n * rows * width * 6),
        name="sum_cores",
    )(idx, *ops)


def spread(parts, n):
    return [parts[0]] + [xor_pp(parts[e], e, n) for e in range(1, n // 4)]


def sum_parts_kernel(*refs):
    total = refs[0][...].astype(F32)
    for x in refs[1:-1]:
        total = total + x[...].astype(F32)
    refs[-1][...] = total.astype(BF)


def sum_parts(parts):
    shape = (1,) + parts[0].shape[1:]
    spec = pl.BlockSpec(shape, lambda i: (i, 0, 0))
    return pl.pallas_call(
        sum_parts_kernel,
        grid=(4,),
        in_specs=[spec] * len(parts),
        out_specs=spec,
        out_shape=pltpu.HBM(parts[0].shape, BF),
        compiler_params=params(),
        cost_estimate=cost(4 * len(parts) * math.prod(shape), 8 * len(parts) * math.prod(shape)),
        name="sum_parts",
    )(*parts)


def sum_qkv_kernel(idx_ref, *refs, q):
    outs = refs[2 * q + 1 :]
    for d in range(4):
        at = lax.bitwise_xor(idx_ref[0] // q, jnp.int32(d))
        start = 0
        for parts in (refs[:q], refs[q : 2 * q]):
            total = parts[0][at].astype(F32)
            for x in parts[1:]:
                total = total + x[at].astype(F32)
            w = total.shape[1]
            outs[d][:, start : start + w] = total.astype(BF)
            start += w
    last = refs[2 * q]
    outs[4][...] = (
        last[0].astype(F32) + last[1].astype(F32) + last[2].astype(F32) + last[3].astype(F32)
    ).astype(BF)


def sum_qkv(idx, far, vecs, last, n):
    _, rows, w = far[0].shape
    width = w + vecs[0].shape[2]
    ops = list(far) + list(vecs) + [last]
    *near, total = pl.pallas_call(
        functools.partial(sum_qkv_kernel, q=n // 4),
        grid_spec=pltpu.PrefetchScalarGridSpec(
            num_scalar_prefetch=1,
            grid=(1,),
            in_specs=[whole(x.shape) for x in ops],
            out_specs=[fixed((rows, width))] * 4 + [fixed(last.shape[1:])],
        ),
        out_shape=[pltpu.HBM((rows, width), BF)] * 4 + [pltpu.HBM(last.shape[1:], BF)],
        compiler_params=params(),
        cost_estimate=cost(n * rows * width, n * rows * width * 3),
        name="sum_qkv",
    )(idx, *ops)
    return near, total


def reduce_last(near, n, m):
    total = near[0].astype(F32)
    for x in near[1:]:
        total = total + x.astype(F32)
    return over_pairs(total, m)


def over_pairs(total, m):
    b = 2
    while b < m:
        total = total + lax.ppermute(total.astype(BF), "dp", [(i, i ^ b) for i in range(m)]).astype(F32)
        b *= 2
    return total


def local(
    tokens,
    sensor_tag,
    owner_order,
    ln1_gain,
    ln1_bias,
    w_qkv,
    b_query,
    b_value,
    w_out,
    b_out,
    ln2_gain,
    ln2_bias,
    w_up,
    b_up,
    w_down,
    b_down,
    out_grad,
    *,
    n,
    m,
):
    t, d = tokens.shape
    ff = w_up.shape[1]
    rows = d // n
    wide = ff // d
    f = lax.axis_index("fsdp")
    c = lax.axis_index("dp") % 2
    idx = jnp.stack([f, c]).astype(jnp.int32)
    use = idx if fits(rows, n) else jnp.zeros_like(idx)

    def core_half(x):
        h = x.shape[1] // 2
        return jnp.where(c == 0, x[:, :h], x[:, h:])

    vec = jnp.stack([ln1_gain, ln1_bias, b_query, b_value, b_out, ln2_gain, ln2_bias, b_down], axis=1)
    vec = jnp.concatenate([vec, b_up.reshape(wide, rows).T], axis=1)
    vec = jnp.pad(vec, ((0, 0), (0, 128 - vec.shape[1])))
    shard_a = jnp.concatenate([core_half(w_qkv), vec], axis=1)
    shard_b = jnp.concatenate(
        [core_half(jnp.concatenate([w_out, w_up], axis=1))]
        + [core_half(w_down[j * rows : (j + 1) * rows]) for j in range(wide)],
        axis=1,
    )
    q = n // 4
    everyone = jnp.arange(n)

    near_a = gather_near(shard_a, n)
    near_b = hop(jnp.broadcast_to(after(shard_b, near_a)[None], (4,) + shard_b.shape), tops(n))
    own_a = gather_far(near_a, n)
    cast = after(out_grad, near_a).astype(BF)
    own_a[1:] = after(own_a[1:], cast)
    swap_a = [core_swap(near_a, m), core_swap(jnp.stack(own_a[1:]), m)]
    if fits(rows, n):
        pieces_a = own_a + swap_a
    else:
        pieces_a = settle(own_a + swap_a[:1] + [swap_a[1][e] for e in range(q - 1)], f ^ everyone, c, n)
    near_b = after(near_b, own_a[1:])
    qh, kh, vh, h1, vt, bu, qn, kn = qkv(use, after(tokens, near_b), pieces_a)
    pairs = d // 128
    early = pairs * 2 // 3
    cut = (d + ff) // 2
    if fits(rows, n):
        x, y = near_b[..., :cut], near_b[..., cut:]
        x1, y2 = after((xor_pp(x, 1, n), xor_pp(y, 2, n)), vt)
        x2, y1 = xor_pp(x, 2, n), xor_pp(y, 1, n)
        x3, y3 = xor_pp(x1, 2, n), xor_pp(y2, 1, n)
        part = attend(sensor_tag, qn, kn, after(qh, x1, y2), kh, vh, 0, early)
        side = [near_b] + after([x1, x2, x3, y1, y2, y3], part[0])
        pieces_b = []
        for x in side:
            pieces_b += [x, core_swap(x, m)]
        gate = side[1:]
    else:
        far_b = gather_far(near_b, n)
        side = settle(
            far_b + [core_swap(x, m) for x in far_b], everyone // q * q + (everyone ^ f) % q, c, n, wide
        )
        part = attend(sensor_tag, qn, kn, qh, kh, vh, 0, early)
        pieces_b = [side[0], side[4]]
        for e in range(1, 4):
            pieces_b += [side[e][..., :cut], side[4 + e][..., :cut]]
        for e in range(1, 4):
            pieces_b += [side[e][..., cut:], side[4 + e][..., cut:]]
        gate = far_b
    returned = lax.all_to_all(after(cast, gate), "fsdp", split_axis=0, concat_axis=0, tiled=True)
    mixed, lse = attend(sensor_tag, qn, kn, qh, kh, vh, early, pairs - early, part)

    x2, active, slope, sent = mlp(use, tokens, mixed, vt, bu, owner_order, pieces_b)
    encoded = lax.all_to_all(sent, "fsdp", split_axis=0, concat_axis=0, tiled=True)

    returned = after(returned, sent)
    dm, du, dx2, do, h2, s_mlp, gbu, out_own, out_other = mlp_back(
        use, owner_order, returned, slope, x2, mixed, vt, pieces_b
    )
    out_recv = core_swap(out_other, m)
    down_own, down_other, up_own, up_other, bias = grad_mlp(idx, active, dm, h2, du, gbu, rows)
    down_recv = core_swap(down_other, m)
    up_recv = core_swap(up_other, m)
    part = attend_back(sensor_tag, qh, kh, vh, after(do, up_own, encoded), mixed, lse, 0, 1)
    out_recv, down_recv, up_recv = after((out_recv, down_recv, up_recv), part[0])
    pairs_b = [(up_own, up_recv), (out_own, out_recv), (down_own, down_recv)]
    far_b = sum_cores(idx, pairs_b, rows, n)
    do = after(do, far_b[0])
    far_b = spread(far_b, n)
    dj = attend_back(sensor_tag, qh, kh, vh, do, mixed, lse, 1, pairs - 1, part)
    (qkv_other,) = grad_qkv(idx, h1, *dj)
    qkv_recv = core_swap(qkv_other, m)
    far_b = after(far_b, dj[0])
    near_b = sum_parts([after(far_b[0], qkv_other)] + far_b[1:])
    total_b = hop(near_b, tops(n))
    far_a = grad_qkv(idx, after(h1, near_b), *dj, qkv_recv, n)
    dj = after(dj, far_a[0])
    far_a = spread(far_a, n)
    tokens_grad, *far_v = tokens_back(use, idx, *dj, tokens, vt, dx2, s_mlp, bias, pieces_a, n)
    far_a, total_b = after((far_a, total_b), tokens_grad)
    far_v = spread([far_v[0]] + after(far_v[1:], far_a), n)

    near_a, total_b = sum_qkv(idx, far_a, far_v, total_b, n)
    if m > 2:
        total_b = over_pairs(total_b.astype(F32), m).astype(BF)
    other_b = core_swap(total_b, m)
    encoded = after(encoded, near_a[0]).astype(F32)
    near_a = [near_a[0]] + [xor_pp(near_a[i], i * q, n) for i in range(1, 4)]
    def both(mine, other):
        first = c == 0
        return jnp.where(first, mine, other).astype(F32), jnp.where(first, other, mine).astype(F32)

    def join(pair, start, width, parts, axis=1):
        out = []
        for p in range(parts):
            at = slice(start + p * width, start + (p + 1) * width)
            out.append(jnp.concatenate([pair[0][:, at], pair[1][:, at]], axis=1))
        return jnp.concatenate(out, axis=axis)

    h = d // 2
    g_mlp = both(total_b, other_b)
    grad_up_out = join(g_mlp, 0, h, wide)
    grad_out_out = join(g_mlp, ff // 2, h, 1)
    grad_down_out = join(g_mlp, (d + ff) // 2, h, wide, 0)
    near_a = after(near_a, grad_up_out, grad_out_out, grad_down_out, encoded)
    total_a = reduce_last(near_a, n, m)
    other_a = core_swap(total_a.astype(BF), m)
    cut = 3 * d // 2
    vecs = (total_a[:, cut:] + other_a[:, cut:].astype(F32)).T
    total_a, other_a = total_a[:, :cut].astype(BF), other_a[:, :cut]

    grad_qkv_out = join(both(total_a, other_a), 0, h, 3)
    return (
        encoded,
        tokens_grad,
        vecs[0],
        vecs[1],
        grad_qkv_out,
        vecs[2],
        vecs[3],
        grad_out_out,
        vecs[4],
        vecs[5],
        vecs[6],
        grad_up_out,
        vecs[8 : 8 + wide].reshape(ff // n),
        grad_down_out,
        vecs[7],
    )


def solution(mesh):
    n = mesh.shape["fsdp"]
    m = mesh.shape["dp"]
    both = P(("dp", "fsdp"), None)
    vec = P("fsdp")
    mat = P("fsdp", None)
    in_specs = (both, P(("dp", "fsdp")), both, vec, vec, mat, vec, vec, mat, vec, vec, vec, mat, vec, mat, vec, both)
    out_specs = (both, both, vec, vec, mat, vec, vec, mat, vec, vec, vec, mat, vec, mat, vec)
    return jax.shard_map(
        functools.partial(local, n=n, m=m), mesh=mesh, in_specs=in_specs, out_specs=out_specs, check_vma=False
    )
```
